32 devices in a mesh: seq: 4 (over z), mp: 2 (over core), dp: 4 (over y, x).
Axes of the slice: x: 2, y: 2, z: 4, core: 2. Of those that a mesh axis runs over, the one named last changes fastest.
Arguments:
- tokens: bfloat16 [8, 1024, 2048], P('dp', 'seq'), may hold values from -6 to 6
- cotangent: bfloat16 [8, 1024, 2048], P('dp', 'seq'), may hold values from -6 to 6
- attention_norm_gain: bfloat16 [2048], replicated, may hold values from 0.5 to 1.5
- feedforward_norm_gain: bfloat16 [2048], replicated, may hold values from 0.5 to 1.5
- query_weight: bfloat16 [2048, 2048], P('seq', 'mp'), may hold values from -0.125 to 0.125
- key_weight: bfloat16 [2048, 512], P('seq', 'mp'), may hold values from -0.125 to 0.125
- value_weight: bfloat16 [2048, 512], P('seq', 'mp'), may hold values from -0.125 to 0.125
- output_weight: bfloat16 [2048, 2048], P('mp', 'seq'), may hold values from -0.5 to 0.5
- gate_weight: bfloat16 [2048, 8192], P('seq', 'mp'), may hold values from -0.125 to 0.125
- up_weight: bfloat16 [2048, 8192], P('seq', 'mp'), may hold values from -0.125 to 0.125
- down_weight: bfloat16 [8192, 2048], P('mp', 'seq'), may hold values from -0.0625 to 0.0625
- query_adapter_down: bfloat16 [2048, 8], replicated, may hold values from -0.125 to 0.125
- query_adapter_up: bfloat16 [8, 2048], P(None, 'mp'), may hold values from -2 to 2
- key_adapter_down: bfloat16 [2048, 8], replicated, may hold values from -0.125 to 0.125
- key_adapter_up: bfloat16 [8, 512], P(None, 'mp'), may hold values from -2 to 2
- value_adapter_down: bfloat16 [2048, 8], replicated, may hold values from -0.125 to 0.125
- value_adapter_up: bfloat16 [8, 512], P(None, 'mp'), may hold values from -2 to 2
- output_adapter_down: bfloat16 [2048, 8], P('mp'), may hold values from -0.5 to 0.5
- output_adapter_up: bfloat16 [8, 2048], replicated, may hold values from -2 to 2
- query_feature_matrix: bfloat16 [32, 64, 64], P('mp'), may hold values from -0.75 to 0.75
- key_feature_matrix: bfloat16 [8, 64, 64], P('mp'), may hold values from -0.75 to 0.75
Outputs:
- output: bfloat16 [8, 1024, 2048], P('dp', 'seq')
- tokens_grad: float32 [8, 1024, 2048], P('dp', 'seq')
- attn_gain_grad: float32 [2048], replicated
- mlp_gain_grad: float32 [2048], replicated
- qdown_grad: float32 [2048, 8], replicated
- qup_grad: float32 [8, 2048], P(None, 'mp')
- kdown_grad: float32 [2048, 8], replicated
- kup_grad: float32 [8, 512], P(None, 'mp')
- vdown_grad: float32 [2048, 8], replicated
- vup_grad: float32 [8, 512], P(None, 'mp')
- odown_grad: float32 [2048, 8], P('mp')
- oup_grad: float32 [8, 2048], replicated
- query_maps_grad: float32 [32, 64, 64], P('mp')
- key_maps_grad: float32 [8, 64, 64], P('mp')
The draws below stay inside these ranges and needn't reach their ends.
All inputs are finite; a program needn't handle non-finite values.
Results may differ from the reference program's by a relative error of at most 0.018.
Values may be sent and summed in bfloat16 or wider, within the bound.
A program may use at most 320 MiB of HBM per device.

```python
import math
import jax
import jax.numpy as jnp
from jax import lax

MODEL_WIDTH = 2048
QUERY_HEADS = 32
KEY_VALUE_HEADS = 8
HEAD_WIDTH = 64
FF = 8192
ADAPTER_RANK = 8
SOFTMAX_SPAN = 64
TOKENS_PER_BLOCK = 256
LENGTH = 1024
SEQS = 8


def level_of(rng, shape, split, least, high):
    def one(dim, blocks):
        heights = jax.random.uniform(jax.random.fold_in(jax.random.fold_in(rng, 6), dim), (blocks,), jnp.float32, least / len(split), high / len(split))
        return jnp.repeat(jnp.exp(heights), shape[dim] // blocks).reshape((-1,) + (1,) * (len(shape) - dim - 1))

    factor_of = one(*split[0])
    for cut in split[1:]:
        factor_of = factor_of * one(*cut)
    return factor_of


def bell_draw(key, shape, width, limit, split=(), kind=jnp.bfloat16):
    level = level_of(key, shape, split, -0.22, 0.18) if split else 1.0
    values = jax.random.normal(key, shape, jnp.float32) * width * level
    return jnp.minimum(jnp.maximum(values, -limit), limit).astype(kind)


def setup_inputs(seed: int = 0) -> dict:
    key_list = jax.random.split(jax.random.key(seed), 22)
    tokens = bell_draw(key_list[0], (SEQS, LENGTH, MODEL_WIDTH), 1.0, 6.0, ((0, 4), (1, 4)))
    cotangent = bell_draw(key_list[1], (SEQS, LENGTH, MODEL_WIDTH), 1.0, 6.0, ((0, 4), (1, 4)))
    attention_norm_gain = jnp.clip(1.0 + 0.1 * jax.random.normal(key_list[2], (MODEL_WIDTH,), jnp.float32), 0.5, 1.5).astype(jnp.bfloat16)
    feedforward_norm_gain = jnp.clip(1.0 + 0.1 * jax.random.normal(key_list[3], (MODEL_WIDTH,), jnp.float32), 0.5, 1.5).astype(jnp.bfloat16)
    query_weight = bell_draw(key_list[4], (MODEL_WIDTH, QUERY_HEADS * HEAD_WIDTH), MODEL_WIDTH ** -0.5, 0.125, ((0, 4), (1, 2)))
    key_weight = bell_draw(key_list[5], (MODEL_WIDTH, KEY_VALUE_HEADS * HEAD_WIDTH), MODEL_WIDTH ** -0.5, 0.125, ((0, 4), (1, 2)))
    value_weight = bell_draw(key_list[6], (MODEL_WIDTH, KEY_VALUE_HEADS * HEAD_WIDTH), MODEL_WIDTH ** -0.5, 0.125, ((0, 4), (1, 2)))
    output_weight = bell_draw(key_list[7], (QUERY_HEADS * HEAD_WIDTH, MODEL_WIDTH), (MODEL_WIDTH // 16) ** -0.5, 0.5, ((0, 2), (1, 4)))
    gate_weight = bell_draw(key_list[8], (MODEL_WIDTH, FF), MODEL_WIDTH ** -0.5, 0.125, ((0, 4), (1, 2)))
    up_weight = bell_draw(key_list[9], (MODEL_WIDTH, FF), MODEL_WIDTH ** -0.5, 0.125, ((0, 4), (1, 2)))
    down_weight = bell_draw(key_list[10], (FF, MODEL_WIDTH), FF ** -0.5, 0.0625, ((0, 2), (1, 4)))
    query_adapter_down = bell_draw(key_list[11], (MODEL_WIDTH, ADAPTER_RANK), MODEL_WIDTH ** -0.5, 0.125)
    query_adapter_up = bell_draw(key_list[12], (ADAPTER_RANK, QUERY_HEADS * HEAD_WIDTH), ADAPTER_RANK ** -0.5, 2.0, ((1, 2),))
    key_adapter_down = bell_draw(key_list[13], (MODEL_WIDTH, ADAPTER_RANK), MODEL_WIDTH ** -0.5, 0.125)
    key_adapter_up = bell_draw(key_list[14], (ADAPTER_RANK, KEY_VALUE_HEADS * HEAD_WIDTH), ADAPTER_RANK ** -0.5, 2.0, ((1, 2),))
    value_adapter_down = bell_draw(key_list[15], (MODEL_WIDTH, ADAPTER_RANK), MODEL_WIDTH ** -0.5, 0.125)
    value_adapter_up = bell_draw(key_list[16], (ADAPTER_RANK, KEY_VALUE_HEADS * HEAD_WIDTH), ADAPTER_RANK ** -0.5, 2.0, ((1, 2),))
    output_adapter_down = bell_draw(key_list[17], (QUERY_HEADS * HEAD_WIDTH, ADAPTER_RANK), (MODEL_WIDTH // 16) ** -0.5, 0.5, ((0, 2),))
    output_adapter_up = bell_draw(key_list[18], (ADAPTER_RANK, MODEL_WIDTH), ADAPTER_RANK ** -0.5, 2.0)
    query_feature_matrix = bell_draw(key_list[19], (QUERY_HEADS, HEAD_WIDTH, HEAD_WIDTH), HEAD_WIDTH ** -0.5, 0.75, ((0, 2),))
    key_feature_matrix = bell_draw(key_list[20], (KEY_VALUE_HEADS, HEAD_WIDTH, HEAD_WIDTH), HEAD_WIDTH ** -0.5, 0.75, ((0, 2),))
    return {"tokens": tokens, "cotangent": cotangent, "attention_norm_gain": attention_norm_gain, "feedforward_norm_gain": feedforward_norm_gain, "query_weight": query_weight, "key_weight": key_weight, "value_weight": value_weight, "output_weight": output_weight, "gate_weight": gate_weight, "up_weight": up_weight, "down_weight": down_weight, "query_adapter_down": query_adapter_down, "query_adapter_up": query_adapter_up, "key_adapter_down": key_adapter_down, "key_adapter_up": key_adapter_up, "value_adapter_down": value_adapter_down, "value_adapter_up": value_adapter_up, "output_adapter_down": output_adapter_down, "output_adapter_up": output_adapter_up, "query_feature_matrix": query_feature_matrix, "key_feature_matrix": key_feature_matrix}


highest = lax.Precision.HIGHEST
epsilon = 1e-05

@jax.custom_vjp
def low(v):
    return lax.optimization_barrier(v.astype(jnp.bfloat16)).astype(jnp.float32)

@jax.custom_vjp
def low_back(v):
    return v

def low_keep(v):
    return (low(v), None)

def low_pass(kept, grad):
    return (grad,)

def back_keep(v):
    return (v, None)

def back_low(kept, grad):
    return (low(grad),)
low.defvjp(low_keep, low_pass)
low_back.defvjp(back_keep, back_low)

def key_features(key_block, feature_maps):
    logits = jnp.einsum('ekd,kdf->ekf', key_block, feature_maps, precision=highest)
    return jnp.concatenate([jax.nn.softmax(logits, -1), jax.nn.softmax(-logits, -1)], -1)

def query_features(query_rows, feature_maps):
    logits = jnp.einsum('tkgd,kgdf->tkgf', query_rows, feature_maps, precision=highest)
    return jnp.concatenate([jax.nn.softmax(logits, -1), jax.nn.softmax(-logits, -1)], -1)

def state_piece(features, values, valid_mask, rows_here):
    kept_feats = jnp.where(valid_mask[:rows_here, None, None], features[:rows_here], 0.0)
    state_sum = jnp.einsum('ekf,ekd->kfd', kept_feats, values[:rows_here], precision=highest)
    return (state_sum, lax.optimization_barrier(jnp.sum(kept_feats, 0)))

def attend(query_rows, key_block, values, features, state_sum, totals, feature_maps, valid_mask):
    rows_here = query_rows.shape[0]
    extent = key_block.shape[0]
    reach_back = extent - rows_here
    query_feats = query_features(query_rows, feature_maps)
    scores = jnp.einsum('tkgd,ekd->kgte', query_rows, key_block, precision=highest) / math.sqrt(query_rows.shape[-1])
    rowpos = jnp.arange(rows_here, dtype=jnp.int32)[:, None]
    colpos = jnp.arange(extent, dtype=jnp.int32)[None, :]
    inside = (colpos > rowpos) & (colpos <= rowpos + reach_back) & valid_mask[None, :]
    older_mask = (colpos <= rowpos) & valid_mask[None, :]
    window_part = jnp.where(inside, jnp.exp(jnp.where(inside, scores, 0.0)), 0.0)
    linear_part = jnp.where(older_mask, jnp.einsum('tkgf,ekf->kgte', query_feats, features, precision=highest), 0.0)
    weights = window_part + linear_part
    numerator = jnp.einsum('kgte,ekd->tkgd', weights, values, precision=highest)
    numerator = numerator + jnp.einsum('tkgf,kfd->tkgd', query_feats, state_sum, precision=highest)
    denominator = jnp.transpose(lax.optimization_barrier(jnp.sum(weights, -1)), (2, 0, 1))
    denominator = denominator + jnp.einsum('tkgf,kf->tkg', query_feats, totals, precision=highest)
    return numerator / denominator[..., None]

def matmul_exact(left, right):
    return jnp.dot(left, right, precision=highest)

def norm_rows(values_in, gain):
    return values_in * lax.rsqrt(lax.optimization_barrier(jnp.mean(values_in * values_in, -1, keepdims=True)) + epsilon) * gain

def sequence_forward(inputs, learned_params, frozen):
    attention_norm_gain, feedforward_norm_gain, query_down_factor, query_up_factor, key_down_factor, key_up_factor, value_down_factor, value_up_factor, odown, oup, query_feature_set, kmaps = learned_params
    query_weight, key_weight, value_weight, output_weight, gate_weight, up_weight, down_weight = frozen
    query_group_count = QUERY_HEADS // KEY_VALUE_HEADS
    block_list = LENGTH // TOKENS_PER_BLOCK
    normed = low(norm_rows(inputs, attention_norm_gain))

    def apply_projection(weight_matrix, first, second):
        return low(low_back(matmul_exact(normed, weight_matrix) + matmul_exact(matmul_exact(normed, first), second)))
    query_rows = apply_projection(query_weight, query_down_factor, query_up_factor).reshape(block_list, TOKENS_PER_BLOCK, KEY_VALUE_HEADS, query_group_count, HEAD_WIDTH)
    every_key_row = apply_projection(key_weight, key_down_factor, key_up_factor).reshape(block_list, TOKENS_PER_BLOCK, KEY_VALUE_HEADS, HEAD_WIDTH)
    every_value_row = apply_projection(value_weight, value_down_factor, value_up_factor).reshape(block_list, TOKENS_PER_BLOCK, KEY_VALUE_HEADS, HEAD_WIDTH)
    query_feature_matrix4 = query_feature_set.reshape(KEY_VALUE_HEADS, query_group_count, HEAD_WIDTH, HEAD_WIDTH)

    def block_step(carry, block_in):
        state_sum, totals, key_edge, value_edge = carry
        block_q, block_k, block_v, position = block_in
        key_ext = jnp.concatenate([key_edge, block_k], 0)
        value_ext = jnp.concatenate([value_edge, block_v], 0)
        valid_mask = position * TOKENS_PER_BLOCK - SOFTMAX_SPAN + jnp.arange(TOKENS_PER_BLOCK + SOFTMAX_SPAN, dtype=jnp.int32) >= 0
        features = key_features(key_ext, kmaps)
        result = attend(block_q, key_ext, value_ext, features, state_sum, totals, query_feature_matrix4, valid_mask)
        piece_state, piece_totals = state_piece(features, value_ext, valid_mask, TOKENS_PER_BLOCK)
        carry_next = (state_sum + piece_state, totals + piece_totals, block_k[TOKENS_PER_BLOCK - SOFTMAX_SPAN:], block_v[TOKENS_PER_BLOCK - SOFTMAX_SPAN:])
        return (carry_next, result)
    initial_state_pair = (jnp.zeros((KEY_VALUE_HEADS, 2 * HEAD_WIDTH, HEAD_WIDTH), jnp.float32), jnp.zeros((KEY_VALUE_HEADS, 2 * HEAD_WIDTH), jnp.float32), jnp.zeros((SOFTMAX_SPAN, KEY_VALUE_HEADS, HEAD_WIDTH), jnp.float32), jnp.zeros((SOFTMAX_SPAN, KEY_VALUE_HEADS, HEAD_WIDTH), jnp.float32))
    final_carry, attn = lax.scan(jax.checkpoint(block_step), initial_state_pair, (query_rows, every_key_row, every_value_row, jnp.arange(block_list, dtype=jnp.int32)))
    attn = low(low_back(attn.reshape(LENGTH, QUERY_HEADS * HEAD_WIDTH)))
    branch = low_back(matmul_exact(attn, output_weight) + matmul_exact(matmul_exact(attn, odown), oup))
    resid = inputs + branch
    normed_mlp = low(norm_rows(resid, feedforward_norm_gain))
    gate = low_back(matmul_exact(normed_mlp, gate_weight))
    up_vals = low_back(matmul_exact(normed_mlp, up_weight))
    hidden = low(jax.nn.silu(gate) * up_vals)
    return resid + low_back(matmul_exact(hidden, down_weight))

def reference(tokens, cotangent, attention_norm_gain, feedforward_norm_gain, query_weight, key_weight, value_weight, output_weight, gate_weight, up_weight, down_weight, query_adapter_down, query_adapter_up, key_adapter_down, key_adapter_up, value_adapter_down, value_adapter_up, output_adapter_down, output_adapter_up, query_feature_matrix, key_feature_matrix):
    frozen = tuple((weight_matrix.astype(jnp.float32) for weight_matrix in (query_weight, key_weight, value_weight, output_weight, gate_weight, up_weight, down_weight)))
    learned_params = tuple((weight_matrix.astype(jnp.float32) for weight_matrix in (attention_norm_gain, feedforward_norm_gain, query_adapter_down, query_adapter_up, key_adapter_down, key_adapter_up, value_adapter_down, value_adapter_up, output_adapter_down, output_adapter_up, query_feature_matrix, key_feature_matrix)))
    inputs = tokens.astype(jnp.float32)

    def whole(all_inputs, params):

        def per_sequence(single_seq):
            return sequence_forward(single_seq, params, frozen)
        return lax.map(jax.checkpoint(per_sequence), all_inputs)
    result, pullback = jax.vjp(whole, inputs, learned_params)
    grad_inputs, grad_trained = pullback(cotangent.astype(jnp.float32))
    return (result.astype(jnp.bfloat16), grad_inputs, grad_trained[0], grad_trained[1], grad_trained[2], grad_trained[3], grad_trained[4], grad_trained[5], grad_trained[6], grad_trained[7], grad_trained[8], grad_trained[9], grad_trained[10], grad_trained[11])
```

```python
import math
import functools
import jax
import jax.numpy as jnp
from jax import lax
from jax.experimental import pallas as pl
from jax.experimental.pallas import tpu as pltpu
from jax.sharding import PartitionSpec as P

SOFTMAX_SPAN = 64
epsilon = 1e-05

MESH = pl.DeviceIdType.MESH
ANY = pl.ANY


class Spot:
    def __init__(self):
        self.s, self.m, self.d = (lax.axis_index(a) for a in ("seq", "mp", "dp"))
        self.x = self.d + 1 - 2 * (self.d % 2)
        self.y = (self.d + 2) % 4
        self.diag = (self.x + 2) % 4

    def to(self, kind):
        s, m, d = self.s, self.m, self.d
        if kind == "x":
            d = self.x
        elif kind == "y":
            d = self.y
        elif kind == "c":
            m = 1 - m
        elif kind == "up":
            s = s + 1
        elif kind == "dn":
            s = s - 1
        return {"seq": s, "mp": m, "dp": d}


def remote(src, dst, send, recv, where):
    return pltpu.make_async_remote_copy(
        src_ref=src, dst_ref=dst, send_sem=send, recv_sem=recv, device_id=where, device_id_type=MESH
    )


def greet(spot, n, kinds):
    bar = pltpu.get_barrier_semaphore()
    count = 0
    for kind in kinds:
        if kind in ("up", "dn"):
            there = spot.s + 1 < n if kind == "up" else spot.s > 0

            @pl.when(there)
            def _(kind=kind):
                pl.semaphore_signal(bar, inc=1, device_id=spot.to(kind), device_id_type=MESH)

            count = count + there.astype(jnp.int32)
        else:
            pl.semaphore_signal(bar, inc=1, device_id=spot.to(kind), device_id_type=MESH)
            count = count + 1
    pl.semaphore_wait(bar, count)


def gather_weights_kernel(n, k, *refs):
    ins, outs = refs[:k], refs[k : 2 * k]
    own_sem, z_send, z_recv, p_send, p_recv = refs[2 * k :]
    spot = Spot()
    s, d = spot.s, spot.d
    own = [pltpu.make_async_copy(ins[a], outs[a].at[s], own_sem.at[a]) for a in range(k)]
    for c in own:
        c.start()
    greet(spot, n, ("x", "y", "up", "dn"))

    def rows(a, who, part=None):
        size = ins[a].shape[0] // 4
        if part is None:
            return pl.ds(who * size, size)
        return pl.ds(who * size + part * (size // 2), size // 2)

    def sends(up, t):
        return ((s - t >= 0) & (s + 1 < n)) if up else ((s + t < n) & (s > 0))

    def receives(up, t):
        return s - 1 - t >= 0 if up else s + 1 + t < n

    def z_copy(a, up, t, sending):
        way = 0 if up else 1
        piece = (s - t if up else s + t) if sending else (s - 1 - t if up else s + 1 + t)
        dst = outs[a].at[piece, rows(a, d)]
        src = ins[a].at[rows(a, d)] if (t == 0 and sending) else dst
        return remote(src, dst, z_send.at[a, way, t], z_recv.at[a, way, t], spot.to("up" if up else "dn"))

    def piece_of(up, t):
        return s - 1 - t if up else s + 1 + t

    def plane_copy(a, up, t, kind):
        way = 0 if up else 1
        who = (d, d, spot.y, spot.x)[kind]
        part = (None, None, 0, 1)[kind]
        ref = outs[a].at[piece_of(up, t), rows(a, who, part)]
        return remote(ref, ref, p_send.at[a, way, t, kind], p_recv.at[a, way, t, kind], spot.to("xyxy"[kind]))

    def landed(a, up, t, kind):
        way = 0 if up else 1
        who = (spot.x, spot.y, spot.diag, spot.diag)[kind]
        part = (None, None, 0, 1)[kind]
        ref = outs[a].at[piece_of(up, t), rows(a, who, part)]
        return remote(ref, ref, p_send.at[a, way, t, kind], p_recv.at[a, way, t, kind], spot.to("xyxy"[kind]))

    for a in range(k):
        for up in (True, False):

            @pl.when(sends(up, 0))
            def _():
                z_copy(a, up, 0, True).start()

    for t in range(n):
        if t < n - 1:
            for a in range(k):
                for up in (True, False):

                    @pl.when(receives(up, t))
                    def _():
                        z_copy(a, up, t, False).wait_recv()
                        if t + 1 < n - 1:

                            @pl.when(sends(up, t + 1))
                            def _():
                                z_copy(a, up, t + 1, True).start()

                        plane_copy(a, up, t, 0).start()
                        plane_copy(a, up, t, 1).start()

        if t > 0:
            for a in range(k):
                for up in (True, False):

                    @pl.when(receives(up, t - 1))
                    def _():
                        landed(a, up, t - 1, 0).wait_recv()
                        plane_copy(a, up, t - 1, 3).start()
                        landed(a, up, t - 1, 1).wait_recv()
                        plane_copy(a, up, t - 1, 2).start()

    for t in range(n - 1):
        for a in range(k):
            for up in (True, False):

                @pl.when(sends(up, t))
                def _():
                    z_copy(a, up, t, True).wait_send()

                @pl.when(receives(up, t))
                def _():
                    landed(a, up, t, 2).wait_recv()
                    landed(a, up, t, 3).wait_recv()
                    for kind in range(4):
                        plane_copy(a, up, t, kind).wait_send()

    for c in own:
        c.wait()


def gather_weights(n, arrays, cid):
    k = len(arrays)
    DMA = pltpu.SemaphoreType.DMA
    return pl.pallas_call(
        functools.partial(gather_weights_kernel, n, k),
        out_shape=[jax.ShapeDtypeStruct((n,) + a.shape, a.dtype) for a in arrays],
        in_specs=[pl.BlockSpec(memory_space=ANY)] * k,
        out_specs=[pl.BlockSpec(memory_space=ANY)] * k,
        scratch_shapes=[DMA((k,)), DMA((k, 2, n - 1)), DMA((k, 2, n - 1)), DMA((k, 2, n - 1, 4)), DMA((k, 2, n - 1, 4))],
        compiler_params=pltpu.CompilerParams(collective_id=cid, has_side_effects=True),
        name="gather_weights",
    )(*arrays)


def plane_gather_kernel(own, out, own_sem, c_send, c_recv, p_send, p_recv):
    spot = Spot()
    m, d = spot.m, spot.d
    half = own.shape[0] // 2
    mine = pltpu.make_async_copy(own, out.at[d, m], own_sem)
    mine.start()
    greet(spot, 0, ("x", "y", "c"))
    parts = (pl.ds(0, half), pl.ds(half, half))

    def copy(kind, sending):
        who = (d, d, spot.y, spot.x)[kind] if sending else (spot.x, spot.y, spot.diag, spot.diag)[kind]
        if kind < 2:
            dst = out.at[who, m]
            src = own if sending else dst
        else:
            dst = out.at[who, m, parts[kind - 2]]
            src = dst
        return remote(src, dst, p_send.at[kind], p_recv.at[kind], spot.to("xyxy"[kind]))

    def core(index, sending):
        who = (d, spot.x, spot.y, spot.diag, spot.diag)[index]
        col = m if sending else 1 - m
        if index < 3:
            dst = out.at[who, col]
            src = own if (sending and index == 0) else dst
        else:
            dst = out.at[who, col, parts[index - 3]]
            src = dst
        return remote(src, dst, c_send.at[index], c_recv.at[index], spot.to("c"))

    copy(0, True).start()
    copy(1, True).start()
    core(0, True).start()
    copy(0, False).wait_recv()
    copy(3, True).start()
    core(1, True).start()
    copy(1, False).wait_recv()
    copy(2, True).start()
    core(2, True).start()
    copy(2, False).wait_recv()
    core(3, True).start()
    copy(3, False).wait_recv()
    core(4, True).start()
    for index in range(5):
        core(index, False).wait_recv()
        core(index, True).wait_send()
    for kind in range(4):
        copy(kind, True).wait_send()
    mine.wait()


def plane_gather(own, cid):
    DMA = pltpu.SemaphoreType.DMA
    return pl.pallas_call(
        plane_gather_kernel,
        out_shape=jax.ShapeDtypeStruct((4, 2) + own.shape, own.dtype),
        in_specs=[pl.BlockSpec(memory_space=ANY)],
        out_specs=pl.BlockSpec(memory_space=ANY),
        scratch_shapes=[DMA, DMA((5,)), DMA((5,)), DMA((4,)), DMA((4,))],
        compiler_params=pltpu.CompilerParams(collective_id=cid, has_side_effects=True),
        name=f"plane_gather_{cid}",
    )(own)


def plane_scatter_kernel(
    part, out, mine, theirs, s1, xin, yin, t2, xin2, yin2, l_sem, c_send, c_recv, p_send, p_recv
):
    spot = Spot()
    m, d = spot.m, spot.d
    half = out.shape[0] // 2
    A, B = pl.ds(0, half), pl.ds(half, half)
    order = (spot.diag, spot.x, spot.y, d)
    loads = [pltpu.make_async_copy(part.at[who, m], mine.at[i], l_sem.at[i]) for i, who in enumerate(order)]
    for c in loads:
        c.start()
    greet(spot, 0, ("x", "y", "c"))

    def core(i):
        return remote(part.at[order[i], 1 - m], theirs.at[i], c_send.at[i], c_recv.at[i], spot.to("c"))

    for i in range(4):
        core(i).start()

    first = {
        "xdiag": remote(s1.at[0, A], xin.at[1], p_send.at[0], p_recv.at[0], spot.to("x")),
        "ydiag": remote(s1.at[0, B], yin.at[1], p_send.at[1], p_recv.at[1], spot.to("y")),
        "x": remote(s1.at[1, A], xin.at[0], p_send.at[2], p_recv.at[2], spot.to("x")),
        "y": remote(s1.at[2, B], yin.at[0], p_send.at[3], p_recv.at[3], spot.to("y")),
    }
    for i in range(4):
        loads[i].wait()
        core(i).wait_recv()
        s1[i] = (mine[i].astype(jnp.float32) + theirs[i].astype(jnp.float32)).astype(s1.dtype)
        if i == 0:
            first["xdiag"].start()
            first["ydiag"].start()
        elif i == 1:
            first["x"].start()
        elif i == 2:
            first["y"].start()
    second = (
        remote(t2.at[0], yin2, p_send.at[4], p_recv.at[4], spot.to("y")),
        remote(t2.at[1], xin2, p_send.at[5], p_recv.at[5], spot.to("x")),
    )
    first["xdiag"].wait_recv()
    t2[0] = (s1[2, A].astype(jnp.float32) + xin[1].astype(jnp.float32)).astype(t2.dtype)
    second[0].start()
    first["ydiag"].wait_recv()
    t2[1] = (s1[1, B].astype(jnp.float32) + yin[1].astype(jnp.float32)).astype(t2.dtype)
    second[1].start()
    first["x"].wait_recv()
    first["y"].wait_recv()
    second[0].wait_recv()
    out[A] = s1[3, A].astype(jnp.float32) + xin[0].astype(jnp.float32) + yin2[...].astype(jnp.float32)
    second[1].wait_recv()
    out[B] = s1[3, B].astype(jnp.float32) + yin[0].astype(jnp.float32) + xin2[...].astype(jnp.float32)
    for i in range(4):
        core(i).wait_send()
    for c in list(first.values()) + list(second):
        c.wait_send()


def plane_scatter(part, cid):
    DMA = pltpu.SemaphoreType.DMA
    r, w = part.shape[2:]
    b = jnp.bfloat16
    V = pltpu.VMEM
    return pl.pallas_call(
        plane_scatter_kernel,
        out_shape=jax.ShapeDtypeStruct((r, w), jnp.float32),
        in_specs=[pl.BlockSpec(memory_space=ANY)],
        out_specs=pl.BlockSpec(memory_space=pltpu.VMEM),
        scratch_shapes=[
            V((4, r, w), b),
            V((4, r, w), b),
            V((4, r, w), b),
            V((2, r // 2, w), b),
            V((2, r // 2, w), b),
            V((2, r // 2, w), b),
            V((r // 2, w), b),
            V((r // 2, w), b),
            DMA((4,)),
            DMA((4,)),
            DMA((4,)),
            DMA((6,)),
            DMA((6,)),
        ],
        compiler_params=pltpu.CompilerParams(collective_id=cid, has_side_effects=True, vmem_limit_bytes=40 << 20),
        name=f"plane_scatter_{cid}",
    )(part)


def line_sum_kernel(n, up, own, out, box, send, recv):
    spot = Spot()
    s = spot.s
    greet(spot, n, ("up", "dn"))
    go = "up" if up else "dn"

    def sends(t):
        return ((s - t >= 0) & (s + 1 < n)) if up else ((s + t < n) & (s > 0))

    def receives(t):
        return s - 1 - t >= 0 if up else s + 1 + t < n

    def copy(t):
        src = own if t == 0 else box.at[t - 1]
        return remote(src, box.at[t], send.at[t], recv.at[t], spot.to(go))

    @pl.when(sends(0))
    def _():
        copy(0).start()

    out[...] = jnp.zeros_like(out)
    for t in range(n - 1):

        @pl.when(receives(t))
        def _():
            copy(t).wait_recv()
            if t + 1 < n - 1:

                @pl.when(sends(t + 1))
                def _():
                    copy(t + 1).start()

            out[...] += box[t].astype(jnp.float32)

    for t in range(n - 1):

        @pl.when(sends(t))
        def _():
            copy(t).wait_send()


def line_sum(n, own, up, cid):
    DMA = pltpu.SemaphoreType.DMA
    return pl.pallas_call(
        functools.partial(line_sum_kernel, n, up),
        out_shape=jax.ShapeDtypeStruct(own.shape, jnp.float32),
        in_specs=[pl.BlockSpec(memory_space=pltpu.VMEM)],
        out_specs=pl.BlockSpec(memory_space=pltpu.VMEM),
        scratch_shapes=[pltpu.VMEM((n - 1,) + own.shape, own.dtype), DMA((n - 1,)), DMA((n - 1,))],
        compiler_params=pltpu.CompilerParams(collective_id=cid, has_side_effects=True, vmem_limit_bytes=40 << 20),
        name=f"line_sum_{cid}",
    )(own)
def plane_total_kernel(
    n, shared, part, out, mine, core_in, xin, yin, t2, xin2, yin2, line, c_send, c_recv, p_send, p_recv, z_send, z_recv, g_send, g_recv
):
    spot = Spot()
    s, d = spot.s, spot.d
    h = out.shape[1] // 2
    A, B = pl.ds(0, h), pl.ds(h, h)
    f32, b16 = jnp.float32, jnp.bfloat16
    mine[...] = part[...].astype(b16)
    greet(spot, n, ("x", "y", "c", "up", "dn"))
    core = remote(mine.at[pl.ds(0, shared)], core_in, c_send, c_recv, spot.to("c"))
    core.start()
    core.wait()
    mine[:shared] = (mine[:shared].astype(f32) + core_in[...].astype(f32)).astype(b16)

    def block(who, part):
        return mine.at[pl.ds(who * 2 * h + part * h, h)]

    def read(who, part):
        return mine[pl.ds(who * 2 * h + part * h, h)].astype(f32)

    first = (
        remote(block(spot.diag, 0), xin.at[1], p_send.at[0], p_recv.at[0], spot.to("x")),
        remote(block(spot.diag, 1), yin.at[1], p_send.at[1], p_recv.at[1], spot.to("y")),
        remote(block(spot.x, 0), xin.at[0], p_send.at[2], p_recv.at[2], spot.to("x")),
        remote(block(spot.y, 1), yin.at[0], p_send.at[3], p_recv.at[3], spot.to("y")),
    )
    for c in first:
        c.start()
    second = (
        remote(t2.at[0], yin2, p_send.at[4], p_recv.at[4], spot.to("y")),
        remote(t2.at[1], xin2, p_send.at[5], p_recv.at[5], spot.to("x")),
    )
    first[0].wait_recv()
    t2[0] = (read(spot.y, 0) + xin[1].astype(f32)).astype(b16)
    second[0].start()
    first[1].wait_recv()
    t2[1] = (read(spot.x, 1) + yin[1].astype(f32)).astype(b16)
    second[1].start()
    first[2].wait_recv()
    first[3].wait_recv()
    second[0].wait_recv()
    line[s, A] = (read(d, 0) + xin[0].astype(f32) + yin2[...].astype(f32)).astype(b16)
    second[1].wait_recv()
    line[s, B] = (read(d, 1) + yin[0].astype(f32) + xin2[...].astype(f32)).astype(b16)

    def sends(up, t):
        return ((s - t >= 0) & (s + 1 < n)) if up else ((s + t < n) & (s > 0))

    def receives(up, t):
        return s - 1 - t >= 0 if up else s + 1 + t < n

    def z_copy(up, t, sending):
        way = 0 if up else 1
        piece = (s - t if up else s + t) if sending else (s - 1 - t if up else s + 1 + t)
        return remote(line.at[piece], line.at[piece], z_send.at[way, t], z_recv.at[way, t], spot.to("up" if up else "dn"))

    for up in (True, False):

        @pl.when(sends(up, 0))
        def _():
            z_copy(up, 0, True).start()

    for t in range(n - 1):
        for up in (True, False):

            @pl.when(receives(up, t))
            def _():
                z_copy(up, t, False).wait_recv()
                if t + 1 < n - 1:

                    @pl.when(sends(up, t + 1))
                    def _():
                        z_copy(up, t + 1, True).start()

    total = line[0].astype(f32)
    for i in range(1, n):
        total = total + line[i].astype(f32)
    out[d] = total.astype(b16)

    parts = (A, B)

    def back(kind, sending):
        who = (d, d, spot.y, spot.x)[kind] if sending else (spot.x, spot.y, spot.diag, spot.diag)[kind]
        ref = out.at[who] if kind < 2 else out.at[who, parts[kind - 2]]
        return remote(ref, ref, g_send.at[kind], g_recv.at[kind], spot.to("xyxy"[kind]))

    back(0, True).start()
    back(1, True).start()
    back(0, False).wait_recv()
    back(3, True).start()
    back(1, False).wait_recv()
    back(2, True).start()
    back(2, False).wait_recv()
    back(3, False).wait_recv()
    for kind in range(4):
        back(kind, True).wait_send()
    for c in first + second:
        c.wait_send()
    for t in range(n - 1):
        for up in (True, False):

            @pl.when(sends(up, t))
            def _():
                z_copy(up, t, True).wait_send()


def plane_total(n, part, shared, cid):
    DMA = pltpu.SemaphoreType.DMA
    V = pltpu.VMEM
    b = jnp.bfloat16
    rows, w = part.shape
    h = rows // 8
    return pl.pallas_call(
        functools.partial(plane_total_kernel, n, shared),
        out_shape=jax.ShapeDtypeStruct((4, 2 * h, w), b),
        in_specs=[pl.BlockSpec(memory_space=pltpu.VMEM)],
        out_specs=pl.BlockSpec(memory_space=pltpu.VMEM),
        scratch_shapes=[
            V((rows, w), b),
            V((shared, w), b),
            V((2, h, w), b),
            V((2, h, w), b),
            V((2, h, w), b),
            V((h, w), b),
            V((h, w), b),
            V((n, 2 * h, w), b),
            DMA,
            DMA,
            DMA((6,)),
            DMA((6,)),
            DMA((2, n - 1)),
            DMA((2, n - 1)),
            DMA((4,)),
            DMA((4,)),
        ],
        compiler_params=pltpu.CompilerParams(collective_id=cid, has_side_effects=True, vmem_limit_bytes=40 << 20),
        name=f"plane_total_{cid}",
    )(part)


def key_features(key_block, feature_maps):
    logits = jnp.einsum("ekd,kdf->ekf", key_block, feature_maps, preferred_element_type=jnp.float32)
    return jnp.concatenate([jax.nn.softmax(logits, -1), jax.nn.softmax(-logits, -1)], -1)


def query_features(query_rows, feature_maps):
    logits = jnp.einsum(
        "tkgd,kgdf->tkgf", query_rows, feature_maps, preferred_element_type=jnp.float32
    )
    return jnp.concatenate([jax.nn.softmax(logits, -1), jax.nn.softmax(-logits, -1)], -1)


def state_piece(features, values, valid_mask, rows_here):
    kept_feats = jnp.where(valid_mask[:rows_here, None, None], features[:rows_here], 0.0)
    state_sum = jnp.einsum(
        "ekf,ekd->kfd", kept_feats, values[:rows_here], preferred_element_type=jnp.float32
    )
    return (state_sum, jnp.sum(kept_feats, 0))


def attend(query_rows, key_block, values, features, state_sum, totals, feature_maps, valid_mask):
    rows_here = query_rows.shape[0]
    extent = key_block.shape[0]
    reach_back = extent - rows_here
    query_feats = query_features(query_rows, feature_maps)
    scores = jnp.einsum(
        "tkgd,ekd->kgte", query_rows, key_block, preferred_element_type=jnp.float32
    ) / math.sqrt(query_rows.shape[-1])
    rowpos = jnp.arange(rows_here, dtype=jnp.int32)[:, None]
    colpos = jnp.arange(extent, dtype=jnp.int32)[None, :]
    inside = (colpos > rowpos) & (colpos <= rowpos + reach_back) & valid_mask[None, :]
    older_mask = (colpos <= rowpos) & valid_mask[None, :]
    window_part = jnp.where(inside, jnp.exp(jnp.where(inside, scores, 0.0)), 0.0)
    linear_part = jnp.where(
        older_mask,
        jnp.einsum("tkgf,ekf->kgte", query_feats, features, preferred_element_type=jnp.float32),
        0.0,
    )
    weights = window_part + linear_part
    numerator = jnp.einsum("kgte,ekd->tkgd", weights, values, preferred_element_type=jnp.float32)
    numerator = numerator + jnp.einsum(
        "tkgf,kfd->tkgd", query_feats, state_sum, preferred_element_type=jnp.float32
    )
    denominator = jnp.transpose(jnp.sum(weights, -1), (2, 0, 1))
    denominator = denominator + jnp.einsum(
        "tkgf,kf->tkg", query_feats, totals, preferred_element_type=jnp.float32
    )
    return numerator / denominator[..., None]


f32, b16 = jnp.float32, jnp.bfloat16


def dot(left, right):
    return jnp.dot(left, right, preferred_element_type=f32)


def dot_t(left, right):
    return lax.dot_general(left, right, (((1,), (1,)), ((), ())), preferred_element_type=f32)


def t_dot(left, right):
    return lax.dot_general(left, right, (((0,), (0,)), ((), ())), preferred_element_type=f32)


def norm_back(inputs, inv_rms, gain, dnormed):
    return inv_rms * gain * dnormed - inputs * inv_rms**3 * jnp.mean(
        gain * dnormed * inputs, -1, keepdims=True
    )


def from_behind(value, axis, steps):
    count = lax.axis_size(axis)
    first, last = (max(0, -steps), min(count, count - steps))
    return lax.ppermute(value, axis, [(source, source + steps) for source in range(first, last)])


def swap_core(value):
    return lax.ppermute(value, "mp", [(0, 1), (1, 0)])


def per_device(
    tokens,
    cotangent,
    attention_norm_gain,
    feedforward_norm_gain,
    query_weight,
    key_weight,
    value_weight,
    output_weight,
    gate_weight,
    up_weight,
    down_weight,
    query_adapter_down,
    query_adapter_up,
    key_adapter_down,
    key_adapter_up,
    value_adapter_down,
    value_adapter_up,
    output_adapter_down,
    output_adapter_up,
    query_feature_matrix,
    key_feature_matrix,
):
    n = lax.axis_size("seq")
    position, m, d = (lax.axis_index(a) for a in ("seq", "mp", "dp"))
    seq_count, rows_here, width = tokens.shape
    total_rows = seq_count * rows_here
    half = total_rows // 2
    heads_kv = key_feature_matrix.shape[0]
    head_size = key_feature_matrix.shape[1]
    groups = query_feature_matrix.shape[0] // heads_kv
    extent = rows_here + SOFTMAX_SPAN

    units = gate_weight.shape[1] // 4
    gate_w = lax.all_gather(lax.dynamic_slice_in_dim(gate_weight, d * units, units, 1), "seq", axis=0, tiled=True)
    up_w = lax.all_gather(lax.dynamic_slice_in_dim(up_weight, d * units, units, 1), "seq", axis=0, tiled=True)
    down_w = lax.all_gather(lax.dynamic_slice_in_dim(down_weight, d * units, units, 0), "seq", axis=1, tiled=True)

    qkv_own = jnp.concatenate([query_weight, key_weight, value_weight], 1)
    qkv_g, out_g = gather_weights(n, [qkv_own, output_weight], 1)
    qkv_w = qkv_g.reshape(width, -1)
    wide = query_weight.shape[1]
    kv_wide = key_weight.shape[1]

    def my_half(a):
        return lax.dynamic_slice_in_dim(a, m * half, half, 0)

    def both_halves(own):
        other = swap_core(own)
        return jnp.concatenate([jnp.where(m == 0, own, other), jnp.where(m == 0, other, own)], 0)

    tok2 = tokens.reshape(total_rows, width)
    inputs = tok2.astype(f32)
    gain_attn = attention_norm_gain.astype(f32)
    rms_attn = lax.rsqrt(jnp.mean(inputs * inputs, -1, keepdims=True) + epsilon)
    normed = (inputs * rms_attn * gain_attn).astype(b16)

    cot2 = cotangent.reshape(total_rows, width)
    cot_all = plane_gather(my_half(cot2), 2).reshape(8 * half, width)

    downs = jnp.concatenate([query_adapter_down, key_adapter_down, value_adapter_down], 1)
    inner = dot(normed, downs)
    rank = query_adapter_down.shape[1]
    full = dot(normed, qkv_w)

    def project(index, first, last, second):
        return (
            full[:, first:last] + dot(inner[:, index * rank : (index + 1) * rank].astype(b16), second)
        ).astype(b16)

    query_half = project(0, 0, wide, query_adapter_up)
    key_half = project(1, wide, wide + kv_wide, key_adapter_up)
    value_half = project(2, wide + kv_wide, wide + 2 * kv_wide, value_adapter_up)
    key3 = key_half.reshape(seq_count, rows_here, heads_kv * head_size)
    value3 = value_half.reshape(seq_count, rows_here, heads_kv * head_size)
    kv3 = jnp.concatenate([key3, value3], -1)
    kv_prev = from_behind(kv3[:, rows_here - SOFTMAX_SPAN :], "seq", 1)
    kv_ext = jnp.concatenate([kv_prev, kv3], 1).astype(f32)
    key_ext = kv_ext[..., :kv_wide].reshape(seq_count, extent, heads_kv, head_size)
    value_ext = kv_ext[..., kv_wide:].reshape(seq_count, extent, heads_kv, head_size)
    valid_mask = position * rows_here - SOFTMAX_SPAN + jnp.arange(extent, dtype=jnp.int32) >= 0
    kmaps = key_feature_matrix.astype(f32)
    qmaps = query_feature_matrix.astype(f32).reshape(heads_kv, groups, head_size, head_size)

    def features_all(key_in, maps_in):
        return jax.vmap(key_features, (0, None))(key_in, maps_in)

    features, features_back = jax.vjp(features_all, key_ext, kmaps)

    def pieces_all(feats_in, values_in):
        return jax.vmap(state_piece, (0, 0, None, None))(feats_in, values_in, valid_mask, rows_here)

    (piece_state, piece_totals), pieces_back = jax.vjp(pieces_all, features, value_ext)

    def line_totals(state, totals, up, cid):
        flat = jnp.concatenate([state.reshape(-1, 128), totals.reshape(-1, 128)], 0)
        flat = jnp.pad(flat, ((0, -flat.shape[0] % 16), (0, 0))).astype(b16)
        summed = line_sum(n, flat, up, cid)
        rows = state.size // 128
        return summed[:rows].reshape(state.shape), summed[rows : rows + totals.size // 128].reshape(totals.shape)

    state_sum, totals = line_totals(piece_state, piece_totals, True, 3)
    queries5 = query_half.reshape(seq_count, rows_here, heads_kv, groups, head_size).astype(f32)

    def attend_all(query_in, key_in, value_in, feats_in, state_in, totals_in, maps_in):
        return jax.vmap(attend, (0, 0, 0, 0, 0, 0, None, None))(
            query_in, key_in, value_in, feats_in, state_in, totals_in, maps_in, valid_mask
        )

    attn5, attend_back = jax.vjp(
        attend_all, queries5, key_ext, value_ext, features, state_sum, totals, qmaps
    )
    attn16 = attn5.reshape(total_rows, -1).astype(b16)
    inner_output = dot(attn16, output_adapter_down)
    branch = jnp.concatenate([dot(attn16, out_g[i]) for i in range(n)], 1) + dot(
        inner_output.astype(b16), output_adapter_up
    )
    branch16 = branch.astype(b16)
    from_other = swap_core(lax.dynamic_slice_in_dim(branch16, (1 - m) * half, half, 0))
    resid = my_half(inputs) + my_half(branch) + from_other.astype(f32)
    gain_mlp = feedforward_norm_gain.astype(f32)
    rms_mlp = lax.rsqrt(jnp.mean(resid * resid, -1, keepdims=True) + epsilon)
    normed_mlp = (resid * rms_mlp * gain_mlp).astype(b16)
    normed_all = plane_gather(normed_mlp, 4).reshape(8 * half, width)

    gate = dot(normed_all, gate_w)
    up_vals = dot(normed_all, up_w)
    dhidden = dot_t(cot_all, down_w)
    sig = jax.nn.sigmoid(gate)
    act = gate * sig
    hidden = (act * up_vals).astype(b16)
    dgate = (dhidden * up_vals * sig * (1.0 + gate * (1.0 - sig))).astype(b16)
    dup = (dhidden * act).astype(b16)
    dn_part = (dot_t(dgate, gate_w) + dot_t(dup, up_w)).astype(b16)
    out_part = dot(hidden, down_w).astype(b16)
    dnormed_mlp = plane_scatter(dn_part.reshape(4, 2, half, width), 5)
    mlp_out = plane_scatter(out_part.reshape(4, 2, half, width), 6)
    output = both_halves((resid + mlp_out).astype(b16)).reshape(seq_count, rows_here, width)

    mlp_gain_term = jnp.sum(dnormed_mlp * resid * rms_mlp, 0)
    dresid = my_half(cot2).astype(f32) + norm_back(resid, rms_mlp, gain_mlp, dnormed_mlp)
    dresid16 = both_halves(dresid.astype(b16))
    du_o = dot_t(dresid16, output_adapter_up)
    oup_term = t_dot(inner_output.astype(b16), dresid16)
    odown_term = t_dot(du_o.astype(b16), attn16)
    dattn = dot_t(du_o.astype(b16), output_adapter_down)
    step = output_weight.shape[1]
    for i in range(n):
        dattn = dattn + dot_t(dresid16[:, i * step : (i + 1) * step], out_g[i])
    dattn16 = dattn.astype(b16).astype(f32).reshape(attn5.shape)
    dqueries, dkey_ext, dvalue_ext, dfeatures, dstate, dtotals, dqmaps = attend_back(dattn16)
    later_state, later_totals = line_totals(dstate, dtotals, False, 7)
    dfeatures_more, dvalue_more = pieces_back((later_state, later_totals))
    dkey_more, dkmaps = features_back(dfeatures + dfeatures_more)
    dkey_ext = (dkey_ext + dkey_more).reshape(seq_count, extent, heads_kv * head_size)
    dvalue_ext = (dvalue_ext + dvalue_more).reshape(seq_count, extent, heads_kv * head_size)
    dkv_ext = jnp.concatenate([dkey_ext, dvalue_ext], -1)
    back = from_behind(dkv_ext[:, :SOFTMAX_SPAN].astype(b16), "seq", -1).astype(f32)
    dkv = dkv_ext[:, SOFTMAX_SPAN:]
    dkv = jnp.concatenate(
        [dkv[:, : rows_here - SOFTMAX_SPAN], dkv[:, rows_here - SOFTMAX_SPAN :] + back], 1
    )
    dqkv16 = jnp.concatenate(
        [dqueries.reshape(total_rows, -1).astype(b16), dkv.reshape(total_rows, -1).astype(b16)], 1
    )
    bounds = ((0, wide), (wide, wide + kv_wide), (wide + kv_wide, wide + 2 * kv_wide))
    seconds = (query_adapter_up, key_adapter_up, value_adapter_up)
    dinner = jnp.concatenate(
        [dot_t(dqkv16[:, a:b], second) for (a, b), second in zip(bounds, seconds)], 1
    ).astype(b16)
    dnormed = (dot_t(dqkv16, qkv_w) + dot_t(dinner, downs)).astype(b16)
    down_terms = t_dot(dinner, normed)
    inner16 = inner.astype(b16)
    up_terms = [
        t_dot(inner16[:, i * rank : (i + 1) * rank], dqkv16[:, a:b]) for i, (a, b) in enumerate(bounds)
    ]
    from_other = swap_core(lax.dynamic_slice_in_dim(dnormed, (1 - m) * half, half, 0))
    dnormed = my_half(dnormed).astype(f32) + from_other.astype(f32)
    x_half, r_half = my_half(inputs), my_half(rms_attn)
    attn_gain_term = jnp.sum(dnormed * x_half * r_half, 0)
    tokens_grad = both_halves(dresid + norm_back(x_half, r_half, gain_attn, dnormed)).reshape(
        seq_count, rows_here, width
    )

    shared = [attn_gain_term, mlp_gain_term, down_terms, oup_term]
    split = up_terms + [odown_term, dqmaps, dkmaps]
    flat = [a.reshape(-1, 128) for a in shared + split]
    sizes = [a.shape[0] for a in flat]
    shared_rows = sum(sizes[:4])
    flat = jnp.concatenate(flat, 0)
    flat = jnp.pad(flat, ((0, -flat.shape[0] % 128), (0, 0)))
    summed = plane_total(n, flat, shared_rows, 8).reshape(-1, 128).astype(f32)
    parts, at = [], 0
    for term, size in zip(shared + split, sizes):
        parts.append(summed[at : at + size].reshape(term.shape))
        at += size
    attn_gain, mlp_gain, downs_g, oup, qup, kup, vup, odown, qmaps_g, kmaps_g = parts
    downs_g = downs_g.T
    return (
        output,
        tokens_grad,
        attn_gain,
        mlp_gain,
        downs_g[:, :rank],
        qup,
        downs_g[:, rank : 2 * rank],
        kup,
        downs_g[:, 2 * rank :],
        vup,
        odown.T,
        oup,
        qmaps_g.reshape(query_feature_matrix.shape),
        kmaps_g,
    )


def solution(mesh):
    placed = (
        P("dp", "seq", None),
        P("dp", "seq", None),
        P(),
        P(),
        P("seq", "mp"),
        P("seq", "mp"),
        P("seq", "mp"),
        P("mp", "seq"),
        P("seq", "mp"),
        P("seq", "mp"),
        P("mp", "seq"),
        P(),
        P(None, "mp"),
        P(),
        P(None, "mp"),
        P(),
        P(None, "mp"),
        P("mp", None),
        P(),
        P("mp", None, None),
        P("mp", None, None),
    )
    return jax.shard_map(
        per_device,
        mesh=mesh,
        in_specs=placed,
        out_specs=(
            P("dp", "seq", None),
            P("dp", "seq", None),
            P(),
            P(),
            P(),
            P(None, "mp"),
            P(),
            P(None, "mp"),
            P(),
            P(None, "mp"),
            P("mp", None),
            P(),
            P("mp", None, None),
            P("mp", None, None),
        ),
        check_vma=False,
    )
```

```python
import math
import functools
import jax
import jax.numpy as jnp
from jax import lax
from jax.experimental import pallas as pl
from jax.experimental.pallas import tpu as pltpu
from jax.sharding import PartitionSpec as P

SOFTMAX_SPAN = 64
epsilon = 1e-05

MESH = pl.DeviceIdType.MESH
ANY = pl.ANY


class Spot:
    def __init__(self):
        self.s, self.m, self.d = (lax.axis_index(a) for a in ("seq", "mp", "dp"))
        self.x = self.d + 1 - 2 * (self.d % 2)
        self.y = (self.d + 2) % 4
        self.diag = (self.x + 2) % 4

    def to(self, kind):
        s, m, d = self.s, self.m, self.d
        if kind == "x":
            d = self.x
        elif kind == "y":
            d = self.y
        elif kind == "c":
            m = 1 - m
        elif kind == "up":
            s = s + 1
        elif kind == "dn":
            s = s - 1
        return {"seq": s, "mp": m, "dp": d}


def remote(src, dst, send, recv, where):
    return pltpu.make_async_remote_copy(
        src_ref=src, dst_ref=dst, send_sem=send, recv_sem=recv, device_id=where, device_id_type=MESH
    )


def greet(spot, n, kinds):
    bar = pltpu.get_barrier_semaphore()
    count = 0
    for kind in kinds:
        if kind in ("up", "dn"):
            there = spot.s + 1 < n if kind == "up" else spot.s > 0

            @pl.when(there)
            def _(kind=kind):
                pl.semaphore_signal(bar, inc=1, device_id=spot.to(kind), device_id_type=MESH)

            count = count + there.astype(jnp.int32)
        else:
            pl.semaphore_signal(bar, inc=1, device_id=spot.to(kind), device_id_type=MESH)
            count = count + 1
    pl.semaphore_wait(bar, count)


def gather_weights_kernel(n, k, *refs):
    ins, outs = refs[:k], refs[k : 2 * k]
    own_sem, z_send, z_recv, p_send, p_recv = refs[2 * k :]
    spot = Spot()
    s, d = spot.s, spot.d
    own = [pltpu.make_async_copy(ins[a], outs[a].at[s], own_sem.at[a]) for a in range(k)]
    for c in own:
        c.start()
    greet(spot, n, ("x", "y", "up", "dn"))

    def rows(a, who, part=None):
        size = ins[a].shape[0] // 4
        if part is None:
            return pl.ds(who * size, size)
        return pl.ds(who * size + part * (size // 2), size // 2)

    def sends(up, t):
        return ((s - t >= 0) & (s + 1 < n)) if up else ((s + t < n) & (s > 0))

    def receives(up, t):
        return s - 1 - t >= 0 if up else s + 1 + t < n

    def z_copy(a, up, t, sending):
        way = 0 if up else 1
        piece = (s - t if up else s + t) if sending else (s - 1 - t if up else s + 1 + t)
        dst = outs[a].at[piece, rows(a, d)]
        src = ins[a].at[rows(a, d)] if (t == 0 and sending) else dst
        return remote(src, dst, z_send.at[a, way, t], z_recv.at[a, way, t], spot.to("up" if up else "dn"))

    def piece_of(up, t):
        return s - 1 - t if up else s + 1 + t

    def plane_copy(a, up, t, kind):
        way = 0 if up else 1
        who = (d, d, spot.y, spot.x)[kind]
        part = (None, None, 0, 1)[kind]
        ref = outs[a].at[piece_of(up, t), rows(a, who, part)]
        return remote(ref, ref, p_send.at[a, way, t, kind], p_recv.at[a, way, t, kind], spot.to("xyxy"[kind]))

    def landed(a, up, t, kind):
        way = 0 if up else 1
        who = (spot.x, spot.y, spot.diag, spot.diag)[kind]
        part = (None, None, 0, 1)[kind]
        ref = outs[a].at[piece_of(up, t), rows(a, who, part)]
        return remote(ref, ref, p_send.at[a, way, t, kind], p_recv.at[a, way, t, kind], spot.to("xyxy"[kind]))

    for a in range(k):
        for up in (True, False):

            @pl.when(sends(up, 0))
            def _():
                z_copy(a, up, 0, True).start()

    for t in range(n):
        if t < n - 1:
            for a in range(k):
                for up in (True, False):

                    @pl.when(receives(up, t))
                    def _():
                        z_copy(a, up, t, False).wait_recv()
                        if t + 1 < n - 1:

                            @pl.when(sends(up, t + 1))
                            def _():
                                z_copy(a, up, t + 1, True).start()

                        plane_copy(a, up, t, 0).start()
                        plane_copy(a, up, t, 1).start()

        if t > 0:
            for a in range(k):
                for up in (True, False):

                    @pl.when(receives(up, t - 1))
                    def _():
                        landed(a, up, t - 1, 0).wait_recv()
                        plane_copy(a, up, t - 1, 3).start()
                        landed(a, up, t - 1, 1).wait_recv()
                        plane_copy(a, up, t - 1, 2).start()

    for t in range(n - 1):
        for a in range(k):
            for up in (True, False):

                @pl.when(sends(up, t))
                def _():
                    z_copy(a, up, t, True).wait_send()

                @pl.when(receives(up, t))
                def _():
                    landed(a, up, t, 2).wait_recv()
                    landed(a, up, t, 3).wait_recv()
                    for kind in range(4):
                        plane_copy(a, up, t, kind).wait_send()

    for c in own:
        c.wait()


def gather_weights(n, arrays, cid):
    k = len(arrays)
    DMA = pltpu.SemaphoreType.DMA
    return pl.pallas_call(
        functools.partial(gather_weights_kernel, n, k),
        out_shape=[jax.ShapeDtypeStruct((n,) + a.shape, a.dtype) for a in arrays],
        in_specs=[pl.BlockSpec(memory_space=ANY)] * k,
        out_specs=[pl.BlockSpec(memory_space=ANY)] * k,
        scratch_shapes=[DMA((k,)), DMA((k, 2, n - 1)), DMA((k, 2, n - 1)), DMA((k, 2, n - 1, 4)), DMA((k, 2, n - 1, 4))],
        compiler_params=pltpu.CompilerParams(collective_id=cid, has_side_effects=True),
        name="gather_weights",
    )(*arrays)


def plane_gather_kernel(own, out, own_sem, c_send, c_recv, p_send, p_recv):
    spot = Spot()
    m, d = spot.m, spot.d
    half = own.shape[0] // 2
    mine = pltpu.make_async_copy(own, out.at[d, m], own_sem)
    mine.start()
    greet(spot, 0, ("x", "y", "c"))
    parts = (pl.ds(0, half), pl.ds(half, half))

    def copy(kind, sending):
        who = (d, d, spot.y, spot.x)[kind] if sending else (spot.x, spot.y, spot.diag, spot.diag)[kind]
        if kind < 2:
            dst = out.at[who, m]
            src = own if sending else dst
        else:
            dst = out.at[who, m, parts[kind - 2]]
            src = dst
        return remote(src, dst, p_send.at[kind], p_recv.at[kind], spot.to("xyxy"[kind]))

    def core(index, sending):
        who = (d, spot.x, spot.y, spot.diag, spot.diag)[index]
        col = m if sending else 1 - m
        if index < 3:
            dst = out.at[who, col]
            src = own if (sending and index == 0) else dst
        else:
            dst = out.at[who, col, parts[index - 3]]
            src = dst
        return remote(src, dst, c_send.at[index], c_recv.at[index], spot.to("c"))

    copy(0, True).start()
    copy(1, True).start()
    core(0, True).start()
    copy(0, False).wait_recv()
    copy(3, True).start()
    core(1, True).start()
    copy(1, False).wait_recv()
    copy(2, True).start()
    core(2, True).start()
    copy(2, False).wait_recv()
    core(3, True).start()
    copy(3, False).wait_recv()
    core(4, True).start()
    for index in range(5):
        core(index, False).wait_recv()
        core(index, True).wait_send()
    for kind in range(4):
        copy(kind, True).wait_send()
    mine.wait()


def plane_gather(own, cid):
    DMA = pltpu.SemaphoreType.DMA
    return pl.pallas_call(
        plane_gather_kernel,
        out_shape=jax.ShapeDtypeStruct((4, 2) + own.shape, own.dtype),
        in_specs=[pl.BlockSpec(memory_space=ANY)],
        out_specs=pl.BlockSpec(memory_space=ANY),
        scratch_shapes=[DMA, DMA((5,)), DMA((5,)), DMA((4,)), DMA((4,))],
        compiler_params=pltpu.CompilerParams(collective_id=cid, has_side_effects=True),
        name=f"plane_gather_{cid}",
    )(own)


def plane_scatter_kernel(
    part, out, mine, theirs, s1, xin, yin, t2, xin2, yin2, l_sem, c_send, c_recv, p_send, p_recv
):
    spot = Spot()
    m, d = spot.m, spot.d
    half = out.shape[0] // 2
    A, B = pl.ds(0, half), pl.ds(half, half)
    order = (spot.diag, spot.x, spot.y, d)
    loads = [pltpu.make_async_copy(part.at[who, m], mine.at[i], l_sem.at[i]) for i, who in enumerate(order)]
    for c in loads:
        c.start()
    greet(spot, 0, ("x", "y", "c"))

    def core(i):
        return remote(part.at[order[i], 1 - m], theirs.at[i], c_send.at[i], c_recv.at[i], spot.to("c"))

    for i in range(4):
        core(i).start()

    first = {
        "xdiag": remote(s1.at[0, A], xin.at[1], p_send.at[0], p_recv.at[0], spot.to("x")),
        "ydiag": remote(s1.at[0, B], yin.at[1], p_send.at[1], p_recv.at[1], spot.to("y")),
        "x": remote(s1.at[1, A], xin.at[0], p_send.at[2], p_recv.at[2], spot.to("x")),
        "y": remote(s1.at[2, B], yin.at[0], p_send.at[3], p_recv.at[3], spot.to("y")),
    }
    for i in range(4):
        loads[i].wait()
        core(i).wait_recv()
        s1[i] = (mine[i].astype(jnp.float32) + theirs[i].astype(jnp.float32)).astype(s1.dtype)
        if i == 0:
            first["xdiag"].start()
            first["ydiag"].start()
        elif i == 1:
            first["x"].start()
        elif i == 2:
            first["y"].start()
    second = (
        remote(t2.at[0], yin2, p_send.at[4], p_recv.at[4], spot.to("y")),
        remote(t2.at[1], xin2, p_send.at[5], p_recv.at[5], spot.to("x")),
    )
    first["xdiag"].wait_recv()
    t2[0] = (s1[2, A].astype(jnp.float32) + xin[1].astype(jnp.float32)).astype(t2.dtype)
    second[0].start()
    first["ydiag"].wait_recv()
    t2[1] = (s1[1, B].astype(jnp.float32) + yin[1].astype(jnp.float32)).astype(t2.dtype)
    second[1].start()
    first["x"].wait_recv()
    first["y"].wait_recv()
    second[0].wait_recv()
    out[A] = s1[3, A].astype(jnp.float32) + xin[0].astype(jnp.float32) + yin2[...].astype(jnp.float32)
    second[1].wait_recv()
    out[B] = s1[3, B].astype(jnp.float32) + yin[0].astype(jnp.float32) + xin2[...].astype(jnp.float32)
    for i in range(4):
        core(i).wait_send()
    for c in list(first.values()) + list(second):
        c.wait_send()


def plane_scatter(part, cid):
    DMA = pltpu.SemaphoreType.DMA
    r, w = part.shape[2:]
    b = jnp.bfloat16
    V = pltpu.VMEM
    return pl.pallas_call(
        plane_scatter_kernel,
        out_shape=jax.ShapeDtypeStruct((r, w), jnp.float32),
        in_specs=[pl.BlockSpec(memory_space=ANY)],
        out_specs=pl.BlockSpec(memory_space=pltpu.VMEM),
        scratch_shapes=[
            V((4, r, w), b),
            V((4, r, w), b),
            V((4, r, w), b),
            V((2, r // 2, w), b),
            V((2, r // 2, w), b),
            V((2, r // 2, w), b),
            V((r // 2, w), b),
            V((r // 2, w), b),
            DMA((4,)),
            DMA((4,)),
            DMA((4,)),
            DMA((6,)),
            DMA((6,)),
        ],
        compiler_params=pltpu.CompilerParams(collective_id=cid, has_side_effects=True, vmem_limit_bytes=40 << 20),
        name=f"plane_scatter_{cid}",
    )(part)


def line_sum_kernel(n, up, own, out, box, send, recv):
    spot = Spot()
    s = spot.s
    greet(spot, n, ("up", "dn"))
    go = "up" if up else "dn"

    def sends(t):
        return ((s - t >= 0) & (s + 1 < n)) if up else ((s + t < n) & (s > 0))

    def receives(t):
        return s - 1 - t >= 0 if up else s + 1 + t < n

    def copy(t):
        src = own if t == 0 else box.at[t - 1]
        return remote(src, box.at[t], send.at[t], recv.at[t], spot.to(go))

    @pl.when(sends(0))
    def _():
        copy(0).start()

    out[...] = jnp.zeros_like(out)
    for t in range(n - 1):

        @pl.when(receives(t))
        def _():
            copy(t).wait_recv()
            if t + 1 < n - 1:

                @pl.when(sends(t + 1))
                def _():
                    copy(t + 1).start()

            out[...] += box[t].astype(jnp.float32)

    for t in range(n - 1):

        @pl.when(sends(t))
        def _():
            copy(t).wait_send()


def line_sum(n, own, up, cid):
    DMA = pltpu.SemaphoreType.DMA
    return pl.pallas_call(
        functools.partial(line_sum_kernel, n, up),
        out_shape=jax.ShapeDtypeStruct(own.shape, jnp.float32),
        in_specs=[pl.BlockSpec(memory_space=pltpu.VMEM)],
        out_specs=pl.BlockSpec(memory_space=pltpu.VMEM),
        scratch_shapes=[pltpu.VMEM((n - 1,) + own.shape, own.dtype), DMA((n - 1,)), DMA((n - 1,))],
        compiler_params=pltpu.CompilerParams(collective_id=cid, has_side_effects=True, vmem_limit_bytes=40 << 20),
        name=f"line_sum_{cid}",
    )(own)
def plane_total_kernel(
    n, shared, part, out, mine, core_in, xin, yin, t2, xin2, yin2, line, c_send, c_recv, p_send, p_recv, z_send, z_recv, g_send, g_recv
):
    spot = Spot()
    s, d = spot.s, spot.d
    h = out.shape[1] // 2
    A, B = pl.ds(0, h), pl.ds(h, h)
    f32, b16 = jnp.float32, jnp.bfloat16
    mine[...] = part[...].astype(b16)
    greet(spot, n, ("x", "y", "c", "up", "dn"))
    core = remote(mine.at[pl.ds(0, shared)], core_in, c_send, c_recv, spot.to("c"))
    core.start()
    core.wait()
    mine[:shared] = (mine[:shared].astype(f32) + core_in[...].astype(f32)).astype(b16)

    def block(who, part):
        return mine.at[pl.ds(who * 2 * h + part * h, h)]

    def read(who, part):
        return mine[pl.ds(who * 2 * h + part * h, h)].astype(f32)

    first = (
        remote(block(spot.diag, 0), xin.at[1], p_send.at[0], p_recv.at[0], spot.to("x")),
        remote(block(spot.diag, 1), yin.at[1], p_send.at[1], p_recv.at[1], spot.to("y")),
        remote(block(spot.x, 0), xin.at[0], p_send.at[2], p_recv.at[2], spot.to("x")),
        remote(block(spot.y, 1), yin.at[0], p_send.at[3], p_recv.at[3], spot.to("y")),
    )
    for c in first:
        c.start()
    second = (
        remote(t2.at[0], yin2, p_send.at[4], p_recv.at[4], spot.to("y")),
        remote(t2.at[1], xin2, p_send.at[5], p_recv.at[5], spot.to("x")),
    )
    first[0].wait_recv()
    t2[0] = (read(spot.y, 0) + xin[1].astype(f32)).astype(b16)
    second[0].start()
    first[1].wait_recv()
    t2[1] = (read(spot.x, 1) + yin[1].astype(f32)).astype(b16)
    second[1].start()
    first[2].wait_recv()
    first[3].wait_recv()
    second[0].wait_recv()
    line[s, A] = (read(d, 0) + xin[0].astype(f32) + yin2[...].astype(f32)).astype(b16)
    second[1].wait_recv()
    line[s, B] = (read(d, 1) + yin[0].astype(f32) + xin2[...].astype(f32)).astype(b16)

    def sends(up, t):
        return ((s - t >= 0) & (s + 1 < n)) if up else ((s + t < n) & (s > 0))

    def receives(up, t):
        return s - 1 - t >= 0 if up else s + 1 + t < n

    def z_copy(up, t, sending):
        way = 0 if up else 1
        piece = (s - t if up else s + t) if sending else (s - 1 - t if up else s + 1 + t)
        return remote(line.at[piece], line.at[piece], z_send.at[way, t], z_recv.at[way, t], spot.to("up" if up else "dn"))

    for up in (True, False):

        @pl.when(sends(up, 0))
        def _():
            z_copy(up, 0, True).start()

    for t in range(n - 1):
        for up in (True, False):

            @pl.when(receives(up, t))
            def _():
                z_copy(up, t, False).wait_recv()
                if t + 1 < n - 1:

                    @pl.when(sends(up, t + 1))
                    def _():
                        z_copy(up, t + 1, True).start()

    total = line[0].astype(f32)
    for i in range(1, n):
        total = total + line[i].astype(f32)
    out[d] = total.astype(b16)

    parts = (A, B)

    def back(kind, sending):
        who = (d, d, spot.y, spot.x)[kind] if sending else (spot.x, spot.y, spot.diag, spot.diag)[kind]
        ref = out.at[who] if kind < 2 else out.at[who, parts[kind - 2]]
        return remote(ref, ref, g_send.at[kind], g_recv.at[kind], spot.to("xyxy"[kind]))

    back(0, True).start()
    back(1, True).start()
    back(0, False).wait_recv()
    back(3, True).start()
    back(1, False).wait_recv()
    back(2, True).start()
    back(2, False).wait_recv()
    back(3, False).wait_recv()
    for kind in range(4):
        back(kind, True).wait_send()
    for c in first + second:
        c.wait_send()
    for t in range(n - 1):
        for up in (True, False):

            @pl.when(sends(up, t))
            def _():
                z_copy(up, t, True).wait_send()


def plane_total(n, part, shared, cid):
    DMA = pltpu.SemaphoreType.DMA
    V = pltpu.VMEM
    b = jnp.bfloat16
    rows, w = part.shape
    h = rows // 8
    return pl.pallas_call(
        functools.partial(plane_total_kernel, n, shared),
        out_shape=jax.ShapeDtypeStruct((4, 2 * h, w), b),
        in_specs=[pl.BlockSpec(memory_space=pltpu.VMEM)],
        out_specs=pl.BlockSpec(memory_space=pltpu.VMEM),
        scratch_shapes=[
            V((rows, w), b),
            V((shared, w), b),
            V((2, h, w), b),
            V((2, h, w), b),
            V((2, h, w), b),
            V((h, w), b),
            V((h, w), b),
            V((n, 2 * h, w), b),
            DMA,
            DMA,
            DMA((6,)),
            DMA((6,)),
            DMA((2, n - 1)),
            DMA((2, n - 1)),
            DMA((4,)),
            DMA((4,)),
        ],
        compiler_params=pltpu.CompilerParams(collective_id=cid, has_side_effects=True, vmem_limit_bytes=40 << 20),
        name=f"plane_total_{cid}",
    )(part)


SPAN, TILE = 64, 128
REACH = TILE + SPAN


def mm(left, right, contract=((1,), (0,))):
    return lax.dot_general(left, right, (contract, ((), ())), preferred_element_type=jnp.float32)


def halves(shape, value):
    r = lax.broadcasted_iota(jnp.int32, shape, 0) // 64
    c = lax.broadcasted_iota(jnp.int32, shape, 1) // 64
    return jnp.where(r == c, value, 0.0).astype(jnp.bfloat16)


def signed_map(matrix):
    return jnp.concatenate([matrix, -matrix], 1)


def maps_of(logits):
    left = lax.broadcasted_iota(jnp.int32, logits.shape, 1) < 64
    low = jnp.max(jnp.where(left, logits, -jnp.inf), -1, keepdims=True)
    high = jnp.max(jnp.where(left, -jnp.inf, logits), -1, keepdims=True)
    e = jnp.exp(logits - jnp.where(left, low, high))
    sums = mm(e.astype(jnp.bfloat16), halves((128, 128), 1.0))
    return e / sums


def maps_back(maps, dmaps):
    p = (maps * dmaps).astype(jnp.bfloat16)
    return maps * (dmaps - mm(p, halves((128, 128), 1.0)))


def with_ones(values, first):
    rows = values.shape[0]
    r = lax.broadcasted_iota(jnp.int32, (rows, 64), 0)
    c = lax.broadcasted_iota(jnp.int32, (rows, 64), 1)
    ones = jnp.where((c == 0) & (r >= first), 1.0, 0.0).astype(jnp.bfloat16)
    return jnp.concatenate([values, ones], 1)


def pick(column):
    r = lax.broadcasted_iota(jnp.int32, (8, 128), 0)
    c = lax.broadcasted_iota(jnp.int32, (8, 128), 1)
    return jnp.where((r == 0) & (c == column), 1.0, 0.0).astype(jnp.bfloat16)


def identity():
    r = lax.broadcasted_iota(jnp.int32, (128, 128), 0)
    c = lax.broadcasted_iota(jnp.int32, (128, 128), 1)
    return jnp.where(r == c, 1.0, 0.0).astype(jnp.bfloat16)


def start_row():
    return jnp.where(lax.axis_index("seq") == 0, SPAN, 0)


def key_state_kernel(kv, kmaps, out):
    first = start_row()
    b16 = jnp.bfloat16
    out[512:] = jnp.zeros((16, 128), b16)
    for e in range(2):
        for gp in range(2):
            parts = []
            for j in range(2):
                g = 2 * gp + j
                keys = kv[e, :256, g * 64 : g * 64 + 64]
                values = with_ones(kv[e, :256, 256 + g * 64 : 320 + g * 64], first)
                feats = maps_of(mm(keys, signed_map(kmaps[g]))).astype(b16)
                state = mm(feats, values, ((0,), (0,)))
                parts.append(state[:, :64])
                total = mm(pick(64), state.astype(b16), ((1,), (1,)))
                out[512 + e * 4 + g : 513 + e * 4 + g] = total[:1].astype(b16)
            block = jnp.concatenate(parts, 1).astype(b16)
            out[(e * 2 + gp) * 128 : (e * 2 + gp) * 128 + 128] = block


def key_state(kv_ext, kmaps):
    return pl.pallas_call(
        key_state_kernel,
        out_shape=jax.ShapeDtypeStruct((528, 128), jnp.bfloat16),
        in_specs=[pl.BlockSpec(memory_space=pltpu.VMEM)] * 2,
        out_specs=pl.BlockSpec(memory_space=pltpu.VMEM),
        compiler_params=pltpu.CompilerParams(vmem_limit_bytes=40 << 20),
        name="key_state",
    )(kv_ext, kmaps)


def masks():
    r = lax.broadcasted_iota(jnp.int32, (TILE, REACH), 0)
    c = lax.broadcasted_iota(jnp.int32, (TILE, REACH), 1)
    return (c > r) & (c <= r + SPAN), c <= r


def state_of(states, totals, e, gp, j):
    b16 = jnp.bfloat16
    column = mm(identity(), totals[...].astype(b16), ((1,), (1,)))
    row = e * 4 + 2 * gp + j
    pickcol = lax.broadcasted_iota(jnp.int32, column.shape, 1) == row
    one = jnp.sum(jnp.where(pickcol, column, 0.0), -1, keepdims=True)
    c = lax.broadcasted_iota(jnp.int32, (128, 64), 1)
    return jnp.concatenate([states[:, j * 64 : j * 64 + 64], jnp.where(c == 0, one, 0.0)], 1)


def attend_kernel(q, k, v, st, tot, qmaps, kmaps, out):
    gp, e = pl.program_id(0), pl.program_id(1)
    first = start_row()
    b16 = jnp.bfloat16
    window, older = masks()
    for j in range(2):
        keys = k[0, :, j * 64 : j * 64 + 64]
        values = with_ones(v[0, :, j * 64 : j * 64 + 64], first)
        kfeats = maps_of(mm(keys, signed_map(kmaps[j]))).astype(b16)
        keys8 = keys * jnp.asarray(0.125, b16)
        state = state_of(st, tot, e, gp, j)
        for i in range(2):
            if i:
                state = state + mm(kfeats[:TILE], values[:TILE], ((0,), (0,)))
            state16 = state.astype(b16)
            reach = slice(i * TILE, i * TILE + REACH)
            for h in range(0, 4, 2):
                pair = []
                for hh in (h, h + 1):
                    col = (j * 4 + hh) * 64
                    query = q[i * TILE : (i + 1) * TILE, col : col + 64]
                    qfeats = maps_of(mm(query, signed_map(qmaps[j * 4 + hh]))).astype(b16)
                    near = mm(query, keys8[reach], ((1,), (1,)))
                    far = mm(qfeats, kfeats[reach], ((1,), (1,)))
                    weights = jnp.where(window, jnp.exp(jnp.where(window, near, 0.0)), jnp.where(older, far, 0.0))
                    both = mm(weights.astype(b16), values[reach]) + mm(qfeats, state16)
                    pair.append(both[:, :64] / both[:, 64:65])
                col = (j * 4 + h) * 64
                out[i * TILE : (i + 1) * TILE, col : col + 128] = jnp.concatenate(pair, 1).astype(b16)


def attend(q, kv_ext, st, qmaps, kmaps):
    return pl.pallas_call(
        attend_kernel,
        grid=(2, 2),
        out_shape=jax.ShapeDtypeStruct(q.shape, jnp.bfloat16),
        in_specs=[
            pl.BlockSpec((256, 512), lambda g, e: (e, g)),
            pl.BlockSpec((1, 320, 128), lambda g, e: (e, 0, g)),
            pl.BlockSpec((1, 320, 128), lambda g, e: (e, 0, 2 + g)),
            pl.BlockSpec((128, 128), lambda g, e: (e * 2 + g, 0)),
            pl.BlockSpec((16, 128), lambda g, e: (32, 0)),
            pl.BlockSpec((8, 64, 64), lambda g, e: (g, 0, 0)),
            pl.BlockSpec((2, 64, 64), lambda g, e: (g, 0, 0)),
        ],
        out_specs=pl.BlockSpec((256, 512), lambda g, e: (e, g)),
        compiler_params=pltpu.CompilerParams(vmem_limit_bytes=40 << 20),
        name="attend",
    )(q, kv_ext, kv_ext, st, st, qmaps, kmaps)


def attend_back_kernel(q, k, v, st, tot, qmaps, kmaps, dattn, dq, dk, dv, dkf, dst, dtot, dqm):
    gp, e = pl.program_id(0), pl.program_id(1)
    first = start_row()
    b16, f32 = jnp.bfloat16, jnp.float32
    window, older = masks()
    eighth = jnp.asarray(0.125, b16)
    dk[...] = jnp.zeros_like(dk)
    dv[...] = jnp.zeros_like(dv)
    dkf[...] = jnp.zeros_like(dkf)

    @pl.when(e == 0)
    def _():
        dqm[...] = jnp.zeros_like(dqm)

    dstates = []
    for j in range(2):
        keys = k[0, :, j * 64 : j * 64 + 64]
        values = with_ones(v[0, :, j * 64 : j * 64 + 64], first)
        kfeats = maps_of(mm(keys, signed_map(kmaps[j]))).astype(b16)
        keys8 = keys * eighth
        state = state_of(st, tot, e, gp, j)
        gsum = None
        for i in range(2):
            if i:
                state = state + mm(kfeats[:TILE], values[:TILE], ((0,), (0,)))
            state16 = state.astype(b16)
            reach = slice(i * TILE, i * TILE + REACH)
            rows = slice(i * TILE, (i + 1) * TILE)
            dvalue = dkey = dkfeat = g = None
            for h in range(0, 4, 2):
                dqs = []
                for hh in (h, h + 1):
                    head = j * 4 + hh
                    query = q[rows, head * 64 : head * 64 + 64]
                    grad = dattn[rows, head * 64 : head * 64 + 64].astype(f32)
                    signed = signed_map(qmaps[head])
                    qmap = maps_of(mm(query, signed))
                    qfeats = qmap.astype(b16)
                    near = mm(query, keys8[reach], ((1,), (1,)))
                    far = mm(qfeats, kfeats[reach], ((1,), (1,)))
                    close = jnp.where(window, jnp.exp(jnp.where(window, near, 0.0)), 0.0)
                    weights = (close + jnp.where(older, far, 0.0)).astype(b16)
                    both = mm(weights, values[reach]) + mm(qfeats, state16)
                    inv = 1.0 / both[:, 64:65]
                    grad = grad * inv
                    c = jnp.sum(grad * both[:, :64], -1, keepdims=True) * inv
                    lane = lax.broadcasted_iota(jnp.int32, (TILE, 64), 1)
                    grad1 = jnp.concatenate([grad, jnp.where(lane == 0, -c, 0.0)], 1).astype(b16)
                    dweights = mm(grad1, values[reach], ((1,), (1,)))
                    ds = (close * dweights).astype(b16)
                    dl = jnp.where(older, dweights, 0.0).astype(b16)
                    dqmap = mm(dl, kfeats[reach]) + mm(grad1, state16, ((1,), (1,)))
                    da = maps_back(qmap, dqmap).astype(b16)
                    dqs.append(mm(ds, keys8[reach]) + mm(da, signed, ((1,), (1,))))
                    x = mm(query, da, ((0,), (0,)))
                    dqm[head] += x[:, :64] - x[:, 64:]
                    a1 = mm(weights, grad1, ((0,), (0,)))
                    a2 = mm(ds, query * eighth, ((0,), (0,)))
                    a3 = mm(dl, qfeats, ((0,), (0,)))
                    a4 = mm(qfeats, grad1, ((0,), (0,)))
                    if dvalue is None:
                        dvalue, dkey, dkfeat, g = a1, a2, a3, a4
                    else:
                        dvalue, dkey, dkfeat, g = dvalue + a1, dkey + a2, dkfeat + a3, g + a4
                col = (j * 4 + h) * 64
                dq[rows, col : col + 128] = jnp.concatenate(dqs, 1).astype(b16)
            dv[0, reach, j * 64 : j * 64 + 64] += dvalue[:, :64]
            dk[0, reach, j * 64 : j * 64 + 64] += dkey
            dkf[0, j, reach] += dkfeat
            if i:
                g16 = g.astype(b16)
                dkf[0, j, :TILE] += mm(values[:TILE], g16, ((1,), (1,)))
                dv[0, :TILE, j * 64 : j * 64 + 64] += mm(kfeats[:TILE], g16)[:, :64]
            gsum = g if gsum is None else gsum + g
        dstates.append(gsum[:, :64])
        dtot[0, 0, j * 8 : j * 8 + 8] = mm(pick(64), gsum.astype(b16), ((1,), (1,))).astype(b16)
    dst[...] = jnp.concatenate(dstates, 1).astype(b16)


def attend_back(q, kv_ext, st, qmaps, kmaps, dattn):
    f32, b16 = jnp.float32, jnp.bfloat16
    e2, ext = kv_ext.shape[:2]
    return pl.pallas_call(
        attend_back_kernel,
        grid=(2, 2),
        out_shape=[
            jax.ShapeDtypeStruct(q.shape, b16),
            jax.ShapeDtypeStruct((e2, ext, 256), f32),
            jax.ShapeDtypeStruct((e2, ext, 256), f32),
            jax.ShapeDtypeStruct((e2, 4, ext, 128), f32),
            jax.ShapeDtypeStruct((512, 128), b16),
            jax.ShapeDtypeStruct((2, 2, 16, 128), b16),
            jax.ShapeDtypeStruct((16, 64, 64), f32),
        ],
        in_specs=[
            pl.BlockSpec((256, 512), lambda g, e: (e, g)),
            pl.BlockSpec((1, 320, 128), lambda g, e: (e, 0, g)),
            pl.BlockSpec((1, 320, 128), lambda g, e: (e, 0, 2 + g)),
            pl.BlockSpec((128, 128), lambda g, e: (e * 2 + g, 0)),
            pl.BlockSpec((16, 128), lambda g, e: (32, 0)),
            pl.BlockSpec((8, 64, 64), lambda g, e: (g, 0, 0)),
            pl.BlockSpec((2, 64, 64), lambda g, e: (g, 0, 0)),
            pl.BlockSpec((256, 512), lambda g, e: (e, g)),
        ],
        out_specs=[
            pl.BlockSpec((256, 512), lambda g, e: (e, g)),
            pl.BlockSpec((1, 320, 128), lambda g, e: (e, 0, g)),
            pl.BlockSpec((1, 320, 128), lambda g, e: (e, 0, g)),
            pl.BlockSpec((1, 2, 320, 128), lambda g, e: (e, g, 0, 0)),
            pl.BlockSpec((128, 128), lambda g, e: (e * 2 + g, 0)),
            pl.BlockSpec((1, 1, 16, 128), lambda g, e: (e, g, 0, 0)),
            pl.BlockSpec((8, 64, 64), lambda g, e: (g, 0, 0)),
        ],
        compiler_params=pltpu.CompilerParams(vmem_limit_bytes=40 << 20),
        name="attend_back",
    )(q, kv_ext, kv_ext, st, st, qmaps, kmaps, dattn)


def key_back_kernel(k, v, later, tot, kmaps, dk_in, dv_in, dkf, dk, dv, dkm):
    gp, e = pl.program_id(0), pl.program_id(1)
    first = start_row()
    b16 = jnp.bfloat16

    @pl.when(e == 0)
    def _():
        dkm[...] = jnp.zeros_like(dkm)

    dks, dvs = [], []
    for j in range(2):
        cols = slice(j * 64, j * 64 + 64)
        keys = k[0, :, cols]
        values = with_ones(v[0, :, cols], first)
        signed = signed_map(kmaps[j])
        kmap = maps_of(mm(keys, signed))
        g = state_of(later, tot, e, gp, j).astype(b16)
        more = mm(values[:256], g, ((1,), (1,)))
        dmap = jnp.concatenate([dkf[0, j, :256] + more, dkf[0, j, 256:]], 0)
        da = maps_back(kmap, dmap).astype(b16)
        dks.append(dk_in[0, :, cols] + mm(da, signed, ((1,), (1,))))
        moved = mm(kmap[:256].astype(b16), g)[:, :64]
        dvs.append(jnp.concatenate([dv_in[0, :256, cols] + moved, dv_in[0, 256:, cols]], 0))
        x = mm(keys, da, ((0,), (0,)))
        dkm[j] += x[:, :64] - x[:, 64:]
    dk[0] = jnp.concatenate(dks, 1)
    dv[0] = jnp.concatenate(dvs, 1)


def key_back(kv_ext, later, kmaps, dk, dv, dkf):
    f32 = jnp.float32
    piece = pl.BlockSpec((1, 320, 128), lambda g, e: (e, 0, g))
    return pl.pallas_call(
        key_back_kernel,
        grid=(2, 2),
        out_shape=[
            jax.ShapeDtypeStruct(dk.shape, f32),
            jax.ShapeDtypeStruct(dv.shape, f32),
            jax.ShapeDtypeStruct((4, 64, 64), f32),
        ],
        in_specs=[
            piece,
            pl.BlockSpec((1, 320, 128), lambda g, e: (e, 0, 2 + g)),
            pl.BlockSpec((128, 128), lambda g, e: (e * 2 + g, 0)),
            pl.BlockSpec((16, 128), lambda g, e: (32, 0)),
            pl.BlockSpec((2, 64, 64), lambda g, e: (g, 0, 0)),
            piece,
            piece,
            pl.BlockSpec((1, 2, 320, 128), lambda g, e: (e, g, 0, 0)),
        ],
        out_specs=[piece, piece, pl.BlockSpec((2, 64, 64), lambda g, e: (g, 0, 0))],
        compiler_params=pltpu.CompilerParams(vmem_limit_bytes=40 << 20),
        name="key_back",
    )(kv_ext, kv_ext, later, later, kmaps, dk, dv, dkf)


CHUNKS = 4


def feed_kernel(n, k, early, xn_own, ct_own, packed, gate, up, down, dxn, out_part, *scratch):
    (xn, ct, gw, uw, dw, da, oa, xin, yin, t2, xin2, yin2) = scratch[:12]
    (o_sem, a_send, a_recv, w_sem, w_send, w_recv, z_sem, z_send, z_recv, c_send, c_recv, p_send, p_recv, st_sem) = scratch[12:]
    spot = Spot()
    s, m, d = spot.s, spot.m, spot.d
    f32, b16 = jnp.float32, jnp.bfloat16
    unit = gw.shape[3] // 2
    wd = min(unit, k)
    gs, ds = unit // wd, k // wd
    half = xn.shape[1] // 2
    A, B = pl.ds(0, half), pl.ds(half, half)

    own = [pltpu.make_async_copy(xn_own, xn.at[3], o_sem.at[0]), pltpu.make_async_copy(ct_own, ct.at[3], o_sem.at[1])]
    for c in own:
        c.start()

    lanes = pl.ds(pl.multiple_of(m * unit, unit), unit)

    def own_piece(q):
        start = pl.multiple_of(d * (CHUNKS * unit) + q * unit, unit)
        return (
            (gate.at[:, pl.ds(start, unit)], gw.at[q, s, :, lanes]),
            (up.at[:, pl.ds(start, unit)], uw.at[q, s, :, lanes]),
            (down.at[pl.ds(start, unit)], dw.at[q, s, lanes]),
        )

    def piece(q, w, who):
        return (gw.at[q, who, :, lanes], uw.at[q, who, :, lanes], dw.at[q, who, lanes])[w]

    late = tuple(range(early, CHUNKS))
    own_weights = [
        pltpu.make_async_copy(src, dst, z_sem.at[i, w])
        for i, q in enumerate(late)
        for w, (src, dst) in enumerate(own_piece(q))
    ]
    for c in own_weights:
        c.start()

    def early_parts(q):
        parts = []
        at = 0
        for ref in (gw, uw):
            for i in range(gs):
                cols = pl.ds(pl.multiple_of(m * unit + i * wd, wd), wd)
                parts.append((packed.at[:, q, pl.ds(at, k)], ref.at[q, :, :, cols]))
                at += k
        for i in range(ds):
            parts.append((packed.at[:, q, pl.ds(at, unit)], dw.at[q, :, lanes, pl.ds(i * wd, wd)]))
            at += unit
        return parts

    early_own = [
        [pltpu.make_async_copy(src, dst, w_sem.at[q, i]) for i, (src, dst) in enumerate(early_parts(q))]
        for q in range(early)
    ]
    for copies in early_own:
        for c in copies:
            c.start()

    greet(spot, n, ("x", "y", "c", "up", "dn"))

    def block_copy(a, kind, sending):
        ref, src_own = ((xn, xn_own), (ct, ct_own))[a]
        if kind < 2:
            dst = ref.at[kind + 1]
            src = src_own if sending else dst
        else:
            rows = (A, B)[kind - 2]
            dst = ref.at[0, rows]
            src = ref.at[(2, 1)[kind - 2], rows] if sending else dst
        return remote(src, dst, a_send.at[a, kind], a_recv.at[a, kind], spot.to("xyxy"[kind]))

    for a in range(2):
        block_copy(a, 0, True).start()
        block_copy(a, 1, True).start()

    def sends(upward, t):
        return ((s - t >= 0) & (s + 1 < n)) if upward else ((s + t < n) & (s > 0))

    def receives(upward, t):
        return s - 1 - t >= 0 if upward else s + 1 + t < n

    def z_copy(i, w, upward, t, sending):
        q = late[i]
        way = 0 if upward else 1
        who = (s - t if upward else s + t) if sending else (s - 1 - t if upward else s + 1 + t)
        dst = piece(q, w, who)
        src = own_piece(q)[w][0] if (t == 0 and sending) else dst
        return remote(src, dst, z_send.at[i, w, way, t], z_recv.at[i, w, way, t], spot.to("up" if upward else "dn"))

    for i in range(len(late)):
        for w in range(3):
            for upward in (True, False):

                @pl.when(sends(upward, 0))
                def _():
                    z_copy(i, w, upward, 0, True).start()

    def early_core(q):
        return [
            remote(src, dst, w_send.at[q, i], w_recv.at[q, i], spot.to("c")) for i, (src, dst) in enumerate(early_parts(q))
        ]

    def theirs(q, w, who):
        other = pl.ds(pl.multiple_of((1 - m) * unit, unit), unit)
        return (gw.at[q, who, :, other], uw.at[q, who, :, other], dw.at[q, who, other])[w]

    def core_copy(i, w, who, sending):
        q = late[i]
        ref = piece(q, w, who) if sending else theirs(q, w, who)
        return remote(ref, ref, c_send.at[i, w, who], c_recv.at[i, w, who], spot.to("c"))

    for q in range(early):
        for c in early_core(q):
            c.start()

    def relay(i, t):
        for w in range(3):
            for upward in (True, False):

                @pl.when(receives(upward, t))
                def _():
                    z_copy(i, w, upward, t, False).wait_recv()
                    if t + 1 < n - 1:

                        @pl.when(sends(upward, t + 1))
                        def _():
                            z_copy(i, w, upward, t + 1, True).start()

                    core_copy(i, w, s - 1 - t if upward else s + 1 + t, True).start()

    for i in range(len(late)):
        for w in range(3):
            own_weights[3 * i + w].wait()
            core_copy(i, w, s, True).start()

    for c in own:
        c.wait()

    first = (
        remote(xn.at[0, A], xin.at[1], p_send.at[0], p_recv.at[0], spot.to("x")),
        remote(xn.at[0, B], yin.at[1], p_send.at[1], p_recv.at[1], spot.to("y")),
        remote(xn.at[1, A], xin.at[0], p_send.at[2], p_recv.at[2], spot.to("x")),
        remote(xn.at[2, B], yin.at[0], p_send.at[3], p_recv.at[3], spot.to("y")),
    )
    stores = [pltpu.make_async_copy(ct.at[i], out_part.at[i], st_sem.at[i]) for i in range(4)]

    steps = 4 * CHUNKS
    turns = {}
    total = len(late) * (n - 1)
    for j in range(total):
        i, t = j // (n - 1), j % (n - 1)
        at = min(4 * late[i], 2 + (4 * late[i] - 2) * (j + 1) // (i * (n - 1) + n - 1))
        turns.setdefault(at, []).append((i, t))

    @pl.loop(0, steps)
    def _(step):
        c = step // 4
        last = step >= steps - 4
        t = jnp.where(last, step % 4, 3 - step % 4)

        for q in range(early):

            @pl.when(step == 4 * q)
            def _():
                for copy in early_own[q]:
                    copy.wait()
                for copy in early_core(q):
                    copy.wait_recv()

        for at, jobs in turns.items():

            @pl.when(step == at)
            def _():
                for i, t in jobs:
                    relay(i, t)

        for i, q in enumerate(late):

            @pl.when(step == 4 * q)
            def _():
                for w in range(3):
                    for who in range(n):
                        core_copy(i, w, who, False).wait_recv()

        @pl.when(step == 1)
        def _():
            for a in range(2):
                block_copy(a, 1, False).wait_recv()
                block_copy(a, 2, True).start()
                block_copy(a, 0, False).wait_recv()
                block_copy(a, 3, True).start()

        @pl.when(step == 3)
        def _():
            for a in range(2):
                for kind in (2, 3):
                    block_copy(a, kind, False).wait_recv()
                for kind in range(4):
                    block_copy(a, kind, True).wait_send()

        x, cot = xn[t], ct[t]
        g_all = gw[c].reshape(n * k, 2 * unit)
        u_all = uw[c].reshape(n * k, 2 * unit)
        g = mm(x, g_all)
        u = mm(x, u_all)
        dh = mm(cot[:, :k], dw[c, 0], ((1,), (1,)))
        for i in range(1, n):
            dh = dh + mm(cot[:, i * k : (i + 1) * k], dw[c, i], ((1,), (1,)))
        sig = 1.0 / (1.0 + jnp.exp(-g))
        act = g * sig
        hid = (act * u).astype(b16)
        dg = (dh * u * sig * (1.0 + g * (1.0 - sig))).astype(b16)
        du = (dh * act).astype(b16)
        for i in range(n):
            cols = slice(i * k, (i + 1) * k)
            o = mm(hid, dw[c, i])
            e = mm(dg, gw[c, i], ((1,), (1,))) + mm(du, uw[c, i], ((1,), (1,)))

            @pl.when(step < 4)
            def _():
                oa[t, :, cols] = o
                da[t, :, cols] = e

            @pl.when(step >= 4)
            def _():
                oa[t, :, cols] += o
                da[t, :, cols] += e

        @pl.when(last)
        def _():
            xn[t] = da[t].astype(b16)
            ct[t] = oa[t].astype(b16)

        for i in range(4):

            @pl.when(step == steps - 4 + i)
            def _():
                stores[i].start()
                if i == 0:
                    first[0].start()
                    first[1].start()
                elif i < 3:
                    first[i + 1].start()

    second = (
        remote(t2.at[0], yin2, p_send.at[4], p_recv.at[4], spot.to("y")),
        remote(t2.at[1], xin2, p_send.at[5], p_recv.at[5], spot.to("x")),
    )
    first[0].wait_recv()
    t2[0] = (xn[2, A].astype(f32) + xin[1].astype(f32)).astype(b16)
    second[0].start()
    first[1].wait_recv()
    t2[1] = (xn[1, B].astype(f32) + yin[1].astype(f32)).astype(b16)
    second[1].start()
    first[2].wait_recv()
    first[3].wait_recv()
    second[0].wait_recv()
    dxn[A] = da[3, A] + xin[0].astype(f32) + yin2[...].astype(f32)
    second[1].wait_recv()
    dxn[B] = da[3, B] + yin[0].astype(f32) + xin2[...].astype(f32)

    for c in stores:
        c.wait()
    for c in first + second:
        c.wait_send()
    for q in range(early):
        for c in early_core(q):
            c.wait_send()
    for i in range(len(late)):
        for w in range(3):
            for who in range(n):
                core_copy(i, w, who, True).wait_send()
            for t in range(n - 1):
                for upward in (True, False):

                    @pl.when(sends(upward, t))
                    def _():
                        z_copy(i, w, upward, t, True).wait_send()


def feed(n, early, xn_own, ct_own, packed, gate, up, down, cid):
    DMA, V = pltpu.SemaphoreType.DMA, pltpu.VMEM
    b, f32 = jnp.bfloat16, jnp.float32
    r, w = xn_own.shape
    k = gate.shape[0]
    unit = gate.shape[1] // (4 * CHUNKS)
    wd = min(unit, k)
    pieces = 2 * (unit // wd) + k // wd
    late = CHUNKS - early
    scratch = [V((4, r, w), b), V((4, r, w), b)]
    scratch += [V((CHUNKS, n, k, 2 * unit), b), V((CHUNKS, n, k, 2 * unit), b), V((CHUNKS, n, 2 * unit, k), b)]
    scratch += [V((4, r, w), f32), V((4, r, w), f32)]
    scratch += [V((2, r // 2, w), b), V((2, r // 2, w), b), V((2, r // 2, w), b), V((r // 2, w), b), V((r // 2, w), b)]
    scratch += [DMA((2,)), DMA((2, 4)), DMA((2, 4))]
    scratch += [DMA((max(early, 1), pieces))] * 3
    scratch += [DMA((late, 3)), DMA((late, 3, 2, n - 1)), DMA((late, 3, 2, n - 1)), DMA((late, 3, n)), DMA((late, 3, n))]
    scratch += [DMA((6,)), DMA((6,)), DMA((4,))]
    return pl.pallas_call(
        functools.partial(feed_kernel, n, k, early),
        out_shape=[jax.ShapeDtypeStruct((r, w), f32), jax.ShapeDtypeStruct((4, r, w), b)],
        in_specs=[pl.BlockSpec(memory_space=ANY)] * 6,
        out_specs=[pl.BlockSpec(memory_space=pltpu.VMEM), pl.BlockSpec(memory_space=ANY)],
        scratch_shapes=scratch,
        compiler_params=pltpu.CompilerParams(collective_id=cid, has_side_effects=True, vmem_limit_bytes=62 << 20),
        name="feed",
    )(xn_own, ct_own, packed, gate, up, down)


def pack_early(k, early, gate, up, down, d):
    unit = gate.shape[1] // (4 * CHUNKS)
    wd = min(unit, k)
    at = d * (CHUNKS * unit)
    g = lax.dynamic_slice_in_dim(gate, at, early * unit, 1)
    u = lax.dynamic_slice_in_dim(up, at, early * unit, 1)
    dn = lax.dynamic_slice_in_dim(down, at, early * unit, 0)
    chunks = []
    for q in range(early):
        rows = [a[:, q * unit + i : q * unit + i + wd] for a in (g, u) for i in range(0, unit, wd)]
        rows += [dn[q * unit : (q + 1) * unit, i : i + wd] for i in range(0, k, wd)]
        chunks.append(jnp.concatenate(rows, 0))
    return jnp.stack(chunks)


EARLY = 3


f32, b16 = jnp.float32, jnp.bfloat16


def dot(left, right):
    return jnp.dot(left, right, preferred_element_type=f32)


def dot_t(left, right):
    return lax.dot_general(left, right, (((1,), (1,)), ((), ())), preferred_element_type=f32)


def t_dot(left, right):
    return lax.dot_general(left, right, (((0,), (0,)), ((), ())), preferred_element_type=f32)


def norm_back(inputs, inv_rms, gain, dnormed):
    return inv_rms * gain * dnormed - inputs * inv_rms**3 * jnp.mean(
        gain * dnormed * inputs, -1, keepdims=True
    )


def from_behind(value, axis, steps):
    count = lax.axis_size(axis)
    first, last = (max(0, -steps), min(count, count - steps))
    return lax.ppermute(value, axis, [(source, source + steps) for source in range(first, last)])


def swap_core(value):
    return lax.ppermute(value, "mp", [(0, 1), (1, 0)])


def per_device(
    tokens,
    cotangent,
    attention_norm_gain,
    feedforward_norm_gain,
    query_weight,
    key_weight,
    value_weight,
    output_weight,
    gate_weight,
    up_weight,
    down_weight,
    query_adapter_down,
    query_adapter_up,
    key_adapter_down,
    key_adapter_up,
    value_adapter_down,
    value_adapter_up,
    output_adapter_down,
    output_adapter_up,
    query_feature_matrix,
    key_feature_matrix,
):
    n = lax.axis_size("seq")
    position, m, d = (lax.axis_index(a) for a in ("seq", "mp", "dp"))
    seq_count, rows_here, width = tokens.shape
    total_rows = seq_count * rows_here
    half = total_rows // 2
    heads_kv = key_feature_matrix.shape[0]
    head_size = key_feature_matrix.shape[1]
    groups = query_feature_matrix.shape[0] // heads_kv
    extent = rows_here + SOFTMAX_SPAN

    packed = lax.all_gather(
        pack_early(gate_weight.shape[0], EARLY, gate_weight, up_weight, down_weight, d), "seq"
    )
    qkv_own = jnp.concatenate([query_weight, key_weight, value_weight], 1)
    qkv_g, out_g = gather_weights(n, [qkv_own, output_weight], 1)
    qkv_w = qkv_g.reshape(width, -1)
    wide = query_weight.shape[1]
    kv_wide = key_weight.shape[1]

    def my_half(a):
        return lax.dynamic_slice_in_dim(a, m * half, half, 0)

    def both_halves(own):
        other = swap_core(own)
        return jnp.concatenate([jnp.where(m == 0, own, other), jnp.where(m == 0, other, own)], 0)

    tok2 = tokens.reshape(total_rows, width)
    inputs = tok2.astype(f32)
    gain_attn = attention_norm_gain.astype(f32)
    rms_attn = lax.rsqrt(jnp.mean(inputs * inputs, -1, keepdims=True) + epsilon)
    normed = (inputs * rms_attn * gain_attn).astype(b16)

    cot2 = cotangent.reshape(total_rows, width)
    cot_half = my_half(cot2)

    downs = jnp.concatenate([query_adapter_down, key_adapter_down, value_adapter_down], 1)
    inner = dot(normed, downs)
    rank = query_adapter_down.shape[1]
    full = dot(normed, qkv_w)

    def project(index, first, last, second):
        return (
            full[:, first:last] + dot(inner[:, index * rank : (index + 1) * rank].astype(b16), second)
        ).astype(b16)

    query_half = project(0, 0, wide, query_adapter_up)
    key_half = project(1, wide, wide + kv_wide, key_adapter_up)
    value_half = project(2, wide + kv_wide, wide + 2 * kv_wide, value_adapter_up)
    key3 = key_half.reshape(seq_count, rows_here, heads_kv * head_size)
    value3 = value_half.reshape(seq_count, rows_here, heads_kv * head_size)
    kv3 = jnp.concatenate([key3, value3], -1)
    kv_prev = from_behind(kv3[:, rows_here - SOFTMAX_SPAN :], "seq", 1)
    kv_ext = jnp.concatenate([kv_prev, kv3], 1)
    states = line_sum(n, key_state(kv_ext, key_feature_matrix), True, 3)
    attn16 = attend(query_half, kv_ext, states, query_feature_matrix, key_feature_matrix)
    inner_output = dot(attn16, output_adapter_down)
    branch = jnp.concatenate([dot(attn16, out_g[i]) for i in range(n)], 1) + dot(
        inner_output.astype(b16), output_adapter_up
    )
    branch16 = branch.astype(b16)
    from_other = swap_core(lax.dynamic_slice_in_dim(branch16, (1 - m) * half, half, 0))
    resid = my_half(inputs) + my_half(branch) + from_other.astype(f32)
    gain_mlp = feedforward_norm_gain.astype(f32)
    rms_mlp = lax.rsqrt(jnp.mean(resid * resid, -1, keepdims=True) + epsilon)
    normed_mlp = (resid * rms_mlp * gain_mlp).astype(b16)
    dnormed_mlp, out_part = feed(
        n, EARLY, normed_mlp, cot_half, packed, gate_weight, up_weight, down_weight, 4
    )

    def swap_chip(value, bit):
        return lax.ppermute(value, "dp", [(i, i ^ bit) for i in range(4)])

    cut = half // 2
    upper_in = swap_chip(out_part[0:2, :cut], 1)
    lower_in = swap_chip(out_part[0::2, cut:], 2)
    upper_in2 = swap_chip((out_part[2, :cut].astype(f32) + upper_in[0].astype(f32)).astype(b16), 2)
    lower_in2 = swap_chip((out_part[1, cut:].astype(f32) + lower_in[0].astype(f32)).astype(b16), 1)
    mlp_out = out_part[3].astype(f32) + jnp.concatenate(
        [
            upper_in[1].astype(f32) + upper_in2.astype(f32),
            lower_in[1].astype(f32) + lower_in2.astype(f32),
        ],
        0,
    )
    output = both_halves((resid + mlp_out).astype(b16)).reshape(seq_count, rows_here, width)

    mlp_gain_term = jnp.sum(dnormed_mlp * resid * rms_mlp, 0)
    dresid = cot_half.astype(f32) + norm_back(resid, rms_mlp, gain_mlp, dnormed_mlp)
    dresid16 = both_halves(dresid.astype(b16))
    du_o = dot_t(dresid16, output_adapter_up)
    oup_term = t_dot(inner_output.astype(b16), dresid16)
    odown_term = t_dot(du_o.astype(b16), attn16)
    dattn = dot_t(du_o.astype(b16), output_adapter_down)
    step = output_weight.shape[1]
    for i in range(n):
        dattn = dattn + dot_t(dresid16[:, i * step : (i + 1) * step], out_g[i])
    dq16, dk_ext, dv_ext, dkfeats, dstates, dtotals, dqmaps = attend_back(
        query_half, kv_ext, states, query_feature_matrix, key_feature_matrix, dattn.astype(b16)
    )
    dtotals = jnp.pad(dtotals[:, :, ::8].reshape(-1, 128), ((0, 8), (0, 0)))
    later = line_sum(n, jnp.concatenate([dstates, dtotals], 0), False, 7)
    dk_ext, dv_ext, dkmaps = key_back(kv_ext, later, key_feature_matrix, dk_ext, dv_ext, dkfeats)
    dkv_ext = jnp.concatenate([dk_ext, dv_ext], -1)
    back = from_behind(dkv_ext[:, :SOFTMAX_SPAN].astype(b16), "seq", -1).astype(f32)
    dkv = dkv_ext[:, SOFTMAX_SPAN:]
    dkv = jnp.concatenate(
        [dkv[:, : rows_here - SOFTMAX_SPAN], dkv[:, rows_here - SOFTMAX_SPAN :] + back], 1
    )
    dqkv16 = jnp.concatenate(
        [dq16, dkv.reshape(total_rows, -1).astype(b16)], 1
    )
    bounds = ((0, wide), (wide, wide + kv_wide), (wide + kv_wide, wide + 2 * kv_wide))
    seconds = (query_adapter_up, key_adapter_up, value_adapter_up)
    dinner = jnp.concatenate(
        [dot_t(dqkv16[:, a:b], second) for (a, b), second in zip(bounds, seconds)], 1
    ).astype(b16)
    dnormed = (dot_t(dqkv16, qkv_w) + dot_t(dinner, downs)).astype(b16)
    down_terms = t_dot(dinner, normed)
    inner16 = inner.astype(b16)
    up_terms = [
        t_dot(inner16[:, i * rank : (i + 1) * rank], dqkv16[:, a:b]) for i, (a, b) in enumerate(bounds)
    ]
    from_other = swap_core(lax.dynamic_slice_in_dim(dnormed, (1 - m) * half, half, 0))
    dnormed = my_half(dnormed).astype(f32) + from_other.astype(f32)
    x_half, r_half = my_half(inputs), my_half(rms_attn)
    attn_gain_term = jnp.sum(dnormed * x_half * r_half, 0)
    tokens_grad = both_halves(dresid + norm_back(x_half, r_half, gain_attn, dnormed)).reshape(
        seq_count, rows_here, width
    )

    shared = [attn_gain_term, mlp_gain_term, down_terms, oup_term]
    split = up_terms + [odown_term, dqmaps, dkmaps]
    flat = [a.reshape(-1, 128) for a in shared + split]
    sizes = [a.shape[0] for a in flat]
    shared_rows = sum(sizes[:4])
    flat = jnp.concatenate(flat, 0)
    flat = jnp.pad(flat, ((0, -flat.shape[0] % 128), (0, 0)))
    summed = plane_total(n, flat, shared_rows, 8).reshape(-1, 128).astype(f32)
    parts, at = [], 0
    for term, size in zip(shared + split, sizes):
        parts.append(summed[at : at + size].reshape(term.shape))
        at += size
    attn_gain, mlp_gain, downs_g, oup, qup, kup, vup, odown, qmaps_g, kmaps_g = parts
    downs_g = downs_g.T
    return (
        output,
        tokens_grad,
        attn_gain,
        mlp_gain,
        downs_g[:, :rank],
        qup,
        downs_g[:, rank : 2 * rank],
        kup,
        downs_g[:, 2 * rank :],
        vup,
        odown.T,
        oup,
        qmaps_g.reshape(query_feature_matrix.shape),
        kmaps_g,
    )


def solution(mesh):
    placed = (
        P("dp", "seq", None),
        P("dp", "seq", None),
        P(),
        P(),
        P("seq", "mp"),
        P("seq", "mp"),
        P("seq", "mp"),
        P("mp", "seq"),
        P("seq", "mp"),
        P("seq", "mp"),
        P("mp", "seq"),
        P(),
        P(None, "mp"),
        P(),
        P(None, "mp"),
        P(),
        P(None, "mp"),
        P("mp", None),
        P(),
        P("mp", None, None),
        P("mp", None, None),
    )
    return jax.shard_map(
        per_device,
        mesh=mesh,
        in_specs=placed,
        out_specs=(
            P("dp", "seq", None),
            P("dp", "seq", None),
            P(),
            P(),
            P(),
            P(None, "mp"),
            P(),
            P(None, "mp"),
            P(),
            P(None, "mp"),
            P("mp", None),
            P(),
            P("mp", None, None),
            P("mp", None, None),
        ),
        check_vma=False,
    )
```

```python
import math
import functools
import jax
import jax.numpy as jnp
from jax import lax
from jax.experimental import pallas as pl
from jax.experimental.pallas import tpu as pltpu
from jax.sharding import PartitionSpec as P

SOFTMAX_SPAN = 64
epsilon = 1e-05

MESH = pl.DeviceIdType.MESH
ANY = pl.ANY


class Spot:
    def __init__(self):
        self.s, self.m, self.d = (lax.axis_index(a) for a in ("seq", "mp", "dp"))
        self.x = self.d + 1 - 2 * (self.d % 2)
        self.y = (self.d + 2) % 4
        self.diag = (self.x + 2) % 4

    def to(self, kind):
        s, m, d = self.s, self.m, self.d
        if kind == "x":
            d = self.x
        elif kind == "y":
            d = self.y
        elif kind == "c":
            m = 1 - m
        elif kind == "up":
            s = s + 1
        elif kind == "dn":
            s = s - 1
        return {"seq": s, "mp": m, "dp": d}


def remote(src, dst, send, recv, where):
    return pltpu.make_async_remote_copy(
        src_ref=src, dst_ref=dst, send_sem=send, recv_sem=recv, device_id=where, device_id_type=MESH
    )


def greet(spot, n, kinds):
    bar = pltpu.get_barrier_semaphore()
    count = 0
    for kind in kinds:
        if kind in ("up", "dn"):
            there = spot.s + 1 < n if kind == "up" else spot.s > 0

            @pl.when(there)
            def _(kind=kind):
                pl.semaphore_signal(bar, inc=1, device_id=spot.to(kind), device_id_type=MESH)

            count = count + there.astype(jnp.int32)
        else:
            pl.semaphore_signal(bar, inc=1, device_id=spot.to(kind), device_id_type=MESH)
            count = count + 1
    pl.semaphore_wait(bar, count)


def gather_weights_kernel(n, k, *refs):
    ins, block, outs, blocks = refs[:k], refs[k], refs[k + 1 : 2 * k + 1], refs[2 * k + 1]
    own_sem, z_send, z_recv, p_send, p_recv, b_send, b_recv = refs[2 * k + 2 :]
    spot = Spot()
    s, d = spot.s, spot.d
    own = [pltpu.make_async_copy(ins[a], outs[a].at[s], own_sem.at[a]) for a in range(k)]
    own.append(pltpu.make_async_copy(block, blocks.at[3], own_sem.at[k]))
    for c in own:
        c.start()
    greet(spot, n, ("x", "y", "up", "dn"))

    cut = block.shape[0] // 2
    parts = (pl.ds(0, cut), pl.ds(cut, cut))

    def block_copy(kind, sending):
        if kind < 2:
            dst = blocks.at[kind + 1]
            src = block if sending else dst
        else:
            dst = blocks.at[0, parts[kind - 2]]
            src = blocks.at[(2, 1)[kind - 2], parts[kind - 2]] if sending else dst
        return remote(src, dst, b_send.at[kind], b_recv.at[kind], spot.to("xyxy"[kind]))

    def rows(a, who, part=None):
        size = ins[a].shape[0] // 4
        if part is None:
            return pl.ds(who * size, size)
        return pl.ds(who * size + part * (size // 2), size // 2)

    def sends(up, t):
        return ((s - t >= 0) & (s + 1 < n)) if up else ((s + t < n) & (s > 0))

    def receives(up, t):
        return s - 1 - t >= 0 if up else s + 1 + t < n

    def z_copy(a, up, t, sending):
        way = 0 if up else 1
        piece = (s - t if up else s + t) if sending else (s - 1 - t if up else s + 1 + t)
        dst = outs[a].at[piece, rows(a, d)]
        src = ins[a].at[rows(a, d)] if (t == 0 and sending) else dst
        return remote(src, dst, z_send.at[a, way, t], z_recv.at[a, way, t], spot.to("up" if up else "dn"))

    def piece_of(up, t):
        return s - 1 - t if up else s + 1 + t

    def plane_copy(a, up, t, kind):
        way = 0 if up else 1
        who = (d, d, spot.y, spot.x)[kind]
        part = (None, None, 0, 1)[kind]
        ref = outs[a].at[piece_of(up, t), rows(a, who, part)]
        return remote(ref, ref, p_send.at[a, way, t, kind], p_recv.at[a, way, t, kind], spot.to("xyxy"[kind]))

    def landed(a, up, t, kind):
        way = 0 if up else 1
        who = (spot.x, spot.y, spot.diag, spot.diag)[kind]
        part = (None, None, 0, 1)[kind]
        ref = outs[a].at[piece_of(up, t), rows(a, who, part)]
        return remote(ref, ref, p_send.at[a, way, t, kind], p_recv.at[a, way, t, kind], spot.to("xyxy"[kind]))

    for a in range(k):
        for up in (True, False):

            @pl.when(sends(up, 0))
            def _():
                z_copy(a, up, 0, True).start()

    block_copy(0, True).start()
    block_copy(1, True).start()

    for t in range(n):
        if t == n - 1:
            block_copy(1, False).wait_recv()
            block_copy(2, True).start()
            block_copy(0, False).wait_recv()
            block_copy(3, True).start()
        if t < n - 1:
            for a in range(k):
                for up in (True, False):

                    @pl.when(receives(up, t))
                    def _():
                        z_copy(a, up, t, False).wait_recv()
                        if t + 1 < n - 1:

                            @pl.when(sends(up, t + 1))
                            def _():
                                z_copy(a, up, t + 1, True).start()

                        plane_copy(a, up, t, 0).start()
                        plane_copy(a, up, t, 1).start()

        if t > 0:
            for a in range(k):
                for up in (True, False):

                    @pl.when(receives(up, t - 1))
                    def _():
                        landed(a, up, t - 1, 0).wait_recv()
                        plane_copy(a, up, t - 1, 3).start()
                        landed(a, up, t - 1, 1).wait_recv()
                        plane_copy(a, up, t - 1, 2).start()

    for t in range(n - 1):
        for a in range(k):
            for up in (True, False):

                @pl.when(sends(up, t))
                def _():
                    z_copy(a, up, t, True).wait_send()

                @pl.when(receives(up, t))
                def _():
                    landed(a, up, t, 2).wait_recv()
                    landed(a, up, t, 3).wait_recv()
                    for kind in range(4):
                        plane_copy(a, up, t, kind).wait_send()

    for kind in (2, 3):
        block_copy(kind, False).wait_recv()
    for kind in range(4):
        block_copy(kind, True).wait_send()
    for c in own:
        c.wait()


def gather_weights(n, arrays, block, cid):
    k = len(arrays)
    DMA = pltpu.SemaphoreType.DMA
    return pl.pallas_call(
        functools.partial(gather_weights_kernel, n, k),
        out_shape=[jax.ShapeDtypeStruct((n,) + a.shape, a.dtype) for a in arrays]
        + [jax.ShapeDtypeStruct((4,) + block.shape, block.dtype)],
        in_specs=[pl.BlockSpec(memory_space=ANY)] * (k + 1),
        out_specs=[pl.BlockSpec(memory_space=ANY)] * (k + 1),
        scratch_shapes=[DMA((k + 1,)), DMA((k, 2, n - 1)), DMA((k, 2, n - 1)), DMA((k, 2, n - 1, 4)), DMA((k, 2, n - 1, 4)), DMA((4,)), DMA((4,))],
        compiler_params=pltpu.CompilerParams(collective_id=cid, has_side_effects=True),
        name="gather_weights",
    )(*arrays, block)


def line_sum_kernel(n, up, own, out, box, send, recv):
    spot = Spot()
    s = spot.s
    greet(spot, n, ("up", "dn"))
    go = "up" if up else "dn"

    def sends(t):
        return ((s - t >= 0) & (s + 1 < n)) if up else ((s + t < n) & (s > 0))

    def receives(t):
        return s - 1 - t >= 0 if up else s + 1 + t < n

    def copy(t):
        src = own if t == 0 else box.at[t - 1]
        return remote(src, box.at[t], send.at[t], recv.at[t], spot.to(go))

    @pl.when(sends(0))
    def _():
        copy(0).start()

    out[...] = jnp.zeros_like(out)
    for t in range(n - 1):

        @pl.when(receives(t))
        def _():
            copy(t).wait_recv()
            if t + 1 < n - 1:

                @pl.when(sends(t + 1))
                def _():
                    copy(t + 1).start()

            out[...] += box[t].astype(jnp.float32)

    for t in range(n - 1):

        @pl.when(sends(t))
        def _():
            copy(t).wait_send()


def line_sum(n, own, up, cid):
    DMA = pltpu.SemaphoreType.DMA
    return pl.pallas_call(
        functools.partial(line_sum_kernel, n, up),
        out_shape=jax.ShapeDtypeStruct(own.shape, jnp.float32),
        in_specs=[pl.BlockSpec(memory_space=pltpu.VMEM)],
        out_specs=pl.BlockSpec(memory_space=pltpu.VMEM),
        scratch_shapes=[pltpu.VMEM((n - 1,) + own.shape, own.dtype), DMA((n - 1,)), DMA((n - 1,))],
        compiler_params=pltpu.CompilerParams(collective_id=cid, has_side_effects=True, vmem_limit_bytes=40 << 20),
        name=f"line_sum_{cid}",
    )(own)
def plane_total_kernel(
    n, shared, part, out, mine, core_in, xin, yin, t2, xin2, yin2, line, c_send, c_recv, p_send, p_recv, z_send, z_recv, g_send, g_recv
):
    spot = Spot()
    s, d = spot.s, spot.d
    h = out.shape[1] // 2
    A, B = pl.ds(0, h), pl.ds(h, h)
    f32, b16 = jnp.float32, jnp.bfloat16
    mine[...] = part[...].astype(b16)
    greet(spot, n, ("x", "y", "c", "up", "dn"))
    core = remote(mine.at[pl.ds(0, shared)], core_in, c_send, c_recv, spot.to("c"))
    core.start()
    core.wait()
    mine[:shared] = (mine[:shared].astype(f32) + core_in[...].astype(f32)).astype(b16)

    def block(who, part):
        return mine.at[pl.ds(who * 2 * h + part * h, h)]

    def read(who, part):
        return mine[pl.ds(who * 2 * h + part * h, h)].astype(f32)

    first = (
        remote(block(spot.diag, 0), xin.at[1], p_send.at[0], p_recv.at[0], spot.to("x")),
        remote(block(spot.diag, 1), yin.at[1], p_send.at[1], p_recv.at[1], spot.to("y")),
        remote(block(spot.x, 0), xin.at[0], p_send.at[2], p_recv.at[2], spot.to("x")),
        remote(block(spot.y, 1), yin.at[0], p_send.at[3], p_recv.at[3], spot.to("y")),
    )
    for c in first:
        c.start()
    second = (
        remote(t2.at[0], yin2, p_send.at[4], p_recv.at[4], spot.to("y")),
        remote(t2.at[1], xin2, p_send.at[5], p_recv.at[5], spot.to("x")),
    )
    first[0].wait_recv()
    t2[0] = (read(spot.y, 0) + xin[1].astype(f32)).astype(b16)
    second[0].start()
    first[1].wait_recv()
    t2[1] = (read(spot.x, 1) + yin[1].astype(f32)).astype(b16)
    second[1].start()
    first[2].wait_recv()
    first[3].wait_recv()
    second[0].wait_recv()
    line[s, A] = (read(d, 0) + xin[0].astype(f32) + yin2[...].astype(f32)).astype(b16)
    second[1].wait_recv()
    line[s, B] = (read(d, 1) + yin[0].astype(f32) + xin2[...].astype(f32)).astype(b16)

    def sends(up, t):
        return ((s - t >= 0) & (s + 1 < n)) if up else ((s + t < n) & (s > 0))

    def receives(up, t):
        return s - 1 - t >= 0 if up else s + 1 + t < n

    def z_copy(up, t, sending):
        way = 0 if up else 1
        piece = (s - t if up else s + t) if sending else (s - 1 - t if up else s + 1 + t)
        return remote(line.at[piece], line.at[piece], z_send.at[way, t], z_recv.at[way, t], spot.to("up" if up else "dn"))

    for up in (True, False):

        @pl.when(sends(up, 0))
        def _():
            z_copy(up, 0, True).start()

    for t in range(n - 1):
        for up in (True, False):

            @pl.when(receives(up, t))
            def _():
                z_copy(up, t, False).wait_recv()
                if t + 1 < n - 1:

                    @pl.when(sends(up, t + 1))
                    def _():
                        z_copy(up, t + 1, True).start()

    total = line[0].astype(f32)
    for i in range(1, n):
        total = total + line[i].astype(f32)
    out[d] = total.astype(b16)

    parts = (A, B)

    def back(kind, sending):
        who = (d, d, spot.y, spot.x)[kind] if sending else (spot.x, spot.y, spot.diag, spot.diag)[kind]
        ref = out.at[who] if kind < 2 else out.at[who, parts[kind - 2]]
        return remote(ref, ref, g_send.at[kind], g_recv.at[kind], spot.to("xyxy"[kind]))

    back(0, True).start()
    back(1, True).start()
    back(0, False).wait_recv()
    back(3, True).start()
    back(1, False).wait_recv()
    back(2, True).start()
    back(2, False).wait_recv()
    back(3, False).wait_recv()
    for kind in range(4):
        back(kind, True).wait_send()
    for c in first + second:
        c.wait_send()
    for t in range(n - 1):
        for up in (True, False):

            @pl.when(sends(up, t))
            def _():
                z_copy(up, t, True).wait_send()


def plane_total(n, part, shared, cid):
    DMA = pltpu.SemaphoreType.DMA
    V = pltpu.VMEM
    b = jnp.bfloat16
    rows, w = part.shape
    h = rows // 8
    return pl.pallas_call(
        functools.partial(plane_total_kernel, n, shared),
        out_shape=jax.ShapeDtypeStruct((4, 2 * h, w), b),
        in_specs=[pl.BlockSpec(memory_space=pltpu.VMEM)],
        out_specs=pl.BlockSpec(memory_space=pltpu.VMEM),
        scratch_shapes=[
            V((rows, w), b),
            V((shared, w), b),
            V((2, h, w), b),
            V((2, h, w), b),
            V((2, h, w), b),
            V((h, w), b),
            V((h, w), b),
            V((n, 2 * h, w), b),
            DMA,
            DMA,
            DMA((6,)),
            DMA((6,)),
            DMA((2, n - 1)),
            DMA((2, n - 1)),
            DMA((4,)),
            DMA((4,)),
        ],
        compiler_params=pltpu.CompilerParams(collective_id=cid, has_side_effects=True, vmem_limit_bytes=40 << 20),
        name=f"plane_total_{cid}",
    )(part)


SPAN, TILE = 64, 128
REACH = TILE + SPAN


def mm(left, right, contract=((1,), (0,))):
    return lax.dot_general(left, right, (contract, ((), ())), preferred_element_type=jnp.float32)


def halves(shape, value):
    r = lax.broadcasted_iota(jnp.int32, shape, 0) // 64
    c = lax.broadcasted_iota(jnp.int32, shape, 1) // 64
    return jnp.where(r == c, value, 0.0).astype(jnp.bfloat16)


def signed_map(matrix):
    return jnp.concatenate([matrix, -matrix], 1)


def maps_of(logits):
    left = lax.broadcasted_iota(jnp.int32, logits.shape, 1) < 64
    low = jnp.max(jnp.where(left, logits, -jnp.inf), -1, keepdims=True)
    high = jnp.max(jnp.where(left, -jnp.inf, logits), -1, keepdims=True)
    e = jnp.exp(logits - jnp.where(left, low, high))
    sums = mm(e.astype(jnp.bfloat16), halves((128, 128), 1.0))
    return e / sums


def maps_back(maps, dmaps):
    p = (maps * dmaps).astype(jnp.bfloat16)
    return maps * (dmaps - mm(p, halves((128, 128), 1.0)))


def with_ones(values, first):
    rows = values.shape[0]
    r = lax.broadcasted_iota(jnp.int32, (rows, 64), 0)
    c = lax.broadcasted_iota(jnp.int32, (rows, 64), 1)
    ones = jnp.where((c == 0) & (r >= first), 1.0, 0.0).astype(jnp.bfloat16)
    return jnp.concatenate([values, ones], 1)


def pick(column):
    r = lax.broadcasted_iota(jnp.int32, (8, 128), 0)
    c = lax.broadcasted_iota(jnp.int32, (8, 128), 1)
    return jnp.where((r == 0) & (c == column), 1.0, 0.0).astype(jnp.bfloat16)


def identity():
    r = lax.broadcasted_iota(jnp.int32, (128, 128), 0)
    c = lax.broadcasted_iota(jnp.int32, (128, 128), 1)
    return jnp.where(r == c, 1.0, 0.0).astype(jnp.bfloat16)


def start_row():
    return jnp.where(lax.axis_index("seq") == 0, SPAN, 0)


def key_state_kernel(kv, kmaps, out):
    first = start_row()
    b16 = jnp.bfloat16
    out[512:] = jnp.zeros((16, 128), b16)
    for e in range(2):
        for gp in range(2):
            parts = []
            for j in range(2):
                g = 2 * gp + j
                keys = kv[e, :256, g * 64 : g * 64 + 64]
                values = with_ones(kv[e, :256, 256 + g * 64 : 320 + g * 64], first)
                feats = maps_of(mm(keys, signed_map(kmaps[g]))).astype(b16)
                state = mm(feats, values, ((0,), (0,)))
                parts.append(state[:, :64])
                total = mm(pick(64), state.astype(b16), ((1,), (1,)))
                out[512 + e * 4 + g : 513 + e * 4 + g] = total[:1].astype(b16)
            block = jnp.concatenate(parts, 1).astype(b16)
            out[(e * 2 + gp) * 128 : (e * 2 + gp) * 128 + 128] = block


def key_state(kv_ext, kmaps):
    return pl.pallas_call(
        key_state_kernel,
        out_shape=jax.ShapeDtypeStruct((528, 128), jnp.bfloat16),
        in_specs=[pl.BlockSpec(memory_space=pltpu.VMEM)] * 2,
        out_specs=pl.BlockSpec(memory_space=pltpu.VMEM),
        compiler_params=pltpu.CompilerParams(vmem_limit_bytes=40 << 20),
        name="key_state",
    )(kv_ext, kmaps)


STACK = 4


def masks():
    r = lax.broadcasted_iota(jnp.int32, (STACK * TILE, REACH), 0) % TILE
    c = lax.broadcasted_iota(jnp.int32, (STACK * TILE, REACH), 1)
    return (c > r) & (c <= r + SPAN), c <= r


def stacked(ref, rows, head):
    return jnp.concatenate([ref[rows, (head + i) * 64 : (head + i) * 64 + 64] for i in range(STACK)], 0)


def beside(value):
    return jnp.concatenate([value[i * TILE : (i + 1) * TILE] for i in range(STACK)], 1)


def query_logits(queries, qmaps, head):
    return jnp.concatenate(
        [mm(queries[i * TILE : (i + 1) * TILE], signed_map(qmaps[head + i])) for i in range(STACK)], 0
    )


def state_of(states, totals, e, gp, j):
    b16 = jnp.bfloat16
    column = mm(identity(), totals[...].astype(b16), ((1,), (1,)))
    row = e * 4 + 2 * gp + j
    pickcol = lax.broadcasted_iota(jnp.int32, column.shape, 1) == row
    one = jnp.sum(jnp.where(pickcol, column, 0.0), -1, keepdims=True)
    c = lax.broadcasted_iota(jnp.int32, (128, 64), 1)
    return jnp.concatenate([states[:, j * 64 : j * 64 + 64], jnp.where(c == 0, one, 0.0)], 1)


def attend_kernel(q, k, v, st, tot, qmaps, kmaps, out, qf, inv):
    gp, e = pl.program_id(0), pl.program_id(1)
    first = start_row()
    b16 = jnp.bfloat16
    window, older = masks()
    for j in range(2):
        keys = k[0, :, j * 64 : j * 64 + 64]
        values = with_ones(v[0, :, j * 64 : j * 64 + 64], first)
        kfeats = maps_of(mm(keys, signed_map(kmaps[j]))).astype(b16)
        keys8 = keys * jnp.asarray(0.125, b16)
        state = state_of(st, tot, e, gp, j)
        for i in range(2):
            if i:
                state = state + mm(kfeats[:TILE], values[:TILE], ((0,), (0,)))
            state16 = state.astype(b16)
            reach = slice(i * TILE, i * TILE + REACH)
            rows = slice(i * TILE, (i + 1) * TILE)
            for h in range(0, 4, STACK):
                head = j * 4 + h
                query = stacked(q, rows, head)
                qfeats = maps_of(query_logits(query, qmaps, head)).astype(b16)
                near = mm(query, keys8[reach], ((1,), (1,)))
                far = mm(qfeats, kfeats[reach], ((1,), (1,)))
                weights = jnp.where(window, jnp.exp(near), jnp.where(older, far, 0.0))
                both = mm(weights.astype(b16), values[reach]) + mm(qfeats, state16)
                part = 1.0 / both[:, 64:65]
                out[rows, head * 64 : (head + STACK) * 64] = beside((both[:, :64] * part).astype(b16))
                inv[0, rows, head : head + STACK] = beside(part)
                qf[0, 0, head // STACK, i] = qfeats


STACKED = pl.BlockSpec((1, 1, 8 // STACK, 2, STACK * TILE, 128), lambda g, e: (e, g, 0, 0, 0, 0))


def attend(q, kv_ext, st, qmaps, kmaps):
    return pl.pallas_call(
        attend_kernel,
        grid=(2, 2),
        out_shape=[
            jax.ShapeDtypeStruct(q.shape, jnp.bfloat16),
            jax.ShapeDtypeStruct((2, 2, 8 // STACK, 2, STACK * TILE, 128), jnp.bfloat16),
            jax.ShapeDtypeStruct((2, 512, 8), jnp.float32),
        ],
        in_specs=[
            pl.BlockSpec((256, 512), lambda g, e: (e, g)),
            pl.BlockSpec((1, 320, 128), lambda g, e: (e, 0, g)),
            pl.BlockSpec((1, 320, 128), lambda g, e: (e, 0, 2 + g)),
            pl.BlockSpec((128, 128), lambda g, e: (e * 2 + g, 0)),
            pl.BlockSpec((16, 128), lambda g, e: (32, 0)),
            pl.BlockSpec((8, 64, 64), lambda g, e: (g, 0, 0)),
            pl.BlockSpec((2, 64, 64), lambda g, e: (g, 0, 0)),
        ],
        out_specs=[
            pl.BlockSpec((256, 512), lambda g, e: (e, g)),
            STACKED,
            pl.BlockSpec((1, 256, 8), lambda g, e: (g, e, 0)),
        ],
        compiler_params=pltpu.CompilerParams(vmem_limit_bytes=40 << 20),
        name="attend",
    )(q, kv_ext, kv_ext, st, st, qmaps, kmaps)


def state_back_kernel(attn, dattn, inv, qf, grad1, dst, dtot):
    b16, f32 = jnp.bfloat16, jnp.float32
    lane = lax.broadcasted_iota(jnp.int32, (STACK * TILE, 64), 1)
    states = []
    for j in range(2):
        total = None
        for h in range(0, 4, STACK):
            head = j * 4 + h
            for i in range(2):
                rows = slice(i * TILE, (i + 1) * TILE)
                part = jnp.concatenate([inv[0, rows, head + z : head + z + 1] for z in range(STACK)], 0)
                grad = stacked(dattn, rows, head).astype(f32) * part
                c = jnp.sum(grad * stacked(attn, rows, head).astype(f32), -1, keepdims=True)
                one = jnp.concatenate([grad, jnp.where(lane == 0, -c, 0.0)], 1).astype(b16)
                grad1[0, 0, head // STACK, i] = one
                g = mm(qf[0, 0, head // STACK, i], one, ((0,), (0,)))
                total = g if total is None else total + g
        states.append(total[:, :64])
        dtot[0, 0, j * 8 : j * 8 + 8] = mm(pick(64), total.astype(b16), ((1,), (1,))).astype(b16)
    dst[...] = jnp.concatenate(states, 1).astype(b16)


def state_back(attn, dattn, inv, qf):
    b16 = jnp.bfloat16
    rows = pl.BlockSpec((256, 512), lambda g, e: (e, g))
    return pl.pallas_call(
        state_back_kernel,
        grid=(2, 2),
        out_shape=[
            jax.ShapeDtypeStruct(qf.shape, b16),
            jax.ShapeDtypeStruct((512, 128), b16),
            jax.ShapeDtypeStruct((2, 2, 16, 128), b16),
        ],
        in_specs=[rows, rows, pl.BlockSpec((1, 256, 8), lambda g, e: (g, e, 0)), STACKED],
        out_specs=[
            STACKED,
            pl.BlockSpec((128, 128), lambda g, e: (e * 2 + g, 0)),
            pl.BlockSpec((1, 1, 16, 128), lambda g, e: (e, g, 0, 0)),
        ],
        compiler_params=pltpu.CompilerParams(vmem_limit_bytes=40 << 20),
        name="state_back",
    )(attn, dattn, inv, qf)


def attend_back_kernel(q, k, v, st, tot, qmaps, kmaps, qf, gr, dq, dk, dv, dkf, dqm):
    gp, e = pl.program_id(0), pl.program_id(1)
    first = start_row()
    b16, f32 = jnp.bfloat16, jnp.float32
    window, older = masks()
    eighth = jnp.asarray(0.125, b16)
    dk[...] = jnp.zeros_like(dk)
    dv[...] = jnp.zeros_like(dv)
    dkf[...] = jnp.zeros_like(dkf)

    @pl.when(e == 0)
    def _():
        dqm[...] = jnp.zeros_like(dqm)

    for j in range(2):
        keys = k[0, :, j * 64 : j * 64 + 64]
        values = with_ones(v[0, :, j * 64 : j * 64 + 64], first)
        kfeats = maps_of(mm(keys, signed_map(kmaps[j]))).astype(b16)
        keys8 = keys * eighth
        state = state_of(st, tot, e, gp, j)
        for i in range(2):
            if i:
                state = state + mm(kfeats[:TILE], values[:TILE], ((0,), (0,)))
            state16 = state.astype(b16)
            reach = slice(i * TILE, i * TILE + REACH)
            rows = slice(i * TILE, (i + 1) * TILE)
            dvalue = dkey = dkfeat = g = None
            for h in range(0, 4, STACK):
                head = j * 4 + h
                query = stacked(q, rows, head)
                grad1 = gr[0, 0, head // STACK, i]
                qfeats = qf[0, 0, head // STACK, i]
                qmap = qfeats.astype(f32)
                near = mm(query, keys8[reach], ((1,), (1,)))
                far = mm(qfeats, kfeats[reach], ((1,), (1,)))
                close = jnp.where(window, jnp.exp(near), 0.0)
                weights = (close + jnp.where(older, far, 0.0)).astype(b16)
                dweights = mm(grad1, values[reach], ((1,), (1,)))
                ds = (close * dweights).astype(b16)
                dl = jnp.where(older, dweights, 0.0).astype(b16)
                dqmap = mm(dl, kfeats[reach]) + mm(grad1, state16, ((1,), (1,)))
                da = maps_back(qmap, dqmap).astype(b16)
                dmaps = []
                for z in range(STACK):
                    part = slice(z * TILE, (z + 1) * TILE)
                    dmaps.append(mm(da[part], signed_map(qmaps[head + z]), ((1,), (1,))))
                    x = mm(query[part], da[part], ((0,), (0,)))
                    dqm[head + z] += x[:, :64] - x[:, 64:]
                dquery = mm(ds, keys8[reach]) + jnp.concatenate(dmaps, 0)
                dq[rows, head * 64 : (head + STACK) * 64] = beside(dquery.astype(b16))
                a1 = mm(weights, grad1, ((0,), (0,)))
                a2 = mm(ds, query * eighth, ((0,), (0,)))
                a3 = mm(dl, qfeats, ((0,), (0,)))
                a4 = mm(qfeats, grad1, ((0,), (0,))) if i else None
                if dvalue is None:
                    dvalue, dkey, dkfeat, g = a1, a2, a3, a4
                else:
                    dvalue, dkey, dkfeat = dvalue + a1, dkey + a2, dkfeat + a3
                    g = g + a4 if i else None
            dv[0, reach, j * 64 : j * 64 + 64] += dvalue[:, :64]
            dk[0, reach, j * 64 : j * 64 + 64] += dkey
            dkf[0, j, reach] += dkfeat
            if i:
                g16 = g.astype(b16)
                dkf[0, j, :TILE] += mm(values[:TILE], g16, ((1,), (1,)))
                dv[0, :TILE, j * 64 : j * 64 + 64] += mm(kfeats[:TILE], g16)[:, :64]


def attend_back(q, kv_ext, st, qmaps, kmaps, qf, grad1):
    f32, b16 = jnp.float32, jnp.bfloat16
    e2, ext = kv_ext.shape[:2]
    return pl.pallas_call(
        attend_back_kernel,
        grid=(2, 2),
        out_shape=[
            jax.ShapeDtypeStruct(q.shape, b16),
            jax.ShapeDtypeStruct((e2, ext, 256), f32),
            jax.ShapeDtypeStruct((e2, ext, 256), f32),
            jax.ShapeDtypeStruct((e2, 4, ext, 128), f32),
            jax.ShapeDtypeStruct((16, 64, 64), f32),
        ],
        in_specs=[
            pl.BlockSpec((256, 512), lambda g, e: (e, g)),
            pl.BlockSpec((1, 320, 128), lambda g, e: (e, 0, g)),
            pl.BlockSpec((1, 320, 128), lambda g, e: (e, 0, 2 + g)),
            pl.BlockSpec((128, 128), lambda g, e: (e * 2 + g, 0)),
            pl.BlockSpec((16, 128), lambda g, e: (32, 0)),
            pl.BlockSpec((8, 64, 64), lambda g, e: (g, 0, 0)),
            pl.BlockSpec((2, 64, 64), lambda g, e: (g, 0, 0)),
            STACKED,
            STACKED,
        ],
        out_specs=[
            pl.BlockSpec((256, 512), lambda g, e: (e, g)),
            pl.BlockSpec((1, 320, 128), lambda g, e: (e, 0, g)),
            pl.BlockSpec((1, 320, 128), lambda g, e: (e, 0, g)),
            pl.BlockSpec((1, 2, 320, 128), lambda g, e: (e, g, 0, 0)),
            pl.BlockSpec((8, 64, 64), lambda g, e: (g, 0, 0)),
        ],
        compiler_params=pltpu.CompilerParams(vmem_limit_bytes=40 << 20),
        cost_estimate=pl.CostEstimate(flops=40 * 10**9, bytes_accessed=10**7, transcendentals=4 * 10**6),
        name="attend_back",
    )(q, kv_ext, kv_ext, st, st, qmaps, kmaps, qf, grad1)


def key_back_kernel(k, v, later, tot, kmaps, dk_in, dv_in, dkf, dk, dv, dkm):
    gp, e = pl.program_id(0), pl.program_id(1)
    first = start_row()
    b16 = jnp.bfloat16

    @pl.when(e == 0)
    def _():
        dkm[...] = jnp.zeros_like(dkm)

    dks, dvs = [], []
    for j in range(2):
        cols = slice(j * 64, j * 64 + 64)
        keys = k[0, :, cols]
        values = with_ones(v[0, :, cols], first)
        signed = signed_map(kmaps[j])
        kmap = maps_of(mm(keys, signed))
        g = state_of(later, tot, e, gp, j).astype(b16)
        more = mm(values[:256], g, ((1,), (1,)))
        dmap = jnp.concatenate([dkf[0, j, :256] + more, dkf[0, j, 256:]], 0)
        da = maps_back(kmap, dmap).astype(b16)
        dks.append(dk_in[0, :, cols] + mm(da, signed, ((1,), (1,))))
        moved = mm(kmap[:256].astype(b16), g)[:, :64]
        dvs.append(jnp.concatenate([dv_in[0, :256, cols] + moved, dv_in[0, 256:, cols]], 0))
        x = mm(keys, da, ((0,), (0,)))
        dkm[j] += x[:, :64] - x[:, 64:]
    dk[0] = jnp.concatenate(dks, 1)
    dv[0] = jnp.concatenate(dvs, 1)


def key_back(kv_ext, later, kmaps, dk, dv, dkf):
    f32 = jnp.float32
    piece = pl.BlockSpec((1, 320, 128), lambda g, e: (e, 0, g))
    return pl.pallas_call(
        key_back_kernel,
        grid=(2, 2),
        out_shape=[
            jax.ShapeDtypeStruct(dk.shape, f32),
            jax.ShapeDtypeStruct(dv.shape, f32),
            jax.ShapeDtypeStruct((4, 64, 64), f32),
        ],
        in_specs=[
            piece,
            pl.BlockSpec((1, 320, 128), lambda g, e: (e, 0, 2 + g)),
            pl.BlockSpec((128, 128), lambda g, e: (e * 2 + g, 0)),
            pl.BlockSpec((16, 128), lambda g, e: (32, 0)),
            pl.BlockSpec((2, 64, 64), lambda g, e: (g, 0, 0)),
            piece,
            piece,
            pl.BlockSpec((1, 2, 320, 128), lambda g, e: (e, g, 0, 0)),
        ],
        out_specs=[piece, piece, pl.BlockSpec((2, 64, 64), lambda g, e: (g, 0, 0))],
        compiler_params=pltpu.CompilerParams(vmem_limit_bytes=40 << 20),
        name="key_back",
    )(kv_ext, kv_ext, later, later, kmaps, dk, dv, dkf)


CHUNKS = 4


def feed_kernel(n, k, early, xn_own, ct_all, packed, gate, up, down, dxn, out_part, *scratch):
    (xn, ct, gw, uw, dw, da, oa, xin, yin, t2, xin2, yin2) = scratch[:12]
    (o_sem, a_send, a_recv, w_sem, w_send, w_recv, z_sem, z_send, z_recv, c_send, c_recv, p_send, p_recv, st_sem) = scratch[12:]
    spot = Spot()
    s, m, d = spot.s, spot.m, spot.d
    f32, b16 = jnp.float32, jnp.bfloat16
    unit = gw.shape[3] // 2
    wd = min(unit, k)
    gs, ds = unit // wd, k // wd
    half = xn.shape[1] // 2
    A, B = pl.ds(0, half), pl.ds(half, half)

    own = [pltpu.make_async_copy(xn_own, xn.at[3], o_sem.at[0]), pltpu.make_async_copy(ct_all, ct, o_sem.at[1])]
    for c in own:
        c.start()

    lanes = pl.ds(pl.multiple_of(m * unit, unit), unit)

    def own_piece(q):
        start = pl.multiple_of(d * (CHUNKS * unit) + q * unit, unit)
        return (
            (gate.at[:, pl.ds(start, unit)], gw.at[q, s, :, lanes]),
            (up.at[:, pl.ds(start, unit)], uw.at[q, s, :, lanes]),
            (down.at[pl.ds(start, unit)], dw.at[q, s, lanes]),
        )

    def piece(q, w, who):
        return (gw.at[q, who, :, lanes], uw.at[q, who, :, lanes], dw.at[q, who, lanes])[w]

    late = tuple(range(early, CHUNKS))
    own_weights = [
        pltpu.make_async_copy(src, dst, z_sem.at[i, w])
        for i, q in enumerate(late)
        for w, (src, dst) in enumerate(own_piece(q))
    ]
    for c in own_weights:
        c.start()

    def early_parts(q):
        parts = []
        at = 0
        for ref in (gw, uw):
            for i in range(gs):
                cols = pl.ds(pl.multiple_of(m * unit + i * wd, wd), wd)
                parts.append((packed.at[:, q, pl.ds(at, k)], ref.at[q, :, :, cols]))
                at += k
        for i in range(ds):
            parts.append((packed.at[:, q, pl.ds(at, unit)], dw.at[q, :, lanes, pl.ds(i * wd, wd)]))
            at += unit
        return parts

    early_own = [
        [pltpu.make_async_copy(src, dst, w_sem.at[q, i]) for i, (src, dst) in enumerate(early_parts(q))]
        for q in range(early)
    ]
    for copies in early_own:
        for c in copies:
            c.start()

    greet(spot, n, ("x", "y", "c", "up", "dn"))

    def block_copy(kind, sending):
        if kind < 2:
            dst = xn.at[kind + 1]
            src = xn_own if sending else dst
        else:
            rows = (A, B)[kind - 2]
            dst = xn.at[0, rows]
            src = xn.at[(2, 1)[kind - 2], rows] if sending else dst
        return remote(src, dst, a_send.at[kind], a_recv.at[kind], spot.to("xyxy"[kind]))

    block_copy(0, True).start()
    block_copy(1, True).start()

    def sends(upward, t):
        return ((s - t >= 0) & (s + 1 < n)) if upward else ((s + t < n) & (s > 0))

    def receives(upward, t):
        return s - 1 - t >= 0 if upward else s + 1 + t < n

    def z_copy(i, w, upward, t, sending):
        q = late[i]
        way = 0 if upward else 1
        who = (s - t if upward else s + t) if sending else (s - 1 - t if upward else s + 1 + t)
        dst = piece(q, w, who)
        src = own_piece(q)[w][0] if (t == 0 and sending) else dst
        return remote(src, dst, z_send.at[i, w, way, t], z_recv.at[i, w, way, t], spot.to("up" if upward else "dn"))

    for i in range(len(late)):
        for w in range(3):
            for upward in (True, False):

                @pl.when(sends(upward, 0))
                def _():
                    z_copy(i, w, upward, 0, True).start()

    def early_core(q):
        return [
            remote(src, dst, w_send.at[q, i], w_recv.at[q, i], spot.to("c")) for i, (src, dst) in enumerate(early_parts(q))
        ]

    def theirs(q, w, who):
        other = pl.ds(pl.multiple_of((1 - m) * unit, unit), unit)
        return (gw.at[q, who, :, other], uw.at[q, who, :, other], dw.at[q, who, other])[w]

    def core_copy(i, w, who, sending):
        q = late[i]
        ref = piece(q, w, who) if sending else theirs(q, w, who)
        return remote(ref, ref, c_send.at[i, w, who], c_recv.at[i, w, who], spot.to("c"))

    for q in range(early):
        for c in early_core(q):
            c.start()

    def relay(i, t, w):
        for upward in (True, False):

            @pl.when(receives(upward, t))
            def _():
                z_copy(i, w, upward, t, False).wait_recv()
                if t + 1 < n - 1:

                    @pl.when(sends(upward, t + 1))
                    def _():
                        z_copy(i, w, upward, t + 1, True).start()

                core_copy(i, w, s - 1 - t if upward else s + 1 + t, True).start()

    for i in range(len(late)):
        for w in range(3):
            own_weights[3 * i + w].wait()
            core_copy(i, w, s, True).start()

    for c in own:
        c.wait()

    first = (
        remote(xn.at[0, A], xin.at[1], p_send.at[0], p_recv.at[0], spot.to("x")),
        remote(xn.at[0, B], yin.at[1], p_send.at[1], p_recv.at[1], spot.to("y")),
        remote(xn.at[1, A], xin.at[0], p_send.at[2], p_recv.at[2], spot.to("x")),
        remote(xn.at[2, B], yin.at[0], p_send.at[3], p_recv.at[3], spot.to("y")),
    )
    stores = [pltpu.make_async_copy(ct.at[i], out_part.at[i], st_sem.at[i]) for i in range(4)]

    steps = 4 * CHUNKS
    turns = {}
    total = len(late) * (n - 1) * 3
    for j in range(total):
        i, t, w = j // (3 * n - 3), j // 3 % (n - 1), j % 3
        at = min(4 * late[i], 1 + (4 * late[i] - 1) * j // ((i + 1) * (n - 1) * 3))
        turns.setdefault(at, []).append((i, t, w))

    @pl.loop(0, steps)
    def _(step):
        last = step >= steps - 4
        c = jnp.where(step < 4 * early, step % early, step // 4)
        t = jnp.where(step < 4 * early, 3 - step // early, step % 4)

        for q in range(early):

            @pl.when(step == q)
            def _():
                for copy in early_own[q]:
                    copy.wait()
                for copy in early_core(q):
                    copy.wait_recv()

        for at, jobs in turns.items():

            @pl.when(step == at)
            def _():
                for i, t, w in jobs:
                    relay(i, t, w)

        for i, q in enumerate(late):

            @pl.when(step == 4 * q)
            def _():
                for w in range(3):
                    for who in range(n):
                        core_copy(i, w, who, False).wait_recv()

        @pl.when(step == early)
        def _():
            block_copy(1, False).wait_recv()
            block_copy(2, True).start()
            block_copy(0, False).wait_recv()
            block_copy(3, True).start()

        @pl.when(step == 3 * early)
        def _():
            for kind in (2, 3):
                block_copy(kind, False).wait_recv()
            for kind in range(4):
                block_copy(kind, True).wait_send()

        x, cot = xn[t], ct[t]
        g_all = gw[c].reshape(n * k, 2 * unit)
        u_all = uw[c].reshape(n * k, 2 * unit)
        g = mm(x, g_all)
        u = mm(x, u_all)
        dh = mm(cot[:, :k], dw[c, 0], ((1,), (1,)))
        for i in range(1, n):
            dh = dh + mm(cot[:, i * k : (i + 1) * k], dw[c, i], ((1,), (1,)))
        sig = 1.0 / (1.0 + jnp.exp(-g))
        act = g * sig
        hid = (act * u).astype(b16)
        dg = (dh * u * sig * (1.0 + g * (1.0 - sig))).astype(b16)
        du = (dh * act).astype(b16)
        for i in range(n):
            cols = slice(i * k, (i + 1) * k)
            o = mm(hid, dw[c, i])
            e = mm(dg, gw[c, i], ((1,), (1,))) + mm(du, uw[c, i], ((1,), (1,)))

            @pl.when(c == 0)
            def _():
                oa[t, :, cols] = o
                da[t, :, cols] = e

            @pl.when(c > 0)
            def _():
                oa[t, :, cols] += o
                da[t, :, cols] += e

        @pl.when(last)
        def _():
            xn[t] = da[t].astype(b16)
            ct[t] = oa[t].astype(b16)

        for i in range(4):

            @pl.when(step == steps - 4 + i)
            def _():
                stores[i].start()
                if i == 0:
                    first[0].start()
                    first[1].start()
                elif i < 3:
                    first[i + 1].start()

    second = (
        remote(t2.at[0], yin2, p_send.at[4], p_recv.at[4], spot.to("y")),
        remote(t2.at[1], xin2, p_send.at[5], p_recv.at[5], spot.to("x")),
    )
    first[0].wait_recv()
    t2[0] = (xn[2, A].astype(f32) + xin[1].astype(f32)).astype(b16)
    second[0].start()
    first[1].wait_recv()
    t2[1] = (xn[1, B].astype(f32) + yin[1].astype(f32)).astype(b16)
    second[1].start()
    first[2].wait_recv()
    first[3].wait_recv()
    second[0].wait_recv()
    dxn[A] = da[3, A] + xin[0].astype(f32) + yin2[...].astype(f32)
    second[1].wait_recv()
    dxn[B] = da[3, B] + yin[0].astype(f32) + xin2[...].astype(f32)

    for c in stores:
        c.wait()
    for c in first + second:
        c.wait_send()
    for q in range(early):
        for c in early_core(q):
            c.wait_send()
    for i in range(len(late)):
        for w in range(3):
            for who in range(n):
                core_copy(i, w, who, True).wait_send()
            for t in range(n - 1):
                for upward in (True, False):

                    @pl.when(sends(upward, t))
                    def _():
                        z_copy(i, w, upward, t, True).wait_send()


def feed(n, early, xn_own, ct_all, packed, gate, up, down, cid):
    DMA, V = pltpu.SemaphoreType.DMA, pltpu.VMEM
    b, f32 = jnp.bfloat16, jnp.float32
    r, w = xn_own.shape
    k = gate.shape[0]
    unit = gate.shape[1] // (4 * CHUNKS)
    wd = min(unit, k)
    pieces = 2 * (unit // wd) + k // wd
    late = CHUNKS - early
    scratch = [V((4, r, w), b), V((4, r, w), b)]
    scratch += [V((CHUNKS, n, k, 2 * unit), b), V((CHUNKS, n, k, 2 * unit), b), V((CHUNKS, n, 2 * unit, k), b)]
    scratch += [V((4, r, w), f32), V((4, r, w), f32)]
    scratch += [V((2, r // 2, w), b), V((2, r // 2, w), b), V((2, r // 2, w), b), V((r // 2, w), b), V((r // 2, w), b)]
    scratch += [DMA((2,)), DMA((4,)), DMA((4,))]
    scratch += [DMA((max(early, 1), pieces))] * 3
    scratch += [DMA((late, 3)), DMA((late, 3, 2, n - 1)), DMA((late, 3, 2, n - 1)), DMA((late, 3, n)), DMA((late, 3, n))]
    scratch += [DMA((6,)), DMA((6,)), DMA((4,))]
    return pl.pallas_call(
        functools.partial(feed_kernel, n, k, early),
        out_shape=[jax.ShapeDtypeStruct((r, w), f32), jax.ShapeDtypeStruct((4, r, w), b)],
        in_specs=[pl.BlockSpec(memory_space=ANY)] * 6,
        out_specs=[pl.BlockSpec(memory_space=pltpu.VMEM), pl.BlockSpec(memory_space=ANY)],
        scratch_shapes=scratch,
        compiler_params=pltpu.CompilerParams(collective_id=cid, has_side_effects=True, vmem_limit_bytes=62 << 20),
        name="feed",
    )(xn_own, ct_all, packed, gate, up, down)


def pack_early(k, early, gate, up, down, d):
    unit = gate.shape[1] // (4 * CHUNKS)
    wd = min(unit, k)
    at = d * (CHUNKS * unit)
    g = lax.dynamic_slice_in_dim(gate, at, early * unit, 1)
    u = lax.dynamic_slice_in_dim(up, at, early * unit, 1)
    dn = lax.dynamic_slice_in_dim(down, at, early * unit, 0)
    chunks = []
    for q in range(early):
        rows = [a[:, q * unit + i : q * unit + i + wd] for a in (g, u) for i in range(0, unit, wd)]
        rows += [dn[q * unit : (q + 1) * unit, i : i + wd] for i in range(0, k, wd)]
        chunks.append(jnp.concatenate(rows, 0))
    return jnp.stack(chunks)


EARLY = 3


f32, b16 = jnp.float32, jnp.bfloat16


def dot(left, right):
    return jnp.dot(left, right, preferred_element_type=f32)


def dot_t(left, right):
    return lax.dot_general(left, right, (((1,), (1,)), ((), ())), preferred_element_type=f32)


def t_dot(left, right):
    return lax.dot_general(left, right, (((0,), (0,)), ((), ())), preferred_element_type=f32)


def norm_back(inputs, inv_rms, gain, dnormed):
    return inv_rms * gain * dnormed - inputs * inv_rms**3 * jnp.mean(
        gain * dnormed * inputs, -1, keepdims=True
    )


def from_behind(value, axis, steps):
    count = lax.axis_size(axis)
    first, last = (max(0, -steps), min(count, count - steps))
    return lax.ppermute(value, axis, [(source, source + steps) for source in range(first, last)])


def swap_core(value):
    return lax.ppermute(value, "mp", [(0, 1), (1, 0)])


def per_device(
    tokens,
    cotangent,
    attention_norm_gain,
    feedforward_norm_gain,
    query_weight,
    key_weight,
    value_weight,
    output_weight,
    gate_weight,
    up_weight,
    down_weight,
    query_adapter_down,
    query_adapter_up,
    key_adapter_down,
    key_adapter_up,
    value_adapter_down,
    value_adapter_up,
    output_adapter_down,
    output_adapter_up,
    query_feature_matrix,
    key_feature_matrix,
):
    n = lax.axis_size("seq")
    position, m, d = (lax.axis_index(a) for a in ("seq", "mp", "dp"))
    seq_count, rows_here, width = tokens.shape
    total_rows = seq_count * rows_here
    half = total_rows // 2
    heads_kv = key_feature_matrix.shape[0]
    head_size = key_feature_matrix.shape[1]
    groups = query_feature_matrix.shape[0] // heads_kv
    extent = rows_here + SOFTMAX_SPAN

    packed = lax.all_gather(
        pack_early(gate_weight.shape[0], EARLY, gate_weight, up_weight, down_weight, d), "seq"
    )
    def my_half(a):
        return lax.dynamic_slice_in_dim(a, m * half, half, 0)

    cot_half = my_half(cotangent.reshape(total_rows, width))
    qkv_own = jnp.concatenate([query_weight, key_weight, value_weight], 1)
    qkv_g, out_g, cot_blocks = gather_weights(n, [qkv_own, output_weight], cot_half, 1)
    qkv_w = qkv_g.reshape(width, -1)
    wide = query_weight.shape[1]
    kv_wide = key_weight.shape[1]

    def both_halves(own):
        other = swap_core(own)
        return jnp.concatenate([jnp.where(m == 0, own, other), jnp.where(m == 0, other, own)], 0)

    tok2 = tokens.reshape(total_rows, width)
    inputs = tok2.astype(f32)
    gain_attn = attention_norm_gain.astype(f32)
    rms_attn = lax.rsqrt(jnp.mean(inputs * inputs, -1, keepdims=True) + epsilon)
    normed = (inputs * rms_attn * gain_attn).astype(b16)

    downs = jnp.concatenate([query_adapter_down, key_adapter_down, value_adapter_down], 1)
    inner = dot(normed, downs)
    rank = query_adapter_down.shape[1]
    full = dot(normed, qkv_w)

    def project(index, first, last, second):
        return (
            full[:, first:last] + dot(inner[:, index * rank : (index + 1) * rank].astype(b16), second)
        ).astype(b16)

    query_half = project(0, 0, wide, query_adapter_up)
    key_half = project(1, wide, wide + kv_wide, key_adapter_up)
    value_half = project(2, wide + kv_wide, wide + 2 * kv_wide, value_adapter_up)
    key3 = key_half.reshape(seq_count, rows_here, heads_kv * head_size)
    value3 = value_half.reshape(seq_count, rows_here, heads_kv * head_size)
    kv3 = jnp.concatenate([key3, value3], -1)
    kv_prev = from_behind(kv3[:, rows_here - SOFTMAX_SPAN :], "seq", 1)
    kv_ext = jnp.concatenate([kv_prev, kv3], 1)
    states = line_sum(n, key_state(kv_ext, key_feature_matrix), True, 3)
    attn16, qfeats, inv_weights = attend(query_half, kv_ext, states, query_feature_matrix, key_feature_matrix)
    inner_output = dot(attn16, output_adapter_down)
    branch = jnp.concatenate([dot(attn16, out_g[i]) for i in range(n)], 1) + dot(
        inner_output.astype(b16), output_adapter_up
    )
    branch16 = branch.astype(b16)
    from_other = swap_core(lax.dynamic_slice_in_dim(branch16, (1 - m) * half, half, 0))
    resid = my_half(inputs) + my_half(branch) + from_other.astype(f32)
    gain_mlp = feedforward_norm_gain.astype(f32)
    rms_mlp = lax.rsqrt(jnp.mean(resid * resid, -1, keepdims=True) + epsilon)
    normed_mlp = (resid * rms_mlp * gain_mlp).astype(b16)
    dnormed_mlp, out_part = feed(
        n, EARLY, normed_mlp, cot_blocks, packed, gate_weight, up_weight, down_weight, 4
    )

    def swap_chip(value, bit):
        return lax.ppermute(value, "dp", [(i, i ^ bit) for i in range(4)])

    cut = half // 2
    upper_in = swap_chip(out_part[0:2, :cut], 1)
    lower_in = swap_chip(out_part[0::2, cut:], 2)


    mlp_gain_term = jnp.sum(dnormed_mlp * resid * rms_mlp, 0)
    dresid = cot_half.astype(f32) + norm_back(resid, rms_mlp, gain_mlp, dnormed_mlp)
    dresid16 = both_halves(dresid.astype(b16))
    du_o = dot_t(dresid16, output_adapter_up)
    oup_term = t_dot(inner_output.astype(b16), dresid16)
    odown_term = t_dot(du_o.astype(b16), attn16)
    dattn = dot_t(du_o.astype(b16), output_adapter_down)
    step = output_weight.shape[1]
    for i in range(n):
        dattn = dattn + dot_t(dresid16[:, i * step : (i + 1) * step], out_g[i])
    grad1, dstates, dtotals = state_back(attn16, dattn.astype(b16), inv_weights, qfeats)
    dtotals = jnp.pad(dtotals[:, :, ::8].reshape(-1, 128), ((0, 8), (0, 0)))
    dstates = jnp.concatenate([dstates, dtotals], 0)
    later = [from_behind(dstates, "seq", -i) for i in range(1, n)]
    dresid_other = swap_core(dresid)
    dq16, dk_ext, dv_ext, dkfeats, dqmaps = attend_back(
        query_half, kv_ext, states, query_feature_matrix, key_feature_matrix, qfeats, grad1
    )
    dq16, later, upper_in, lower_in, dresid_other = lax.optimization_barrier(
        (dq16, later, upper_in, lower_in, dresid_other)
    )
    upper_in2 = swap_chip((out_part[2, :cut].astype(f32) + upper_in[0].astype(f32)).astype(b16), 2)
    lower_in2 = swap_chip((out_part[1, cut:].astype(f32) + lower_in[0].astype(f32)).astype(b16), 1)
    later = functools.reduce(jnp.add, [a.astype(f32) for a in later])
    dk_ext, dv_ext, dkmaps = key_back(kv_ext, later, key_feature_matrix, dk_ext, dv_ext, dkfeats)
    dk_ext, upper_in2, lower_in2 = lax.optimization_barrier((dk_ext, upper_in2, lower_in2))
    mlp_out = out_part[3].astype(f32) + jnp.concatenate(
        [
            upper_in[1].astype(f32) + upper_in2.astype(f32),
            lower_in[1].astype(f32) + lower_in2.astype(f32),
        ],
        0,
    )
    output = both_halves((resid + mlp_out).astype(b16)).reshape(seq_count, rows_here, width)
    dkv_ext = jnp.concatenate([dk_ext, dv_ext], -1)
    back = from_behind(dkv_ext[:, :SOFTMAX_SPAN].astype(b16), "seq", -1).astype(f32)
    dkv = dkv_ext[:, SOFTMAX_SPAN:]
    dkv = jnp.concatenate(
        [dkv[:, : rows_here - SOFTMAX_SPAN], dkv[:, rows_here - SOFTMAX_SPAN :] + back], 1
    )
    dqkv16 = jnp.concatenate(
        [dq16, dkv.reshape(total_rows, -1).astype(b16)], 1
    )
    bounds = ((0, wide), (wide, wide + kv_wide), (wide + kv_wide, wide + 2 * kv_wide))
    seconds = (query_adapter_up, key_adapter_up, value_adapter_up)
    dinner = jnp.concatenate(
        [dot_t(dqkv16[:, a:b], second) for (a, b), second in zip(bounds, seconds)], 1
    ).astype(b16)
    dnormed = (dot_t(dqkv16, qkv_w) + dot_t(dinner, downs)).astype(b16)
    down_terms = t_dot(dinner, normed)
    inner16 = inner.astype(b16)
    up_terms = [
        t_dot(inner16[:, i * rank : (i + 1) * rank], dqkv16[:, a:b]) for i, (a, b) in enumerate(bounds)
    ]
    dnormed = dnormed.astype(f32) + swap_core(dnormed).astype(f32)
    attn_gain_term = jnp.sum(my_half(dnormed * inputs * rms_attn), 0)
    dresid_both = jnp.concatenate(
        [jnp.where(m == 0, dresid, dresid_other), jnp.where(m == 0, dresid_other, dresid)], 0
    )
    tokens_grad = (dresid_both + norm_back(inputs, rms_attn, gain_attn, dnormed)).reshape(
        seq_count, rows_here, width
    )

    shared = [attn_gain_term, mlp_gain_term, down_terms, oup_term]
    split = up_terms + [odown_term, dqmaps, dkmaps]
    flat = [a.reshape(-1, 128) for a in shared + split]
    sizes = [a.shape[0] for a in flat]
    shared_rows = sum(sizes[:4])
    flat = jnp.concatenate(flat, 0)
    flat = jnp.pad(flat, ((0, -flat.shape[0] % 128), (0, 0)))
    summed = plane_total(n, flat, shared_rows, 8).reshape(-1, 128).astype(f32)
    parts, at = [], 0
    for term, size in zip(shared + split, sizes):
        parts.append(summed[at : at + size].reshape(term.shape))
        at += size
    attn_gain, mlp_gain, downs_g, oup, qup, kup, vup, odown, qmaps_g, kmaps_g = parts
    downs_g = downs_g.T
    return (
        output,
        tokens_grad,
        attn_gain,
        mlp_gain,
        downs_g[:, :rank],
        qup,
        downs_g[:, rank : 2 * rank],
        kup,
        downs_g[:, 2 * rank :],
        vup,
        odown.T,
        oup,
        qmaps_g.reshape(query_feature_matrix.shape),
        kmaps_g,
    )


def solution(mesh):
    placed = (
        P("dp", "seq", None),
        P("dp", "seq", None),
        P(),
        P(),
        P("seq", "mp"),
        P("seq", "mp"),
        P("seq", "mp"),
        P("mp", "seq"),
        P("seq", "mp"),
        P("seq", "mp"),
        P("mp", "seq"),
        P(),
        P(None, "mp"),
        P(),
        P(None, "mp"),
        P(),
        P(None, "mp"),
        P("mp", None),
        P(),
        P("mp", None, None),
        P("mp", None, None),
    )
    return jax.shard_map(
        per_device,
        mesh=mesh,
        in_specs=placed,
        out_specs=(
            P("dp", "seq", None),
            P("dp", "seq", None),
            P(),
            P(),
            P(),
            P(None, "mp"),
            P(),
            P(None, "mp"),
            P(),
            P(None, "mp"),
            P("mp", None),
            P(),
            P("mp", None, None),
            P("mp", None, None),
        ),
        check_vma=False,
    )
```

```python
import math
import functools
import jax
import jax.numpy as jnp
from jax import lax
from jax.experimental import pallas as pl
from jax.experimental.pallas import tpu as pltpu
from jax.sharding import PartitionSpec as P

SOFTMAX_SPAN = 64
epsilon = 1e-05

MESH = pl.DeviceIdType.MESH
ANY = pl.ANY


class Spot:
    def __init__(self):
        self.s, self.m, self.d = (lax.axis_index(a) for a in ("seq", "mp", "dp"))
        self.x = self.d + 1 - 2 * (self.d % 2)
        self.y = (self.d + 2) % 4
        self.diag = (self.x + 2) % 4

    def to(self, kind):
        s, m, d = self.s, self.m, self.d
        if kind == "x":
            d = self.x
        elif kind == "y":
            d = self.y
        elif kind == "c":
            m = 1 - m
        elif kind == "up":
            s = s + 1
        elif kind == "dn":
            s = s - 1
        return {"seq": s, "mp": m, "dp": d}


def remote(src, dst, send, recv, where):
    return pltpu.make_async_remote_copy(
        src_ref=src, dst_ref=dst, send_sem=send, recv_sem=recv, device_id=where, device_id_type=MESH
    )


def greet(spot, n, kinds):
    bar = pltpu.get_barrier_semaphore()
    count = 0
    for kind in kinds:
        if kind in ("up", "dn"):
            there = spot.s + 1 < n if kind == "up" else spot.s > 0

            @pl.when(there)
            def _(kind=kind):
                pl.semaphore_signal(bar, inc=1, device_id=spot.to(kind), device_id_type=MESH)

            count = count + there.astype(jnp.int32)
        else:
            pl.semaphore_signal(bar, inc=1, device_id=spot.to(kind), device_id_type=MESH)
            count = count + 1
    pl.semaphore_wait(bar, count)


def gather_weights_kernel(n, k, *refs):
    ins, block, outs, blocks = refs[:k], refs[k], refs[k + 1 : 2 * k + 1], refs[2 * k + 1]
    own_sem, z_send, z_recv, p_send, p_recv, b_send, b_recv = refs[2 * k + 2 :]
    spot = Spot()
    s, d = spot.s, spot.d
    own = [pltpu.make_async_copy(ins[a], outs[a].at[s], own_sem.at[a]) for a in range(k)]
    own.append(pltpu.make_async_copy(block, blocks.at[3], own_sem.at[k]))
    for c in own:
        c.start()
    greet(spot, n, ("x", "y", "up", "dn"))

    cut = block.shape[0] // 2
    parts = (pl.ds(0, cut), pl.ds(cut, cut))

    def block_copy(kind, sending):
        if kind < 2:
            dst = blocks.at[kind + 1]
            src = block if sending else dst
        else:
            dst = blocks.at[0, parts[kind - 2]]
            src = blocks.at[(2, 1)[kind - 2], parts[kind - 2]] if sending else dst
        return remote(src, dst, b_send.at[kind], b_recv.at[kind], spot.to("xyxy"[kind]))

    def rows(a, who, part=None):
        size = ins[a].shape[0] // 4
        if part is None:
            return pl.ds(who * size, size)
        return pl.ds(who * size + part * (size // 2), size // 2)

    def sends(up, t):
        return ((s - t >= 0) & (s + 1 < n)) if up else ((s + t < n) & (s > 0))

    def receives(up, t):
        return s - 1 - t >= 0 if up else s + 1 + t < n

    def z_copy(a, up, t, sending):
        way = 0 if up else 1
        piece = (s - t if up else s + t) if sending else (s - 1 - t if up else s + 1 + t)
        dst = outs[a].at[piece, rows(a, d)]
        src = ins[a].at[rows(a, d)] if (t == 0 and sending) else dst
        return remote(src, dst, z_send.at[a, way, t], z_recv.at[a, way, t], spot.to("up" if up else "dn"))

    def piece_of(up, t):
        return s - 1 - t if up else s + 1 + t

    def plane_copy(a, up, t, kind):
        way = 0 if up else 1
        who = (d, d, spot.y, spot.x)[kind]
        part = (None, None, 0, 1)[kind]
        ref = outs[a].at[piece_of(up, t), rows(a, who, part)]
        return remote(ref, ref, p_send.at[a, way, t, kind], p_recv.at[a, way, t, kind], spot.to("xyxy"[kind]))

    def landed(a, up, t, kind):
        way = 0 if up else 1
        who = (spot.x, spot.y, spot.diag, spot.diag)[kind]
        part = (None, None, 0, 1)[kind]
        ref = outs[a].at[piece_of(up, t), rows(a, who, part)]
        return remote(ref, ref, p_send.at[a, way, t, kind], p_recv.at[a, way, t, kind], spot.to("xyxy"[kind]))

    def begin(a):
        for up in (True, False):

            @pl.when(sends(up, 0))
            def _():
                z_copy(a, up, 0, True).start()

    begin(0)
    for step in range(n + k - 1):
        for a in range(k):
            t = step - a
            if 0 <= t < n - 1:
                for up in (True, False):

                    @pl.when(receives(up, t))
                    def _():
                        z_copy(a, up, t, False).wait_recv()
                        if t + 1 < n - 1:

                            @pl.when(sends(up, t + 1))
                            def _():
                                z_copy(a, up, t + 1, True).start()

                        plane_copy(a, up, t, 0).start()
                        plane_copy(a, up, t, 1).start()

            if t == 0 and a + 1 < k:
                begin(a + 1)
                block_copy(0, True).start()
                block_copy(1, True).start()

            if 0 < t < n:
                for up in (True, False):

                    @pl.when(receives(up, t - 1))
                    def _():
                        landed(a, up, t - 1, 0).wait_recv()
                        plane_copy(a, up, t - 1, 3).start()
                        landed(a, up, t - 1, 1).wait_recv()
                        plane_copy(a, up, t - 1, 2).start()

    block_copy(1, False).wait_recv()
    block_copy(2, True).start()
    block_copy(0, False).wait_recv()
    block_copy(3, True).start()

    for t in range(n - 1):
        for a in range(k):
            for up in (True, False):

                @pl.when(sends(up, t))
                def _():
                    z_copy(a, up, t, True).wait_send()

                @pl.when(receives(up, t))
                def _():
                    landed(a, up, t, 2).wait_recv()
                    landed(a, up, t, 3).wait_recv()
                    for kind in range(4):
                        plane_copy(a, up, t, kind).wait_send()

    for kind in (2, 3):
        block_copy(kind, False).wait_recv()
    for kind in range(4):
        block_copy(kind, True).wait_send()
    for c in own:
        c.wait()


def gather_weights(n, arrays, block, cid):
    k = len(arrays)
    DMA = pltpu.SemaphoreType.DMA
    return pl.pallas_call(
        functools.partial(gather_weights_kernel, n, k),
        out_shape=[jax.ShapeDtypeStruct((n,) + a.shape, a.dtype) for a in arrays]
        + [jax.ShapeDtypeStruct((4,) + block.shape, block.dtype)],
        in_specs=[pl.BlockSpec(memory_space=ANY)] * (k + 1),
        out_specs=[pl.BlockSpec(memory_space=ANY)] * (k + 1),
        scratch_shapes=[DMA((k + 1,)), DMA((k, 2, n - 1)), DMA((k, 2, n - 1)), DMA((k, 2, n - 1, 4)), DMA((k, 2, n - 1, 4)), DMA((4,)), DMA((4,))],
        compiler_params=pltpu.CompilerParams(collective_id=cid, has_side_effects=True),
        name="gather_weights",
    )(*arrays, block)


def look_back_kernel(n, near, whole, edge, states, before, box, send, recv, e_send, e_recv):
    spot = Spot()
    s = spot.s
    bar = pltpu.get_barrier_semaphore()
    for i in range(1, n):
        pl.semaphore_signal(
            bar, inc=1, device_id={"seq": (s + i) % n, "mp": spot.m, "dp": spot.d}, device_id_type=MESH
        )
    pl.semaphore_wait(bar, n - 1)
    edge_copy = remote(edge, before, e_send, e_recv, spot.to("up"))

    def copy(i):
        return remote(
            near if i == 1 else whole,
            box.at[i - 1],
            send.at[i - 1],
            recv.at[i - 1],
            {"seq": s + i, "mp": spot.m, "dp": spot.d},
        )

    @pl.when(s + 1 < n)
    def _():
        edge_copy.start()

    for i in range(1, n):

        @pl.when(s + i < n)
        def _():
            copy(i).start()

    states[...] = jnp.zeros_like(states)

    @pl.when(s > 0)
    def _():
        edge_copy.wait_recv()

    @pl.when(s == 0)
    def _():
        before[...] = jnp.zeros_like(before)

    for i in range(1, n):

        @pl.when(s - i >= 0)
        def _():
            copy(i).wait_recv()
            states[...] += box[i - 1].astype(jnp.float32)

    @pl.when(s + 1 < n)
    def _():
        edge_copy.wait_send()

    for i in range(1, n):

        @pl.when(s + i < n)
        def _():
            copy(i).wait_send()


def look_back(n, near, whole, edge, cid):
    DMA = pltpu.SemaphoreType.DMA
    vmem = pl.BlockSpec(memory_space=pltpu.VMEM)
    return pl.pallas_call(
        functools.partial(look_back_kernel, n),
        out_shape=[
            jax.ShapeDtypeStruct(whole.shape, jnp.float32),
            jax.ShapeDtypeStruct(edge.shape, edge.dtype),
        ],
        in_specs=[vmem] * 3,
        out_specs=[vmem] * 2,
        scratch_shapes=[pltpu.VMEM((n - 1,) + whole.shape, whole.dtype), DMA((n - 1,)), DMA((n - 1,)), DMA, DMA],
        compiler_params=pltpu.CompilerParams(collective_id=cid, has_side_effects=True, vmem_limit_bytes=40 << 20),
        name="look_back",
    )(near, whole, edge)


def plane_total_kernel(
    n, shared, part, out, mine, core_in, near, line, c_send, c_recv, p_send, p_recv, z_send, z_recv, g_send, g_recv
):
    spot = Spot()
    s, m, d = spot.s, spot.m, spot.d
    h = out.shape[1]
    f32, b16 = jnp.float32, jnp.bfloat16
    mine[...] = part[...].astype(b16)
    bar = pltpu.get_barrier_semaphore()
    plane = [{"seq": s, "mp": m, "dp": (d + i) % 4} for i in range(1, 4)]
    lines = [{"seq": (s + i) % n, "mp": m, "dp": d} for i in range(1, n)]
    for where in plane + lines + [spot.to("c")]:
        pl.semaphore_signal(bar, inc=1, device_id=where, device_id_type=MESH)
    pl.semaphore_wait(bar, n + 3)
    core = remote(mine.at[pl.ds(0, shared)], core_in, c_send, c_recv, spot.to("c"))
    core.start()
    core.wait()
    mine[:shared] = (mine[:shared].astype(f32) + core_in[...].astype(f32)).astype(b16)

    def rows(who):
        return pl.ds(pl.multiple_of(who * h, h), h)

    def scatter(i):
        return remote(mine.at[rows((d + i) % 4)], near.at[i - 1], p_send.at[i - 1], p_recv.at[i - 1], plane[i - 1])

    for i in (2, 1, 3):
        scatter(i).start()
    total = mine[rows(d)].astype(f32)
    for i in range(1, 4):
        scatter(i).wait_recv()
        total = total + near[i - 1].astype(f32)
    line[s] = total.astype(b16)

    def along(i, sending):
        who = s if sending else (s - i) % n
        return remote(line.at[who], line.at[who], z_send.at[i - 1], z_recv.at[i - 1], lines[i - 1])

    for i in range(1, n):
        along(i, True).start()
    for i in range(1, n):
        along(i, False).wait_recv()
    total = line[0].astype(f32)
    for i in range(1, n):
        total = total + line[i].astype(f32)
    out[d] = total.astype(b16)

    def back(i, sending):
        who = d if sending else (d - i) % 4
        return remote(out.at[who], out.at[who], g_send.at[i - 1], g_recv.at[i - 1], plane[i - 1])

    for i in (2, 1, 3):
        back(i, True).start()
    for i in range(1, 4):
        back(i, False).wait_recv()
    for i in range(1, 4):
        scatter(i).wait_send()
        back(i, True).wait_send()
    for i in range(1, n):
        along(i, True).wait_send()


def plane_total(n, part, shared, cid):
    DMA = pltpu.SemaphoreType.DMA
    V = pltpu.VMEM
    b = jnp.bfloat16
    rows, w = part.shape
    h = rows // 4
    return pl.pallas_call(
        functools.partial(plane_total_kernel, n, shared),
        out_shape=jax.ShapeDtypeStruct((4, h, w), b),
        in_specs=[pl.BlockSpec(memory_space=pltpu.VMEM)],
        out_specs=pl.BlockSpec(memory_space=pltpu.VMEM),
        scratch_shapes=[
            V((rows, w), b),
            V((shared, w), b),
            V((3, h, w), b),
            V((n, h, w), b),
            DMA,
            DMA,
            DMA((3,)),
            DMA((3,)),
            DMA((n - 1,)),
            DMA((n - 1,)),
            DMA((3,)),
            DMA((3,)),
        ],
        compiler_params=pltpu.CompilerParams(collective_id=cid, has_side_effects=True, vmem_limit_bytes=40 << 20),
        name="plane_total",
    )(part)


SPAN, TILE = 64, 128
REACH = TILE + SPAN


def mm(left, right, contract=((1,), (0,))):
    return lax.dot_general(left, right, (contract, ((), ())), preferred_element_type=jnp.float32)


def halves(shape, value):
    r = lax.broadcasted_iota(jnp.int32, shape, 0) // 64
    c = lax.broadcasted_iota(jnp.int32, shape, 1) // 64
    return jnp.where(r == c, value, 0.0).astype(jnp.bfloat16)


def signed_map(matrix):
    return jnp.concatenate([matrix, -matrix], 1)


def maps_of(logits):
    left = lax.broadcasted_iota(jnp.int32, logits.shape, 1) < 64
    low = jnp.max(jnp.where(left, logits, -jnp.inf), -1, keepdims=True)
    high = jnp.max(jnp.where(left, -jnp.inf, logits), -1, keepdims=True)
    e = jnp.exp(logits - jnp.where(left, low, high))
    sums = mm(e.astype(jnp.bfloat16), halves((128, 128), 1.0))
    return e / sums


def maps_back(maps, dmaps):
    p = (maps * dmaps).astype(jnp.bfloat16)
    return maps * (dmaps - mm(p, halves((128, 128), 1.0)))


def with_ones(values, first):
    rows = values.shape[0]
    r = lax.broadcasted_iota(jnp.int32, (rows, 64), 0)
    c = lax.broadcasted_iota(jnp.int32, (rows, 64), 1)
    ones = jnp.where((c == 0) & (r >= first), 1.0, 0.0).astype(jnp.bfloat16)
    return jnp.concatenate([values, ones], 1)


def pick(column):
    r = lax.broadcasted_iota(jnp.int32, (8, 128), 0)
    c = lax.broadcasted_iota(jnp.int32, (8, 128), 1)
    return jnp.where((r == 0) & (c == column), 1.0, 0.0).astype(jnp.bfloat16)


def identity():
    r = lax.broadcasted_iota(jnp.int32, (128, 128), 0)
    c = lax.broadcasted_iota(jnp.int32, (128, 128), 1)
    return jnp.where(r == c, 1.0, 0.0).astype(jnp.bfloat16)


def start_row():
    return jnp.where(lax.axis_index("seq") == 0, SPAN, 0)


def key_state_kernel(kv, kmaps, near, whole):
    b16 = jnp.bfloat16
    rows = kv.shape[1]
    near[512:] = jnp.zeros((16, 128), b16)
    whole[512:] = jnp.zeros((16, 128), b16)
    for e in range(2):
        for gp in range(2):
            parts = ([], [])
            for j in range(2):
                g = 2 * gp + j
                keys = kv[e, :, g * 64 : g * 64 + 64]
                values = with_ones(kv[e, :, 256 + g * 64 : 320 + g * 64], 0)
                feats = maps_of(mm(keys, signed_map(kmaps[g]))).astype(b16)
                cut = rows - SPAN
                state = mm(feats[:cut], values[:cut], ((0,), (0,)))
                for out, part in ((near, 0), (whole, 1)):
                    if part:
                        state = state + mm(feats[cut:], values[cut:], ((0,), (0,)))
                    parts[part].append(state[:, :64])
                    total = mm(pick(64), state.astype(b16), ((1,), (1,)))
                    out[512 + e * 4 + g : 513 + e * 4 + g] = total[:1].astype(b16)
            for out, part in ((near, 0), (whole, 1)):
                block = jnp.concatenate(parts[part], 1).astype(b16)
                out[(e * 2 + gp) * 128 : (e * 2 + gp) * 128 + 128] = block


def key_state(kv, kmaps):
    vmem = pl.BlockSpec(memory_space=pltpu.VMEM)
    return pl.pallas_call(
        key_state_kernel,
        out_shape=[jax.ShapeDtypeStruct((528, 128), jnp.bfloat16)] * 2,
        in_specs=[vmem] * 2,
        out_specs=[vmem] * 2,
        compiler_params=pltpu.CompilerParams(vmem_limit_bytes=40 << 20),
        name="key_state",
    )(kv, kmaps)


STACK = 4


def masks():
    r = lax.broadcasted_iota(jnp.int32, (STACK * TILE, REACH), 0) % TILE
    c = lax.broadcasted_iota(jnp.int32, (STACK * TILE, REACH), 1)
    return (c > r) & (c <= r + SPAN), c <= r


def stacked(ref, rows, head):
    return jnp.concatenate([ref[rows, (head + i) * 64 : (head + i) * 64 + 64] for i in range(STACK)], 0)


def beside(value):
    return jnp.concatenate([value[i * TILE : (i + 1) * TILE] for i in range(STACK)], 1)


def query_logits(queries, qmaps, head):
    return jnp.concatenate(
        [mm(queries[i * TILE : (i + 1) * TILE], signed_map(qmaps[head + i])) for i in range(STACK)], 0
    )


def state_of(states, totals, e, gp, j):
    b16 = jnp.bfloat16
    column = mm(identity(), totals[...].astype(b16), ((1,), (1,)))
    row = e * 4 + 2 * gp + j
    pickcol = lax.broadcasted_iota(jnp.int32, column.shape, 1) == row
    one = jnp.sum(jnp.where(pickcol, column, 0.0), -1, keepdims=True)
    c = lax.broadcasted_iota(jnp.int32, (128, 64), 1)
    return jnp.concatenate([states[:, j * 64 : j * 64 + 64], jnp.where(c == 0, one, 0.0)], 1)


def attend_kernel(q, k, v, st, tot, qmaps, kmaps, out, qf, inv):
    gp, e = pl.program_id(0), pl.program_id(1)
    first = start_row()
    b16 = jnp.bfloat16
    window, older = masks()
    for j in range(2):
        keys = k[0, :, j * 64 : j * 64 + 64]
        values = with_ones(v[0, :, j * 64 : j * 64 + 64], first)
        kfeats = maps_of(mm(keys, signed_map(kmaps[j]))).astype(b16)
        keys8 = keys * jnp.asarray(0.125, b16)
        state = state_of(st, tot, e, gp, j)
        for i in range(2):
            if i:
                state = state + mm(kfeats[:TILE], values[:TILE], ((0,), (0,)))
            state16 = state.astype(b16)
            reach = slice(i * TILE, i * TILE + REACH)
            rows = slice(i * TILE, (i + 1) * TILE)
            for h in range(0, 4, STACK):
                head = j * 4 + h
                query = stacked(q, rows, head)
                qfeats = maps_of(query_logits(query, qmaps, head)).astype(b16)
                near = mm(query, keys8[reach], ((1,), (1,)))
                far = mm(qfeats, kfeats[reach], ((1,), (1,)))
                weights = jnp.where(window, jnp.exp(near), jnp.where(older, far, 0.0))
                both = mm(weights.astype(b16), values[reach]) + mm(qfeats, state16)
                part = 1.0 / both[:, 64:65]
                out[rows, head * 64 : (head + STACK) * 64] = beside((both[:, :64] * part).astype(b16))
                inv[0, rows, head : head + STACK] = beside(part)
                qf[0, 0, head // STACK, i] = qfeats


STACKED = pl.BlockSpec((1, 1, 8 // STACK, 2, STACK * TILE, 128), lambda g, e: (e, g, 0, 0, 0, 0))


def attend(q, kv_ext, st, qmaps, kmaps):
    return pl.pallas_call(
        attend_kernel,
        grid=(2, 2),
        out_shape=[
            jax.ShapeDtypeStruct(q.shape, jnp.bfloat16),
            jax.ShapeDtypeStruct((2, 2, 8 // STACK, 2, STACK * TILE, 128), jnp.bfloat16),
            jax.ShapeDtypeStruct((2, 512, 8), jnp.float32),
        ],
        in_specs=[
            pl.BlockSpec((256, 512), lambda g, e: (e, g)),
            pl.BlockSpec((1, 320, 128), lambda g, e: (e, 0, g)),
            pl.BlockSpec((1, 320, 128), lambda g, e: (e, 0, 2 + g)),
            pl.BlockSpec((128, 128), lambda g, e: (e * 2 + g, 0)),
            pl.BlockSpec((16, 128), lambda g, e: (32, 0)),
            pl.BlockSpec((8, 64, 64), lambda g, e: (g, 0, 0)),
            pl.BlockSpec((2, 64, 64), lambda g, e: (g, 0, 0)),
        ],
        out_specs=[
            pl.BlockSpec((256, 512), lambda g, e: (e, g)),
            STACKED,
            pl.BlockSpec((1, 256, 8), lambda g, e: (g, e, 0)),
        ],
        compiler_params=pltpu.CompilerParams(vmem_limit_bytes=40 << 20),
        name="attend",
    )(q, kv_ext, kv_ext, st, st, qmaps, kmaps)


def state_back_kernel(attn, dattn, inv, qf, grad1, dst, dtot):
    b16, f32 = jnp.bfloat16, jnp.float32
    lane = lax.broadcasted_iota(jnp.int32, (STACK * TILE, 64), 1)
    states = []
    for j in range(2):
        total = None
        for h in range(0, 4, STACK):
            head = j * 4 + h
            for i in range(2):
                rows = slice(i * TILE, (i + 1) * TILE)
                part = jnp.concatenate([inv[0, rows, head + z : head + z + 1] for z in range(STACK)], 0)
                grad = stacked(dattn, rows, head).astype(f32) * part
                c = jnp.sum(grad * stacked(attn, rows, head).astype(f32), -1, keepdims=True)
                one = jnp.concatenate([grad, jnp.where(lane == 0, -c, 0.0)], 1).astype(b16)
                grad1[0, 0, head // STACK, i] = one
                g = mm(qf[0, 0, head // STACK, i], one, ((0,), (0,)))
                total = g if total is None else total + g
        states.append(total[:, :64])
        dtot[0, 0, j * 8 : j * 8 + 8] = mm(pick(64), total.astype(b16), ((1,), (1,))).astype(b16)
    dst[...] = jnp.concatenate(states, 1).astype(b16)


def state_back(attn, dattn, inv, qf):
    b16 = jnp.bfloat16
    rows = pl.BlockSpec((256, 512), lambda g, e: (e, g))
    return pl.pallas_call(
        state_back_kernel,
        grid=(2, 2),
        out_shape=[
            jax.ShapeDtypeStruct(qf.shape, b16),
            jax.ShapeDtypeStruct((512, 128), b16),
            jax.ShapeDtypeStruct((2, 2, 16, 128), b16),
        ],
        in_specs=[rows, rows, pl.BlockSpec((1, 256, 8), lambda g, e: (g, e, 0)), STACKED],
        out_specs=[
            STACKED,
            pl.BlockSpec((128, 128), lambda g, e: (e * 2 + g, 0)),
            pl.BlockSpec((1, 1, 16, 128), lambda g, e: (e, g, 0, 0)),
        ],
        compiler_params=pltpu.CompilerParams(vmem_limit_bytes=40 << 20),
        cost_estimate=pl.CostEstimate(flops=8 * 10**9, bytes_accessed=10**6, transcendentals=0),
        name="state_back",
    )(attn, dattn, inv, qf)


def attend_back_kernel(q, k, v, st, tot, qmaps, kmaps, qf, gr, dq, dk, dv, dkf, dqm):
    gp, e = pl.program_id(0), pl.program_id(1)
    first = start_row()
    b16, f32 = jnp.bfloat16, jnp.float32
    window, older = masks()
    eighth = jnp.asarray(0.125, b16)
    dk[...] = jnp.zeros_like(dk)
    dv[...] = jnp.zeros_like(dv)
    dkf[...] = jnp.zeros_like(dkf)

    @pl.when(e == 0)
    def _():
        dqm[...] = jnp.zeros_like(dqm)

    for j in range(2):
        keys = k[0, :, j * 64 : j * 64 + 64]
        values = with_ones(v[0, :, j * 64 : j * 64 + 64], first)
        kfeats = maps_of(mm(keys, signed_map(kmaps[j]))).astype(b16)
        keys8 = keys * eighth
        state = state_of(st, tot, e, gp, j)
        for i in range(2):
            if i:
                state = state + mm(kfeats[:TILE], values[:TILE], ((0,), (0,)))
            state16 = state.astype(b16)
            reach = slice(i * TILE, i * TILE + REACH)
            rows = slice(i * TILE, (i + 1) * TILE)
            dvalue = dkey = dkfeat = g = None
            for h in range(0, 4, STACK):
                head = j * 4 + h
                query = stacked(q, rows, head)
                grad1 = gr[0, 0, head // STACK, i]
                qfeats = qf[0, 0, head // STACK, i]
                qmap = qfeats.astype(f32)
                near = mm(query, keys8[reach], ((1,), (1,)))
                far = mm(qfeats, kfeats[reach], ((1,), (1,)))
                close = jnp.where(window, jnp.exp(near), 0.0)
                weights = (close + jnp.where(older, far, 0.0)).astype(b16)
                dweights = mm(grad1, values[reach], ((1,), (1,)))
                ds = (close * dweights).astype(b16)
                dl = jnp.where(older, dweights, 0.0).astype(b16)
                dqmap = mm(dl, kfeats[reach]) + mm(grad1, state16, ((1,), (1,)))
                da = maps_back(qmap, dqmap).astype(b16)
                dmaps = []
                for z in range(STACK):
                    part = slice(z * TILE, (z + 1) * TILE)
                    dmaps.append(mm(da[part], signed_map(qmaps[head + z]), ((1,), (1,))))
                    x = mm(query[part], da[part], ((0,), (0,)))
                    dqm[head + z] += x[:, :64] - x[:, 64:]
                dquery = mm(ds, keys8[reach]) + jnp.concatenate(dmaps, 0)
                dq[rows, head * 64 : (head + STACK) * 64] = beside(dquery.astype(b16))
                a1 = mm(weights, grad1, ((0,), (0,)))
                a2 = mm(ds, query * eighth, ((0,), (0,)))
                a3 = mm(dl, qfeats, ((0,), (0,)))
                a4 = mm(qfeats, grad1, ((0,), (0,))) if i else None
                if dvalue is None:
                    dvalue, dkey, dkfeat, g = a1, a2, a3, a4
                else:
                    dvalue, dkey, dkfeat = dvalue + a1, dkey + a2, dkfeat + a3
                    g = g + a4 if i else None
            dv[0, reach, j * 64 : j * 64 + 64] += dvalue[:, :64]
            dk[0, reach, j * 64 : j * 64 + 64] += dkey
            dkf[0, j, reach] += dkfeat
            if i:
                g16 = g.astype(b16)
                dkf[0, j, :TILE] += mm(values[:TILE], g16, ((1,), (1,)))
                dv[0, :TILE, j * 64 : j * 64 + 64] += mm(kfeats[:TILE], g16)[:, :64]


def attend_back(q, kv_ext, st, qmaps, kmaps, qf, grad1):
    f32, b16 = jnp.float32, jnp.bfloat16
    e2, ext = kv_ext.shape[:2]
    return pl.pallas_call(
        attend_back_kernel,
        grid=(2, 2),
        out_shape=[
            jax.ShapeDtypeStruct(q.shape, b16),
            jax.ShapeDtypeStruct((e2, ext, 256), f32),
            jax.ShapeDtypeStruct((e2, ext, 256), f32),
            jax.ShapeDtypeStruct((e2, 4, ext, 128), f32),
            jax.ShapeDtypeStruct((16, 64, 64), f32),
        ],
        in_specs=[
            pl.BlockSpec((256, 512), lambda g, e: (e, g)),
            pl.BlockSpec((1, 320, 128), lambda g, e: (e, 0, g)),
            pl.BlockSpec((1, 320, 128), lambda g, e: (e, 0, 2 + g)),
            pl.BlockSpec((128, 128), lambda g, e: (e * 2 + g, 0)),
            pl.BlockSpec((16, 128), lambda g, e: (32, 0)),
            pl.BlockSpec((8, 64, 64), lambda g, e: (g, 0, 0)),
            pl.BlockSpec((2, 64, 64), lambda g, e: (g, 0, 0)),
            STACKED,
            STACKED,
        ],
        out_specs=[
            pl.BlockSpec((256, 512), lambda g, e: (e, g)),
            pl.BlockSpec((1, 320, 128), lambda g, e: (e, 0, g)),
            pl.BlockSpec((1, 320, 128), lambda g, e: (e, 0, g)),
            pl.BlockSpec((1, 2, 320, 128), lambda g, e: (e, g, 0, 0)),
            pl.BlockSpec((8, 64, 64), lambda g, e: (g, 0, 0)),
        ],
        compiler_params=pltpu.CompilerParams(vmem_limit_bytes=40 << 20),
        cost_estimate=pl.CostEstimate(flops=8 * 10**9, bytes_accessed=10**7, transcendentals=4 * 10**6),
        name="attend_back",
    )(q, kv_ext, kv_ext, st, st, qmaps, kmaps, qf, grad1)


def key_back_kernel(k, v, later, tot, kmaps, dk_in, dv_in, dkf, dk, dv, dkm):
    gp, e = pl.program_id(0), pl.program_id(1)
    first = start_row()
    b16 = jnp.bfloat16

    @pl.when(e == 0)
    def _():
        dkm[...] = jnp.zeros_like(dkm)

    dks, dvs = [], []
    for j in range(2):
        cols = slice(j * 64, j * 64 + 64)
        keys = k[0, :, cols]
        values = with_ones(v[0, :, cols], first)
        signed = signed_map(kmaps[j])
        kmap = maps_of(mm(keys, signed))
        g = state_of(later, tot, e, gp, j).astype(b16)
        more = mm(values[:256], g, ((1,), (1,)))
        dmap = jnp.concatenate([dkf[0, j, :256] + more, dkf[0, j, 256:]], 0)
        da = maps_back(kmap, dmap).astype(b16)
        dks.append(dk_in[0, :, cols] + mm(da, signed, ((1,), (1,))))
        moved = mm(kmap[:256].astype(b16), g)[:, :64]
        dvs.append(jnp.concatenate([dv_in[0, :256, cols] + moved, dv_in[0, 256:, cols]], 0))
        x = mm(keys, da, ((0,), (0,)))
        dkm[j] += x[:, :64] - x[:, 64:]
    dk[0] = jnp.concatenate(dks, 1)
    dv[0] = jnp.concatenate(dvs, 1)


def key_back(kv_ext, later, kmaps, dk, dv, dkf):
    f32 = jnp.float32
    piece = pl.BlockSpec((1, 320, 128), lambda g, e: (e, 0, g))
    return pl.pallas_call(
        key_back_kernel,
        grid=(2, 2),
        out_shape=[
            jax.ShapeDtypeStruct(dk.shape, f32),
            jax.ShapeDtypeStruct(dv.shape, f32),
            jax.ShapeDtypeStruct((4, 64, 64), f32),
        ],
        in_specs=[
            piece,
            pl.BlockSpec((1, 320, 128), lambda g, e: (e, 0, 2 + g)),
            pl.BlockSpec((128, 128), lambda g, e: (e * 2 + g, 0)),
            pl.BlockSpec((16, 128), lambda g, e: (32, 0)),
            pl.BlockSpec((2, 64, 64), lambda g, e: (g, 0, 0)),
            piece,
            piece,
            pl.BlockSpec((1, 2, 320, 128), lambda g, e: (e, g, 0, 0)),
        ],
        out_specs=[piece, piece, pl.BlockSpec((2, 64, 64), lambda g, e: (g, 0, 0))],
        compiler_params=pltpu.CompilerParams(vmem_limit_bytes=40 << 20),
        name="key_back",
    )(kv_ext, kv_ext, later, later, kmaps, dk, dv, dkf)


CHUNKS = 4


def feed_kernel(n, k, early, xn_own, ct_all, packed, gate, up, down, res, gain, gsum, dres16, out_part, *scratch):
    (xn, ct, gw, uw, dw, da, oa, xin, yin, t2, xin2, yin2) = scratch[:12]
    (o_sem, a_send, a_recv, w_sem, w_send, w_recv, z_sem, z_send, z_recv, c_send, c_recv, p_send, p_recv, st_sem, e_sem) = scratch[12:]
    spot = Spot()
    s, m, d = spot.s, spot.m, spot.d
    f32, b16 = jnp.float32, jnp.bfloat16
    unit = gw.shape[3] // 2
    wd = min(unit, k)
    gs, ds = unit // wd, k // wd
    half = xn.shape[1] // 2
    A, B = pl.ds(0, half), pl.ds(half, half)

    own = [pltpu.make_async_copy(xn_own, xn.at[3], o_sem.at[0]), pltpu.make_async_copy(ct_all, ct, o_sem.at[1])]
    for c in own:
        c.start()

    lanes = pl.ds(pl.multiple_of(m * unit, unit), unit)

    def own_piece(q):
        start = pl.multiple_of(d * (CHUNKS * unit) + q * unit, unit)
        return (
            (gate.at[:, pl.ds(start, unit)], gw.at[q, s, :, lanes]),
            (up.at[:, pl.ds(start, unit)], uw.at[q, s, :, lanes]),
            (down.at[pl.ds(start, unit)], dw.at[q, s, lanes]),
        )

    def piece(q, w, who):
        return (gw.at[q, who, :, lanes], uw.at[q, who, :, lanes], dw.at[q, who, lanes])[w]

    late = tuple(range(early, CHUNKS))
    own_weights = [
        pltpu.make_async_copy(src, dst, z_sem.at[i, w])
        for i, q in enumerate(late)
        for w, (src, dst) in enumerate(own_piece(q))
    ]
    for c in own_weights:
        c.start()

    def early_parts(q):
        parts = []
        at = 0
        for ref in (gw, uw):
            for i in range(gs):
                cols = pl.ds(pl.multiple_of(m * unit + i * wd, wd), wd)
                parts.append((packed.at[:, q, pl.ds(at, k)], ref.at[q, :, :, cols]))
                at += k
        for i in range(ds):
            parts.append((packed.at[:, q, pl.ds(at, unit)], dw.at[q, :, lanes, pl.ds(i * wd, wd)]))
            at += unit
        return parts

    early_own = [
        [pltpu.make_async_copy(src, dst, w_sem.at[q, i]) for i, (src, dst) in enumerate(early_parts(q))]
        for q in range(early)
    ]
    for copies in early_own:
        for c in copies:
            c.start()

    greet(spot, n, ("x", "y", "c", "up", "dn"))

    def block_copy(kind, sending):
        if kind < 2:
            dst = xn.at[kind + 1]
            src = xn_own if sending else dst
        else:
            rows = (A, B)[kind - 2]
            dst = xn.at[0, rows]
            src = xn.at[(2, 1)[kind - 2], rows] if sending else dst
        return remote(src, dst, a_send.at[kind], a_recv.at[kind], spot.to("xyxy"[kind]))

    block_copy(0, True).start()
    block_copy(1, True).start()

    def sends(upward, t):
        return ((s - t >= 0) & (s + 1 < n)) if upward else ((s + t < n) & (s > 0))

    def receives(upward, t):
        return s - 1 - t >= 0 if upward else s + 1 + t < n

    def z_copy(i, w, upward, t, sending):
        q = late[i]
        way = 0 if upward else 1
        who = (s - t if upward else s + t) if sending else (s - 1 - t if upward else s + 1 + t)
        dst = piece(q, w, who)
        src = own_piece(q)[w][0] if (t == 0 and sending) else dst
        return remote(src, dst, z_send.at[i, w, way, t], z_recv.at[i, w, way, t], spot.to("up" if upward else "dn"))

    for i in range(len(late)):
        for w in range(3):
            for upward in (True, False):

                @pl.when(sends(upward, 0))
                def _():
                    z_copy(i, w, upward, 0, True).start()

    def early_core(q):
        return [
            remote(src, dst, w_send.at[q, i], w_recv.at[q, i], spot.to("c")) for i, (src, dst) in enumerate(early_parts(q))
        ]

    def theirs(q, w, who):
        other = pl.ds(pl.multiple_of((1 - m) * unit, unit), unit)
        return (gw.at[q, who, :, other], uw.at[q, who, :, other], dw.at[q, who, other])[w]

    def core_copy(i, w, who, sending):
        q = late[i]
        ref = piece(q, w, who) if sending else theirs(q, w, who)
        return remote(ref, ref, c_send.at[i, w, who], c_recv.at[i, w, who], spot.to("c"))

    for q in range(early):
        for c in early_core(q):
            c.start()

    def relay(i, t, w):
        for upward in (True, False):

            @pl.when(receives(upward, t))
            def _():
                z_copy(i, w, upward, t, False).wait_recv()
                if t + 1 < n - 1:

                    @pl.when(sends(upward, t + 1))
                    def _():
                        z_copy(i, w, upward, t + 1, True).start()

                core_copy(i, w, s - 1 - t if upward else s + 1 + t, True).start()

    for i in range(len(late)):
        for w in range(3):
            own_weights[3 * i + w].wait()
            core_copy(i, w, s, True).start()

    for c in own:
        c.wait()

    first = (
        remote(xn.at[0, A], xin.at[1], p_send.at[0], p_recv.at[0], spot.to("x")),
        remote(xn.at[0, B], yin.at[1], p_send.at[1], p_recv.at[1], spot.to("y")),
        remote(xn.at[1, A], xin.at[0], p_send.at[2], p_recv.at[2], spot.to("x")),
        remote(xn.at[2, B], yin.at[0], p_send.at[3], p_recv.at[3], spot.to("y")),
    )
    stores = [pltpu.make_async_copy(ct.at[i], out_part.at[i], st_sem.at[i]) for i in range(4)]

    again = (
        pltpu.make_async_copy(res, da.at[0], e_sem.at[0]),
        pltpu.make_async_copy(ct_all.at[3], ct.at[0], e_sem.at[1]),
    )

    steps = 4 * CHUNKS
    turns = {}
    total = len(late) * (n - 1) * 3
    for j in range(total):
        i, t, w = j // (3 * n - 3), j // 3 % (n - 1), j % 3
        at = min(4 * late[i], 1 + (4 * late[i] - 1) * j // ((i + 1) * (n - 1) * 3))
        turns.setdefault(at, []).append((i, t, w))

    @pl.loop(0, steps)
    def _(step):
        last = step >= steps - 4
        c = jnp.where(step < 4 * early, step % early, step // 4)
        t = jnp.where(step < 4 * early, 3 - step // early, step % 4)

        for q in range(early):

            @pl.when(step == q)
            def _():
                for copy in early_own[q]:
                    copy.wait()
                for copy in early_core(q):
                    copy.wait_recv()

        for at, jobs in turns.items():

            @pl.when(step == at)
            def _():
                for i, t, w in jobs:
                    relay(i, t, w)

        for i, q in enumerate(late):

            @pl.when(step == 4 * q)
            def _():
                for w in range(3):
                    for who in range(n):
                        core_copy(i, w, who, False).wait_recv()

        @pl.when(step == early)
        def _():
            block_copy(1, False).wait_recv()
            block_copy(2, True).start()
            block_copy(0, False).wait_recv()
            block_copy(3, True).start()

        @pl.when(step == 3 * early)
        def _():
            for kind in (2, 3):
                block_copy(kind, False).wait_recv()
            for kind in range(4):
                block_copy(kind, True).wait_send()

        x, cot = xn[t], ct[t]
        g_all = gw[c].reshape(n * k, 2 * unit)
        u_all = uw[c].reshape(n * k, 2 * unit)
        g = mm(x, g_all)
        u = mm(x, u_all)
        dh = mm(cot[:, :k], dw[c, 0], ((1,), (1,)))
        for i in range(1, n):
            dh = dh + mm(cot[:, i * k : (i + 1) * k], dw[c, i], ((1,), (1,)))
        sig = 1.0 / (1.0 + jnp.exp(-g))
        act = g * sig
        hid = (act * u).astype(b16)
        dg = (dh * u * sig * (1.0 + g * (1.0 - sig))).astype(b16)
        du = (dh * act).astype(b16)
        for i in range(n):
            cols = slice(i * k, (i + 1) * k)
            o = mm(hid, dw[c, i])
            e = mm(dg, gw[c, i], ((1,), (1,))) + mm(du, uw[c, i], ((1,), (1,)))

            @pl.when(c == 0)
            def _():
                oa[t, :, cols] = o
                da[t, :, cols] = e

            @pl.when(c > 0)
            def _():
                oa[t, :, cols] += o
                da[t, :, cols] += e

        @pl.when(last)
        def _():
            xn[t] = da[t].astype(b16)
            ct[t] = oa[t].astype(b16)

        for i in range(4):

            @pl.when(step == steps - 4 + i)
            def _():
                stores[i].start()
                if i == 1:
                    again[0].start()
                if i == 0:
                    first[0].start()
                    first[1].start()
                elif i < 3:
                    first[i + 1].start()

    second = (
        remote(t2.at[0], yin2, p_send.at[4], p_recv.at[4], spot.to("y")),
        remote(t2.at[1], xin2, p_send.at[5], p_recv.at[5], spot.to("x")),
    )
    stores[0].wait()
    again[1].start()
    first[0].wait_recv()
    t2[0] = (xn[2, A].astype(f32) + xin[1].astype(f32)).astype(b16)
    second[0].start()
    first[1].wait_recv()
    t2[1] = (xn[1, B].astype(f32) + yin[1].astype(f32)).astype(b16)
    second[1].start()
    for c in first:
        c.wait_send()
    for c in again:
        c.wait()
    first[2].wait_recv()
    first[3].wait_recv()
    second[0].wait_recv()
    second[1].wait_recv()
    scale = gain[...].astype(f32)
    chunk = half // 4
    gsum[...] = jnp.zeros_like(gsum)
    for part, inner, outer in ((0, xin, yin2), (1, yin, xin2)):

        @pl.loop(0, 4)
        def _(i):
            at = pl.ds(pl.multiple_of(i * chunk, chunk), chunk)
            rows = pl.ds(pl.multiple_of(part * half + i * chunk, chunk), chunk)
            dxn = da[3, rows] + inner[0, at].astype(f32) + outer[at].astype(f32)
            r = da[0, rows]
            inv = lax.rsqrt(jnp.mean(r * r, -1, keepdims=True) + epsilon)
            ri = r * inv
            gsum[...] += jnp.sum((dxn * ri).reshape(chunk // 8, 8, -1), 0)
            gx = scale * dxn
            grad = ct[0, rows].astype(f32) + inv * (gx - ri * jnp.mean(gx * ri, -1, keepdims=True))
            xn[0, rows] = grad.astype(b16)

    swap = remote(xn.at[0], dres16.at[m], e_sem.at[2], e_sem.at[3], spot.to("c"))
    keep = pltpu.make_async_copy(xn.at[0], dres16.at[m], e_sem.at[4])
    swap.start()
    keep.start()
    keep.wait()
    swap.wait_send()
    remote(xn.at[0], dres16.at[1 - m], e_sem.at[2], e_sem.at[3], spot.to("c")).wait_recv()
    for c in stores[1:]:
        c.wait()
    for c in second:
        c.wait_send()
    for q in range(early):
        for c in early_core(q):
            c.wait_send()
    for i in range(len(late)):
        for w in range(3):
            for who in range(n):
                core_copy(i, w, who, True).wait_send()
            for t in range(n - 1):
                for upward in (True, False):

                    @pl.when(sends(upward, t))
                    def _():
                        z_copy(i, w, upward, t, True).wait_send()


def feed(n, early, xn_own, ct_all, packed, gate, up, down, res, gain, cid):
    DMA, V = pltpu.SemaphoreType.DMA, pltpu.VMEM
    b, f32 = jnp.bfloat16, jnp.float32
    r, w = xn_own.shape
    k = gate.shape[0]
    unit = gate.shape[1] // (4 * CHUNKS)
    wd = min(unit, k)
    pieces = 2 * (unit // wd) + k // wd
    late = CHUNKS - early
    scratch = [V((4, r, w), b), V((4, r, w), b)]
    scratch += [V((CHUNKS, n, k, 2 * unit), b), V((CHUNKS, n, k, 2 * unit), b), V((CHUNKS, n, 2 * unit, k), b)]
    scratch += [V((4, r, w), f32), V((4, r, w), f32)]
    scratch += [V((2, r // 2, w), b), V((2, r // 2, w), b), V((2, r // 2, w), b), V((r // 2, w), b), V((r // 2, w), b)]
    scratch += [DMA((2,)), DMA((4,)), DMA((4,))]
    scratch += [DMA((max(early, 1), pieces))] * 3
    scratch += [DMA((late, 3)), DMA((late, 3, 2, n - 1)), DMA((late, 3, 2, n - 1)), DMA((late, 3, n)), DMA((late, 3, n))]
    scratch += [DMA((6,)), DMA((6,)), DMA((4,)), DMA((5,))]
    return pl.pallas_call(
        functools.partial(feed_kernel, n, k, early),
        out_shape=[
            jax.ShapeDtypeStruct((8, w), f32),
            jax.ShapeDtypeStruct((2, r, w), b),
            jax.ShapeDtypeStruct((4, r, w), b),
        ],
        in_specs=[pl.BlockSpec(memory_space=ANY)] * 7 + [pl.BlockSpec(memory_space=pltpu.VMEM)],
        out_specs=[pl.BlockSpec(memory_space=pltpu.VMEM)] + [pl.BlockSpec(memory_space=ANY)] * 2,
        scratch_shapes=scratch,
        compiler_params=pltpu.CompilerParams(collective_id=cid, has_side_effects=True, vmem_limit_bytes=62 << 20),
        name="feed",
    )(xn_own, ct_all, packed, gate, up, down, res, gain)


def pack_early(k, early, gate, up, down, d):
    unit = gate.shape[1] // (4 * CHUNKS)
    wd = min(unit, k)
    at = d * (CHUNKS * unit)
    g = lax.dynamic_slice_in_dim(gate, at, early * unit, 1)
    u = lax.dynamic_slice_in_dim(up, at, early * unit, 1)
    dn = lax.dynamic_slice_in_dim(down, at, early * unit, 0)
    chunks = []
    for q in range(early):
        rows = [a[:, q * unit + i : q * unit + i + wd] for a in (g, u) for i in range(0, unit, wd)]
        rows += [dn[q * unit : (q + 1) * unit, i : i + wd] for i in range(0, k, wd)]
        chunks.append(jnp.concatenate(rows, 0))
    return jnp.stack(chunks)


def branch_kernel(n, attn, weight, first, second, tok, gain, res, xn, inner, part, other, send, recv):
    spot = Spot()
    m = spot.m
    f32, b16 = jnp.float32, jnp.bfloat16
    half = attn.shape[0] // 2
    k = weight.shape[2]
    greet(spot, n, ("c",))
    low = mm(attn[...], first[...])
    inner[...] = low

    def terms(who, i):
        rows = pl.ds(pl.multiple_of(who * half, half), half)
        return mm(attn[rows], weight[i]) + mm(
            inner[rows].astype(b16), second[:, i * k : (i + 1) * k]
        )

    for i in range(n):
        part[:, i * k : (i + 1) * k] = terms(1 - m, i).astype(b16)
    swap = remote(part, other, send, recv, spot.to("c"))
    swap.start()
    mine = pl.ds(pl.multiple_of(m * half, half), half)
    for i in range(n):
        cols = slice(i * k, (i + 1) * k)
        res[:, cols] = tok[mine, cols].astype(f32) + terms(m, i)
    swap.wait_recv()
    scale = gain[...].astype(f32)
    step = 64

    @pl.loop(0, half // step)
    def _(i):
        at = pl.ds(pl.multiple_of(i * step, step), step)
        r = res[at] + other[at].astype(f32)
        res[at] = r
        xn[at] = (r * lax.rsqrt(jnp.mean(r * r, -1, keepdims=True) + epsilon) * scale).astype(b16)

    swap.wait_send()


def branch(n, attn, weight, first, second, tok, gain, cid):
    DMA, V = pltpu.SemaphoreType.DMA, pltpu.VMEM
    b, f32 = jnp.bfloat16, jnp.float32
    total, width = tok.shape
    half = total // 2
    vmem = pl.BlockSpec(memory_space=pltpu.VMEM)
    return pl.pallas_call(
        functools.partial(branch_kernel, n),
        out_shape=[
            jax.ShapeDtypeStruct((half, width), f32),
            jax.ShapeDtypeStruct((half, width), b),
            jax.ShapeDtypeStruct((total, first.shape[1]), f32),
        ],
        in_specs=[vmem] * 6,
        out_specs=[vmem] * 3,
        scratch_shapes=[V((half, width), b), V((half, width), b), DMA, DMA],
        compiler_params=pltpu.CompilerParams(collective_id=cid, has_side_effects=True, vmem_limit_bytes=48 << 20),
        name="branch",
    )(attn, weight, first, second, tok, gain)


EARLY = 3


f32, b16 = jnp.float32, jnp.bfloat16


def dot(left, right):
    return jnp.dot(left, right, preferred_element_type=f32)


def dot_t(left, right):
    return lax.dot_general(left, right, (((1,), (1,)), ((), ())), preferred_element_type=f32)


def t_dot(left, right):
    return lax.dot_general(left, right, (((0,), (0,)), ((), ())), preferred_element_type=f32)


def norm_back(inputs, inv_rms, gain, dnormed):
    return inv_rms * gain * dnormed - inputs * inv_rms**3 * jnp.mean(
        gain * dnormed * inputs, -1, keepdims=True
    )


def from_behind(value, axis, steps):
    count = lax.axis_size(axis)
    first, last = (max(0, -steps), min(count, count - steps))
    return lax.ppermute(value, axis, [(source, source + steps) for source in range(first, last)])


def swap_core(value):
    return lax.ppermute(value, "mp", [(0, 1), (1, 0)])


def per_device(
    tokens,
    cotangent,
    attention_norm_gain,
    feedforward_norm_gain,
    query_weight,
    key_weight,
    value_weight,
    output_weight,
    gate_weight,
    up_weight,
    down_weight,
    query_adapter_down,
    query_adapter_up,
    key_adapter_down,
    key_adapter_up,
    value_adapter_down,
    value_adapter_up,
    output_adapter_down,
    output_adapter_up,
    query_feature_matrix,
    key_feature_matrix,
):
    n = lax.axis_size("seq")
    position, m, d = (lax.axis_index(a) for a in ("seq", "mp", "dp"))
    seq_count, rows_here, width = tokens.shape
    total_rows = seq_count * rows_here
    half = total_rows // 2
    heads_kv = key_feature_matrix.shape[0]
    head_size = key_feature_matrix.shape[1]
    groups = query_feature_matrix.shape[0] // heads_kv
    extent = rows_here + SOFTMAX_SPAN

    packed = lax.all_gather(
        pack_early(gate_weight.shape[0], EARLY, gate_weight, up_weight, down_weight, d), "seq"
    )
    def my_half(a):
        return lax.dynamic_slice_in_dim(a, m * half, half, 0)

    cot_half = my_half(cotangent.reshape(total_rows, width))
    qkv_own = jnp.concatenate([query_weight, key_weight, value_weight], 1)
    qkv_g, out_g, cot_blocks = gather_weights(n, [qkv_own, output_weight], cot_half, 1)
    qkv_w = qkv_g.reshape(width, -1)
    wide = query_weight.shape[1]
    kv_wide = key_weight.shape[1]

    def both_halves(own):
        other = swap_core(own)
        return jnp.concatenate([jnp.where(m == 0, own, other), jnp.where(m == 0, other, own)], 0)

    tok2 = tokens.reshape(total_rows, width)
    inputs = tok2.astype(f32)
    gain_attn = attention_norm_gain.astype(f32)
    rms_attn = lax.rsqrt(jnp.mean(inputs * inputs, -1, keepdims=True) + epsilon)
    normed = (inputs * rms_attn * gain_attn).astype(b16)

    downs = jnp.concatenate([query_adapter_down, key_adapter_down, value_adapter_down], 1)
    inner = dot(normed, downs)
    rank = query_adapter_down.shape[1]
    full = dot(normed, qkv_w)

    def project(index, first, last, second):
        return (
            full[:, first:last] + dot(inner[:, index * rank : (index + 1) * rank].astype(b16), second)
        ).astype(b16)

    query_half = project(0, 0, wide, query_adapter_up)
    key_half = project(1, wide, wide + kv_wide, key_adapter_up)
    value_half = project(2, wide + kv_wide, wide + 2 * kv_wide, value_adapter_up)
    key3 = key_half.reshape(seq_count, rows_here, heads_kv * head_size)
    value3 = value_half.reshape(seq_count, rows_here, heads_kv * head_size)
    kv3 = jnp.concatenate([key3, value3], -1)
    near, whole = key_state(kv3, key_feature_matrix)
    states, kv_prev = look_back(n, near, whole, kv3[:, rows_here - SOFTMAX_SPAN :], 3)
    kv_ext = jnp.concatenate([kv_prev, kv3], 1)
    attn16, qfeats, inv_weights = attend(query_half, kv_ext, states, query_feature_matrix, key_feature_matrix)
    resid, normed_mlp, inner_output = branch(
        n,
        attn16,
        out_g,
        output_adapter_down,
        output_adapter_up,
        tok2,
        feedforward_norm_gain.reshape(1, width),
        5,
    )
    mlp_gain_rows, dresid16, out_part = feed(
        n,
        EARLY,
        normed_mlp,
        cot_blocks,
        packed,
        gate_weight,
        up_weight,
        down_weight,
        resid,
        feedforward_norm_gain.reshape(1, width),
        4,
    )
    dresid16 = dresid16.reshape(total_rows, width)

    def swap_chip(value, bit):
        return lax.ppermute(value, "dp", [(i, i ^ bit) for i in range(4)])

    cut = half // 2
    upper_in = swap_chip(out_part[0:2, :cut], 1)
    lower_in = swap_chip(out_part[0::2, cut:], 2)


    mlp_gain_term = jnp.sum(mlp_gain_rows, 0)
    du_o = dot_t(dresid16, output_adapter_up)
    oup_term = t_dot(inner_output.astype(b16), dresid16)
    odown_term = t_dot(du_o.astype(b16), attn16)
    dattn = dot_t(du_o.astype(b16), output_adapter_down)
    step = output_weight.shape[1]
    for i in range(n):
        dattn = dattn + dot_t(dresid16[:, i * step : (i + 1) * step], out_g[i])
    grad1, dstates, dtotals = state_back(attn16, dattn.astype(b16), inv_weights, qfeats)
    dtotals = jnp.pad(dtotals[:, :, ::8].reshape(-1, 128), ((0, 8), (0, 0)))
    dstates = jnp.concatenate([dstates, dtotals], 0)
    later = [from_behind(dstates, "seq", -i) for i in range(1, n)]
    dq16, dk_ext, dv_ext, dkfeats, dqmaps = attend_back(
        query_half, kv_ext, states, query_feature_matrix, key_feature_matrix, qfeats, grad1
    )
    dq16, later, upper_in, lower_in = lax.optimization_barrier((dq16, later, upper_in, lower_in))
    upper_in2 = swap_chip((out_part[2, :cut].astype(f32) + upper_in[0].astype(f32)).astype(b16), 2)
    lower_in2 = swap_chip((out_part[1, cut:].astype(f32) + lower_in[0].astype(f32)).astype(b16), 1)
    later = functools.reduce(jnp.add, [a.astype(f32) for a in later])
    dk_ext, dv_ext, dkmaps = key_back(kv_ext, later, key_feature_matrix, dk_ext, dv_ext, dkfeats)
    dk_ext, upper_in2, lower_in2 = lax.optimization_barrier((dk_ext, upper_in2, lower_in2))
    mlp_out = out_part[3].astype(f32) + jnp.concatenate(
        [
            upper_in[1].astype(f32) + upper_in2.astype(f32),
            lower_in[1].astype(f32) + lower_in2.astype(f32),
        ],
        0,
    )
    output = both_halves((resid + mlp_out).astype(b16)).reshape(seq_count, rows_here, width)
    dkv_ext = jnp.concatenate([dk_ext, dv_ext], -1)
    back = from_behind(dkv_ext[:, :SOFTMAX_SPAN].astype(b16), "seq", -1).astype(f32)
    dkv = dkv_ext[:, SOFTMAX_SPAN:]
    dkv = jnp.concatenate(
        [dkv[:, : rows_here - SOFTMAX_SPAN], dkv[:, rows_here - SOFTMAX_SPAN :] + back], 1
    )
    dqkv16 = jnp.concatenate(
        [dq16, dkv.reshape(total_rows, -1).astype(b16)], 1
    )
    bounds = ((0, wide), (wide, wide + kv_wide), (wide + kv_wide, wide + 2 * kv_wide))
    seconds = (query_adapter_up, key_adapter_up, value_adapter_up)
    dinner = jnp.concatenate(
        [dot_t(dqkv16[:, a:b], second) for (a, b), second in zip(bounds, seconds)], 1
    ).astype(b16)
    dnormed = (dot_t(dqkv16, qkv_w) + dot_t(dinner, downs)).astype(b16)
    down_terms = t_dot(dinner, normed)
    inner16 = inner.astype(b16)
    up_terms = [
        t_dot(inner16[:, i * rank : (i + 1) * rank], dqkv16[:, a:b]) for i, (a, b) in enumerate(bounds)
    ]
    dnormed = dnormed.astype(f32) + swap_core(dnormed).astype(f32)
    attn_gain_term = jnp.sum(my_half(dnormed * inputs * rms_attn), 0)
    tokens_grad = (dresid16.astype(f32) + norm_back(inputs, rms_attn, gain_attn, dnormed)).reshape(
        seq_count, rows_here, width
    )

    shared = [attn_gain_term, mlp_gain_term, down_terms, oup_term]
    split = up_terms + [odown_term, dqmaps, dkmaps]
    flat = [a.reshape(-1, 128) for a in shared + split]
    sizes = [a.shape[0] for a in flat]
    shared_rows = sum(sizes[:4])
    flat = jnp.concatenate(flat, 0)
    flat = jnp.pad(flat, ((0, -flat.shape[0] % 128), (0, 0)))
    summed = plane_total(n, flat, shared_rows, 8).reshape(-1, 128).astype(f32)
    parts, at = [], 0
    for term, size in zip(shared + split, sizes):
        parts.append(summed[at : at + size].reshape(term.shape))
        at += size
    attn_gain, mlp_gain, downs_g, oup, qup, kup, vup, odown, qmaps_g, kmaps_g = parts
    downs_g = downs_g.T
    return (
        output,
        tokens_grad,
        attn_gain,
        mlp_gain,
        downs_g[:, :rank],
        qup,
        downs_g[:, rank : 2 * rank],
        kup,
        downs_g[:, 2 * rank :],
        vup,
        odown.T,
        oup,
        qmaps_g.reshape(query_feature_matrix.shape),
        kmaps_g,
    )


def solution(mesh):
    placed = (
        P("dp", "seq", None),
        P("dp", "seq", None),
        P(),
        P(),
        P("seq", "mp"),
        P("seq", "mp"),
        P("seq", "mp"),
        P("mp", "seq"),
        P("seq", "mp"),
        P("seq", "mp"),
        P("mp", "seq"),
        P(),
        P(None, "mp"),
        P(),
        P(None, "mp"),
        P(),
        P(None, "mp"),
        P("mp", None),
        P(),
        P("mp", None, None),
        P("mp", None, None),
    )
    return jax.shard_map(
        per_device,
        mesh=mesh,
        in_specs=placed,
        out_specs=(
            P("dp", "seq", None),
            P("dp", "seq", None),
            P(),
            P(),
            P(),
            P(None, "mp"),
            P(),
            P(None, "mp"),
            P(),
            P(None, "mp"),
            P("mp", None),
            P(),
            P("mp", None, None),
            P("mp", None, None),
        ),
        check_vma=False,
    )
```

```python
import math
import functools
import jax
import jax.numpy as jnp
from jax import lax
from jax.experimental import pallas as pl
from jax.experimental.pallas import tpu as pltpu
from jax.sharding import PartitionSpec as P

SOFTMAX_SPAN = 64
epsilon = 1e-05

MESH = pl.DeviceIdType.MESH
ANY = pl.ANY


class Spot:
    def __init__(self):
        self.s, self.m, self.d = (lax.axis_index(a) for a in ("seq", "mp", "dp"))
        self.x = self.d + 1 - 2 * (self.d % 2)
        self.y = (self.d + 2) % 4
        self.diag = (self.x + 2) % 4

    def to(self, kind):
        s, m, d = self.s, self.m, self.d
        if kind == "x":
            d = self.x
        elif kind == "y":
            d = self.y
        elif kind == "c":
            m = 1 - m
        elif kind == "up":
            s = s + 1
        elif kind == "dn":
            s = s - 1
        return {"seq": s, "mp": m, "dp": d}


def remote(src, dst, send, recv, where):
    return pltpu.make_async_remote_copy(
        src_ref=src, dst_ref=dst, send_sem=send, recv_sem=recv, device_id=where, device_id_type=MESH
    )


def greet(spot, n, kinds):
    bar = pltpu.get_barrier_semaphore()
    count = 0
    for kind in kinds:
        if kind in ("up", "dn"):
            there = spot.s + 1 < n if kind == "up" else spot.s > 0

            @pl.when(there)
            def _(kind=kind):
                pl.semaphore_signal(bar, inc=1, device_id=spot.to(kind), device_id_type=MESH)

            count = count + there.astype(jnp.int32)
        else:
            pl.semaphore_signal(bar, inc=1, device_id=spot.to(kind), device_id_type=MESH)
            count = count + 1
    pl.semaphore_wait(bar, count)


def opening_kernel(n, k, *refs):
    ins, block, tok, gain, downs, seconds, kmaps = refs[:k], *refs[k : k + 6]
    refs = refs[k + 6 :]
    outs, blocks, normed, inner, query, kv, states, before = refs[:k], *refs[k : k + 7]
    weight, near, whole, box = refs[k + 7 : k + 11]
    own_sem, z_send, z_recv, p_send, p_recv, b_send, b_recv, w_sem, l_send, l_recv, e_send, e_recv = refs[k + 11 :]
    spot = Spot()
    s, d = spot.s, spot.d
    block = block.at[spot.m]
    own = [pltpu.make_async_copy(ins[a], outs[a].at[s], own_sem.at[a]) for a in range(k)]
    own.append(pltpu.make_async_copy(block, blocks.at[3], own_sem.at[k]))
    for c in own:
        c.start()
    bar = pltpu.get_barrier_semaphore()
    others = [{"seq": (s + i) % n, "mp": spot.m, "dp": d} for i in range(1, n)]
    for where in [spot.to("x"), spot.to("y")] + others:
        pl.semaphore_signal(bar, inc=1, device_id=where, device_id_type=MESH)
    pl.semaphore_wait(bar, n + 1)

    cut = block.shape[0] // 2
    parts = (pl.ds(0, cut), pl.ds(cut, cut))

    def block_copy(kind, sending):
        if kind < 2:
            dst = blocks.at[kind + 1]
            src = block if sending else dst
        else:
            dst = blocks.at[0, parts[kind - 2]]
            src = blocks.at[(2, 1)[kind - 2], parts[kind - 2]] if sending else dst
        return remote(src, dst, b_send.at[kind], b_recv.at[kind], spot.to("xyxy"[kind]))

    def rows(a, who, part=None):
        size = ins[a].shape[0] // 4
        if part is None:
            return pl.ds(who * size, size)
        return pl.ds(who * size + part * (size // 2), size // 2)

    def sends(up, t):
        return ((s - t >= 0) & (s + 1 < n)) if up else ((s + t < n) & (s > 0))

    def receives(up, t):
        return s - 1 - t >= 0 if up else s + 1 + t < n

    def z_copy(a, up, t, sending):
        way = 0 if up else 1
        piece = (s - t if up else s + t) if sending else (s - 1 - t if up else s + 1 + t)
        dst = outs[a].at[piece, rows(a, d)]
        src = ins[a].at[rows(a, d)] if (t == 0 and sending) else dst
        return remote(src, dst, z_send.at[a, way, t], z_recv.at[a, way, t], spot.to("up" if up else "dn"))

    def piece_of(up, t):
        return s - 1 - t if up else s + 1 + t

    def plane_copy(a, up, t, kind):
        way = 0 if up else 1
        who = (d, d, spot.y, spot.x)[kind]
        part = (None, None, 0, 1)[kind]
        ref = outs[a].at[piece_of(up, t), rows(a, who, part)]
        return remote(ref, ref, p_send.at[a, way, t, kind], p_recv.at[a, way, t, kind], spot.to("xyxy"[kind]))

    def landed(a, up, t, kind):
        way = 0 if up else 1
        who = (spot.x, spot.y, spot.diag, spot.diag)[kind]
        part = (None, None, 0, 1)[kind]
        ref = outs[a].at[piece_of(up, t), rows(a, who, part)]
        return remote(ref, ref, p_send.at[a, way, t, kind], p_recv.at[a, way, t, kind], spot.to("xyxy"[kind]))

    def begin(a):
        for up in (True, False):

            @pl.when(sends(up, 0))
            def _():
                z_copy(a, up, 0, True).start()

    begin(0)
    f32, b16 = jnp.float32, jnp.bfloat16
    scale = gain[...].astype(f32)
    total = tok.shape[0]

    @pl.loop(0, total // 64)
    def _(i):
        at = pl.ds(pl.multiple_of(i * 64, 64), 64)
        x = tok[at].astype(f32)
        normed[at] = (x * lax.rsqrt(jnp.mean(x * x, -1, keepdims=True) + epsilon) * scale).astype(b16)

    low = mm(normed[...], downs[...])
    inner[...] = low
    for step in range(n + k - 1):
        for a in range(k):
            t = step - a
            if 0 <= t < n - 1:
                for up in (True, False):

                    @pl.when(receives(up, t))
                    def _():
                        z_copy(a, up, t, False).wait_recv()
                        if t + 1 < n - 1:

                            @pl.when(sends(up, t + 1))
                            def _():
                                z_copy(a, up, t + 1, True).start()

                        plane_copy(a, up, t, 0).start()
                        plane_copy(a, up, t, 1).start()

            if t == 0 and a + 1 < k:
                begin(a + 1)
                block_copy(0, True).start()
                block_copy(1, True).start()

            if 0 < t < n:
                for up in (True, False):

                    @pl.when(receives(up, t - 1))
                    def _():
                        landed(a, up, t - 1, 0).wait_recv()
                        plane_copy(a, up, t - 1, 3).start()
                        landed(a, up, t - 1, 1).wait_recv()
                        plane_copy(a, up, t - 1, 2).start()

    block_copy(1, False).wait_recv()
    block_copy(2, True).start()
    block_copy(0, False).wait_recv()
    block_copy(3, True).start()

    own[0].wait()
    for t in range(n - 1):
        for up in (True, False):

            @pl.when(receives(up, t))
            def _():
                landed(0, up, t, 2).wait_recv()
                landed(0, up, t, 3).wait_recv()

    loads = [pltpu.make_async_copy(outs[0].at[i], weight.at[i], w_sem.at[i]) for i in range(n)]
    for c in loads:
        c.start()
    for c in loads:
        c.wait()
    wide = query.shape[1]
    length = kv.shape[1]
    cols = weight.shape[2]
    low16 = low.astype(b16)
    for at in range(0, cols, 512):
        full = mm(normed[...], weight[:, :, at : at + 512].reshape(-1, 512)) + mm(low16, seconds[:, at : at + 512])
        if at < wide:
            query[:, at : at + 512] = full.astype(b16)
        else:
            kv[...] = full.astype(b16).reshape(kv.shape)
    key_states(kv, kmaps, near, whole)

    edge_copy = remote(kv.at[:, pl.ds(length - before.shape[1], before.shape[1])], before, e_send, e_recv, spot.to("up"))

    def state_copy(i):
        return remote(
            near if i == 1 else whole,
            box.at[i - 1],
            l_send.at[i - 1],
            l_recv.at[i - 1],
            {"seq": s + i, "mp": spot.m, "dp": d},
        )

    @pl.when(s + 1 < n)
    def _():
        edge_copy.start()

    for i in range(1, n):

        @pl.when(s + i < n)
        def _():
            state_copy(i).start()

    for t in range(n - 1):
        for a in range(k):
            for up in (True, False):

                @pl.when(sends(up, t))
                def _():
                    z_copy(a, up, t, True).wait_send()

                @pl.when(receives(up, t))
                def _():
                    if a:
                        landed(a, up, t, 2).wait_recv()
                        landed(a, up, t, 3).wait_recv()
                    for kind in range(4):
                        plane_copy(a, up, t, kind).wait_send()

    for kind in (2, 3):
        block_copy(kind, False).wait_recv()
    for kind in range(4):
        block_copy(kind, True).wait_send()
    for c in own[1:]:
        c.wait()

    states[...] = jnp.zeros_like(states)

    @pl.when(s > 0)
    def _():
        edge_copy.wait_recv()

    @pl.when(s == 0)
    def _():
        before[...] = jnp.zeros_like(before)

    for i in range(1, n):

        @pl.when(s - i >= 0)
        def _():
            state_copy(i).wait_recv()
            states[...] += box[i - 1].astype(f32)

    @pl.when(s + 1 < n)
    def _():
        edge_copy.wait_send()

    for i in range(1, n):

        @pl.when(s + i < n)
        def _():
            state_copy(i).wait_send()


def opening(n, arrays, block, tok, gain, downs, seconds, kmaps, wide, cid):
    k = len(arrays)
    DMA, V = pltpu.SemaphoreType.DMA, pltpu.VMEM
    b, f32 = jnp.bfloat16, jnp.float32
    total, width = tok.shape
    cols = arrays[0].shape[1]
    depth = arrays[0].shape[0]
    seqs, rows = block.shape[:2]
    vmem = pl.BlockSpec(memory_space=pltpu.VMEM)
    far = pl.BlockSpec(memory_space=ANY)
    return pl.pallas_call(
        functools.partial(opening_kernel, n, k),
        out_shape=[jax.ShapeDtypeStruct((n,) + a.shape, a.dtype) for a in arrays]
        + [
            jax.ShapeDtypeStruct((4,) + block.shape[1:], b),
            jax.ShapeDtypeStruct((total, width), b),
            jax.ShapeDtypeStruct((total, downs.shape[1]), f32),
            jax.ShapeDtypeStruct((total, wide), b),
            jax.ShapeDtypeStruct((seqs, rows, cols - wide), b),
            jax.ShapeDtypeStruct((528, 128), f32),
            jax.ShapeDtypeStruct((seqs, SPAN, cols - wide), b),
        ],
        in_specs=[far] * (k + 1) + [vmem] * 5,
        out_specs=[far] * (k + 1) + [vmem] * 6,
        scratch_shapes=[
            V((n, depth, cols), b),
            V((528, 128), b),
            V((528, 128), b),
            V((n - 1, 528, 128), b),
            DMA((k + 1,)),
            DMA((k, 2, n - 1)),
            DMA((k, 2, n - 1)),
            DMA((k, 2, n - 1, 4)),
            DMA((k, 2, n - 1, 4)),
            DMA((4,)),
            DMA((4,)),
            DMA((n,)),
            DMA((n - 1,)),
            DMA((n - 1,)),
            DMA,
            DMA,
        ],
        compiler_params=pltpu.CompilerParams(collective_id=cid, has_side_effects=True, vmem_limit_bytes=48 << 20),
        name="opening",
    )(*arrays, block, tok, gain, downs, seconds, kmaps)


def plane_total_kernel(
    n, shared, part, out, mine, core_in, near, line, c_send, c_recv, p_send, p_recv, z_send, z_recv, g_send, g_recv
):
    spot = Spot()
    s, m, d = spot.s, spot.m, spot.d
    h = out.shape[1]
    f32, b16 = jnp.float32, jnp.bfloat16
    mine[...] = part[...].astype(b16)
    bar = pltpu.get_barrier_semaphore()
    plane = [{"seq": s, "mp": m, "dp": (d + i) % 4} for i in range(1, 4)]
    lines = [{"seq": (s + i) % n, "mp": m, "dp": d} for i in range(1, n)]
    for where in plane + lines + [spot.to("c")]:
        pl.semaphore_signal(bar, inc=1, device_id=where, device_id_type=MESH)
    pl.semaphore_wait(bar, n + 3)
    core = remote(mine.at[pl.ds(0, shared)], core_in, c_send, c_recv, spot.to("c"))
    core.start()
    core.wait()
    mine[:shared] = (mine[:shared].astype(f32) + core_in[...].astype(f32)).astype(b16)

    def rows(who):
        return pl.ds(pl.multiple_of(who * h, h), h)

    def scatter(i):
        return remote(mine.at[rows((d + i) % 4)], near.at[i - 1], p_send.at[i - 1], p_recv.at[i - 1], plane[i - 1])

    for i in (2, 1, 3):
        scatter(i).start()
    total = mine[rows(d)].astype(f32)
    for i in range(1, 4):
        scatter(i).wait_recv()
        total = total + near[i - 1].astype(f32)
    line[s] = total.astype(b16)

    def along(i, sending):
        who = s if sending else (s - i) % n
        return remote(line.at[who], line.at[who], z_send.at[i - 1], z_recv.at[i - 1], lines[i - 1])

    for i in range(1, n):
        along(i, True).start()
    for i in range(1, n):
        along(i, False).wait_recv()
    total = line[0].astype(f32)
    for i in range(1, n):
        total = total + line[i].astype(f32)
    out[d] = total.astype(b16)

    def back(i, sending):
        who = d if sending else (d - i) % 4
        return remote(out.at[who], out.at[who], g_send.at[i - 1], g_recv.at[i - 1], plane[i - 1])

    for i in (2, 1, 3):
        back(i, True).start()
    for i in range(1, 4):
        back(i, False).wait_recv()
    for i in range(1, 4):
        scatter(i).wait_send()
        back(i, True).wait_send()
    for i in range(1, n):
        along(i, True).wait_send()


def plane_total(n, part, shared, cid):
    DMA = pltpu.SemaphoreType.DMA
    V = pltpu.VMEM
    b = jnp.bfloat16
    rows, w = part.shape
    h = rows // 4
    return pl.pallas_call(
        functools.partial(plane_total_kernel, n, shared),
        out_shape=jax.ShapeDtypeStruct((4, h, w), b),
        in_specs=[pl.BlockSpec(memory_space=pltpu.VMEM)],
        out_specs=pl.BlockSpec(memory_space=pltpu.VMEM),
        scratch_shapes=[
            V((rows, w), b),
            V((shared, w), b),
            V((3, h, w), b),
            V((n, h, w), b),
            DMA,
            DMA,
            DMA((3,)),
            DMA((3,)),
            DMA((n - 1,)),
            DMA((n - 1,)),
            DMA((3,)),
            DMA((3,)),
        ],
        compiler_params=pltpu.CompilerParams(collective_id=cid, has_side_effects=True, vmem_limit_bytes=40 << 20),
        name="plane_total",
    )(part)


SPAN, TILE = 64, 128
REACH = TILE + SPAN


def mm(left, right, contract=((1,), (0,))):
    return lax.dot_general(left, right, (contract, ((), ())), preferred_element_type=jnp.float32)


def halves(shape, value):
    r = lax.broadcasted_iota(jnp.int32, shape, 0) // 64
    c = lax.broadcasted_iota(jnp.int32, shape, 1) // 64
    return jnp.where(r == c, value, 0.0).astype(jnp.bfloat16)


def signed_map(matrix):
    return jnp.concatenate([matrix, -matrix], 1)


def maps_of(logits):
    left = lax.broadcasted_iota(jnp.int32, logits.shape, 1) < 64
    low = jnp.max(jnp.where(left, logits, -jnp.inf), -1, keepdims=True)
    high = jnp.max(jnp.where(left, -jnp.inf, logits), -1, keepdims=True)
    e = jnp.exp(logits - jnp.where(left, low, high))
    sums = mm(e.astype(jnp.bfloat16), halves((128, 128), 1.0))
    return e / sums


def maps_back(maps, dmaps):
    p = (maps * dmaps).astype(jnp.bfloat16)
    return maps * (dmaps - mm(p, halves((128, 128), 1.0)))


def with_ones(values, first):
    rows = values.shape[0]
    r = lax.broadcasted_iota(jnp.int32, (rows, 64), 0)
    c = lax.broadcasted_iota(jnp.int32, (rows, 64), 1)
    ones = jnp.where((c == 0) & (r >= first), 1.0, 0.0).astype(jnp.bfloat16)
    return jnp.concatenate([values, ones], 1)


def pick(column):
    r = lax.broadcasted_iota(jnp.int32, (8, 128), 0)
    c = lax.broadcasted_iota(jnp.int32, (8, 128), 1)
    return jnp.where((r == 0) & (c == column), 1.0, 0.0).astype(jnp.bfloat16)


def identity():
    r = lax.broadcasted_iota(jnp.int32, (128, 128), 0)
    c = lax.broadcasted_iota(jnp.int32, (128, 128), 1)
    return jnp.where(r == c, 1.0, 0.0).astype(jnp.bfloat16)


def start_row():
    return jnp.where(lax.axis_index("seq") == 0, SPAN, 0)


def key_states(kv, kmaps, near, whole):
    b16 = jnp.bfloat16
    rows = kv.shape[1]
    near[512:] = jnp.zeros((16, 128), b16)
    whole[512:] = jnp.zeros((16, 128), b16)
    for e in range(2):
        for gp in range(2):
            parts = ([], [])
            for j in range(2):
                g = 2 * gp + j
                keys = kv[e, :, g * 64 : g * 64 + 64]
                values = with_ones(kv[e, :, 256 + g * 64 : 320 + g * 64], 0)
                feats = maps_of(mm(keys, signed_map(kmaps[g]))).astype(b16)
                cut = rows - SPAN
                state = mm(feats[:cut], values[:cut], ((0,), (0,)))
                for out, part in ((near, 0), (whole, 1)):
                    if part:
                        state = state + mm(feats[cut:], values[cut:], ((0,), (0,)))
                    parts[part].append(state[:, :64])
                    total = mm(pick(64), state.astype(b16), ((1,), (1,)))
                    out[512 + e * 4 + g : 513 + e * 4 + g] = total[:1].astype(b16)
            for out, part in ((near, 0), (whole, 1)):
                block = jnp.concatenate(parts[part], 1).astype(b16)
                out[(e * 2 + gp) * 128 : (e * 2 + gp) * 128 + 128] = block


STACK = 4


def masks():
    r = lax.broadcasted_iota(jnp.int32, (STACK * TILE, REACH), 0) % TILE
    c = lax.broadcasted_iota(jnp.int32, (STACK * TILE, REACH), 1)
    return (c > r) & (c <= r + SPAN), c <= r


def stacked(ref, rows, head):
    return jnp.concatenate([ref[rows, (head + i) * 64 : (head + i) * 64 + 64] for i in range(STACK)], 0)


def beside(value):
    return jnp.concatenate([value[i * TILE : (i + 1) * TILE] for i in range(STACK)], 1)


def query_logits(queries, qmaps, head):
    return jnp.concatenate(
        [mm(queries[i * TILE : (i + 1) * TILE], signed_map(qmaps[head + i])) for i in range(STACK)], 0
    )


def state_of(states, totals, e, gp, j):
    b16 = jnp.bfloat16
    column = mm(identity(), totals[...].astype(b16), ((1,), (1,)))
    row = e * 4 + 2 * gp + j
    pickcol = lax.broadcasted_iota(jnp.int32, column.shape, 1) == row
    one = jnp.sum(jnp.where(pickcol, column, 0.0), -1, keepdims=True)
    c = lax.broadcasted_iota(jnp.int32, (128, 64), 1)
    return jnp.concatenate([states[:, j * 64 : j * 64 + 64], jnp.where(c == 0, one, 0.0)], 1)


def attend_kernel(q, k, v, st, tot, qmaps, kmaps, out, qf, inv):
    gp, e = pl.program_id(0), pl.program_id(1)
    first = start_row()
    b16 = jnp.bfloat16
    window, older = masks()
    for j in range(2):
        keys = k[0, :, j * 64 : j * 64 + 64]
        values = with_ones(v[0, :, j * 64 : j * 64 + 64], first)
        kfeats = maps_of(mm(keys, signed_map(kmaps[j]))).astype(b16)
        keys8 = keys * jnp.asarray(0.125, b16)
        state = state_of(st, tot, e, gp, j)
        for i in range(2):
            if i:
                state = state + mm(kfeats[:TILE], values[:TILE], ((0,), (0,)))
            state16 = state.astype(b16)
            reach = slice(i * TILE, i * TILE + REACH)
            rows = slice(i * TILE, (i + 1) * TILE)
            for h in range(0, 4, STACK):
                head = j * 4 + h
                query = stacked(q, rows, head)
                qfeats = maps_of(query_logits(query, qmaps, head)).astype(b16)
                near = mm(query, keys8[reach], ((1,), (1,)))
                far = mm(qfeats, kfeats[reach], ((1,), (1,)))
                weights = jnp.where(window, jnp.exp(near), jnp.where(older, far, 0.0))
                both = mm(weights.astype(b16), values[reach]) + mm(qfeats, state16)
                part = 1.0 / both[:, 64:65]
                out[rows, head * 64 : (head + STACK) * 64] = beside((both[:, :64] * part).astype(b16))
                inv[0, rows, head : head + STACK] = beside(part)
                qf[0, 0, head // STACK, i] = qfeats


STACKED = pl.BlockSpec((1, 1, 8 // STACK, 2, STACK * TILE, 128), lambda g, e: (e, g, 0, 0, 0, 0))


def attend(q, kv_ext, st, qmaps, kmaps):
    return pl.pallas_call(
        attend_kernel,
        grid=(2, 2),
        out_shape=[
            jax.ShapeDtypeStruct(q.shape, jnp.bfloat16),
            jax.ShapeDtypeStruct((2, 2, 8 // STACK, 2, STACK * TILE, 128), jnp.bfloat16),
            jax.ShapeDtypeStruct((2, 512, 8), jnp.float32),
        ],
        in_specs=[
            pl.BlockSpec((256, 512), lambda g, e: (e, g)),
            pl.BlockSpec((1, 320, 128), lambda g, e: (e, 0, g)),
            pl.BlockSpec((1, 320, 128), lambda g, e: (e, 0, 2 + g)),
            pl.BlockSpec((128, 128), lambda g, e: (e * 2 + g, 0)),
            pl.BlockSpec((16, 128), lambda g, e: (32, 0)),
            pl.BlockSpec((8, 64, 64), lambda g, e: (g, 0, 0)),
            pl.BlockSpec((2, 64, 64), lambda g, e: (g, 0, 0)),
        ],
        out_specs=[
            pl.BlockSpec((256, 512), lambda g, e: (e, g)),
            STACKED,
            pl.BlockSpec((1, 256, 8), lambda g, e: (g, e, 0)),
        ],
        compiler_params=pltpu.CompilerParams(vmem_limit_bytes=40 << 20),
        name="attend",
    )(q, kv_ext, kv_ext, st, st, qmaps, kmaps)


def state_back_kernel(attn, dres, weight, du, down, inv, qf, grad1, dst, dtot, dattn):
    b16, f32 = jnp.bfloat16, jnp.float32
    k = weight.shape[2]
    grads = mm(du[...], down[...], ((1,), (1,)))
    for i in range(weight.shape[0]):
        grads = grads + mm(dres[:, i * k : (i + 1) * k], weight[i], ((1,), (1,)))
    dattn[...] = grads.astype(b16)
    lane = lax.broadcasted_iota(jnp.int32, (STACK * TILE, 64), 1)
    states = []
    for j in range(2):
        total = None
        for h in range(0, 4, STACK):
            head = j * 4 + h
            for i in range(2):
                rows = slice(i * TILE, (i + 1) * TILE)
                part = jnp.concatenate([inv[0, rows, head + z : head + z + 1] for z in range(STACK)], 0)
                grad = stacked(dattn, rows, head).astype(f32) * part
                c = jnp.sum(grad * stacked(attn, rows, head).astype(f32), -1, keepdims=True)
                one = jnp.concatenate([grad, jnp.where(lane == 0, -c, 0.0)], 1).astype(b16)
                grad1[0, 0, head // STACK, i] = one
                g = mm(qf[0, 0, head // STACK, i], one, ((0,), (0,)))
                total = g if total is None else total + g
        states.append(total[:, :64])
        dtot[0, 0, j * 8 : j * 8 + 8] = mm(pick(64), total.astype(b16), ((1,), (1,))).astype(b16)
    dst[...] = jnp.concatenate(states, 1).astype(b16)


def state_back(attn, dres, weight, du, down, inv, qf):
    b16 = jnp.bfloat16
    n, _, k = weight.shape
    rows = pl.BlockSpec((256, 512), lambda g, e: (e, g))
    return pl.pallas_call(
        state_back_kernel,
        grid=(2, 2),
        out_shape=[
            jax.ShapeDtypeStruct(qf.shape, b16),
            jax.ShapeDtypeStruct((512, 128), b16),
            jax.ShapeDtypeStruct((2, 2, 16, 128), b16),
        ],
        in_specs=[
            rows,
            pl.BlockSpec((256, dres.shape[1]), lambda g, e: (e, 0)),
            pl.BlockSpec((n, 512, k), lambda g, e: (0, g, 0)),
            pl.BlockSpec((256, du.shape[1]), lambda g, e: (e, 0)),
            pl.BlockSpec((512, du.shape[1]), lambda g, e: (g, 0)),
            pl.BlockSpec((1, 256, 8), lambda g, e: (g, e, 0)),
            STACKED,
        ],
        scratch_shapes=[pltpu.VMEM((256, 512), b16)],
        out_specs=[
            STACKED,
            pl.BlockSpec((128, 128), lambda g, e: (e * 2 + g, 0)),
            pl.BlockSpec((1, 1, 16, 128), lambda g, e: (e, g, 0, 0)),
        ],
        compiler_params=pltpu.CompilerParams(vmem_limit_bytes=61 << 20),
        cost_estimate=pl.CostEstimate(flops=8 * 10**9, bytes_accessed=10**6, transcendentals=0),
        name="state_back",
    )(attn, dres, weight, du, down, inv, qf)


def attend_back_kernel(q, k, v, st, tot, qmaps, kmaps, qf, gr, dq, dk, dv, dkf, dqm):
    gp, e = pl.program_id(0), pl.program_id(1)
    first = start_row()
    b16, f32 = jnp.bfloat16, jnp.float32
    window, older = masks()
    eighth = jnp.asarray(0.125, b16)
    dk[...] = jnp.zeros_like(dk)
    dv[...] = jnp.zeros_like(dv)
    dkf[...] = jnp.zeros_like(dkf)

    @pl.when(e == 0)
    def _():
        dqm[...] = jnp.zeros_like(dqm)

    for j in range(2):
        keys = k[0, :, j * 64 : j * 64 + 64]
        values = with_ones(v[0, :, j * 64 : j * 64 + 64], first)
        kfeats = maps_of(mm(keys, signed_map(kmaps[j]))).astype(b16)
        keys8 = keys * eighth
        state = state_of(st, tot, e, gp, j)
        for i in range(2):
            if i:
                state = state + mm(kfeats[:TILE], values[:TILE], ((0,), (0,)))
            state16 = state.astype(b16)
            reach = slice(i * TILE, i * TILE + REACH)
            rows = slice(i * TILE, (i + 1) * TILE)
            dvalue = dkey = dkfeat = g = None
            for h in range(0, 4, STACK):
                head = j * 4 + h
                query = stacked(q, rows, head)
                grad1 = gr[0, 0, head // STACK, i]
                qfeats = qf[0, 0, head // STACK, i]
                qmap = qfeats.astype(f32)
                near = mm(query, keys8[reach], ((1,), (1,)))
                far = mm(qfeats, kfeats[reach], ((1,), (1,)))
                close = jnp.where(window, jnp.exp(near), 0.0)
                weights = (close + jnp.where(older, far, 0.0)).astype(b16)
                dweights = mm(grad1, values[reach], ((1,), (1,)))
                ds = (close * dweights).astype(b16)
                dl = jnp.where(older, dweights, 0.0).astype(b16)
                dqmap = mm(dl, kfeats[reach]) + mm(grad1, state16, ((1,), (1,)))
                da = maps_back(qmap, dqmap).astype(b16)
                dmaps = []
                for z in range(STACK):
                    part = slice(z * TILE, (z + 1) * TILE)
                    dmaps.append(mm(da[part], signed_map(qmaps[head + z]), ((1,), (1,))))
                    x = mm(query[part], da[part], ((0,), (0,)))
                    dqm[head + z] += x[:, :64] - x[:, 64:]
                dquery = mm(ds, keys8[reach]) + jnp.concatenate(dmaps, 0)
                dq[rows, head * 64 : (head + STACK) * 64] = beside(dquery.astype(b16))
                a1 = mm(weights, grad1, ((0,), (0,)))
                a2 = mm(ds, query * eighth, ((0,), (0,)))
                a3 = mm(dl, qfeats, ((0,), (0,)))
                a4 = mm(qfeats, grad1, ((0,), (0,))) if i else None
                if dvalue is None:
                    dvalue, dkey, dkfeat, g = a1, a2, a3, a4
                else:
                    dvalue, dkey, dkfeat = dvalue + a1, dkey + a2, dkfeat + a3
                    g = g + a4 if i else None
            dv[0, reach, j * 64 : j * 64 + 64] += dvalue[:, :64]
            dk[0, reach, j * 64 : j * 64 + 64] += dkey
            dkf[0, j, reach] += dkfeat
            if i:
                g16 = g.astype(b16)
                dkf[0, j, :TILE] += mm(values[:TILE], g16, ((1,), (1,)))
                dv[0, :TILE, j * 64 : j * 64 + 64] += mm(kfeats[:TILE], g16)[:, :64]


def attend_back(q, kv_ext, st, qmaps, kmaps, qf, grad1):
    f32, b16 = jnp.float32, jnp.bfloat16
    e2, ext = kv_ext.shape[:2]
    return pl.pallas_call(
        attend_back_kernel,
        grid=(2, 2),
        out_shape=[
            jax.ShapeDtypeStruct(q.shape, b16),
            jax.ShapeDtypeStruct((e2, ext, 256), f32),
            jax.ShapeDtypeStruct((e2, ext, 256), f32),
            jax.ShapeDtypeStruct((e2, 4, ext, 128), f32),
            jax.ShapeDtypeStruct((16, 64, 64), f32),
        ],
        in_specs=[
            pl.BlockSpec((256, 512), lambda g, e: (e, g)),
            pl.BlockSpec((1, 320, 128), lambda g, e: (e, 0, g)),
            pl.BlockSpec((1, 320, 128), lambda g, e: (e, 0, 2 + g)),
            pl.BlockSpec((128, 128), lambda g, e: (e * 2 + g, 0)),
            pl.BlockSpec((16, 128), lambda g, e: (32, 0)),
            pl.BlockSpec((8, 64, 64), lambda g, e: (g, 0, 0)),
            pl.BlockSpec((2, 64, 64), lambda g, e: (g, 0, 0)),
            STACKED,
            STACKED,
        ],
        out_specs=[
            pl.BlockSpec((256, 512), lambda g, e: (e, g)),
            pl.BlockSpec((1, 320, 128), lambda g, e: (e, 0, g)),
            pl.BlockSpec((1, 320, 128), lambda g, e: (e, 0, g)),
            pl.BlockSpec((1, 2, 320, 128), lambda g, e: (e, g, 0, 0)),
            pl.BlockSpec((8, 64, 64), lambda g, e: (g, 0, 0)),
        ],
        compiler_params=pltpu.CompilerParams(vmem_limit_bytes=40 << 20),
        cost_estimate=pl.CostEstimate(flops=8 * 10**9, bytes_accessed=10**7, transcendentals=4 * 10**6),
        name="attend_back",
    )(q, kv_ext, kv_ext, st, st, qmaps, kmaps, qf, grad1)


def key_back_kernel(k, v, later, tot, kmaps, dk_in, dv_in, dkf, dk, dv, dkm):
    gp, e = pl.program_id(0), pl.program_id(1)
    first = start_row()
    b16 = jnp.bfloat16

    @pl.when(e == 0)
    def _():
        dkm[...] = jnp.zeros_like(dkm)

    dks, dvs = [], []
    for j in range(2):
        cols = slice(j * 64, j * 64 + 64)
        keys = k[0, :, cols]
        values = with_ones(v[0, :, cols], first)
        signed = signed_map(kmaps[j])
        kmap = maps_of(mm(keys, signed))
        g = state_of(later, tot, e, gp, j).astype(b16)
        more = mm(values[:256], g, ((1,), (1,)))
        dmap = jnp.concatenate([dkf[0, j, :256] + more, dkf[0, j, 256:]], 0)
        da = maps_back(kmap, dmap).astype(b16)
        dks.append(dk_in[0, :, cols] + mm(da, signed, ((1,), (1,))))
        moved = mm(kmap[:256].astype(b16), g)[:, :64]
        dvs.append(jnp.concatenate([dv_in[0, :256, cols] + moved, dv_in[0, 256:, cols]], 0))
        x = mm(keys, da, ((0,), (0,)))
        dkm[j] += x[:, :64] - x[:, 64:]
    dk[0] = jnp.concatenate(dks, 1)
    dv[0] = jnp.concatenate(dvs, 1)


def key_back(kv_ext, later, kmaps, dk, dv, dkf):
    f32 = jnp.float32
    piece = pl.BlockSpec((1, 320, 128), lambda g, e: (e, 0, g))
    return pl.pallas_call(
        key_back_kernel,
        grid=(2, 2),
        out_shape=[
            jax.ShapeDtypeStruct(dk.shape, f32),
            jax.ShapeDtypeStruct(dv.shape, f32),
            jax.ShapeDtypeStruct((4, 64, 64), f32),
        ],
        in_specs=[
            piece,
            pl.BlockSpec((1, 320, 128), lambda g, e: (e, 0, 2 + g)),
            pl.BlockSpec((128, 128), lambda g, e: (e * 2 + g, 0)),
            pl.BlockSpec((16, 128), lambda g, e: (32, 0)),
            pl.BlockSpec((2, 64, 64), lambda g, e: (g, 0, 0)),
            piece,
            piece,
            pl.BlockSpec((1, 2, 320, 128), lambda g, e: (e, g, 0, 0)),
        ],
        out_specs=[piece, piece, pl.BlockSpec((2, 64, 64), lambda g, e: (g, 0, 0))],
        compiler_params=pltpu.CompilerParams(vmem_limit_bytes=40 << 20),
        name="key_back",
    )(kv_ext, kv_ext, later, later, kmaps, dk, dv, dkf)


CHUNKS = 4


def feed_kernel(n, k, early, xn_own, ct_all, packed, gate, up, down, res, gain, gsum, dres16, out_part, *scratch):
    (xn, ct, gw, uw, dw, da, oa, xin, yin, t2, xin2, yin2) = scratch[:12]
    (o_sem, a_send, a_recv, w_sem, w_send, w_recv, z_sem, z_send, z_recv, c_send, c_recv, p_send, p_recv, st_sem, e_sem) = scratch[12:]
    spot = Spot()
    s, m, d = spot.s, spot.m, spot.d
    f32, b16 = jnp.float32, jnp.bfloat16
    unit = gw.shape[3] // 2
    wd = min(unit, k)
    gs, ds = unit // wd, k // wd
    half = xn.shape[1] // 2
    A, B = pl.ds(0, half), pl.ds(half, half)

    own = [pltpu.make_async_copy(xn_own, xn.at[3], o_sem.at[0]), pltpu.make_async_copy(ct_all, ct, o_sem.at[1])]
    for c in own:
        c.start()

    lanes = pl.ds(pl.multiple_of(m * unit, unit), unit)

    def own_piece(q):
        start = pl.multiple_of(d * (CHUNKS * unit) + q * unit, unit)
        return (
            (gate.at[:, pl.ds(start, unit)], gw.at[q, s, :, lanes]),
            (up.at[:, pl.ds(start, unit)], uw.at[q, s, :, lanes]),
            (down.at[pl.ds(start, unit)], dw.at[q, s, lanes]),
        )

    def piece(q, w, who):
        return (gw.at[q, who, :, lanes], uw.at[q, who, :, lanes], dw.at[q, who, lanes])[w]

    late = tuple(range(early, CHUNKS))
    own_weights = [
        pltpu.make_async_copy(src, dst, z_sem.at[i, w])
        for i, q in enumerate(late)
        for w, (src, dst) in enumerate(own_piece(q))
    ]
    for c in own_weights:
        c.start()

    def early_parts(q):
        parts = []
        at = 0
        for ref in (gw, uw):
            for i in range(gs):
                cols = pl.ds(pl.multiple_of(m * unit + i * wd, wd), wd)
                parts.append((packed.at[:, q, pl.ds(at, k)], ref.at[q, :, :, cols]))
                at += k
        for i in range(ds):
            parts.append((packed.at[:, q, pl.ds(at, unit)], dw.at[q, :, lanes, pl.ds(i * wd, wd)]))
            at += unit
        return parts

    early_own = [
        [pltpu.make_async_copy(src, dst, w_sem.at[q, i]) for i, (src, dst) in enumerate(early_parts(q))]
        for q in range(early)
    ]
    for copies in early_own:
        for c in copies:
            c.start()

    greet(spot, n, ("x", "y", "c", "up", "dn"))

    def block_copy(kind, sending):
        if kind < 2:
            dst = xn.at[kind + 1]
            src = xn_own if sending else dst
        else:
            rows = (A, B)[kind - 2]
            dst = xn.at[0, rows]
            src = xn.at[(2, 1)[kind - 2], rows] if sending else dst
        return remote(src, dst, a_send.at[kind], a_recv.at[kind], spot.to("xyxy"[kind]))

    block_copy(0, True).start()
    block_copy(1, True).start()

    def sends(upward, t):
        return ((s - t >= 0) & (s + 1 < n)) if upward else ((s + t < n) & (s > 0))

    def receives(upward, t):
        return s - 1 - t >= 0 if upward else s + 1 + t < n

    def z_copy(i, w, upward, t, sending):
        q = late[i]
        way = 0 if upward else 1
        who = (s - t if upward else s + t) if sending else (s - 1 - t if upward else s + 1 + t)
        dst = piece(q, w, who)
        src = own_piece(q)[w][0] if (t == 0 and sending) else dst
        return remote(src, dst, z_send.at[i, w, way, t], z_recv.at[i, w, way, t], spot.to("up" if upward else "dn"))

    for i in range(len(late)):
        for w in range(3):
            for upward in (True, False):

                @pl.when(sends(upward, 0))
                def _():
                    z_copy(i, w, upward, 0, True).start()

    def early_core(q):
        return [
            remote(src, dst, w_send.at[q, i], w_recv.at[q, i], spot.to("c")) for i, (src, dst) in enumerate(early_parts(q))
        ]

    def theirs(q, w, who):
        other = pl.ds(pl.multiple_of((1 - m) * unit, unit), unit)
        return (gw.at[q, who, :, other], uw.at[q, who, :, other], dw.at[q, who, other])[w]

    def core_copy(i, w, who, sending):
        q = late[i]
        ref = piece(q, w, who) if sending else theirs(q, w, who)
        return remote(ref, ref, c_send.at[i, w, who], c_recv.at[i, w, who], spot.to("c"))

    for q in range(early):
        for c in early_core(q):
            c.start()

    def relay(i, t, w):
        for upward in (True, False):

            @pl.when(receives(upward, t))
            def _():
                z_copy(i, w, upward, t, False).wait_recv()
                if t + 1 < n - 1:

                    @pl.when(sends(upward, t + 1))
                    def _():
                        z_copy(i, w, upward, t + 1, True).start()

                core_copy(i, w, s - 1 - t if upward else s + 1 + t, True).start()

    for i in range(len(late)):
        for w in range(3):
            own_weights[3 * i + w].wait()
            core_copy(i, w, s, True).start()

    for c in own:
        c.wait()

    first = (
        remote(xn.at[0, A], xin.at[1], p_send.at[0], p_recv.at[0], spot.to("x")),
        remote(xn.at[0, B], yin.at[1], p_send.at[1], p_recv.at[1], spot.to("y")),
        remote(xn.at[1, A], xin.at[0], p_send.at[2], p_recv.at[2], spot.to("x")),
        remote(xn.at[2, B], yin.at[0], p_send.at[3], p_recv.at[3], spot.to("y")),
    )
    stores = [pltpu.make_async_copy(ct.at[i], out_part.at[i], st_sem.at[i]) for i in range(4)]

    again = (
        pltpu.make_async_copy(res, da.at[0], e_sem.at[0]),
        pltpu.make_async_copy(ct_all.at[3], ct.at[0], e_sem.at[1]),
    )

    steps = 4 * CHUNKS
    turns = {}
    total = len(late) * (n - 1) * 3
    for j in range(total):
        i, t, w = j // (3 * n - 3), j // 3 % (n - 1), j % 3
        at = min(4 * late[i], 1 + (4 * late[i] - 1) * j // ((i + 1) * (n - 1) * 3))
        turns.setdefault(at, []).append((i, t, w))

    @pl.loop(0, steps)
    def _(step):
        last = step >= steps - 4
        c = jnp.where(step < 4 * early, step % early, step // 4)
        t = jnp.where(step < 4 * early, 3 - step // early, step % 4)

        for q in range(early):

            @pl.when(step == q)
            def _():
                for copy in early_own[q]:
                    copy.wait()
                for copy in early_core(q):
                    copy.wait_recv()

        for at, jobs in turns.items():

            @pl.when(step == at)
            def _():
                for i, t, w in jobs:
                    relay(i, t, w)

        for i, q in enumerate(late):

            @pl.when(step == 4 * q)
            def _():
                for w in range(3):
                    for who in range(n):
                        core_copy(i, w, who, False).wait_recv()

        @pl.when(step == early)
        def _():
            block_copy(1, False).wait_recv()
            block_copy(2, True).start()
            block_copy(0, False).wait_recv()
            block_copy(3, True).start()

        @pl.when(step == 3 * early)
        def _():
            for kind in (2, 3):
                block_copy(kind, False).wait_recv()
            for kind in range(4):
                block_copy(kind, True).wait_send()

        x, cot = xn[t], ct[t]
        g_all = gw[c].reshape(n * k, 2 * unit)
        u_all = uw[c].reshape(n * k, 2 * unit)
        g = mm(x, g_all)
        u = mm(x, u_all)
        dh = mm(cot[:, :k], dw[c, 0], ((1,), (1,)))
        for i in range(1, n):
            dh = dh + mm(cot[:, i * k : (i + 1) * k], dw[c, i], ((1,), (1,)))
        sig = 1.0 / (1.0 + jnp.exp(-g))
        act = g * sig
        hid = (act * u).astype(b16)
        dg = (dh * u * sig * (1.0 + g * (1.0 - sig))).astype(b16)
        du = (dh * act).astype(b16)
        for i in range(n):
            cols = slice(i * k, (i + 1) * k)
            o = mm(hid, dw[c, i])
            e = mm(dg, gw[c, i], ((1,), (1,))) + mm(du, uw[c, i], ((1,), (1,)))

            @pl.when(c == 0)
            def _():
                oa[t, :, cols] = o
                da[t, :, cols] = e

            @pl.when(c > 0)
            def _():
                oa[t, :, cols] += o
                da[t, :, cols] += e

        @pl.when(last)
        def _():
            xn[t] = da[t].astype(b16)
            ct[t] = oa[t].astype(b16)

        for i in range(4):

            @pl.when(step == steps - 4 + i)
            def _():
                stores[i].start()
                if i == 1:
                    again[0].start()
                if i == 0:
                    first[0].start()
                    first[1].start()
                elif i < 3:
                    first[i + 1].start()

    second = (
        remote(t2.at[0], yin2, p_send.at[4], p_recv.at[4], spot.to("y")),
        remote(t2.at[1], xin2, p_send.at[5], p_recv.at[5], spot.to("x")),
    )
    stores[0].wait()
    again[1].start()
    first[0].wait_recv()
    t2[0] = (xn[2, A].astype(f32) + xin[1].astype(f32)).astype(b16)
    second[0].start()
    first[1].wait_recv()
    t2[1] = (xn[1, B].astype(f32) + yin[1].astype(f32)).astype(b16)
    second[1].start()
    for c in first:
        c.wait_send()
    for c in again:
        c.wait()
    first[2].wait_recv()
    first[3].wait_recv()
    second[0].wait_recv()
    second[1].wait_recv()
    scale = gain[...].astype(f32)
    chunk = half // 4
    gsum[...] = jnp.zeros_like(gsum)
    for part, inner, outer in ((0, xin, yin2), (1, yin, xin2)):

        @pl.loop(0, 4)
        def _(i):
            at = pl.ds(pl.multiple_of(i * chunk, chunk), chunk)
            rows = pl.ds(pl.multiple_of(part * half + i * chunk, chunk), chunk)
            dxn = da[3, rows] + inner[0, at].astype(f32) + outer[at].astype(f32)
            r = da[0, rows]
            inv = lax.rsqrt(jnp.mean(r * r, -1, keepdims=True) + epsilon)
            ri = r * inv
            gsum[...] += jnp.sum((dxn * ri).reshape(chunk // 8, 8, -1), 0)
            gx = scale * dxn
            grad = ct[0, rows].astype(f32) + inv * (gx - ri * jnp.mean(gx * ri, -1, keepdims=True))
            xn[0, rows] = grad.astype(b16)

    swap = remote(xn.at[0], dres16.at[m], e_sem.at[2], e_sem.at[3], spot.to("c"))
    keep = pltpu.make_async_copy(xn.at[0], dres16.at[m], e_sem.at[4])
    swap.start()
    keep.start()
    keep.wait()
    swap.wait_send()
    remote(xn.at[0], dres16.at[1 - m], e_sem.at[2], e_sem.at[3], spot.to("c")).wait_recv()
    for c in stores[1:]:
        c.wait()
    for c in second:
        c.wait_send()
    for q in range(early):
        for c in early_core(q):
            c.wait_send()
    for i in range(len(late)):
        for w in range(3):
            for who in range(n):
                core_copy(i, w, who, True).wait_send()
            for t in range(n - 1):
                for upward in (True, False):

                    @pl.when(sends(upward, t))
                    def _():
                        z_copy(i, w, upward, t, True).wait_send()


def feed(n, early, xn_own, ct_all, packed, gate, up, down, res, gain, cid):
    DMA, V = pltpu.SemaphoreType.DMA, pltpu.VMEM
    b, f32 = jnp.bfloat16, jnp.float32
    r, w = xn_own.shape
    k = gate.shape[0]
    unit = gate.shape[1] // (4 * CHUNKS)
    wd = min(unit, k)
    pieces = 2 * (unit // wd) + k // wd
    late = CHUNKS - early
    scratch = [V((4, r, w), b), V((4, r, w), b)]
    scratch += [V((CHUNKS, n, k, 2 * unit), b), V((CHUNKS, n, k, 2 * unit), b), V((CHUNKS, n, 2 * unit, k), b)]
    scratch += [V((4, r, w), f32), V((4, r, w), f32)]
    scratch += [V((2, r // 2, w), b), V((2, r // 2, w), b), V((2, r // 2, w), b), V((r // 2, w), b), V((r // 2, w), b)]
    scratch += [DMA((2,)), DMA((4,)), DMA((4,))]
    scratch += [DMA((max(early, 1), pieces))] * 3
    scratch += [DMA((late, 3)), DMA((late, 3, 2, n - 1)), DMA((late, 3, 2, n - 1)), DMA((late, 3, n)), DMA((late, 3, n))]
    scratch += [DMA((6,)), DMA((6,)), DMA((4,)), DMA((5,))]
    return pl.pallas_call(
        functools.partial(feed_kernel, n, k, early),
        out_shape=[
            jax.ShapeDtypeStruct((8, w), f32),
            jax.ShapeDtypeStruct((2, r, w), b),
            jax.ShapeDtypeStruct((4, r, w), b),
        ],
        in_specs=[pl.BlockSpec(memory_space=ANY)] * 7 + [pl.BlockSpec(memory_space=pltpu.VMEM)],
        out_specs=[pl.BlockSpec(memory_space=pltpu.VMEM)] + [pl.BlockSpec(memory_space=ANY)] * 2,
        scratch_shapes=scratch,
        compiler_params=pltpu.CompilerParams(collective_id=cid, has_side_effects=True, vmem_limit_bytes=62 << 20),
        name="feed",
    )(xn_own, ct_all, packed, gate, up, down, res, gain)


def pack_early(k, early, gate, up, down, d):
    unit = gate.shape[1] // (4 * CHUNKS)
    wd = min(unit, k)
    at = d * (CHUNKS * unit)
    g = lax.dynamic_slice_in_dim(gate, at, early * unit, 1)
    u = lax.dynamic_slice_in_dim(up, at, early * unit, 1)
    dn = lax.dynamic_slice_in_dim(down, at, early * unit, 0)
    chunks = []
    for q in range(early):
        rows = [a[:, q * unit + i : q * unit + i + wd] for a in (g, u) for i in range(0, unit, wd)]
        rows += [dn[q * unit : (q + 1) * unit, i : i + wd] for i in range(0, k, wd)]
        chunks.append(jnp.concatenate(rows, 0))
    return jnp.stack(chunks)


def branch_kernel(n, attn, weight, first, second, tok, gain, res, xn, inner, part, other, send, recv):
    spot = Spot()
    m = spot.m
    f32, b16 = jnp.float32, jnp.bfloat16
    half = attn.shape[0] // 2
    k = weight.shape[2]
    greet(spot, n, ("c",))
    low = mm(attn[...], first[...])
    inner[...] = low

    def terms(who, i):
        rows = pl.ds(pl.multiple_of(who * half, half), half)
        return mm(attn[rows], weight[i]) + mm(
            inner[rows].astype(b16), second[:, i * k : (i + 1) * k]
        )

    for i in range(n):
        part[:, i * k : (i + 1) * k] = terms(1 - m, i).astype(b16)
    swap = remote(part, other, send, recv, spot.to("c"))
    swap.start()
    mine = pl.ds(pl.multiple_of(m * half, half), half)
    for i in range(n):
        cols = slice(i * k, (i + 1) * k)
        res[:, cols] = tok[mine, cols].astype(f32) + terms(m, i)
    swap.wait_recv()
    scale = gain[...].astype(f32)
    step = 64

    @pl.loop(0, half // step)
    def _(i):
        at = pl.ds(pl.multiple_of(i * step, step), step)
        r = res[at] + other[at].astype(f32)
        res[at] = r
        xn[at] = (r * lax.rsqrt(jnp.mean(r * r, -1, keepdims=True) + epsilon) * scale).astype(b16)

    swap.wait_send()


def branch(n, attn, weight, first, second, tok, gain, cid):
    DMA, V = pltpu.SemaphoreType.DMA, pltpu.VMEM
    b, f32 = jnp.bfloat16, jnp.float32
    total, width = tok.shape
    half = total // 2
    vmem = pl.BlockSpec(memory_space=pltpu.VMEM)
    return pl.pallas_call(
        functools.partial(branch_kernel, n),
        out_shape=[
            jax.ShapeDtypeStruct((half, width), f32),
            jax.ShapeDtypeStruct((half, width), b),
            jax.ShapeDtypeStruct((total, first.shape[1]), f32),
        ],
        in_specs=[vmem] * 6,
        out_specs=[vmem] * 3,
        scratch_shapes=[V((half, width), b), V((half, width), b), DMA, DMA],
        compiler_params=pltpu.CompilerParams(collective_id=cid, has_side_effects=True, vmem_limit_bytes=48 << 20),
        name="branch",
    )(attn, weight, first, second, tok, gain)


EARLY = 3


f32, b16 = jnp.float32, jnp.bfloat16


def dot(left, right):
    return jnp.dot(left, right, preferred_element_type=f32)


def dot_t(left, right):
    return lax.dot_general(left, right, (((1,), (1,)), ((), ())), preferred_element_type=f32)


def t_dot(left, right):
    return lax.dot_general(left, right, (((0,), (0,)), ((), ())), preferred_element_type=f32)


def norm_back(inputs, inv_rms, gain, dnormed):
    return inv_rms * gain * dnormed - inputs * inv_rms**3 * jnp.mean(
        gain * dnormed * inputs, -1, keepdims=True
    )


def from_behind(value, axis, steps):
    count = lax.axis_size(axis)
    first, last = (max(0, -steps), min(count, count - steps))
    return lax.ppermute(value, axis, [(source, source + steps) for source in range(first, last)])


def swap_core(value):
    return lax.ppermute(value, "mp", [(0, 1), (1, 0)])


def per_device(
    tokens,
    cotangent,
    attention_norm_gain,
    feedforward_norm_gain,
    query_weight,
    key_weight,
    value_weight,
    output_weight,
    gate_weight,
    up_weight,
    down_weight,
    query_adapter_down,
    query_adapter_up,
    key_adapter_down,
    key_adapter_up,
    value_adapter_down,
    value_adapter_up,
    output_adapter_down,
    output_adapter_up,
    query_feature_matrix,
    key_feature_matrix,
):
    n = lax.axis_size("seq")
    position, m, d = (lax.axis_index(a) for a in ("seq", "mp", "dp"))
    seq_count, rows_here, width = tokens.shape
    total_rows = seq_count * rows_here
    half = total_rows // 2
    heads_kv = key_feature_matrix.shape[0]
    head_size = key_feature_matrix.shape[1]
    groups = query_feature_matrix.shape[0] // heads_kv
    extent = rows_here + SOFTMAX_SPAN

    packed = lax.all_gather(
        pack_early(gate_weight.shape[0], EARLY, gate_weight, up_weight, down_weight, d), "seq"
    )
    def my_half(a):
        return lax.dynamic_slice_in_dim(a, m * half, half, 0)

    qkv_own = jnp.concatenate([query_weight, key_weight, value_weight], 1)
    def both_halves(own):
        other = swap_core(own)
        return jnp.concatenate([jnp.where(m == 0, own, other), jnp.where(m == 0, other, own)], 0)

    wide = query_weight.shape[1]
    kv_wide = key_weight.shape[1]
    rank = query_adapter_down.shape[1]
    tok2 = tokens.reshape(total_rows, width)
    downs = jnp.concatenate([query_adapter_down, key_adapter_down, value_adapter_down], 1)
    block_seconds = jnp.concatenate(
        [
            jnp.pad(query_adapter_up, ((0, 0), (0, 2 * kv_wide))),
            jnp.pad(key_adapter_up, ((0, 0), (wide, kv_wide))),
            jnp.pad(value_adapter_up, ((0, 0), (wide + kv_wide, 0))),
        ],
        0,
    )
    qkv_g, out_g, cot_blocks, normed, inner, query_half, kv3, states, kv_prev = opening(
        n,
        [qkv_own, output_weight],
        cotangent,
        tok2,
        attention_norm_gain.reshape(1, width),
        downs,
        block_seconds,
        key_feature_matrix,
        wide,
        1,
    )
    qkv_w = qkv_g.reshape(width, -1)
    kv_ext = jnp.concatenate([kv_prev, kv3], 1)
    attn16, qfeats, inv_weights = attend(query_half, kv_ext, states, query_feature_matrix, key_feature_matrix)
    resid, normed_mlp, inner_output = branch(
        n,
        attn16,
        out_g,
        output_adapter_down,
        output_adapter_up,
        tok2,
        feedforward_norm_gain.reshape(1, width),
        5,
    )
    mlp_gain_rows, dresid16, out_part = feed(
        n,
        EARLY,
        normed_mlp,
        cot_blocks,
        packed,
        gate_weight,
        up_weight,
        down_weight,
        resid,
        feedforward_norm_gain.reshape(1, width),
        4,
    )
    dresid16 = dresid16.reshape(total_rows, width)

    def swap_chip(value, bit):
        return lax.ppermute(value, "dp", [(i, i ^ bit) for i in range(4)])

    cut = half // 2
    upper_in = swap_chip(out_part[0:2, :cut], 1)
    lower_in = swap_chip(out_part[0::2, cut:], 2)


    mlp_gain_term = jnp.sum(mlp_gain_rows, 0)
    du_o = dot_t(dresid16, output_adapter_up)
    oup_term = t_dot(inner_output.astype(b16), dresid16)
    du_o16 = du_o.astype(b16)
    odown_term = t_dot(du_o16, attn16)
    grad1, dstates, dtotals = state_back(
        attn16, dresid16, out_g, du_o16, output_adapter_down, inv_weights, qfeats
    )
    dtotals = jnp.pad(dtotals[:, :, ::8].reshape(-1, 128), ((0, 8), (0, 0)))
    dstates = jnp.concatenate([dstates, dtotals], 0)
    later = [from_behind(dstates, "seq", -i) for i in range(1, n)]
    dq16, dk_ext, dv_ext, dkfeats, dqmaps = attend_back(
        query_half, kv_ext, states, query_feature_matrix, key_feature_matrix, qfeats, grad1
    )
    dq16, later, upper_in, lower_in = lax.optimization_barrier((dq16, later, upper_in, lower_in))
    upper_in2 = swap_chip((out_part[2, :cut].astype(f32) + upper_in[0].astype(f32)).astype(b16), 2)
    lower_in2 = swap_chip((out_part[1, cut:].astype(f32) + lower_in[0].astype(f32)).astype(b16), 1)
    later = functools.reduce(jnp.add, [a.astype(f32) for a in later])
    dk_ext, dv_ext, dkmaps = key_back(kv_ext, later, key_feature_matrix, dk_ext, dv_ext, dkfeats)
    dkv_ext = jnp.concatenate([dk_ext, dv_ext], -1)
    back = from_behind(dkv_ext[:, :SOFTMAX_SPAN].astype(b16), "seq", -1).astype(f32)
    dkv = dkv_ext[:, SOFTMAX_SPAN:]
    dkv = jnp.concatenate(
        [dkv[:, : rows_here - SOFTMAX_SPAN], dkv[:, rows_here - SOFTMAX_SPAN :] + back], 1
    )
    dqkv16 = jnp.concatenate(
        [dq16, dkv.reshape(total_rows, -1).astype(b16)], 1
    )
    bounds = ((0, wide), (wide, wide + kv_wide), (wide + kv_wide, wide + 2 * kv_wide))
    seconds = (query_adapter_up, key_adapter_up, value_adapter_up)
    dinner = jnp.concatenate(
        [dot_t(dqkv16[:, a:b], second) for (a, b), second in zip(bounds, seconds)], 1
    ).astype(b16)
    dnormed = (dot_t(dqkv16, qkv_w) + dot_t(dinner, downs)).astype(b16)
    down_terms = t_dot(dinner, normed)
    inner16 = inner.astype(b16)
    up_terms = [
        t_dot(inner16[:, i * rank : (i + 1) * rank], dqkv16[:, a:b]) for i, (a, b) in enumerate(bounds)
    ]
    inputs = tok2.astype(f32)
    gain_attn = attention_norm_gain.astype(f32)
    rms_attn = lax.rsqrt(jnp.mean(inputs * inputs, -1, keepdims=True) + epsilon)
    dnormed, upper_in2, lower_in2 = lax.optimization_barrier((dnormed, upper_in2, lower_in2))
    mlp_out = out_part[3].astype(f32) + jnp.concatenate(
        [
            upper_in[1].astype(f32) + upper_in2.astype(f32),
            lower_in[1].astype(f32) + lower_in2.astype(f32),
        ],
        0,
    )
    output = both_halves((resid + mlp_out).astype(b16)).reshape(seq_count, rows_here, width)
    dnormed = dnormed.astype(f32) + swap_core(dnormed).astype(f32)
    attn_gain_term = jnp.sum(my_half(dnormed * inputs * rms_attn), 0)
    tokens_grad = (dresid16.astype(f32) + norm_back(inputs, rms_attn, gain_attn, dnormed)).reshape(
        seq_count, rows_here, width
    )

    shared = [attn_gain_term, mlp_gain_term, down_terms, oup_term]
    split = up_terms + [odown_term, dqmaps, dkmaps]
    flat = [a.reshape(-1, 128) for a in shared + split]
    sizes = [a.shape[0] for a in flat]
    shared_rows = sum(sizes[:4])
    flat = jnp.concatenate(flat, 0)
    flat = jnp.pad(flat, ((0, -flat.shape[0] % 128), (0, 0)))
    summed = plane_total(n, flat, shared_rows, 8).reshape(-1, 128).astype(f32)
    parts, at = [], 0
    for term, size in zip(shared + split, sizes):
        parts.append(summed[at : at + size].reshape(term.shape))
        at += size
    attn_gain, mlp_gain, downs_g, oup, qup, kup, vup, odown, qmaps_g, kmaps_g = parts
    downs_g = downs_g.T
    return (
        output,
        tokens_grad,
        attn_gain,
        mlp_gain,
        downs_g[:, :rank],
        qup,
        downs_g[:, rank : 2 * rank],
        kup,
        downs_g[:, 2 * rank :],
        vup,
        odown.T,
        oup,
        qmaps_g.reshape(query_feature_matrix.shape),
        kmaps_g,
    )


def solution(mesh):
    placed = (
        P("dp", "seq", None),
        P("dp", "seq", None),
        P(),
        P(),
        P("seq", "mp"),
        P("seq", "mp"),
        P("seq", "mp"),
        P("mp", "seq"),
        P("seq", "mp"),
        P("seq", "mp"),
        P("mp", "seq"),
        P(),
        P(None, "mp"),
        P(),
        P(None, "mp"),
        P(),
        P(None, "mp"),
        P("mp", None),
        P(),
        P("mp", None, None),
        P("mp", None, None),
    )
    return jax.shard_map(
        per_device,
        mesh=mesh,
        in_specs=placed,
        out_specs=(
            P("dp", "seq", None),
            P("dp", "seq", None),
            P(),
            P(),
            P(),
            P(None, "mp"),
            P(),
            P(None, "mp"),
            P(),
            P(None, "mp"),
            P("mp", None),
            P(),
            P("mp", None, None),
            P("mp", None, None),
        ),
        check_vma=False,
    )
```

```python
import math
import functools
import jax
import jax.numpy as jnp
from jax import lax
from jax.experimental import pallas as pl
from jax.experimental.pallas import tpu as pltpu
from jax.sharding import PartitionSpec as P

SOFTMAX_SPAN = 64
epsilon = 1e-05

MESH = pl.DeviceIdType.MESH
ANY = pl.ANY


class Spot:
    def __init__(self):
        self.s, self.m, self.d = (lax.axis_index(a) for a in ("seq", "mp", "dp"))
        self.x = self.d + 1 - 2 * (self.d % 2)
        self.y = (self.d + 2) % 4
        self.diag = (self.x + 2) % 4

    def to(self, kind):
        s, m, d = self.s, self.m, self.d
        if kind == "x":
            d = self.x
        elif kind == "y":
            d = self.y
        elif kind == "c":
            m = 1 - m
        elif kind == "up":
            s = s + 1
        elif kind == "dn":
            s = s - 1
        return {"seq": s, "mp": m, "dp": d}


def remote(src, dst, send, recv, where):
    return pltpu.make_async_remote_copy(
        src_ref=src, dst_ref=dst, send_sem=send, recv_sem=recv, device_id=where, device_id_type=MESH
    )


def greet(spot, n, kinds):
    bar = pltpu.get_barrier_semaphore()
    count = 0
    for kind in kinds:
        if kind in ("up", "dn"):
            there = spot.s + 1 < n if kind == "up" else spot.s > 0

            @pl.when(there)
            def _(kind=kind):
                pl.semaphore_signal(bar, inc=1, device_id=spot.to(kind), device_id_type=MESH)

            count = count + there.astype(jnp.int32)
        else:
            pl.semaphore_signal(bar, inc=1, device_id=spot.to(kind), device_id_type=MESH)
            count = count + 1
    pl.semaphore_wait(bar, count)


def opening_kernel(n, k, *refs):
    ins, block, tok, gain, downs, seconds, kmaps = refs[:k], *refs[k : k + 6]
    refs = refs[k + 6 :]
    outs, blocks, normed, inner, query, kv, states, before = refs[:k], *refs[k : k + 7]
    weight, near, whole, box = refs[k + 7 : k + 11]
    own_sem, z_send, z_recv, p_send, p_recv, b_send, b_recv, w_sem, l_send, l_recv, e_send, e_recv = refs[k + 11 :]
    spot = Spot()
    s, d = spot.s, spot.d
    block = block.at[spot.m]
    own = [pltpu.make_async_copy(ins[a], outs[a].at[s], own_sem.at[a]) for a in range(k)]
    own.append(pltpu.make_async_copy(block, blocks.at[3], own_sem.at[k]))
    for c in own:
        c.start()
    bar = pltpu.get_barrier_semaphore()
    others = [{"seq": (s + i) % n, "mp": spot.m, "dp": d} for i in range(1, n)]
    for where in [spot.to("x"), spot.to("y")] + others:
        pl.semaphore_signal(bar, inc=1, device_id=where, device_id_type=MESH)
    pl.semaphore_wait(bar, n + 1)

    cut = block.shape[0] // 2
    parts = (pl.ds(0, cut), pl.ds(cut, cut))

    def block_copy(kind, sending):
        if kind < 2:
            dst = blocks.at[kind + 1]
            src = block if sending else dst
        else:
            dst = blocks.at[0, parts[kind - 2]]
            src = blocks.at[(2, 1)[kind - 2], parts[kind - 2]] if sending else dst
        return remote(src, dst, b_send.at[kind], b_recv.at[kind], spot.to("xyxy"[kind]))

    def rows(a, who, part=None):
        size = ins[a].shape[0] // 4
        if part is None:
            return pl.ds(who * size, size)
        return pl.ds(who * size + part * (size // 2), size // 2)

    def sends(up, t):
        return ((s - t >= 0) & (s + 1 < n)) if up else ((s + t < n) & (s > 0))

    def receives(up, t):
        return s - 1 - t >= 0 if up else s + 1 + t < n

    def z_copy(a, up, t, sending):
        way = 0 if up else 1
        piece = (s - t if up else s + t) if sending else (s - 1 - t if up else s + 1 + t)
        dst = outs[a].at[piece, rows(a, d)]
        src = ins[a].at[rows(a, d)] if (t == 0 and sending) else dst
        return remote(src, dst, z_send.at[a, way, t], z_recv.at[a, way, t], spot.to("up" if up else "dn"))

    def piece_of(up, t):
        return s - 1 - t if up else s + 1 + t

    def plane_copy(a, up, t, kind):
        way = 0 if up else 1
        who = (d, d, spot.y, spot.x)[kind]
        part = (None, None, 0, 1)[kind]
        ref = outs[a].at[piece_of(up, t), rows(a, who, part)]
        return remote(ref, ref, p_send.at[a, way, t, kind], p_recv.at[a, way, t, kind], spot.to("xyxy"[kind]))

    def landed(a, up, t, kind):
        way = 0 if up else 1
        who = (spot.x, spot.y, spot.diag, spot.diag)[kind]
        part = (None, None, 0, 1)[kind]
        ref = outs[a].at[piece_of(up, t), rows(a, who, part)]
        return remote(ref, ref, p_send.at[a, way, t, kind], p_recv.at[a, way, t, kind], spot.to("xyxy"[kind]))

    def begin(a):
        for up in (True, False):

            @pl.when(sends(up, 0))
            def _():
                z_copy(a, up, 0, True).start()

    begin(0)
    f32, b16 = jnp.float32, jnp.bfloat16
    scale = gain[...].astype(f32)
    total = tok.shape[0]

    @pl.loop(0, total // 64)
    def _(i):
        at = pl.ds(pl.multiple_of(i * 64, 64), 64)
        x = tok[at].astype(f32)
        normed[at] = (x * lax.rsqrt(jnp.mean(x * x, -1, keepdims=True) + epsilon) * scale).astype(b16)

    low = mm(normed[...], downs[...])
    inner[...] = low
    for step in range(n + k - 1):
        for a in range(k):
            t = step - a
            if 0 <= t < n - 1:
                for up in (True, False):

                    @pl.when(receives(up, t))
                    def _():
                        z_copy(a, up, t, False).wait_recv()
                        if t + 1 < n - 1:

                            @pl.when(sends(up, t + 1))
                            def _():
                                z_copy(a, up, t + 1, True).start()

                        plane_copy(a, up, t, 0).start()
                        plane_copy(a, up, t, 1).start()

            if t == 0 and a + 1 < k:
                begin(a + 1)
                block_copy(0, True).start()
                block_copy(1, True).start()

            if 0 < t < n:
                for up in (True, False):

                    @pl.when(receives(up, t - 1))
                    def _():
                        landed(a, up, t - 1, 0).wait_recv()
                        plane_copy(a, up, t - 1, 3).start()
                        landed(a, up, t - 1, 1).wait_recv()
                        plane_copy(a, up, t - 1, 2).start()

    block_copy(1, False).wait_recv()
    block_copy(2, True).start()
    block_copy(0, False).wait_recv()
    block_copy(3, True).start()

    own[0].wait()
    for t in range(n - 1):
        for up in (True, False):

            @pl.when(receives(up, t))
            def _():
                landed(0, up, t, 2).wait_recv()
                landed(0, up, t, 3).wait_recv()

    loads = [pltpu.make_async_copy(outs[0].at[i], weight.at[i], w_sem.at[i]) for i in range(n)]
    for c in loads:
        c.start()
    for c in loads:
        c.wait()
    wide = query.shape[1]
    length = kv.shape[1]
    cols = weight.shape[2]
    low16 = low.astype(b16)
    for at in range(0, cols, 512):
        full = mm(normed[...], weight[:, :, at : at + 512].reshape(-1, 512)) + mm(low16, seconds[:, at : at + 512])
        if at < wide:
            query[:, at : at + 512] = full.astype(b16)
        else:
            kv[...] = full.astype(b16).reshape(kv.shape)
    key_states(kv, kmaps, near, whole)

    edge_copy = remote(kv.at[:, pl.ds(length - before.shape[1], before.shape[1])], before, e_send, e_recv, spot.to("up"))

    def state_copy(i):
        return remote(
            near if i == 1 else whole,
            box.at[i - 1],
            l_send.at[i - 1],
            l_recv.at[i - 1],
            {"seq": s + i, "mp": spot.m, "dp": d},
        )

    @pl.when(s + 1 < n)
    def _():
        edge_copy.start()

    for i in range(1, n):

        @pl.when(s + i < n)
        def _():
            state_copy(i).start()

    for t in range(n - 1):
        for a in range(k):
            for up in (True, False):

                @pl.when(sends(up, t))
                def _():
                    z_copy(a, up, t, True).wait_send()

                @pl.when(receives(up, t))
                def _():
                    if a:
                        landed(a, up, t, 2).wait_recv()
                        landed(a, up, t, 3).wait_recv()
                    for kind in range(4):
                        plane_copy(a, up, t, kind).wait_send()

    for kind in (2, 3):
        block_copy(kind, False).wait_recv()
    for kind in range(4):
        block_copy(kind, True).wait_send()
    for c in own[1:]:
        c.wait()

    states[...] = jnp.zeros_like(states)

    @pl.when(s > 0)
    def _():
        edge_copy.wait_recv()

    @pl.when(s == 0)
    def _():
        before[...] = jnp.zeros_like(before)

    for i in range(1, n):

        @pl.when(s - i >= 0)
        def _():
            state_copy(i).wait_recv()
            states[...] += box[i - 1].astype(f32)

    @pl.when(s + 1 < n)
    def _():
        edge_copy.wait_send()

    for i in range(1, n):

        @pl.when(s + i < n)
        def _():
            state_copy(i).wait_send()


def opening(n, arrays, block, tok, gain, downs, seconds, kmaps, wide, cid):
    k = len(arrays)
    DMA, V = pltpu.SemaphoreType.DMA, pltpu.VMEM
    b, f32 = jnp.bfloat16, jnp.float32
    total, width = tok.shape
    cols = arrays[0].shape[1]
    depth = arrays[0].shape[0]
    seqs, rows = block.shape[:2]
    vmem = pl.BlockSpec(memory_space=pltpu.VMEM)
    far = pl.BlockSpec(memory_space=ANY)
    return pl.pallas_call(
        functools.partial(opening_kernel, n, k),
        out_shape=[jax.ShapeDtypeStruct((n,) + a.shape, a.dtype) for a in arrays]
        + [
            jax.ShapeDtypeStruct((4,) + block.shape[1:], b),
            jax.ShapeDtypeStruct((total, width), b),
            jax.ShapeDtypeStruct((total, downs.shape[1]), f32),
            jax.ShapeDtypeStruct((total, wide), b),
            jax.ShapeDtypeStruct((seqs, rows, cols - wide), b),
            jax.ShapeDtypeStruct((528, 128), f32),
            jax.ShapeDtypeStruct((seqs, SPAN, cols - wide), b),
        ],
        in_specs=[far] * (k + 1) + [vmem] * 5,
        out_specs=[far] * (k + 1) + [vmem] * 6,
        scratch_shapes=[
            V((n, depth, cols), b),
            V((528, 128), b),
            V((528, 128), b),
            V((n - 1, 528, 128), b),
            DMA((k + 1,)),
            DMA((k, 2, n - 1)),
            DMA((k, 2, n - 1)),
            DMA((k, 2, n - 1, 4)),
            DMA((k, 2, n - 1, 4)),
            DMA((4,)),
            DMA((4,)),
            DMA((n,)),
            DMA((n - 1,)),
            DMA((n - 1,)),
            DMA,
            DMA,
        ],
        compiler_params=pltpu.CompilerParams(collective_id=cid, has_side_effects=True, vmem_limit_bytes=48 << 20),
        name="opening",
    )(*arrays, block, tok, gain, downs, seconds, kmaps)


WIDE = 512


def grad_total_kernel(
    n,
    down_terms,
    oup_term,
    attn_rows,
    mlp_rows,
    q_term,
    k_term,
    v_term,
    odown_term,
    dqm,
    dkm,
    gains_out,
    downs_out,
    oup_out,
    ups_out,
    odown_out,
    qm_out,
    km_out,
    stage,
    mine,
    core_in,
    near,
    line,
    whole,
    c_send,
    c_recv,
    p_send,
    p_recv,
    z_send,
    z_recv,
    g_send,
    g_recv,
):
    spot = Spot()
    s, m, d = spot.s, spot.m, spot.d
    h = whole.shape[1]
    f32, b16 = jnp.float32, jnp.bfloat16
    blocks = down_terms.shape[1] // WIDE
    shared = core_in.shape[0]
    stage[...] = jnp.zeros_like(stage)
    for b in range(blocks):
        at = slice(b * WIDE, (b + 1) * WIDE)
        stage[b * 24 : b * 24 + 24] = down_terms[:, at]
        stage[96 + b * 8 : 104 + b * 8] = oup_term[:, at]
    stage[144:152] = q_term[:, :WIDE]
    stage[152:160] = q_term[:, WIDE:]
    stage[160:168] = jnp.concatenate([k_term[...], v_term[...]], 1)
    stage[168:176] = odown_term[:, :WIDE]
    stage[176:184] = odown_term[:, WIDE:]
    for i in range(2):
        stage[192 + 64 * i : 256 + 64 * i] = jnp.concatenate([dqm[i * 8 + h] for h in range(8)], 1)
    km = jnp.concatenate([dkm[h] for h in range(4)], 1)
    stage[320:352] = jnp.concatenate([km[:32], km[32:]], 1)
    gains = [jnp.sum(v[...], 0, keepdims=True) for v in (attn_rows, mlp_rows)]
    stage[128:136] = jnp.concatenate([v[:, b * WIDE : (b + 1) * WIDE] for v in gains for b in range(blocks)], 0)
    mine[...] = stage[...].astype(b16)
    bar = pltpu.get_barrier_semaphore()
    plane = [{"seq": s, "mp": m, "dp": (d + i) % 4} for i in range(1, 4)]
    lines = [{"seq": (s + i) % n, "mp": m, "dp": d} for i in range(1, n)]
    for where in plane + lines + [spot.to("c")]:
        pl.semaphore_signal(bar, inc=1, device_id=where, device_id_type=MESH)
    pl.semaphore_wait(bar, n + 3)
    core = remote(mine.at[pl.ds(0, shared)], core_in, c_send, c_recv, spot.to("c"))
    core.start()
    core.wait()
    mine[:shared] = (mine[:shared].astype(f32) + core_in[...].astype(f32)).astype(b16)

    def rows(who):
        return pl.ds(pl.multiple_of(who * h, h), h)

    def scatter(i):
        return remote(mine.at[rows((d + i) % 4)], near.at[i - 1], p_send.at[i - 1], p_recv.at[i - 1], plane[i - 1])

    for i in (2, 1, 3):
        scatter(i).start()
    total = mine[rows(d)].astype(f32)
    for i in range(1, 4):
        scatter(i).wait_recv()
        total = total + near[i - 1].astype(f32)
    line[s] = total.astype(b16)

    def along(i, sending):
        who = s if sending else (s - i) % n
        return remote(line.at[who], line.at[who], z_send.at[i - 1], z_recv.at[i - 1], lines[i - 1])

    for i in range(1, n):
        along(i, True).start()
    for i in range(1, n):
        along(i, False).wait_recv()
    total = line[0].astype(f32)
    for i in range(1, n):
        total = total + line[i].astype(f32)
    whole[d] = total.astype(b16)

    def back(i, sending):
        who = d if sending else (d - i) % 4
        return remote(whole.at[who], whole.at[who], g_send.at[i - 1], g_recv.at[i - 1], plane[i - 1])

    for i in (2, 1, 3):
        back(i, True).start()
    for i in range(1, 4):
        back(i, False).wait_recv()
    for i in range(4):
        stage[i * h : (i + 1) * h] = whole[i].astype(f32)
    for b in range(blocks):
        at = slice(b * WIDE, (b + 1) * WIDE)
        downs_out[:, at] = stage[b * 24 : b * 24 + 24]
        oup_out[:, at] = stage[96 + b * 8 : 104 + b * 8]
    gains_out[...] = stage[128:136]
    ups_out[:, :WIDE] = stage[144:152]
    ups_out[:, WIDE : 2 * WIDE] = stage[152:160]
    ups_out[:, 2 * WIDE :] = stage[160:168]
    odown_out[:, :WIDE] = stage[168:176]
    odown_out[:, WIDE:] = stage[176:184]
    for i in range(2):
        for h2 in range(8):
            qm_out[i * 8 + h2] = stage[192 + 64 * i : 256 + 64 * i, h2 * 64 : h2 * 64 + 64]
    for h2 in range(4):
        km_out[h2, :32] = stage[320:352, h2 * 64 : h2 * 64 + 64]
        km_out[h2, 32:] = stage[320:352, 256 + h2 * 64 : 320 + h2 * 64]
    for i in range(1, 4):
        scatter(i).wait_send()
        back(i, True).wait_send()
    for i in range(1, n):
        along(i, True).wait_send()


def grad_total(n, args, cid):
    DMA, V = pltpu.SemaphoreType.DMA, pltpu.VMEM
    b, f32 = jnp.bfloat16, jnp.float32
    width, wide, kv_wide = args[0].shape[1], args[4].shape[1], args[5].shape[1]
    rows, shared = 384, 144
    h = rows // 4
    vmem = pl.BlockSpec(memory_space=pltpu.VMEM)
    shapes = [(8, WIDE), (24, width), (8, width), (8, wide + 2 * kv_wide), (8, wide), (16, 64, 64), (4, 64, 64)]
    return pl.pallas_call(
        functools.partial(grad_total_kernel, n),
        out_shape=[jax.ShapeDtypeStruct(shape, f32) for shape in shapes],
        in_specs=[vmem] * len(args),
        out_specs=[vmem] * len(shapes),
        scratch_shapes=[
            V((rows, WIDE), f32),
            V((rows, WIDE), b),
            V((shared, WIDE), b),
            V((3, h, WIDE), b),
            V((n, h, WIDE), b),
            V((4, h, WIDE), b),
            DMA,
            DMA,
            DMA((3,)),
            DMA((3,)),
            DMA((n - 1,)),
            DMA((n - 1,)),
            DMA((3,)),
            DMA((3,)),
        ],
        compiler_params=pltpu.CompilerParams(collective_id=cid, has_side_effects=True, vmem_limit_bytes=40 << 20),
        name="plane_total",
    )(*args)


SPAN, TILE = 64, 128
REACH = TILE + SPAN


def mm(left, right, contract=((1,), (0,))):
    return lax.dot_general(left, right, (contract, ((), ())), preferred_element_type=jnp.float32)


def halves(shape, value):
    r = lax.broadcasted_iota(jnp.int32, shape, 0) // 64
    c = lax.broadcasted_iota(jnp.int32, shape, 1) // 64
    return jnp.where(r == c, value, 0.0).astype(jnp.bfloat16)


def signed_map(matrix):
    return jnp.concatenate([matrix, -matrix], 1)


def maps_of(logits):
    left = lax.broadcasted_iota(jnp.int32, logits.shape, 1) < 64
    low = jnp.max(jnp.where(left, logits, -jnp.inf), -1, keepdims=True)
    high = jnp.max(jnp.where(left, -jnp.inf, logits), -1, keepdims=True)
    e = jnp.exp(logits - jnp.where(left, low, high))
    sums = mm(e.astype(jnp.bfloat16), halves((128, 128), 1.0))
    return e / sums


def maps_back(maps, dmaps):
    p = (maps * dmaps).astype(jnp.bfloat16)
    return maps * (dmaps - mm(p, halves((128, 128), 1.0)))


def with_ones(values, first):
    rows = values.shape[0]
    r = lax.broadcasted_iota(jnp.int32, (rows, 64), 0)
    c = lax.broadcasted_iota(jnp.int32, (rows, 64), 1)
    ones = jnp.where((c == 0) & (r >= first), 1.0, 0.0).astype(jnp.bfloat16)
    return jnp.concatenate([values, ones], 1)


def pick(column):
    r = lax.broadcasted_iota(jnp.int32, (8, 128), 0)
    c = lax.broadcasted_iota(jnp.int32, (8, 128), 1)
    return jnp.where((r == 0) & (c == column), 1.0, 0.0).astype(jnp.bfloat16)


def identity():
    r = lax.broadcasted_iota(jnp.int32, (128, 128), 0)
    c = lax.broadcasted_iota(jnp.int32, (128, 128), 1)
    return jnp.where(r == c, 1.0, 0.0).astype(jnp.bfloat16)


def start_row():
    return jnp.where(lax.axis_index("seq") == 0, SPAN, 0)


def key_states(kv, kmaps, near, whole):
    b16 = jnp.bfloat16
    rows = kv.shape[1]
    near[512:] = jnp.zeros((16, 128), b16)
    whole[512:] = jnp.zeros((16, 128), b16)
    for e in range(2):
        for gp in range(2):
            parts = ([], [])
            for j in range(2):
                g = 2 * gp + j
                keys = kv[e, :, g * 64 : g * 64 + 64]
                values = with_ones(kv[e, :, 256 + g * 64 : 320 + g * 64], 0)
                feats = maps_of(mm(keys, signed_map(kmaps[g]))).astype(b16)
                cut = rows - SPAN
                state = mm(feats[:cut], values[:cut], ((0,), (0,)))
                for out, part in ((near, 0), (whole, 1)):
                    if part:
                        state = state + mm(feats[cut:], values[cut:], ((0,), (0,)))
                    parts[part].append(state[:, :64])
                    total = mm(pick(64), state.astype(b16), ((1,), (1,)))
                    out[512 + e * 4 + g : 513 + e * 4 + g] = total[:1].astype(b16)
            for out, part in ((near, 0), (whole, 1)):
                block = jnp.concatenate(parts[part], 1).astype(b16)
                out[(e * 2 + gp) * 128 : (e * 2 + gp) * 128 + 128] = block


STACK = 4


def masks():
    r = lax.broadcasted_iota(jnp.int32, (STACK * TILE, REACH), 0) % TILE
    c = lax.broadcasted_iota(jnp.int32, (STACK * TILE, REACH), 1)
    return (c > r) & (c <= r + SPAN), c <= r


def stacked(ref, rows, head):
    return jnp.concatenate([ref[rows, (head + i) * 64 : (head + i) * 64 + 64] for i in range(STACK)], 0)


def beside(value):
    return jnp.concatenate([value[i * TILE : (i + 1) * TILE] for i in range(STACK)], 1)


def query_logits(queries, qmaps, head):
    return jnp.concatenate(
        [mm(queries[i * TILE : (i + 1) * TILE], signed_map(qmaps[head + i])) for i in range(STACK)], 0
    )


def state_of(states, totals, e, gp, j):
    b16 = jnp.bfloat16
    column = mm(identity(), totals[...].astype(b16), ((1,), (1,)))
    row = e * 4 + 2 * gp + j
    pickcol = lax.broadcasted_iota(jnp.int32, column.shape, 1) == row
    one = jnp.sum(jnp.where(pickcol, column, 0.0), -1, keepdims=True)
    c = lax.broadcasted_iota(jnp.int32, (128, 64), 1)
    return jnp.concatenate([states[:, j * 64 : j * 64 + 64], jnp.where(c == 0, one, 0.0)], 1)


def attend_kernel(q, k, v, st, tot, qmaps, kmaps, out, qf, inv):
    gp, e = pl.program_id(0), pl.program_id(1)
    first = start_row()
    b16 = jnp.bfloat16
    window, older = masks()
    for j in range(2):
        keys = k[0, :, j * 64 : j * 64 + 64]
        values = with_ones(v[0, :, j * 64 : j * 64 + 64], first)
        kfeats = maps_of(mm(keys, signed_map(kmaps[j]))).astype(b16)
        keys8 = keys * jnp.asarray(0.125, b16)
        state = state_of(st, tot, e, gp, j)
        for i in range(2):
            if i:
                state = state + mm(kfeats[:TILE], values[:TILE], ((0,), (0,)))
            state16 = state.astype(b16)
            reach = slice(i * TILE, i * TILE + REACH)
            rows = slice(i * TILE, (i + 1) * TILE)
            for h in range(0, 4, STACK):
                head = j * 4 + h
                query = stacked(q, rows, head)
                qfeats = maps_of(query_logits(query, qmaps, head)).astype(b16)
                near = mm(query, keys8[reach], ((1,), (1,)))
                far = mm(qfeats, kfeats[reach], ((1,), (1,)))
                weights = jnp.where(window, jnp.exp(near), jnp.where(older, far, 0.0))
                both = mm(weights.astype(b16), values[reach]) + mm(qfeats, state16)
                part = 1.0 / both[:, 64:65]
                out[rows, head * 64 : (head + STACK) * 64] = beside((both[:, :64] * part).astype(b16))
                inv[0, rows, head : head + STACK] = beside(part)
                qf[0, 0, head // STACK, i] = qfeats


STACKED = pl.BlockSpec((1, 1, 8 // STACK, 2, STACK * TILE, 128), lambda g, e: (e, g, 0, 0, 0, 0))


def attend(q, kv_ext, st, qmaps, kmaps):
    return pl.pallas_call(
        attend_kernel,
        grid=(2, 2),
        out_shape=[
            jax.ShapeDtypeStruct(q.shape, jnp.bfloat16),
            jax.ShapeDtypeStruct((2, 2, 8 // STACK, 2, STACK * TILE, 128), jnp.bfloat16),
            jax.ShapeDtypeStruct((2, 512, 8), jnp.float32),
        ],
        in_specs=[
            pl.BlockSpec((256, 512), lambda g, e: (e, g)),
            pl.BlockSpec((1, 320, 128), lambda g, e: (e, 0, g)),
            pl.BlockSpec((1, 320, 128), lambda g, e: (e, 0, 2 + g)),
            pl.BlockSpec((128, 128), lambda g, e: (e * 2 + g, 0)),
            pl.BlockSpec((16, 128), lambda g, e: (32, 0)),
            pl.BlockSpec((8, 64, 64), lambda g, e: (g, 0, 0)),
            pl.BlockSpec((2, 64, 64), lambda g, e: (g, 0, 0)),
        ],
        out_specs=[
            pl.BlockSpec((256, 512), lambda g, e: (e, g)),
            STACKED,
            pl.BlockSpec((1, 256, 8), lambda g, e: (g, e, 0)),
        ],
        compiler_params=pltpu.CompilerParams(vmem_limit_bytes=40 << 20),
        name="attend",
    )(q, kv_ext, kv_ext, st, st, qmaps, kmaps)


def state_back_kernel(attn, dres, weight, du, down, inv, qf, grad1, dst, dtot, dattn):
    b16, f32 = jnp.bfloat16, jnp.float32
    k = weight.shape[2]
    grads = mm(du[...], down[...], ((1,), (1,)))
    for i in range(weight.shape[0]):
        grads = grads + mm(dres[:, i * k : (i + 1) * k], weight[i], ((1,), (1,)))
    dattn[...] = grads.astype(b16)
    lane = lax.broadcasted_iota(jnp.int32, (STACK * TILE, 64), 1)
    states = []
    for j in range(2):
        total = None
        for h in range(0, 4, STACK):
            head = j * 4 + h
            for i in range(2):
                rows = slice(i * TILE, (i + 1) * TILE)
                part = jnp.concatenate([inv[0, rows, head + z : head + z + 1] for z in range(STACK)], 0)
                grad = stacked(dattn, rows, head).astype(f32) * part
                c = jnp.sum(grad * stacked(attn, rows, head).astype(f32), -1, keepdims=True)
                one = jnp.concatenate([grad, jnp.where(lane == 0, -c, 0.0)], 1).astype(b16)
                grad1[0, 0, head // STACK, i] = one
                g = mm(qf[0, 0, head // STACK, i], one, ((0,), (0,)))
                total = g if total is None else total + g
        states.append(total[:, :64])
        dtot[0, 0, j * 8 : j * 8 + 8] = mm(pick(64), total.astype(b16), ((1,), (1,))).astype(b16)
    dst[...] = jnp.concatenate(states, 1).astype(b16)


def state_back(attn, dres, weight, du, down, inv, qf):
    b16 = jnp.bfloat16
    n, _, k = weight.shape
    rows = pl.BlockSpec((256, 512), lambda g, e: (e, g))
    return pl.pallas_call(
        state_back_kernel,
        grid=(2, 2),
        out_shape=[
            jax.ShapeDtypeStruct(qf.shape, b16),
            jax.ShapeDtypeStruct((512, 128), b16),
            jax.ShapeDtypeStruct((2, 2, 16, 128), b16),
        ],
        in_specs=[
            rows,
            pl.BlockSpec((256, dres.shape[1]), lambda g, e: (e, 0)),
            pl.BlockSpec((n, 512, k), lambda g, e: (0, g, 0)),
            pl.BlockSpec((256, du.shape[1]), lambda g, e: (e, 0)),
            pl.BlockSpec((512, du.shape[1]), lambda g, e: (g, 0)),
            pl.BlockSpec((1, 256, 8), lambda g, e: (g, e, 0)),
            STACKED,
        ],
        scratch_shapes=[pltpu.VMEM((256, 512), b16)],
        out_specs=[
            STACKED,
            pl.BlockSpec((128, 128), lambda g, e: (e * 2 + g, 0)),
            pl.BlockSpec((1, 1, 16, 128), lambda g, e: (e, g, 0, 0)),
        ],
        compiler_params=pltpu.CompilerParams(vmem_limit_bytes=61 << 20),
        cost_estimate=pl.CostEstimate(flops=8 * 10**9, bytes_accessed=10**6, transcendentals=0),
        name="state_back",
    )(attn, dres, weight, du, down, inv, qf)


def attend_back_kernel(q, k, v, st, tot, qmaps, kmaps, qf, gr, dq, dk, dv, dkf, dqm):
    gp, e = pl.program_id(0), pl.program_id(1)
    first = start_row()
    b16, f32 = jnp.bfloat16, jnp.float32
    window, older = masks()
    eighth = jnp.asarray(0.125, b16)
    dk[...] = jnp.zeros_like(dk)
    dv[...] = jnp.zeros_like(dv)
    dkf[...] = jnp.zeros_like(dkf)

    @pl.when(e == 0)
    def _():
        dqm[...] = jnp.zeros_like(dqm)

    for j in range(2):
        keys = k[0, :, j * 64 : j * 64 + 64]
        values = with_ones(v[0, :, j * 64 : j * 64 + 64], first)
        kfeats = maps_of(mm(keys, signed_map(kmaps[j]))).astype(b16)
        keys8 = keys * eighth
        state = state_of(st, tot, e, gp, j)
        for i in range(2):
            if i:
                state = state + mm(kfeats[:TILE], values[:TILE], ((0,), (0,)))
            state16 = state.astype(b16)
            reach = slice(i * TILE, i * TILE + REACH)
            rows = slice(i * TILE, (i + 1) * TILE)
            dvalue = dkey = dkfeat = g = None
            for h in range(0, 4, STACK):
                head = j * 4 + h
                query = stacked(q, rows, head)
                grad1 = gr[0, 0, head // STACK, i]
                qfeats = qf[0, 0, head // STACK, i]
                qmap = qfeats.astype(f32)
                near = mm(query, keys8[reach], ((1,), (1,)))
                far = mm(qfeats, kfeats[reach], ((1,), (1,)))
                close = jnp.where(window, jnp.exp(near), 0.0)
                weights = (close + jnp.where(older, far, 0.0)).astype(b16)
                dweights = mm(grad1, values[reach], ((1,), (1,)))
                ds = (close * dweights).astype(b16)
                dl = jnp.where(older, dweights, 0.0).astype(b16)
                dqmap = mm(dl, kfeats[reach]) + mm(grad1, state16, ((1,), (1,)))
                da = maps_back(qmap, dqmap).astype(b16)
                dmaps = []
                for z in range(STACK):
                    part = slice(z * TILE, (z + 1) * TILE)
                    dmaps.append(mm(da[part], signed_map(qmaps[head + z]), ((1,), (1,))))
                    x = mm(query[part], da[part], ((0,), (0,)))
                    dqm[head + z] += x[:, :64] - x[:, 64:]
                dquery = mm(ds, keys8[reach]) + jnp.concatenate(dmaps, 0)
                dq[rows, head * 64 : (head + STACK) * 64] = beside(dquery.astype(b16))
                a1 = mm(weights, grad1, ((0,), (0,)))
                a2 = mm(ds, query * eighth, ((0,), (0,)))
                a3 = mm(dl, qfeats, ((0,), (0,)))
                a4 = mm(qfeats, grad1, ((0,), (0,))) if i else None
                if dvalue is None:
                    dvalue, dkey, dkfeat, g = a1, a2, a3, a4
                else:
                    dvalue, dkey, dkfeat = dvalue + a1, dkey + a2, dkfeat + a3
                    g = g + a4 if i else None
            dv[0, reach, j * 64 : j * 64 + 64] += dvalue[:, :64]
            dk[0, reach, j * 64 : j * 64 + 64] += dkey
            dkf[0, j, reach] += dkfeat
            if i:
                g16 = g.astype(b16)
                dkf[0, j, :TILE] += mm(values[:TILE], g16, ((1,), (1,)))
                dv[0, :TILE, j * 64 : j * 64 + 64] += mm(kfeats[:TILE], g16)[:, :64]


def attend_back(q, kv_ext, st, qmaps, kmaps, qf, grad1):
    f32, b16 = jnp.float32, jnp.bfloat16
    e2, ext = kv_ext.shape[:2]
    return pl.pallas_call(
        attend_back_kernel,
        grid=(2, 2),
        out_shape=[
            jax.ShapeDtypeStruct(q.shape, b16),
            jax.ShapeDtypeStruct((e2, ext, 256), f32),
            jax.ShapeDtypeStruct((e2, ext, 256), f32),
            jax.ShapeDtypeStruct((e2, 4, ext, 128), f32),
            jax.ShapeDtypeStruct((16, 64, 64), f32),
        ],
        in_specs=[
            pl.BlockSpec((256, 512), lambda g, e: (e, g)),
            pl.BlockSpec((1, 320, 128), lambda g, e: (e, 0, g)),
            pl.BlockSpec((1, 320, 128), lambda g, e: (e, 0, 2 + g)),
            pl.BlockSpec((128, 128), lambda g, e: (e * 2 + g, 0)),
            pl.BlockSpec((16, 128), lambda g, e: (32, 0)),
            pl.BlockSpec((8, 64, 64), lambda g, e: (g, 0, 0)),
            pl.BlockSpec((2, 64, 64), lambda g, e: (g, 0, 0)),
            STACKED,
            STACKED,
        ],
        out_specs=[
            pl.BlockSpec((256, 512), lambda g, e: (e, g)),
            pl.BlockSpec((1, 320, 128), lambda g, e: (e, 0, g)),
            pl.BlockSpec((1, 320, 128), lambda g, e: (e, 0, g)),
            pl.BlockSpec((1, 2, 320, 128), lambda g, e: (e, g, 0, 0)),
            pl.BlockSpec((8, 64, 64), lambda g, e: (g, 0, 0)),
        ],
        compiler_params=pltpu.CompilerParams(vmem_limit_bytes=40 << 20),
        cost_estimate=pl.CostEstimate(flops=8 * 10**9, bytes_accessed=10**7, transcendentals=4 * 10**6),
        name="attend_back",
    )(q, kv_ext, kv_ext, st, st, qmaps, kmaps, qf, grad1)


def key_back_kernel(k, v, later, tot, kmaps, dk_in, dv_in, dkf, dk, dv, dkm):
    gp, e = pl.program_id(0), pl.program_id(1)
    first = start_row()
    b16 = jnp.bfloat16

    @pl.when(e == 0)
    def _():
        dkm[...] = jnp.zeros_like(dkm)

    dks, dvs = [], []
    for j in range(2):
        cols = slice(j * 64, j * 64 + 64)
        keys = k[0, :, cols]
        values = with_ones(v[0, :, cols], first)
        signed = signed_map(kmaps[j])
        kmap = maps_of(mm(keys, signed))
        g = state_of(later, tot, e, gp, j).astype(b16)
        more = mm(values[:256], g, ((1,), (1,)))
        dmap = jnp.concatenate([dkf[0, j, :256] + more, dkf[0, j, 256:]], 0)
        da = maps_back(kmap, dmap).astype(b16)
        dks.append(dk_in[0, :, cols] + mm(da, signed, ((1,), (1,))))
        moved = mm(kmap[:256].astype(b16), g)[:, :64]
        dvs.append(jnp.concatenate([dv_in[0, :256, cols] + moved, dv_in[0, 256:, cols]], 0))
        x = mm(keys, da, ((0,), (0,)))
        dkm[j] += x[:, :64] - x[:, 64:]
    dk[0] = jnp.concatenate(dks, 1)
    dv[0] = jnp.concatenate(dvs, 1)


def key_back(kv_ext, later, kmaps, dk, dv, dkf):
    f32 = jnp.float32
    piece = pl.BlockSpec((1, 320, 128), lambda g, e: (e, 0, g))
    return pl.pallas_call(
        key_back_kernel,
        grid=(2, 2),
        out_shape=[
            jax.ShapeDtypeStruct(dk.shape, f32),
            jax.ShapeDtypeStruct(dv.shape, f32),
            jax.ShapeDtypeStruct((4, 64, 64), f32),
        ],
        in_specs=[
            piece,
            pl.BlockSpec((1, 320, 128), lambda g, e: (e, 0, 2 + g)),
            pl.BlockSpec((128, 128), lambda g, e: (e * 2 + g, 0)),
            pl.BlockSpec((16, 128), lambda g, e: (32, 0)),
            pl.BlockSpec((2, 64, 64), lambda g, e: (g, 0, 0)),
            piece,
            piece,
            pl.BlockSpec((1, 2, 320, 128), lambda g, e: (e, g, 0, 0)),
        ],
        out_specs=[piece, piece, pl.BlockSpec((2, 64, 64), lambda g, e: (g, 0, 0))],
        compiler_params=pltpu.CompilerParams(vmem_limit_bytes=40 << 20),
        name="key_back",
    )(kv_ext, kv_ext, later, later, kmaps, dk, dv, dkf)


def norm_close_kernel(part, other, tok, dres, gain, out, sums):
    f32 = jnp.float32
    i, m = pl.program_id(0), lax.axis_index("mp")
    dn = part[...].astype(f32) + other[...].astype(f32)
    x = tok[...].astype(f32)
    inv = lax.rsqrt(jnp.mean(x * x, -1, keepdims=True) + epsilon)
    xi = x * inv
    t = dn * xi
    gain_wide = gain[...].astype(f32)
    out[...] = dres[...].astype(f32) + inv * (gain_wide * dn - xi * jnp.mean(gain_wide * t, -1, keepdims=True))

    @pl.when(i == 0)
    def _():
        sums[...] = jnp.zeros_like(sums)

    @pl.when(i // (pl.num_programs(0) // 2) == m)
    def _():
        sums[...] += jnp.sum(t.reshape(t.shape[0] // 8, 8, -1), 0)


def norm_close(part, other, tok, dres, gain):
    rows, width = tok.shape
    step = 128
    piece = pl.BlockSpec((step, width), lambda i: (i, 0))
    return pl.pallas_call(
        norm_close_kernel,
        grid=(rows // step,),
        out_shape=[jax.ShapeDtypeStruct((rows, width), jnp.float32), jax.ShapeDtypeStruct((8, width), jnp.float32)],
        in_specs=[piece] * 4 + [pl.BlockSpec((1, width), lambda i: (0, 0))],
        out_specs=[piece, pl.BlockSpec((8, width), lambda i: (0, 0))],
        compiler_params=pltpu.CompilerParams(vmem_limit_bytes=40 << 20),
        name="norm_close",
    )(part, other, tok, dres, gain)


CHUNKS = 4


def feed_kernel(n, k, early, xn_own, ct_all, packed, gate, up, down, res, gain, gsum, dres16, out_part, *scratch):
    (xn, ct, gw, uw, dw, da, oa, xin, yin, t2, xin2, yin2) = scratch[:12]
    (o_sem, a_send, a_recv, w_sem, w_send, w_recv, z_sem, z_send, z_recv, c_send, c_recv, p_send, p_recv, st_sem, e_sem) = scratch[12:]
    spot = Spot()
    s, m, d = spot.s, spot.m, spot.d
    f32, b16 = jnp.float32, jnp.bfloat16
    unit = gw.shape[3] // 2
    wd = min(unit, k)
    gs, ds = unit // wd, k // wd
    half = xn.shape[1] // 2
    A, B = pl.ds(0, half), pl.ds(half, half)

    own = [pltpu.make_async_copy(xn_own, xn.at[3], o_sem.at[0]), pltpu.make_async_copy(ct_all, ct, o_sem.at[1])]
    for c in own:
        c.start()

    lanes = pl.ds(pl.multiple_of(m * unit, unit), unit)

    def own_piece(q):
        start = pl.multiple_of(d * (CHUNKS * unit) + q * unit, unit)
        return (
            (gate.at[:, pl.ds(start, unit)], gw.at[q, s, :, lanes]),
            (up.at[:, pl.ds(start, unit)], uw.at[q, s, :, lanes]),
            (down.at[pl.ds(start, unit)], dw.at[q, s, lanes]),
        )

    def piece(q, w, who):
        return (gw.at[q, who, :, lanes], uw.at[q, who, :, lanes], dw.at[q, who, lanes])[w]

    late = tuple(range(early, CHUNKS))
    own_weights = [
        pltpu.make_async_copy(src, dst, z_sem.at[i, w])
        for i, q in enumerate(late)
        for w, (src, dst) in enumerate(own_piece(q))
    ]
    for c in own_weights:
        c.start()

    def early_parts(q):
        parts = []
        at = 0
        for ref in (gw, uw):
            for i in range(gs):
                cols = pl.ds(pl.multiple_of(m * unit + i * wd, wd), wd)
                parts.append((packed.at[:, q, pl.ds(at, k)], ref.at[q, :, :, cols]))
                at += k
        for i in range(ds):
            parts.append((packed.at[:, q, pl.ds(at, unit)], dw.at[q, :, lanes, pl.ds(i * wd, wd)]))
            at += unit
        return parts

    early_own = [
        [pltpu.make_async_copy(src, dst, w_sem.at[q, i]) for i, (src, dst) in enumerate(early_parts(q))]
        for q in range(early)
    ]
    for copies in early_own:
        for c in copies:
            c.start()

    greet(spot, n, ("x", "y", "c", "up", "dn"))

    def block_copy(kind, sending):
        if kind < 2:
            dst = xn.at[kind + 1]
            src = xn_own if sending else dst
        else:
            rows = (A, B)[kind - 2]
            dst = xn.at[0, rows]
            src = xn.at[(2, 1)[kind - 2], rows] if sending else dst
        return remote(src, dst, a_send.at[kind], a_recv.at[kind], spot.to("xyxy"[kind]))

    block_copy(0, True).start()
    block_copy(1, True).start()

    def sends(upward, t):
        return ((s - t >= 0) & (s + 1 < n)) if upward else ((s + t < n) & (s > 0))

    def receives(upward, t):
        return s - 1 - t >= 0 if upward else s + 1 + t < n

    def z_copy(i, w, upward, t, sending):
        q = late[i]
        way = 0 if upward else 1
        who = (s - t if upward else s + t) if sending else (s - 1 - t if upward else s + 1 + t)
        dst = piece(q, w, who)
        src = own_piece(q)[w][0] if (t == 0 and sending) else dst
        return remote(src, dst, z_send.at[i, w, way, t], z_recv.at[i, w, way, t], spot.to("up" if upward else "dn"))

    for i in range(len(late)):
        for w in range(3):
            for upward in (True, False):

                @pl.when(sends(upward, 0))
                def _():
                    z_copy(i, w, upward, 0, True).start()

    def early_core(q):
        return [
            remote(src, dst, w_send.at[q, i], w_recv.at[q, i], spot.to("c")) for i, (src, dst) in enumerate(early_parts(q))
        ]

    def theirs(q, w, who):
        other = pl.ds(pl.multiple_of((1 - m) * unit, unit), unit)
        return (gw.at[q, who, :, other], uw.at[q, who, :, other], dw.at[q, who, other])[w]

    def core_copy(i, w, who, sending):
        q = late[i]
        ref = piece(q, w, who) if sending else theirs(q, w, who)
        return remote(ref, ref, c_send.at[i, w, who], c_recv.at[i, w, who], spot.to("c"))

    for q in range(early):
        for c in early_core(q):
            c.start()

    def relay(i, t, w):
        for upward in (True, False):

            @pl.when(receives(upward, t))
            def _():
                z_copy(i, w, upward, t, False).wait_recv()
                if t + 1 < n - 1:

                    @pl.when(sends(upward, t + 1))
                    def _():
                        z_copy(i, w, upward, t + 1, True).start()

                core_copy(i, w, s - 1 - t if upward else s + 1 + t, True).start()

    for i in range(len(late)):
        for w in range(3):
            own_weights[3 * i + w].wait()
            core_copy(i, w, s, True).start()

    for c in own:
        c.wait()

    first = (
        remote(xn.at[0, A], xin.at[1], p_send.at[0], p_recv.at[0], spot.to("x")),
        remote(xn.at[0, B], yin.at[1], p_send.at[1], p_recv.at[1], spot.to("y")),
        remote(xn.at[1, A], xin.at[0], p_send.at[2], p_recv.at[2], spot.to("x")),
        remote(xn.at[2, B], yin.at[0], p_send.at[3], p_recv.at[3], spot.to("y")),
    )
    stores = [pltpu.make_async_copy(ct.at[i], out_part.at[i], st_sem.at[i]) for i in range(4)]

    again = (
        pltpu.make_async_copy(res, da.at[0], e_sem.at[0]),
        pltpu.make_async_copy(ct_all.at[3], ct.at[0], e_sem.at[1]),
    )

    steps = 4 * CHUNKS
    turns = {}
    total = len(late) * (n - 1) * 3
    for j in range(total):
        i, t, w = j // (3 * n - 3), j // 3 % (n - 1), j % 3
        at = min(4 * late[i], 1 + (4 * late[i] - 1) * j // ((i + 1) * (n - 1) * 3))
        turns.setdefault(at, []).append((i, t, w))

    @pl.loop(0, steps)
    def _(step):
        last = step >= steps - 4
        c = jnp.where(step < 4 * early, step % early, step // 4)
        t = jnp.where(step < 4 * early, 3 - step // early, step % 4)

        for q in range(early):

            @pl.when(step == q)
            def _():
                for copy in early_own[q]:
                    copy.wait()
                for copy in early_core(q):
                    copy.wait_recv()

        for at, jobs in turns.items():

            @pl.when(step == at)
            def _():
                for i, t, w in jobs:
                    relay(i, t, w)

        for i, q in enumerate(late):

            @pl.when(step == 4 * q)
            def _():
                for w in range(3):
                    for who in range(n):
                        core_copy(i, w, who, False).wait_recv()

        @pl.when(step == early)
        def _():
            block_copy(1, False).wait_recv()
            block_copy(2, True).start()
            block_copy(0, False).wait_recv()
            block_copy(3, True).start()

        @pl.when(step == 3 * early)
        def _():
            for kind in (2, 3):
                block_copy(kind, False).wait_recv()
            for kind in range(4):
                block_copy(kind, True).wait_send()

        x, cot = xn[t], ct[t]
        g_all = gw[c].reshape(n * k, 2 * unit)
        u_all = uw[c].reshape(n * k, 2 * unit)
        g = mm(x, g_all)
        u = mm(x, u_all)
        dh = mm(cot[:, :k], dw[c, 0], ((1,), (1,)))
        for i in range(1, n):
            dh = dh + mm(cot[:, i * k : (i + 1) * k], dw[c, i], ((1,), (1,)))
        sig = 1.0 / (1.0 + jnp.exp(-g))
        act = g * sig
        hid = (act * u).astype(b16)
        dg = (dh * u * sig * (1.0 + g * (1.0 - sig))).astype(b16)
        du = (dh * act).astype(b16)
        for i in range(n):
            cols = slice(i * k, (i + 1) * k)
            o = mm(hid, dw[c, i])
            e = mm(dg, gw[c, i], ((1,), (1,))) + mm(du, uw[c, i], ((1,), (1,)))

            @pl.when(c == 0)
            def _():
                oa[t, :, cols] = o
                da[t, :, cols] = e

            @pl.when(c > 0)
            def _():
                oa[t, :, cols] += o
                da[t, :, cols] += e

        @pl.when(last)
        def _():
            xn[t] = da[t].astype(b16)
            ct[t] = oa[t].astype(b16)

        for i in range(4):

            @pl.when(step == steps - 4 + i)
            def _():
                stores[i].start()
                if i == 1:
                    again[0].start()
                if i == 0:
                    first[0].start()
                    first[1].start()
                elif i < 3:
                    first[i + 1].start()

    second = (
        remote(t2.at[0], yin2, p_send.at[4], p_recv.at[4], spot.to("y")),
        remote(t2.at[1], xin2, p_send.at[5], p_recv.at[5], spot.to("x")),
    )
    stores[0].wait()
    again[1].start()
    first[0].wait_recv()
    t2[0] = (xn[2, A].astype(f32) + xin[1].astype(f32)).astype(b16)
    second[0].start()
    first[1].wait_recv()
    t2[1] = (xn[1, B].astype(f32) + yin[1].astype(f32)).astype(b16)
    second[1].start()
    for c in first:
        c.wait_send()
    for c in again:
        c.wait()
    first[2].wait_recv()
    first[3].wait_recv()
    second[0].wait_recv()
    second[1].wait_recv()
    scale = gain[...].astype(f32)
    chunk = half // 4
    gsum[...] = jnp.zeros_like(gsum)
    for part, inner, outer in ((0, xin, yin2), (1, yin, xin2)):

        @pl.loop(0, 4)
        def _(i):
            at = pl.ds(pl.multiple_of(i * chunk, chunk), chunk)
            rows = pl.ds(pl.multiple_of(part * half + i * chunk, chunk), chunk)
            dxn = da[3, rows] + inner[0, at].astype(f32) + outer[at].astype(f32)
            r = da[0, rows]
            inv = lax.rsqrt(jnp.mean(r * r, -1, keepdims=True) + epsilon)
            ri = r * inv
            gsum[...] += jnp.sum((dxn * ri).reshape(chunk // 8, 8, -1), 0)
            gx = scale * dxn
            grad = ct[0, rows].astype(f32) + inv * (gx - ri * jnp.mean(gx * ri, -1, keepdims=True))
            xn[0, rows] = grad.astype(b16)

    swap = remote(xn.at[0], dres16.at[m], e_sem.at[2], e_sem.at[3], spot.to("c"))
    keep = pltpu.make_async_copy(xn.at[0], dres16.at[m], e_sem.at[4])
    swap.start()
    keep.start()
    keep.wait()
    swap.wait_send()
    remote(xn.at[0], dres16.at[1 - m], e_sem.at[2], e_sem.at[3], spot.to("c")).wait_recv()
    for c in stores[1:]:
        c.wait()
    for c in second:
        c.wait_send()
    for q in range(early):
        for c in early_core(q):
            c.wait_send()
    for i in range(len(late)):
        for w in range(3):
            for who in range(n):
                core_copy(i, w, who, True).wait_send()
            for t in range(n - 1):
                for upward in (True, False):

                    @pl.when(sends(upward, t))
                    def _():
                        z_copy(i, w, upward, t, True).wait_send()


def feed(n, early, xn_own, ct_all, packed, gate, up, down, res, gain, cid):
    DMA, V = pltpu.SemaphoreType.DMA, pltpu.VMEM
    b, f32 = jnp.bfloat16, jnp.float32
    r, w = xn_own.shape
    k = gate.shape[0]
    unit = gate.shape[1] // (4 * CHUNKS)
    wd = min(unit, k)
    pieces = 2 * (unit // wd) + k // wd
    late = CHUNKS - early
    scratch = [V((4, r, w), b), V((4, r, w), b)]
    scratch += [V((CHUNKS, n, k, 2 * unit), b), V((CHUNKS, n, k, 2 * unit), b), V((CHUNKS, n, 2 * unit, k), b)]
    scratch += [V((4, r, w), f32), V((4, r, w), f32)]
    scratch += [V((2, r // 2, w), b), V((2, r // 2, w), b), V((2, r // 2, w), b), V((r // 2, w), b), V((r // 2, w), b)]
    scratch += [DMA((2,)), DMA((4,)), DMA((4,))]
    scratch += [DMA((max(early, 1), pieces))] * 3
    scratch += [DMA((late, 3)), DMA((late, 3, 2, n - 1)), DMA((late, 3, 2, n - 1)), DMA((late, 3, n)), DMA((late, 3, n))]
    scratch += [DMA((6,)), DMA((6,)), DMA((4,)), DMA((5,))]
    return pl.pallas_call(
        functools.partial(feed_kernel, n, k, early),
        out_shape=[
            jax.ShapeDtypeStruct((8, w), f32),
            jax.ShapeDtypeStruct((2, r, w), b),
            jax.ShapeDtypeStruct((4, r, w), b),
        ],
        in_specs=[pl.BlockSpec(memory_space=ANY)] * 7 + [pl.BlockSpec(memory_space=pltpu.VMEM)],
        out_specs=[pl.BlockSpec(memory_space=pltpu.VMEM)] + [pl.BlockSpec(memory_space=ANY)] * 2,
        scratch_shapes=scratch,
        compiler_params=pltpu.CompilerParams(collective_id=cid, has_side_effects=True, vmem_limit_bytes=62 << 20),
        name="feed",
    )(xn_own, ct_all, packed, gate, up, down, res, gain)


def pack_early(k, early, gate, up, down, d):
    unit = gate.shape[1] // (4 * CHUNKS)
    wd = min(unit, k)
    at = d * (CHUNKS * unit)
    g = lax.dynamic_slice_in_dim(gate, at, early * unit, 1)
    u = lax.dynamic_slice_in_dim(up, at, early * unit, 1)
    dn = lax.dynamic_slice_in_dim(down, at, early * unit, 0)
    chunks = []
    for q in range(early):
        rows = [a[:, q * unit + i : q * unit + i + wd] for a in (g, u) for i in range(0, unit, wd)]
        rows += [dn[q * unit : (q + 1) * unit, i : i + wd] for i in range(0, k, wd)]
        chunks.append(jnp.concatenate(rows, 0))
    return jnp.stack(chunks)


def branch_kernel(n, attn, weight, first, second, tok, gain, res, xn, inner, part, other, send, recv):
    spot = Spot()
    m = spot.m
    f32, b16 = jnp.float32, jnp.bfloat16
    half = attn.shape[0] // 2
    k = weight.shape[2]
    greet(spot, n, ("c",))
    low = mm(attn[...], first[...])
    inner[...] = low

    def terms(who, i):
        rows = pl.ds(pl.multiple_of(who * half, half), half)
        return mm(attn[rows], weight[i]) + mm(
            inner[rows].astype(b16), second[:, i * k : (i + 1) * k]
        )

    for i in range(n):
        part[:, i * k : (i + 1) * k] = terms(1 - m, i).astype(b16)
    swap = remote(part, other, send, recv, spot.to("c"))
    swap.start()
    mine = pl.ds(pl.multiple_of(m * half, half), half)
    for i in range(n):
        cols = slice(i * k, (i + 1) * k)
        res[:, cols] = tok[mine, cols].astype(f32) + terms(m, i)
    swap.wait_recv()
    scale = gain[...].astype(f32)
    step = 64

    @pl.loop(0, half // step)
    def _(i):
        at = pl.ds(pl.multiple_of(i * step, step), step)
        r = res[at] + other[at].astype(f32)
        res[at] = r
        xn[at] = (r * lax.rsqrt(jnp.mean(r * r, -1, keepdims=True) + epsilon) * scale).astype(b16)

    swap.wait_send()


def branch(n, attn, weight, first, second, tok, gain, cid):
    DMA, V = pltpu.SemaphoreType.DMA, pltpu.VMEM
    b, f32 = jnp.bfloat16, jnp.float32
    total, width = tok.shape
    half = total // 2
    vmem = pl.BlockSpec(memory_space=pltpu.VMEM)
    return pl.pallas_call(
        functools.partial(branch_kernel, n),
        out_shape=[
            jax.ShapeDtypeStruct((half, width), f32),
            jax.ShapeDtypeStruct((half, width), b),
            jax.ShapeDtypeStruct((total, first.shape[1]), f32),
        ],
        in_specs=[vmem] * 6,
        out_specs=[vmem] * 3,
        scratch_shapes=[V((half, width), b), V((half, width), b), DMA, DMA],
        compiler_params=pltpu.CompilerParams(collective_id=cid, has_side_effects=True, vmem_limit_bytes=48 << 20),
        name="branch",
    )(attn, weight, first, second, tok, gain)


EARLY = 3


f32, b16 = jnp.float32, jnp.bfloat16


def dot(left, right):
    return jnp.dot(left, right, preferred_element_type=f32)


def dot_t(left, right):
    return lax.dot_general(left, right, (((1,), (1,)), ((), ())), preferred_element_type=f32)


def t_dot(left, right):
    return lax.dot_general(left, right, (((0,), (0,)), ((), ())), preferred_element_type=f32)


def norm_back(inputs, inv_rms, gain, dnormed):
    return inv_rms * gain * dnormed - inputs * inv_rms**3 * jnp.mean(
        gain * dnormed * inputs, -1, keepdims=True
    )


def from_behind(value, axis, steps):
    count = lax.axis_size(axis)
    first, last = (max(0, -steps), min(count, count - steps))
    return lax.ppermute(value, axis, [(source, source + steps) for source in range(first, last)])


def swap_core(value):
    return lax.ppermute(value, "mp", [(0, 1), (1, 0)])


def per_device(
    tokens,
    cotangent,
    attention_norm_gain,
    feedforward_norm_gain,
    query_weight,
    key_weight,
    value_weight,
    output_weight,
    gate_weight,
    up_weight,
    down_weight,
    query_adapter_down,
    query_adapter_up,
    key_adapter_down,
    key_adapter_up,
    value_adapter_down,
    value_adapter_up,
    output_adapter_down,
    output_adapter_up,
    query_feature_matrix,
    key_feature_matrix,
):
    n = lax.axis_size("seq")
    position, m, d = (lax.axis_index(a) for a in ("seq", "mp", "dp"))
    seq_count, rows_here, width = tokens.shape
    total_rows = seq_count * rows_here
    half = total_rows // 2
    heads_kv = key_feature_matrix.shape[0]
    head_size = key_feature_matrix.shape[1]
    groups = query_feature_matrix.shape[0] // heads_kv
    extent = rows_here + SOFTMAX_SPAN

    packed = lax.all_gather(
        pack_early(gate_weight.shape[0], EARLY, gate_weight, up_weight, down_weight, d), "seq"
    )
    def my_half(a):
        return lax.dynamic_slice_in_dim(a, m * half, half, 0)

    qkv_own = jnp.concatenate([query_weight, key_weight, value_weight], 1)
    def both_halves(own):
        other = swap_core(own)
        return jnp.concatenate([jnp.where(m == 0, own, other), jnp.where(m == 0, other, own)], 0)

    wide = query_weight.shape[1]
    kv_wide = key_weight.shape[1]
    rank = query_adapter_down.shape[1]
    tok2 = tokens.reshape(total_rows, width)
    downs = jnp.concatenate([query_adapter_down, key_adapter_down, value_adapter_down], 1)
    block_seconds = jnp.concatenate(
        [
            jnp.pad(query_adapter_up, ((0, 0), (0, 2 * kv_wide))),
            jnp.pad(key_adapter_up, ((0, 0), (wide, kv_wide))),
            jnp.pad(value_adapter_up, ((0, 0), (wide + kv_wide, 0))),
        ],
        0,
    )
    qkv_g, out_g, cot_blocks, normed, inner, query_half, kv3, states, kv_prev = opening(
        n,
        [qkv_own, output_weight],
        cotangent,
        tok2,
        attention_norm_gain.reshape(1, width),
        downs,
        block_seconds,
        key_feature_matrix,
        wide,
        1,
    )
    qkv_w = qkv_g.reshape(width, -1)
    kv_ext = jnp.concatenate([kv_prev, kv3], 1)
    attn16, qfeats, inv_weights = attend(query_half, kv_ext, states, query_feature_matrix, key_feature_matrix)
    resid, normed_mlp, inner_output = branch(
        n,
        attn16,
        out_g,
        output_adapter_down,
        output_adapter_up,
        tok2,
        feedforward_norm_gain.reshape(1, width),
        5,
    )
    mlp_gain_rows, dresid16, out_part = feed(
        n,
        EARLY,
        normed_mlp,
        cot_blocks,
        packed,
        gate_weight,
        up_weight,
        down_weight,
        resid,
        feedforward_norm_gain.reshape(1, width),
        4,
    )
    dresid16 = dresid16.reshape(total_rows, width)

    def swap_chip(value, bit):
        return lax.ppermute(value, "dp", [(i, i ^ bit) for i in range(4)])

    cut = half // 2
    upper_in = swap_chip(out_part[0:2, :cut], 1)
    lower_in = swap_chip(out_part[0::2, cut:], 2)


    du_o = dot_t(dresid16, output_adapter_up)
    oup_term = t_dot(inner_output.astype(b16), dresid16)
    du_o16 = du_o.astype(b16)
    odown_term = t_dot(du_o16, attn16)
    grad1, dstates, dtotals = state_back(
        attn16, dresid16, out_g, du_o16, output_adapter_down, inv_weights, qfeats
    )
    dtotals = jnp.pad(dtotals[:, :, ::8].reshape(-1, 128), ((0, 8), (0, 0)))
    dstates = jnp.concatenate([dstates, dtotals], 0)
    later = [from_behind(dstates, "seq", -i) for i in range(1, n)]
    dq16, dk_ext, dv_ext, dkfeats, dqmaps = attend_back(
        query_half, kv_ext, states, query_feature_matrix, key_feature_matrix, qfeats, grad1
    )
    dq16, later, upper_in, lower_in = lax.optimization_barrier((dq16, later, upper_in, lower_in))
    upper_in2 = swap_chip((out_part[2, :cut].astype(f32) + upper_in[0].astype(f32)).astype(b16), 2)
    lower_in2 = swap_chip((out_part[1, cut:].astype(f32) + lower_in[0].astype(f32)).astype(b16), 1)
    later = functools.reduce(jnp.add, [a.astype(f32) for a in later])
    dk_ext, dv_ext, dkmaps = key_back(kv_ext, later, key_feature_matrix, dk_ext, dv_ext, dkfeats)
    dkv_ext = jnp.concatenate([dk_ext, dv_ext], -1)
    back = from_behind(dkv_ext[:, :SOFTMAX_SPAN].astype(b16), "seq", -1).astype(f32)
    dkv = dkv_ext[:, SOFTMAX_SPAN:]
    dkv = jnp.concatenate(
        [dkv[:, : rows_here - SOFTMAX_SPAN], dkv[:, rows_here - SOFTMAX_SPAN :] + back], 1
    )
    dqkv16 = jnp.concatenate(
        [dq16, dkv.reshape(total_rows, -1).astype(b16)], 1
    )
    bounds = ((0, wide), (wide, wide + kv_wide), (wide + kv_wide, wide + 2 * kv_wide))
    seconds = (query_adapter_up, key_adapter_up, value_adapter_up)
    dinner = jnp.concatenate(
        [dot_t(dqkv16[:, a:b], second) for (a, b), second in zip(bounds, seconds)], 1
    ).astype(b16)
    dnormed = (dot_t(dqkv16, qkv_w) + dot_t(dinner, downs)).astype(b16)
    down_terms = t_dot(dinner, normed)
    inner16 = inner.astype(b16)
    up_terms = [
        t_dot(inner16[:, i * rank : (i + 1) * rank], dqkv16[:, a:b]) for i, (a, b) in enumerate(bounds)
    ]
    dnormed, upper_in2, lower_in2 = lax.optimization_barrier((dnormed, upper_in2, lower_in2))
    mlp_out = out_part[3].astype(f32) + jnp.concatenate(
        [
            upper_in[1].astype(f32) + upper_in2.astype(f32),
            lower_in[1].astype(f32) + lower_in2.astype(f32),
        ],
        0,
    )
    output = both_halves((resid + mlp_out).astype(b16)).reshape(seq_count, rows_here, width)
    tokens_grad, attn_gain_rows = norm_close(
        dnormed, swap_core(dnormed), tok2, dresid16, attention_norm_gain.reshape(1, width)
    )
    tokens_grad = tokens_grad.reshape(seq_count, rows_here, width)
    gains, downs_g, oup, ups, odown, qmaps_g, kmaps_g = grad_total(
        n,
        (down_terms, oup_term, attn_gain_rows, mlp_gain_rows, *up_terms, odown_term, dqmaps, dkmaps),
        8,
    )
    gains = gains.reshape(2, width)
    attn_gain, mlp_gain = gains[0], gains[1]
    qup, kup, vup = ups[:, :wide], ups[:, wide : wide + kv_wide], ups[:, wide + kv_wide :]
    downs_g = downs_g.T
    return (
        output,
        tokens_grad,
        attn_gain,
        mlp_gain,
        downs_g[:, :rank],
        qup,
        downs_g[:, rank : 2 * rank],
        kup,
        downs_g[:, 2 * rank :],
        vup,
        odown.T,
        oup,
        qmaps_g,
        kmaps_g,
    )


def solution(mesh):
    placed = (
        P("dp", "seq", None),
        P("dp", "seq", None),
        P(),
        P(),
        P("seq", "mp"),
        P("seq", "mp"),
        P("seq", "mp"),
        P("mp", "seq"),
        P("seq", "mp"),
        P("seq", "mp"),
        P("mp", "seq"),
        P(),
        P(None, "mp"),
        P(),
        P(None, "mp"),
        P(),
        P(None, "mp"),
        P("mp", None),
        P(),
        P("mp", None, None),
        P("mp", None, None),
    )
    return jax.shard_map(
        per_device,
        mesh=mesh,
        in_specs=placed,
        out_specs=(
            P("dp", "seq", None),
            P("dp", "seq", None),
            P(),
            P(),
            P(),
            P(None, "mp"),
            P(),
            P(None, "mp"),
            P(),
            P(None, "mp"),
            P("mp", None),
            P(),
            P("mp", None, None),
            P("mp", None, None),
        ),
        check_vma=False,
    )
```

```python
import math
import functools
import jax
import jax.numpy as jnp
from jax import lax
from jax.experimental import pallas as pl
from jax.experimental.pallas import tpu as pltpu
from jax.sharding import PartitionSpec as P

SOFTMAX_SPAN = 64
epsilon = 1e-05

MESH = pl.DeviceIdType.MESH
ANY = pl.ANY


class Spot:
    def __init__(self):
        self.s, self.m, self.d = (lax.axis_index(a) for a in ("seq", "mp", "dp"))
        self.x = self.d + 1 - 2 * (self.d % 2)
        self.y = (self.d + 2) % 4
        self.diag = (self.x + 2) % 4

    def to(self, kind):
        s, m, d = self.s, self.m, self.d
        if kind == "x":
            d = self.x
        elif kind == "y":
            d = self.y
        elif kind == "c":
            m = 1 - m
        elif kind == "up":
            s = s + 1
        elif kind == "dn":
            s = s - 1
        return {"seq": s, "mp": m, "dp": d}


def remote(src, dst, send, recv, where):
    return pltpu.make_async_remote_copy(
        src_ref=src, dst_ref=dst, send_sem=send, recv_sem=recv, device_id=where, device_id_type=MESH
    )


def greet(spot, n, kinds):
    bar = pltpu.get_barrier_semaphore()
    count = 0
    for kind in kinds:
        if kind in ("up", "dn"):
            there = spot.s + 1 < n if kind == "up" else spot.s > 0

            @pl.when(there)
            def _(kind=kind):
                pl.semaphore_signal(bar, inc=1, device_id=spot.to(kind), device_id_type=MESH)

            count = count + there.astype(jnp.int32)
        else:
            pl.semaphore_signal(bar, inc=1, device_id=spot.to(kind), device_id_type=MESH)
            count = count + 1
    pl.semaphore_wait(bar, count)


def opening_kernel(n, k, *refs):
    ins, block, tok, gain, downs, seconds, kmaps = refs[:k], *refs[k : k + 6]
    refs = refs[k + 6 :]
    outs, blocks, normed, inner, query, kv, states, before = refs[:k], *refs[k : k + 7]
    weight, near, whole, box = refs[k + 7 : k + 11]
    own_sem, z_send, z_recv, p_send, p_recv, b_send, b_recv, w_sem, l_send, l_recv, e_send, e_recv = refs[k + 11 :]
    spot = Spot()
    s, d = spot.s, spot.d
    block = block.at[spot.m]
    own = [pltpu.make_async_copy(ins[a], outs[a].at[s], own_sem.at[a]) for a in range(k)]
    own.append(pltpu.make_async_copy(block, blocks.at[3], own_sem.at[k]))
    for c in own:
        c.start()
    bar = pltpu.get_barrier_semaphore()
    others = [{"seq": (s + i) % n, "mp": spot.m, "dp": d} for i in range(1, n)]
    for where in [spot.to("x"), spot.to("y")] + others:
        pl.semaphore_signal(bar, inc=1, device_id=where, device_id_type=MESH)
    pl.semaphore_wait(bar, n + 1)

    cut = block.shape[0] // 2
    parts = (pl.ds(0, cut), pl.ds(cut, cut))

    def block_copy(kind, sending):
        if kind < 2:
            dst = blocks.at[kind + 1]
            src = block if sending else dst
        else:
            dst = blocks.at[0, parts[kind - 2]]
            src = blocks.at[(2, 1)[kind - 2], parts[kind - 2]] if sending else dst
        return remote(src, dst, b_send.at[kind], b_recv.at[kind], spot.to("xyxy"[kind]))

    def rows(a, who, part=None):
        size = ins[a].shape[0] // 4
        if part is None:
            return pl.ds(who * size, size)
        return pl.ds(who * size + part * (size // 2), size // 2)

    def sends(up, t):
        return ((s - t >= 0) & (s + 1 < n)) if up else ((s + t < n) & (s > 0))

    def receives(up, t):
        return s - 1 - t >= 0 if up else s + 1 + t < n

    def z_copy(a, up, t, sending):
        way = 0 if up else 1
        piece = (s - t if up else s + t) if sending else (s - 1 - t if up else s + 1 + t)
        dst = outs[a].at[piece, rows(a, d)]
        src = ins[a].at[rows(a, d)] if (t == 0 and sending) else dst
        return remote(src, dst, z_send.at[a, way, t], z_recv.at[a, way, t], spot.to("up" if up else "dn"))

    def piece_of(up, t):
        return s - 1 - t if up else s + 1 + t

    def plane_copy(a, up, t, kind):
        way = 0 if up else 1
        who = (d, d, spot.y, spot.x)[kind]
        part = (None, None, 0, 1)[kind]
        ref = outs[a].at[piece_of(up, t), rows(a, who, part)]
        return remote(ref, ref, p_send.at[a, way, t, kind], p_recv.at[a, way, t, kind], spot.to("xyxy"[kind]))

    def landed(a, up, t, kind):
        way = 0 if up else 1
        who = (spot.x, spot.y, spot.diag, spot.diag)[kind]
        part = (None, None, 0, 1)[kind]
        ref = outs[a].at[piece_of(up, t), rows(a, who, part)]
        return remote(ref, ref, p_send.at[a, way, t, kind], p_recv.at[a, way, t, kind], spot.to("xyxy"[kind]))

    def begin(a):
        for up in (True, False):

            @pl.when(sends(up, 0))
            def _():
                z_copy(a, up, 0, True).start()

    begin(0)
    f32, b16 = jnp.float32, jnp.bfloat16
    scale = gain[...].astype(f32)
    total = tok.shape[0]

    @pl.loop(0, total // 64)
    def _(i):
        at = pl.ds(pl.multiple_of(i * 64, 64), 64)
        x = tok[at].astype(f32)
        normed[at] = (x * lax.rsqrt(jnp.mean(x * x, -1, keepdims=True) + epsilon) * scale).astype(b16)

    low = mm(normed[...], downs[...])
    inner[...] = low
    for step in range(n + k - 1):
        for a in range(k):
            t = step - a
            if 0 <= t < n - 1:
                for up in (True, False):

                    @pl.when(receives(up, t))
                    def _():
                        z_copy(a, up, t, False).wait_recv()
                        if t + 1 < n - 1:

                            @pl.when(sends(up, t + 1))
                            def _():
                                z_copy(a, up, t + 1, True).start()

                        plane_copy(a, up, t, 0).start()
                        plane_copy(a, up, t, 1).start()

            if t == 0 and a + 1 < k:
                begin(a + 1)
                block_copy(0, True).start()
                block_copy(1, True).start()

            if 0 < t < n:
                for up in (True, False):

                    @pl.when(receives(up, t - 1))
                    def _():
                        landed(a, up, t - 1, 0).wait_recv()
                        plane_copy(a, up, t - 1, 3).start()
                        landed(a, up, t - 1, 1).wait_recv()
                        plane_copy(a, up, t - 1, 2).start()

    block_copy(1, False).wait_recv()
    block_copy(2, True).start()
    block_copy(0, False).wait_recv()
    block_copy(3, True).start()

    own[0].wait()
    for t in range(n - 1):
        for up in (True, False):

            @pl.when(receives(up, t))
            def _():
                landed(0, up, t, 2).wait_recv()
                landed(0, up, t, 3).wait_recv()

    loads = [pltpu.make_async_copy(outs[0].at[i], weight.at[i], w_sem.at[i]) for i in range(n)]
    for c in loads:
        c.start()
    for c in loads:
        c.wait()
    wide = query.shape[1]
    length = kv.shape[1]
    cols = weight.shape[2]
    low16 = low.astype(b16)
    for at in range(0, cols, 512):
        full = mm(normed[...], weight[:, :, at : at + 512].reshape(-1, 512)) + mm(low16, seconds[:, at : at + 512])
        if at < wide:
            query[:, at : at + 512] = full.astype(b16)
        else:
            kv[...] = full.astype(b16).reshape(kv.shape)
    key_states(kv, kmaps, near, whole)

    edge_copy = remote(kv.at[:, pl.ds(length - before.shape[1], before.shape[1])], before, e_send, e_recv, spot.to("up"))

    def state_copy(i):
        return remote(
            near if i == 1 else whole,
            box.at[i - 1],
            l_send.at[i - 1],
            l_recv.at[i - 1],
            {"seq": s + i, "mp": spot.m, "dp": d},
        )

    @pl.when(s + 1 < n)
    def _():
        edge_copy.start()

    for i in range(1, n):

        @pl.when(s + i < n)
        def _():
            state_copy(i).start()

    for t in range(n - 1):
        for a in range(k):
            for up in (True, False):

                @pl.when(sends(up, t))
                def _():
                    z_copy(a, up, t, True).wait_send()

                @pl.when(receives(up, t))
                def _():
                    if a:
                        landed(a, up, t, 2).wait_recv()
                        landed(a, up, t, 3).wait_recv()
                    for kind in range(4):
                        plane_copy(a, up, t, kind).wait_send()

    for kind in (2, 3):
        block_copy(kind, False).wait_recv()
    for kind in range(4):
        block_copy(kind, True).wait_send()
    for c in own[1:]:
        c.wait()

    states[...] = jnp.zeros_like(states)

    @pl.when(s > 0)
    def _():
        edge_copy.wait_recv()

    @pl.when(s == 0)
    def _():
        before[...] = jnp.zeros_like(before)

    for i in range(1, n):

        @pl.when(s - i >= 0)
        def _():
            state_copy(i).wait_recv()
            states[...] += box[i - 1].astype(f32)

    @pl.when(s + 1 < n)
    def _():
        edge_copy.wait_send()

    for i in range(1, n):

        @pl.when(s + i < n)
        def _():
            state_copy(i).wait_send()


def opening(n, arrays, block, tok, gain, downs, seconds, kmaps, wide, cid):
    k = len(arrays)
    DMA, V = pltpu.SemaphoreType.DMA, pltpu.VMEM
    b, f32 = jnp.bfloat16, jnp.float32
    total, width = tok.shape
    cols = arrays[0].shape[1]
    depth = arrays[0].shape[0]
    seqs, rows = block.shape[:2]
    vmem = pl.BlockSpec(memory_space=pltpu.VMEM)
    far = pl.BlockSpec(memory_space=ANY)
    return pl.pallas_call(
        functools.partial(opening_kernel, n, k),
        out_shape=[jax.ShapeDtypeStruct((n,) + a.shape, a.dtype) for a in arrays]
        + [
            jax.ShapeDtypeStruct((4,) + block.shape[1:], b),
            jax.ShapeDtypeStruct((total, width), b),
            jax.ShapeDtypeStruct((total, downs.shape[1]), f32),
            jax.ShapeDtypeStruct((total, wide), b),
            jax.ShapeDtypeStruct((seqs, rows, cols - wide), b),
            jax.ShapeDtypeStruct((528, 128), f32),
            jax.ShapeDtypeStruct((seqs, SPAN, cols - wide), b),
        ],
        in_specs=[far] * (k + 1) + [vmem] * 5,
        out_specs=[far] * (k + 1) + [vmem] * 6,
        scratch_shapes=[
            V((n, depth, cols), b),
            V((528, 128), b),
            V((528, 128), b),
            V((n - 1, 528, 128), b),
            DMA((k + 1,)),
            DMA((k, 2, n - 1)),
            DMA((k, 2, n - 1)),
            DMA((k, 2, n - 1, 4)),
            DMA((k, 2, n - 1, 4)),
            DMA((4,)),
            DMA((4,)),
            DMA((n,)),
            DMA((n - 1,)),
            DMA((n - 1,)),
            DMA,
            DMA,
        ],
        compiler_params=pltpu.CompilerParams(collective_id=cid, has_side_effects=True, vmem_limit_bytes=48 << 20),
        name="opening",
    )(*arrays, block, tok, gain, downs, seconds, kmaps)


WIDE = 512


def grad_total_kernel(
    n,
    down_terms,
    oup_term,
    attn_rows,
    mlp_rows,
    q_term,
    k_term,
    v_term,
    odown_term,
    dqm,
    dkm,
    gains_out,
    downs_out,
    oup_out,
    ups_out,
    odown_out,
    qm_out,
    km_out,
    stage,
    mine,
    core_in,
    near,
    line,
    whole,
    c_send,
    c_recv,
    p_send,
    p_recv,
    z_send,
    z_recv,
    g_send,
    g_recv,
):
    spot = Spot()
    s, m, d = spot.s, spot.m, spot.d
    h = whole.shape[1]
    f32, b16 = jnp.float32, jnp.bfloat16
    blocks = down_terms.shape[1] // WIDE
    shared = core_in.shape[0]
    stage[...] = jnp.zeros_like(stage)
    for b in range(blocks):
        at = slice(b * WIDE, (b + 1) * WIDE)
        stage[b * 24 : b * 24 + 24] = down_terms[:, at]
        stage[96 + b * 8 : 104 + b * 8] = oup_term[:, at]
    stage[144:152] = q_term[:, :WIDE]
    stage[152:160] = q_term[:, WIDE:]
    stage[160:168] = jnp.concatenate([k_term[...], v_term[...]], 1)
    stage[168:176] = odown_term[:, :WIDE]
    stage[176:184] = odown_term[:, WIDE:]
    for i in range(2):
        stage[192 + 64 * i : 256 + 64 * i] = jnp.concatenate([dqm[i * 8 + h] for h in range(8)], 1)
    km = jnp.concatenate([dkm[h] for h in range(4)], 1)
    stage[320:352] = jnp.concatenate([km[:32], km[32:]], 1)
    gains = [jnp.sum(v[...], 0, keepdims=True) for v in (attn_rows, mlp_rows)]
    stage[128:136] = jnp.concatenate([v[:, b * WIDE : (b + 1) * WIDE] for v in gains for b in range(blocks)], 0)
    mine[...] = stage[...].astype(b16)
    bar = pltpu.get_barrier_semaphore()
    plane = [{"seq": s, "mp": m, "dp": (d + i) % 4} for i in range(1, 4)]
    lines = [{"seq": (s + i) % n, "mp": m, "dp": d} for i in range(1, n)]
    for where in plane + lines + [spot.to("c")]:
        pl.semaphore_signal(bar, inc=1, device_id=where, device_id_type=MESH)
    pl.semaphore_wait(bar, n + 3)
    core = remote(mine.at[pl.ds(0, shared)], core_in, c_send, c_recv, spot.to("c"))
    def rows(who):
        return pl.ds(pl.multiple_of(who * h, h), h)

    def scatter(i):
        return remote(mine.at[rows((d + i) % 4)], near.at[i - 1], p_send.at[i - 1], p_recv.at[i - 1], plane[i - 1])

    free = -(-shared // h)
    core.start()
    for i in (2, 1, 3):

        @pl.when((d + i) % 4 >= free)
        def _():
            scatter(i).start()

    core.wait()
    mine[:shared] = (mine[:shared].astype(f32) + core_in[...].astype(f32)).astype(b16)

    for i in (2, 1, 3):

        @pl.when((d + i) % 4 < free)
        def _():
            scatter(i).start()

    total = mine[rows(d)].astype(f32)
    for i in range(1, 4):
        scatter(i).wait_recv()
        total = total + near[i - 1].astype(f32)
    line[s] = total.astype(b16)

    def along(i, sending):
        who = s if sending else (s - i) % n
        return remote(line.at[who], line.at[who], z_send.at[i - 1], z_recv.at[i - 1], lines[i - 1])

    for i in range(1, n):
        along(i, True).start()
    for i in range(1, n):
        along(i, False).wait_recv()
    total = line[0].astype(f32)
    for i in range(1, n):
        total = total + line[i].astype(f32)
    whole[d] = total.astype(b16)

    def back(i, sending):
        who = d if sending else (d - i) % 4
        return remote(whole.at[who], whole.at[who], g_send.at[i - 1], g_recv.at[i - 1], plane[i - 1])

    for i in (2, 1, 3):
        back(i, True).start()
    for i in range(1, 4):
        back(i, False).wait_recv()
    for i in range(4):
        stage[i * h : (i + 1) * h] = whole[i].astype(f32)
    for b in range(blocks):
        at = slice(b * WIDE, (b + 1) * WIDE)
        downs_out[:, at] = stage[b * 24 : b * 24 + 24]
        oup_out[:, at] = stage[96 + b * 8 : 104 + b * 8]
    gains_out[...] = stage[128:136]
    ups_out[:, :WIDE] = stage[144:152]
    ups_out[:, WIDE : 2 * WIDE] = stage[152:160]
    ups_out[:, 2 * WIDE :] = stage[160:168]
    odown_out[:, :WIDE] = stage[168:176]
    odown_out[:, WIDE:] = stage[176:184]
    for i in range(2):
        for h2 in range(8):
            qm_out[i * 8 + h2] = stage[192 + 64 * i : 256 + 64 * i, h2 * 64 : h2 * 64 + 64]
    for h2 in range(4):
        km_out[h2, :32] = stage[320:352, h2 * 64 : h2 * 64 + 64]
        km_out[h2, 32:] = stage[320:352, 256 + h2 * 64 : 320 + h2 * 64]
    for i in range(1, 4):
        scatter(i).wait_send()
        back(i, True).wait_send()
    for i in range(1, n):
        along(i, True).wait_send()


def grad_total(n, args, cid):
    DMA, V = pltpu.SemaphoreType.DMA, pltpu.VMEM
    b, f32 = jnp.bfloat16, jnp.float32
    width, wide, kv_wide = args[0].shape[1], args[4].shape[1], args[5].shape[1]
    rows, shared = 384, 144
    h = rows // 4
    vmem = pl.BlockSpec(memory_space=pltpu.VMEM)
    shapes = [(8, WIDE), (24, width), (8, width), (8, wide + 2 * kv_wide), (8, wide), (16, 64, 64), (4, 64, 64)]
    return pl.pallas_call(
        functools.partial(grad_total_kernel, n),
        out_shape=[jax.ShapeDtypeStruct(shape, f32) for shape in shapes],
        in_specs=[vmem] * len(args),
        out_specs=[vmem] * len(shapes),
        scratch_shapes=[
            V((rows, WIDE), f32),
            V((rows, WIDE), b),
            V((shared, WIDE), b),
            V((3, h, WIDE), b),
            V((n, h, WIDE), b),
            V((4, h, WIDE), b),
            DMA,
            DMA,
            DMA((3,)),
            DMA((3,)),
            DMA((n - 1,)),
            DMA((n - 1,)),
            DMA((3,)),
            DMA((3,)),
        ],
        compiler_params=pltpu.CompilerParams(collective_id=cid, has_side_effects=True, vmem_limit_bytes=40 << 20),
        name="plane_total",
    )(*args)


SPAN, TILE = 64, 128
REACH = TILE + SPAN


def mm(left, right, contract=((1,), (0,))):
    return lax.dot_general(left, right, (contract, ((), ())), preferred_element_type=jnp.float32)


def halves(shape, value):
    r = lax.broadcasted_iota(jnp.int32, shape, 0) // 64
    c = lax.broadcasted_iota(jnp.int32, shape, 1) // 64
    return jnp.where(r == c, value, 0.0).astype(jnp.bfloat16)


def signed_map(matrix):
    return jnp.concatenate([matrix, -matrix], 1)


def maps_of(logits):
    left = lax.broadcasted_iota(jnp.int32, logits.shape, 1) < 64
    low = jnp.max(jnp.where(left, logits, -jnp.inf), -1, keepdims=True)
    high = jnp.max(jnp.where(left, -jnp.inf, logits), -1, keepdims=True)
    e = jnp.exp(logits - jnp.where(left, low, high))
    sums = mm(e.astype(jnp.bfloat16), halves((128, 128), 1.0))
    return e / sums


def maps_back(maps, dmaps):
    p = (maps * dmaps).astype(jnp.bfloat16)
    return maps * (dmaps - mm(p, halves((128, 128), 1.0)))


def with_ones(values, first):
    rows = values.shape[0]
    r = lax.broadcasted_iota(jnp.int32, (rows, 64), 0)
    c = lax.broadcasted_iota(jnp.int32, (rows, 64), 1)
    ones = jnp.where((c == 0) & (r >= first), 1.0, 0.0).astype(jnp.bfloat16)
    return jnp.concatenate([values, ones], 1)


def pick(column):
    r = lax.broadcasted_iota(jnp.int32, (8, 128), 0)
    c = lax.broadcasted_iota(jnp.int32, (8, 128), 1)
    return jnp.where((r == 0) & (c == column), 1.0, 0.0).astype(jnp.bfloat16)


def identity():
    r = lax.broadcasted_iota(jnp.int32, (128, 128), 0)
    c = lax.broadcasted_iota(jnp.int32, (128, 128), 1)
    return jnp.where(r == c, 1.0, 0.0).astype(jnp.bfloat16)


def start_row():
    return jnp.where(lax.axis_index("seq") == 0, SPAN, 0)


def key_states(kv, kmaps, near, whole):
    b16 = jnp.bfloat16
    rows = kv.shape[1]
    near[512:] = jnp.zeros((16, 128), b16)
    whole[512:] = jnp.zeros((16, 128), b16)
    for e in range(2):
        for gp in range(2):
            parts = ([], [])
            for j in range(2):
                g = 2 * gp + j
                keys = kv[e, :, g * 64 : g * 64 + 64]
                values = with_ones(kv[e, :, 256 + g * 64 : 320 + g * 64], 0)
                feats = maps_of(mm(keys, signed_map(kmaps[g]))).astype(b16)
                cut = rows - SPAN
                state = mm(feats[:cut], values[:cut], ((0,), (0,)))
                for out, part in ((near, 0), (whole, 1)):
                    if part:
                        state = state + mm(feats[cut:], values[cut:], ((0,), (0,)))
                    parts[part].append(state[:, :64])
                    total = mm(pick(64), state.astype(b16), ((1,), (1,)))
                    out[512 + e * 4 + g : 513 + e * 4 + g] = total[:1].astype(b16)
            for out, part in ((near, 0), (whole, 1)):
                block = jnp.concatenate(parts[part], 1).astype(b16)
                out[(e * 2 + gp) * 128 : (e * 2 + gp) * 128 + 128] = block


STACK = 4


def masks():
    r = lax.broadcasted_iota(jnp.int32, (STACK * TILE, REACH), 0) % TILE
    c = lax.broadcasted_iota(jnp.int32, (STACK * TILE, REACH), 1)
    return (c > r) & (c <= r + SPAN), c <= r


def stacked(ref, rows, head):
    return jnp.concatenate([ref[rows, (head + i) * 64 : (head + i) * 64 + 64] for i in range(STACK)], 0)


def beside(value):
    return jnp.concatenate([value[i * TILE : (i + 1) * TILE] for i in range(STACK)], 1)


def query_logits(queries, qmaps, head):
    return jnp.concatenate(
        [mm(queries[i * TILE : (i + 1) * TILE], signed_map(qmaps[head + i])) for i in range(STACK)], 0
    )


def state_of(states, totals, e, gp, j):
    b16 = jnp.bfloat16
    column = mm(identity(), totals[...].astype(b16), ((1,), (1,)))
    row = e * 4 + 2 * gp + j
    pickcol = lax.broadcasted_iota(jnp.int32, column.shape, 1) == row
    one = jnp.sum(jnp.where(pickcol, column, 0.0), -1, keepdims=True)
    c = lax.broadcasted_iota(jnp.int32, (128, 64), 1)
    return jnp.concatenate([states[:, j * 64 : j * 64 + 64], jnp.where(c == 0, one, 0.0)], 1)


def attend_kernel(q, k, v, st, tot, qmaps, kmaps, out, qf, inv):
    gp, e = pl.program_id(0), pl.program_id(1)
    first = start_row()
    b16 = jnp.bfloat16
    window, older = masks()
    for j in range(2):
        keys = k[0, :, j * 64 : j * 64 + 64]
        values = with_ones(v[0, :, j * 64 : j * 64 + 64], first)
        kfeats = maps_of(mm(keys, signed_map(kmaps[j]))).astype(b16)
        keys8 = keys * jnp.asarray(0.125, b16)
        state = state_of(st, tot, e, gp, j)
        for i in range(2):
            if i:
                state = state + mm(kfeats[:TILE], values[:TILE], ((0,), (0,)))
            state16 = state.astype(b16)
            reach = slice(i * TILE, i * TILE + REACH)
            rows = slice(i * TILE, (i + 1) * TILE)
            for h in range(0, 4, STACK):
                head = j * 4 + h
                query = stacked(q, rows, head)
                qfeats = maps_of(query_logits(query, qmaps, head)).astype(b16)
                near = mm(query, keys8[reach], ((1,), (1,)))
                far = mm(qfeats, kfeats[reach], ((1,), (1,)))
                weights = jnp.where(window, jnp.exp(near), jnp.where(older, far, 0.0))
                both = mm(weights.astype(b16), values[reach]) + mm(qfeats, state16)
                part = 1.0 / both[:, 64:65]
                out[rows, head * 64 : (head + STACK) * 64] = beside((both[:, :64] * part).astype(b16))
                inv[0, rows, head : head + STACK] = beside(part)
                qf[0, 0, head // STACK, i] = qfeats


STACKED = pl.BlockSpec((1, 1, 8 // STACK, 2, STACK * TILE, 128), lambda g, e: (e, g, 0, 0, 0, 0))


def attend(q, kv_ext, st, qmaps, kmaps):
    return pl.pallas_call(
        attend_kernel,
        grid=(2, 2),
        out_shape=[
            jax.ShapeDtypeStruct(q.shape, jnp.bfloat16),
            jax.ShapeDtypeStruct((2, 2, 8 // STACK, 2, STACK * TILE, 128), jnp.bfloat16),
            jax.ShapeDtypeStruct((2, 512, 8), jnp.float32),
        ],
        in_specs=[
            pl.BlockSpec((256, 512), lambda g, e: (e, g)),
            pl.BlockSpec((1, 320, 128), lambda g, e: (e, 0, g)),
            pl.BlockSpec((1, 320, 128), lambda g, e: (e, 0, 2 + g)),
            pl.BlockSpec((128, 128), lambda g, e: (e * 2 + g, 0)),
            pl.BlockSpec((16, 128), lambda g, e: (32, 0)),
            pl.BlockSpec((8, 64, 64), lambda g, e: (g, 0, 0)),
            pl.BlockSpec((2, 64, 64), lambda g, e: (g, 0, 0)),
        ],
        out_specs=[
            pl.BlockSpec((256, 512), lambda g, e: (e, g)),
            STACKED,
            pl.BlockSpec((1, 256, 8), lambda g, e: (g, e, 0)),
        ],
        compiler_params=pltpu.CompilerParams(vmem_limit_bytes=40 << 20),
        name="attend",
    )(q, kv_ext, kv_ext, st, st, qmaps, kmaps)


def state_back_kernel(attn, dres, weight, du, down, inv, qf, grad1, dst, dtot, dattn):
    b16, f32 = jnp.bfloat16, jnp.float32
    k = weight.shape[2]
    grads = mm(du[...], down[...], ((1,), (1,)))
    for i in range(weight.shape[0]):
        grads = grads + mm(dres[:, i * k : (i + 1) * k], weight[i], ((1,), (1,)))
    dattn[...] = grads.astype(b16)
    lane = lax.broadcasted_iota(jnp.int32, (STACK * TILE, 64), 1)
    states = []
    for j in range(2):
        total = None
        for h in range(0, 4, STACK):
            head = j * 4 + h
            for i in range(2):
                rows = slice(i * TILE, (i + 1) * TILE)
                part = jnp.concatenate([inv[0, rows, head + z : head + z + 1] for z in range(STACK)], 0)
                grad = stacked(dattn, rows, head).astype(f32) * part
                c = jnp.sum(grad * stacked(attn, rows, head).astype(f32), -1, keepdims=True)
                one = jnp.concatenate([grad, jnp.where(lane == 0, -c, 0.0)], 1).astype(b16)
                grad1[0, 0, head // STACK, i] = one
                g = mm(qf[0, 0, head // STACK, i], one, ((0,), (0,)))
                total = g if total is None else total + g
        states.append(total[:, :64])
        dtot[0, 0, j * 8 : j * 8 + 8] = mm(pick(64), total.astype(b16), ((1,), (1,))).astype(b16)
    dst[...] = jnp.concatenate(states, 1).astype(b16)


def state_back(attn, dres, weight, du, down, inv, qf):
    b16 = jnp.bfloat16
    n, _, k = weight.shape
    rows = pl.BlockSpec((256, 512), lambda g, e: (e, g))
    return pl.pallas_call(
        state_back_kernel,
        grid=(2, 2),
        out_shape=[
            jax.ShapeDtypeStruct(qf.shape, b16),
            jax.ShapeDtypeStruct((512, 128), b16),
            jax.ShapeDtypeStruct((2, 2, 16, 128), b16),
        ],
        in_specs=[
            rows,
            pl.BlockSpec((256, dres.shape[1]), lambda g, e: (e, 0)),
            pl.BlockSpec((n, 512, k), lambda g, e: (0, g, 0)),
            pl.BlockSpec((256, du.shape[1]), lambda g, e: (e, 0)),
            pl.BlockSpec((512, du.shape[1]), lambda g, e: (g, 0)),
            pl.BlockSpec((1, 256, 8), lambda g, e: (g, e, 0)),
            STACKED,
        ],
        scratch_shapes=[pltpu.VMEM((256, 512), b16)],
        out_specs=[
            STACKED,
            pl.BlockSpec((128, 128), lambda g, e: (e * 2 + g, 0)),
            pl.BlockSpec((1, 1, 16, 128), lambda g, e: (e, g, 0, 0)),
        ],
        compiler_params=pltpu.CompilerParams(vmem_limit_bytes=61 << 20),
        cost_estimate=pl.CostEstimate(flops=8 * 10**9, bytes_accessed=10**6, transcendentals=0),
        name="state_back",
    )(attn, dres, weight, du, down, inv, qf)


def attend_back_kernel(q, k, v, st, tot, qmaps, kmaps, qf, gr, dq, dk, dv, dkf, dqm):
    gp, e = pl.program_id(0), pl.program_id(1)
    first = start_row()
    b16, f32 = jnp.bfloat16, jnp.float32
    window, older = masks()
    eighth = jnp.asarray(0.125, b16)
    dk[...] = jnp.zeros_like(dk)
    dv[...] = jnp.zeros_like(dv)
    dkf[...] = jnp.zeros_like(dkf)

    @pl.when(e == 0)
    def _():
        dqm[...] = jnp.zeros_like(dqm)

    for j in range(2):
        keys = k[0, :, j * 64 : j * 64 + 64]
        values = with_ones(v[0, :, j * 64 : j * 64 + 64], first)
        kfeats = maps_of(mm(keys, signed_map(kmaps[j]))).astype(b16)
        keys8 = keys * eighth
        state = state_of(st, tot, e, gp, j)
        for i in range(2):
            if i:
                state = state + mm(kfeats[:TILE], values[:TILE], ((0,), (0,)))
            state16 = state.astype(b16)
            reach = slice(i * TILE, i * TILE + REACH)
            rows = slice(i * TILE, (i + 1) * TILE)
            dvalue = dkey = dkfeat = g = None
            for h in range(0, 4, STACK):
                head = j * 4 + h
                query = stacked(q, rows, head)
                grad1 = gr[0, 0, head // STACK, i]
                qfeats = qf[0, 0, head // STACK, i]
                qmap = qfeats.astype(f32)
                near = mm(query, keys8[reach], ((1,), (1,)))
                far = mm(qfeats, kfeats[reach], ((1,), (1,)))
                close = jnp.where(window, jnp.exp(near), 0.0)
                weights = (close + jnp.where(older, far, 0.0)).astype(b16)
                dweights = mm(grad1, values[reach], ((1,), (1,)))
                ds = (close * dweights).astype(b16)
                dl = jnp.where(older, dweights, 0.0).astype(b16)
                dqmap = mm(dl, kfeats[reach]) + mm(grad1, state16, ((1,), (1,)))
                da = maps_back(qmap, dqmap).astype(b16)
                dmaps = []
                for z in range(STACK):
                    part = slice(z * TILE, (z + 1) * TILE)
                    dmaps.append(mm(da[part], signed_map(qmaps[head + z]), ((1,), (1,))))
                    x = mm(query[part], da[part], ((0,), (0,)))
                    dqm[head + z] += x[:, :64] - x[:, 64:]
                dquery = mm(ds, keys8[reach]) + jnp.concatenate(dmaps, 0)
                dq[rows, head * 64 : (head + STACK) * 64] = beside(dquery.astype(b16))
                a1 = mm(weights, grad1, ((0,), (0,)))
                a2 = mm(ds, query * eighth, ((0,), (0,)))
                a3 = mm(dl, qfeats, ((0,), (0,)))
                a4 = mm(qfeats, grad1, ((0,), (0,))) if i else None
                if dvalue is None:
                    dvalue, dkey, dkfeat, g = a1, a2, a3, a4
                else:
                    dvalue, dkey, dkfeat = dvalue + a1, dkey + a2, dkfeat + a3
                    g = g + a4 if i else None
            dv[0, reach, j * 64 : j * 64 + 64] += dvalue[:, :64]
            dk[0, reach, j * 64 : j * 64 + 64] += dkey
            dkf[0, j, reach] += dkfeat
            if i:
                g16 = g.astype(b16)
                dkf[0, j, :TILE] += mm(values[:TILE], g16, ((1,), (1,)))
                dv[0, :TILE, j * 64 : j * 64 + 64] += mm(kfeats[:TILE], g16)[:, :64]


def attend_back(q, kv_ext, st, qmaps, kmaps, qf, grad1):
    f32, b16 = jnp.float32, jnp.bfloat16
    e2, ext = kv_ext.shape[:2]
    return pl.pallas_call(
        attend_back_kernel,
        grid=(2, 2),
        out_shape=[
            jax.ShapeDtypeStruct(q.shape, b16),
            jax.ShapeDtypeStruct((e2, ext, 256), f32),
            jax.ShapeDtypeStruct((e2, ext, 256), f32),
            jax.ShapeDtypeStruct((e2, 4, ext, 128), f32),
            jax.ShapeDtypeStruct((16, 64, 64), f32),
        ],
        in_specs=[
            pl.BlockSpec((256, 512), lambda g, e: (e, g)),
            pl.BlockSpec((1, 320, 128), lambda g, e: (e, 0, g)),
            pl.BlockSpec((1, 320, 128), lambda g, e: (e, 0, 2 + g)),
            pl.BlockSpec((128, 128), lambda g, e: (e * 2 + g, 0)),
            pl.BlockSpec((16, 128), lambda g, e: (32, 0)),
            pl.BlockSpec((8, 64, 64), lambda g, e: (g, 0, 0)),
            pl.BlockSpec((2, 64, 64), lambda g, e: (g, 0, 0)),
            STACKED,
            STACKED,
        ],
        out_specs=[
            pl.BlockSpec((256, 512), lambda g, e: (e, g)),
            pl.BlockSpec((1, 320, 128), lambda g, e: (e, 0, g)),
            pl.BlockSpec((1, 320, 128), lambda g, e: (e, 0, g)),
            pl.BlockSpec((1, 2, 320, 128), lambda g, e: (e, g, 0, 0)),
            pl.BlockSpec((8, 64, 64), lambda g, e: (g, 0, 0)),
        ],
        compiler_params=pltpu.CompilerParams(vmem_limit_bytes=40 << 20),
        cost_estimate=pl.CostEstimate(flops=8 * 10**9, bytes_accessed=10**7, transcendentals=4 * 10**6),
        name="attend_back",
    )(q, kv_ext, kv_ext, st, st, qmaps, kmaps, qf, grad1)


def key_back_kernel(k, v, later, tot, kmaps, dk_in, dv_in, dkf, dk, dv, dkm):
    gp, e = pl.program_id(0), pl.program_id(1)
    first = start_row()
    b16 = jnp.bfloat16

    @pl.when(e == 0)
    def _():
        dkm[...] = jnp.zeros_like(dkm)

    dks, dvs = [], []
    for j in range(2):
        cols = slice(j * 64, j * 64 + 64)
        keys = k[0, :, cols]
        values = with_ones(v[0, :, cols], first)
        signed = signed_map(kmaps[j])
        kmap = maps_of(mm(keys, signed))
        g = state_of(later, tot, e, gp, j).astype(b16)
        more = mm(values[:256], g, ((1,), (1,)))
        dmap = jnp.concatenate([dkf[0, j, :256] + more, dkf[0, j, 256:]], 0)
        da = maps_back(kmap, dmap).astype(b16)
        dks.append(dk_in[0, :, cols] + mm(da, signed, ((1,), (1,))))
        moved = mm(kmap[:256].astype(b16), g)[:, :64]
        dvs.append(jnp.concatenate([dv_in[0, :256, cols] + moved, dv_in[0, 256:, cols]], 0))
        x = mm(keys, da, ((0,), (0,)))
        dkm[j] += x[:, :64] - x[:, 64:]
    dk[0] = jnp.concatenate(dks, 1)
    dv[0] = jnp.concatenate(dvs, 1)


def key_back(kv_ext, later, kmaps, dk, dv, dkf):
    f32 = jnp.float32
    piece = pl.BlockSpec((1, 320, 128), lambda g, e: (e, 0, g))
    return pl.pallas_call(
        key_back_kernel,
        grid=(2, 2),
        out_shape=[
            jax.ShapeDtypeStruct(dk.shape, f32),
            jax.ShapeDtypeStruct(dv.shape, f32),
            jax.ShapeDtypeStruct((4, 64, 64), f32),
        ],
        in_specs=[
            piece,
            pl.BlockSpec((1, 320, 128), lambda g, e: (e, 0, 2 + g)),
            pl.BlockSpec((128, 128), lambda g, e: (e * 2 + g, 0)),
            pl.BlockSpec((16, 128), lambda g, e: (32, 0)),
            pl.BlockSpec((2, 64, 64), lambda g, e: (g, 0, 0)),
            piece,
            piece,
            pl.BlockSpec((1, 2, 320, 128), lambda g, e: (e, g, 0, 0)),
        ],
        out_specs=[piece, piece, pl.BlockSpec((2, 64, 64), lambda g, e: (g, 0, 0))],
        compiler_params=pltpu.CompilerParams(vmem_limit_bytes=40 << 20),
        name="key_back",
    )(kv_ext, kv_ext, later, later, kmaps, dk, dv, dkf)


def norm_close_kernel(part, other, tok, dres, gain, out, sums):
    f32 = jnp.float32
    i, m = pl.program_id(0), lax.axis_index("mp")
    dn = part[...].astype(f32) + other[...].astype(f32)
    x = tok[...].astype(f32)
    inv = lax.rsqrt(jnp.mean(x * x, -1, keepdims=True) + epsilon)
    xi = x * inv
    t = dn * xi
    gain_wide = gain[...].astype(f32)
    out[...] = dres[...].astype(f32) + inv * (gain_wide * dn - xi * jnp.mean(gain_wide * t, -1, keepdims=True))

    @pl.when(i == 0)
    def _():
        sums[...] = jnp.zeros_like(sums)

    @pl.when(i // (pl.num_programs(0) // 2) == m)
    def _():
        sums[...] += jnp.sum(t.reshape(t.shape[0] // 8, 8, -1), 0)


def norm_close(part, other, tok, dres, gain):
    rows, width = tok.shape
    step = 128
    piece = pl.BlockSpec((step, width), lambda i: (i, 0))
    return pl.pallas_call(
        norm_close_kernel,
        grid=(rows // step,),
        out_shape=[jax.ShapeDtypeStruct((rows, width), jnp.float32), jax.ShapeDtypeStruct((8, width), jnp.float32)],
        in_specs=[piece] * 4 + [pl.BlockSpec((1, width), lambda i: (0, 0))],
        out_specs=[piece, pl.BlockSpec((8, width), lambda i: (0, 0))],
        compiler_params=pltpu.CompilerParams(vmem_limit_bytes=40 << 20),
        name="norm_close",
    )(part, other, tok, dres, gain)


CHUNKS = 4


def feed_kernel(n, k, early, xn_own, ct_all, packed, gate, up, down, res, gain, gsum, dres16, up_go, low_go, up_keep, low_keep, *scratch):
    (xn, ct, gw, uw, dw, da, oa, xin, yin, t2, xin2, yin2) = scratch[:12]
    (o_sem, a_send, a_recv, w_sem, w_send, w_recv, z_sem, z_send, z_recv, c_send, c_recv, p_send, p_recv, st_sem, e_sem) = scratch[12:]
    spot = Spot()
    s, m, d = spot.s, spot.m, spot.d
    f32, b16 = jnp.float32, jnp.bfloat16
    unit = gw.shape[3] // 2
    wd = min(unit, k)
    gs, ds = unit // wd, k // wd
    half = xn.shape[1] // 2
    A, B = pl.ds(0, half), pl.ds(half, half)

    own = [pltpu.make_async_copy(xn_own, xn.at[3], o_sem.at[0]), pltpu.make_async_copy(ct_all, ct, o_sem.at[1])]
    for c in own:
        c.start()

    lanes = pl.ds(pl.multiple_of(m * unit, unit), unit)

    def own_piece(q):
        start = pl.multiple_of(d * (CHUNKS * unit) + q * unit, unit)
        return (
            (gate.at[:, pl.ds(start, unit)], gw.at[q, s, :, lanes]),
            (up.at[:, pl.ds(start, unit)], uw.at[q, s, :, lanes]),
            (down.at[pl.ds(start, unit)], dw.at[q, s, lanes]),
        )

    def piece(q, w, who):
        return (gw.at[q, who, :, lanes], uw.at[q, who, :, lanes], dw.at[q, who, lanes])[w]

    late = tuple(range(early, CHUNKS))
    own_weights = [
        pltpu.make_async_copy(src, dst, z_sem.at[i, w])
        for i, q in enumerate(late)
        for w, (src, dst) in enumerate(own_piece(q))
    ]
    for c in own_weights:
        c.start()

    def early_parts(q):
        parts = []
        at = 0
        for ref in (gw, uw):
            for i in range(gs):
                cols = pl.ds(pl.multiple_of(m * unit + i * wd, wd), wd)
                parts.append((packed.at[:, q, pl.ds(at, k)], ref.at[q, :, :, cols]))
                at += k
        for i in range(ds):
            parts.append((packed.at[:, q, pl.ds(at, unit)], dw.at[q, :, lanes, pl.ds(i * wd, wd)]))
            at += unit
        return parts

    early_own = [
        [pltpu.make_async_copy(src, dst, w_sem.at[q, i]) for i, (src, dst) in enumerate(early_parts(q))]
        for q in range(early)
    ]
    for copies in early_own:
        for c in copies:
            c.start()

    greet(spot, n, ("x", "y", "c", "up", "dn"))

    def block_copy(kind, sending):
        if kind < 2:
            dst = xn.at[kind + 1]
            src = xn_own if sending else dst
        else:
            rows = (A, B)[kind - 2]
            dst = xn.at[0, rows]
            src = xn.at[(2, 1)[kind - 2], rows] if sending else dst
        return remote(src, dst, a_send.at[kind], a_recv.at[kind], spot.to("xyxy"[kind]))

    block_copy(0, True).start()
    block_copy(1, True).start()

    def sends(upward, t):
        return ((s - t >= 0) & (s + 1 < n)) if upward else ((s + t < n) & (s > 0))

    def receives(upward, t):
        return s - 1 - t >= 0 if upward else s + 1 + t < n

    def z_copy(i, w, upward, t, sending):
        q = late[i]
        way = 0 if upward else 1
        who = (s - t if upward else s + t) if sending else (s - 1 - t if upward else s + 1 + t)
        dst = piece(q, w, who)
        src = own_piece(q)[w][0] if (t == 0 and sending) else dst
        return remote(src, dst, z_send.at[i, w, way, t], z_recv.at[i, w, way, t], spot.to("up" if upward else "dn"))

    for i in range(len(late)):
        for w in range(3):
            for upward in (True, False):

                @pl.when(sends(upward, 0))
                def _():
                    z_copy(i, w, upward, 0, True).start()

    def early_core(q):
        return [
            remote(src, dst, w_send.at[q, i], w_recv.at[q, i], spot.to("c")) for i, (src, dst) in enumerate(early_parts(q))
        ]

    def theirs(q, w, who):
        other = pl.ds(pl.multiple_of((1 - m) * unit, unit), unit)
        return (gw.at[q, who, :, other], uw.at[q, who, :, other], dw.at[q, who, other])[w]

    def core_copy(i, w, who, sending):
        q = late[i]
        ref = piece(q, w, who) if sending else theirs(q, w, who)
        return remote(ref, ref, c_send.at[i, w, who], c_recv.at[i, w, who], spot.to("c"))

    for q in range(early):
        for c in early_core(q):
            c.start()

    def relay(i, t, w):
        for upward in (True, False):

            @pl.when(receives(upward, t))
            def _():
                z_copy(i, w, upward, t, False).wait_recv()
                if t + 1 < n - 1:

                    @pl.when(sends(upward, t + 1))
                    def _():
                        z_copy(i, w, upward, t + 1, True).start()

                core_copy(i, w, s - 1 - t if upward else s + 1 + t, True).start()

    for i in range(len(late)):
        for w in range(3):
            own_weights[3 * i + w].wait()
            core_copy(i, w, s, True).start()

    for c in own:
        c.wait()

    first = (
        remote(xn.at[0, A], xin.at[1], p_send.at[0], p_recv.at[0], spot.to("x")),
        remote(xn.at[0, B], yin.at[1], p_send.at[1], p_recv.at[1], spot.to("y")),
        remote(xn.at[1, A], xin.at[0], p_send.at[2], p_recv.at[2], spot.to("x")),
        remote(xn.at[2, B], yin.at[0], p_send.at[3], p_recv.at[3], spot.to("y")),
    )
    places = ((up_go.at[0], low_go.at[0]), (up_go.at[1], low_keep.at[0]), (up_keep.at[0], low_go.at[1]), (up_keep.at[1], low_keep.at[1]))
    stores = [
        [pltpu.make_async_copy(ct.at[i, rows], places[i][j], st_sem.at[i, j]) for j, rows in enumerate((A, B))]
        for i in range(4)
    ]

    again = (
        pltpu.make_async_copy(res, da.at[0], e_sem.at[0]),
        pltpu.make_async_copy(ct_all.at[3], ct.at[0], e_sem.at[1]),
    )

    steps = 4 * CHUNKS
    turns = {}
    total = len(late) * (n - 1) * 3
    for j in range(total):
        i, t, w = j // (3 * n - 3), j // 3 % (n - 1), j % 3
        at = min(4 * late[i], 1 + (4 * late[i] - 1) * j // ((i + 1) * (n - 1) * 3))
        turns.setdefault(at, []).append((i, t, w))

    @pl.loop(0, steps)
    def _(step):
        last = step >= steps - 4
        c = jnp.where(step < 4 * early, step % early, step // 4)
        t = jnp.where(step < 4 * early, 3 - step // early, step % 4)

        for q in range(early):

            @pl.when(step == q)
            def _():
                for copy in early_own[q]:
                    copy.wait()
                for copy in early_core(q):
                    copy.wait_recv()

        for at, jobs in turns.items():

            @pl.when(step == at)
            def _():
                for i, t, w in jobs:
                    relay(i, t, w)

        for i, q in enumerate(late):

            @pl.when(step == 4 * q)
            def _():
                for w in range(3):
                    for who in range(n):
                        core_copy(i, w, who, False).wait_recv()

        @pl.when(step == early)
        def _():
            block_copy(1, False).wait_recv()
            block_copy(2, True).start()
            block_copy(0, False).wait_recv()
            block_copy(3, True).start()

        @pl.when(step == 3 * early)
        def _():
            for kind in (2, 3):
                block_copy(kind, False).wait_recv()
            for kind in range(4):
                block_copy(kind, True).wait_send()

        x, cot = xn[t], ct[t]
        g_all = gw[c].reshape(n * k, 2 * unit)
        u_all = uw[c].reshape(n * k, 2 * unit)
        g = mm(x, g_all)
        u = mm(x, u_all)
        dh = mm(cot[:, :k], dw[c, 0], ((1,), (1,)))
        for i in range(1, n):
            dh = dh + mm(cot[:, i * k : (i + 1) * k], dw[c, i], ((1,), (1,)))
        sig = 1.0 / (1.0 + jnp.exp(-g))
        act = g * sig
        hid = (act * u).astype(b16)
        dg = (dh * u * sig * (1.0 + g * (1.0 - sig))).astype(b16)
        du = (dh * act).astype(b16)
        for i in range(n):
            cols = slice(i * k, (i + 1) * k)
            o = mm(hid, dw[c, i])
            e = mm(dg, gw[c, i], ((1,), (1,))) + mm(du, uw[c, i], ((1,), (1,)))

            @pl.when(c == 0)
            def _():
                oa[t, :, cols] = o
                da[t, :, cols] = e

            @pl.when(c > 0)
            def _():
                oa[t, :, cols] += o
                da[t, :, cols] += e

        @pl.when(last)
        def _():
            xn[t] = da[t].astype(b16)
            ct[t] = oa[t].astype(b16)

        for i in range(4):

            @pl.when(step == steps - 4 + i)
            def _():
                for store in stores[i]:
                    store.start()
                if i == 1:
                    again[0].start()
                if i == 0:
                    first[0].start()
                    first[1].start()
                elif i < 3:
                    first[i + 1].start()

    second = (
        remote(t2.at[0], yin2, p_send.at[4], p_recv.at[4], spot.to("y")),
        remote(t2.at[1], xin2, p_send.at[5], p_recv.at[5], spot.to("x")),
    )
    for store in stores[0]:
        store.wait()
    again[1].start()
    first[0].wait_recv()
    t2[0] = (xn[2, A].astype(f32) + xin[1].astype(f32)).astype(b16)
    second[0].start()
    first[1].wait_recv()
    t2[1] = (xn[1, B].astype(f32) + yin[1].astype(f32)).astype(b16)
    second[1].start()
    for c in first:
        c.wait_send()
    for c in again:
        c.wait()
    first[2].wait_recv()
    first[3].wait_recv()
    second[0].wait_recv()
    second[1].wait_recv()
    scale = gain[...].astype(f32)
    chunk = half // 4
    gsum[...] = jnp.zeros_like(gsum)
    for part, inner, outer in ((0, xin, yin2), (1, yin, xin2)):

        @pl.loop(0, 4)
        def _(i):
            at = pl.ds(pl.multiple_of(i * chunk, chunk), chunk)
            rows = pl.ds(pl.multiple_of(part * half + i * chunk, chunk), chunk)
            dxn = da[3, rows] + inner[0, at].astype(f32) + outer[at].astype(f32)
            r = da[0, rows]
            inv = lax.rsqrt(jnp.mean(r * r, -1, keepdims=True) + epsilon)
            ri = r * inv
            gsum[...] += jnp.sum((dxn * ri).reshape(chunk // 8, 8, -1), 0)
            gx = scale * dxn
            grad = ct[0, rows].astype(f32) + inv * (gx - ri * jnp.mean(gx * ri, -1, keepdims=True))
            xn[0, rows] = grad.astype(b16)

    swap = remote(xn.at[0], dres16.at[m], e_sem.at[2], e_sem.at[3], spot.to("c"))
    keep = pltpu.make_async_copy(xn.at[0], dres16.at[m], e_sem.at[4])
    swap.start()
    keep.start()
    keep.wait()
    swap.wait_send()
    remote(xn.at[0], dres16.at[1 - m], e_sem.at[2], e_sem.at[3], spot.to("c")).wait_recv()
    for pair in stores[1:]:
        for store in pair:
            store.wait()
    for c in second:
        c.wait_send()
    for q in range(early):
        for c in early_core(q):
            c.wait_send()
    for i in range(len(late)):
        for w in range(3):
            for who in range(n):
                core_copy(i, w, who, True).wait_send()
            for t in range(n - 1):
                for upward in (True, False):

                    @pl.when(sends(upward, t))
                    def _():
                        z_copy(i, w, upward, t, True).wait_send()


def feed(n, early, xn_own, ct_all, packed, gate, up, down, res, gain, cid):
    DMA, V = pltpu.SemaphoreType.DMA, pltpu.VMEM
    b, f32 = jnp.bfloat16, jnp.float32
    r, w = xn_own.shape
    k = gate.shape[0]
    unit = gate.shape[1] // (4 * CHUNKS)
    wd = min(unit, k)
    pieces = 2 * (unit // wd) + k // wd
    late = CHUNKS - early
    scratch = [V((4, r, w), b), V((4, r, w), b)]
    scratch += [V((CHUNKS, n, k, 2 * unit), b), V((CHUNKS, n, k, 2 * unit), b), V((CHUNKS, n, 2 * unit, k), b)]
    scratch += [V((4, r, w), f32), V((4, r, w), f32)]
    scratch += [V((2, r // 2, w), b), V((2, r // 2, w), b), V((2, r // 2, w), b), V((r // 2, w), b), V((r // 2, w), b)]
    scratch += [DMA((2,)), DMA((4,)), DMA((4,))]
    scratch += [DMA((max(early, 1), pieces))] * 3
    scratch += [DMA((late, 3)), DMA((late, 3, 2, n - 1)), DMA((late, 3, 2, n - 1)), DMA((late, 3, n)), DMA((late, 3, n))]
    scratch += [DMA((6,)), DMA((6,)), DMA((4, 2)), DMA((5,))]
    return pl.pallas_call(
        functools.partial(feed_kernel, n, k, early),
        out_shape=[
            jax.ShapeDtypeStruct((8, w), f32),
            jax.ShapeDtypeStruct((2, r, w), b),
            *[jax.ShapeDtypeStruct((2, r // 2, w), b)] * 4,
        ],
        in_specs=[pl.BlockSpec(memory_space=ANY)] * 7 + [pl.BlockSpec(memory_space=pltpu.VMEM)],
        out_specs=[pl.BlockSpec(memory_space=pltpu.VMEM)] + [pl.BlockSpec(memory_space=ANY)] * 5,
        scratch_shapes=scratch,
        compiler_params=pltpu.CompilerParams(collective_id=cid, has_side_effects=True, vmem_limit_bytes=62 << 20),
        name="feed",
    )(xn_own, ct_all, packed, gate, up, down, res, gain)


def pack_early(k, early, gate, up, down, d):
    unit = gate.shape[1] // (4 * CHUNKS)
    wd = min(unit, k)
    at = d * (CHUNKS * unit)
    g = lax.dynamic_slice_in_dim(gate, at, early * unit, 1)
    u = lax.dynamic_slice_in_dim(up, at, early * unit, 1)
    dn = lax.dynamic_slice_in_dim(down, at, early * unit, 0)
    chunks = []
    for q in range(early):
        rows = [a[:, q * unit + i : q * unit + i + wd] for a in (g, u) for i in range(0, unit, wd)]
        rows += [dn[q * unit : (q + 1) * unit, i : i + wd] for i in range(0, k, wd)]
        chunks.append(jnp.concatenate(rows, 0))
    return jnp.stack(chunks)


def branch_kernel(n, attn, weight, first, second, tok, gain, res, xn, inner, part, other, send, recv):
    spot = Spot()
    m = spot.m
    f32, b16 = jnp.float32, jnp.bfloat16
    half = attn.shape[0] // 2
    k = weight.shape[2]
    greet(spot, n, ("c",))
    low = mm(attn[...], first[...])
    inner[...] = low

    def terms(who, i):
        rows = pl.ds(pl.multiple_of(who * half, half), half)
        return mm(attn[rows], weight[i]) + mm(
            inner[rows].astype(b16), second[:, i * k : (i + 1) * k]
        )

    for i in range(n):
        part[:, i * k : (i + 1) * k] = terms(1 - m, i).astype(b16)
    swap = remote(part, other, send, recv, spot.to("c"))
    swap.start()
    mine = pl.ds(pl.multiple_of(m * half, half), half)
    for i in range(n):
        cols = slice(i * k, (i + 1) * k)
        res[:, cols] = tok[mine, cols].astype(f32) + terms(m, i)
    swap.wait_recv()
    scale = gain[...].astype(f32)
    step = 64

    @pl.loop(0, half // step)
    def _(i):
        at = pl.ds(pl.multiple_of(i * step, step), step)
        r = res[at] + other[at].astype(f32)
        res[at] = r
        xn[at] = (r * lax.rsqrt(jnp.mean(r * r, -1, keepdims=True) + epsilon) * scale).astype(b16)

    swap.wait_send()


def branch(n, attn, weight, first, second, tok, gain, cid):
    DMA, V = pltpu.SemaphoreType.DMA, pltpu.VMEM
    b, f32 = jnp.bfloat16, jnp.float32
    total, width = tok.shape
    half = total // 2
    vmem = pl.BlockSpec(memory_space=pltpu.VMEM)
    return pl.pallas_call(
        functools.partial(branch_kernel, n),
        out_shape=[
            jax.ShapeDtypeStruct((half, width), f32),
            jax.ShapeDtypeStruct((half, width), b),
            jax.ShapeDtypeStruct((total, first.shape[1]), f32),
        ],
        in_specs=[vmem] * 6,
        out_specs=[vmem] * 3,
        scratch_shapes=[V((half, width), b), V((half, width), b), DMA, DMA],
        compiler_params=pltpu.CompilerParams(collective_id=cid, has_side_effects=True, vmem_limit_bytes=48 << 20),
        name="branch",
    )(attn, weight, first, second, tok, gain)


EARLY = 3


f32, b16 = jnp.float32, jnp.bfloat16


def dot(left, right):
    return jnp.dot(left, right, preferred_element_type=f32)


def dot_t(left, right):
    return lax.dot_general(left, right, (((1,), (1,)), ((), ())), preferred_element_type=f32)


def t_dot(left, right):
    return lax.dot_general(left, right, (((0,), (0,)), ((), ())), preferred_element_type=f32)


def norm_back(inputs, inv_rms, gain, dnormed):
    return inv_rms * gain * dnormed - inputs * inv_rms**3 * jnp.mean(
        gain * dnormed * inputs, -1, keepdims=True
    )


def from_behind(value, axis, steps):
    count = lax.axis_size(axis)
    first, last = (max(0, -steps), min(count, count - steps))
    return lax.ppermute(value, axis, [(source, source + steps) for source in range(first, last)])


def swap_core(value):
    return lax.ppermute(value, "mp", [(0, 1), (1, 0)])


def per_device(
    tokens,
    cotangent,
    attention_norm_gain,
    feedforward_norm_gain,
    query_weight,
    key_weight,
    value_weight,
    output_weight,
    gate_weight,
    up_weight,
    down_weight,
    query_adapter_down,
    query_adapter_up,
    key_adapter_down,
    key_adapter_up,
    value_adapter_down,
    value_adapter_up,
    output_adapter_down,
    output_adapter_up,
    query_feature_matrix,
    key_feature_matrix,
):
    n = lax.axis_size("seq")
    position, m, d = (lax.axis_index(a) for a in ("seq", "mp", "dp"))
    seq_count, rows_here, width = tokens.shape
    total_rows = seq_count * rows_here
    half = total_rows // 2
    heads_kv = key_feature_matrix.shape[0]
    head_size = key_feature_matrix.shape[1]
    groups = query_feature_matrix.shape[0] // heads_kv
    extent = rows_here + SOFTMAX_SPAN

    packed = lax.all_gather(
        pack_early(gate_weight.shape[0], EARLY, gate_weight, up_weight, down_weight, d), "seq"
    )
    def my_half(a):
        return lax.dynamic_slice_in_dim(a, m * half, half, 0)

    qkv_own = jnp.concatenate([query_weight, key_weight, value_weight], 1)
    def both_halves(own):
        other = swap_core(own)
        return jnp.concatenate([jnp.where(m == 0, own, other), jnp.where(m == 0, other, own)], 0)

    wide = query_weight.shape[1]
    kv_wide = key_weight.shape[1]
    rank = query_adapter_down.shape[1]
    tok2 = tokens.reshape(total_rows, width)
    downs = jnp.concatenate([query_adapter_down, key_adapter_down, value_adapter_down], 1)
    block_seconds = jnp.concatenate(
        [
            jnp.pad(query_adapter_up, ((0, 0), (0, 2 * kv_wide))),
            jnp.pad(key_adapter_up, ((0, 0), (wide, kv_wide))),
            jnp.pad(value_adapter_up, ((0, 0), (wide + kv_wide, 0))),
        ],
        0,
    )
    qkv_g, out_g, cot_blocks, normed, inner, query_half, kv3, states, kv_prev = opening(
        n,
        [qkv_own, output_weight],
        cotangent,
        tok2,
        attention_norm_gain.reshape(1, width),
        downs,
        block_seconds,
        key_feature_matrix,
        wide,
        1,
    )
    qkv_w = qkv_g.reshape(width, -1)
    kv_ext = jnp.concatenate([kv_prev, kv3], 1)
    attn16, qfeats, inv_weights = attend(query_half, kv_ext, states, query_feature_matrix, key_feature_matrix)
    resid, normed_mlp, inner_output = branch(
        n,
        attn16,
        out_g,
        output_adapter_down,
        output_adapter_up,
        tok2,
        feedforward_norm_gain.reshape(1, width),
        5,
    )
    mlp_gain_rows, dresid16, up_go, low_go, up_keep, low_keep = feed(
        n,
        EARLY,
        normed_mlp,
        cot_blocks,
        packed,
        gate_weight,
        up_weight,
        down_weight,
        resid,
        feedforward_norm_gain.reshape(1, width),
        4,
    )
    dresid16 = dresid16.reshape(total_rows, width)

    def swap_chip(value, bit):
        return lax.ppermute(value, "dp", [(i, i ^ bit) for i in range(4)])

    upper_in = swap_chip(up_go, 1)
    lower_in = swap_chip(low_go, 2)


    du_o = dot_t(dresid16, output_adapter_up)
    oup_term = t_dot(inner_output.astype(b16), dresid16)
    du_o16 = du_o.astype(b16)
    odown_term = t_dot(du_o16, attn16)
    grad1, dstates, dtotals = state_back(
        attn16, dresid16, out_g, du_o16, output_adapter_down, inv_weights, qfeats
    )
    dtotals = jnp.pad(dtotals[:, :, ::8].reshape(-1, 128), ((0, 8), (0, 0)))
    dstates = jnp.concatenate([dstates, dtotals], 0)
    later = [from_behind(dstates, "seq", -i) for i in range(1, n)]
    dq16, dk_ext, dv_ext, dkfeats, dqmaps = attend_back(
        query_half, kv_ext, states, query_feature_matrix, key_feature_matrix, qfeats, grad1
    )
    dq16, later, upper_in, lower_in = lax.optimization_barrier((dq16, later, upper_in, lower_in))
    upper_in2 = swap_chip((up_keep[0].astype(f32) + upper_in[0].astype(f32)).astype(b16), 2)
    lower_in2 = swap_chip((low_keep[0].astype(f32) + lower_in[0].astype(f32)).astype(b16), 1)
    later = functools.reduce(jnp.add, [a.astype(f32) for a in later])
    dk_ext, dv_ext, dkmaps = key_back(kv_ext, later, key_feature_matrix, dk_ext, dv_ext, dkfeats)
    dkv_ext = jnp.concatenate([dk_ext, dv_ext], -1)
    back = from_behind(dkv_ext[:, :SOFTMAX_SPAN].astype(b16), "seq", -1).astype(f32)
    dkv = dkv_ext[:, SOFTMAX_SPAN:]
    dkv = jnp.concatenate(
        [dkv[:, : rows_here - SOFTMAX_SPAN], dkv[:, rows_here - SOFTMAX_SPAN :] + back], 1
    )
    dqkv16 = jnp.concatenate(
        [dq16, dkv.reshape(total_rows, -1).astype(b16)], 1
    )
    bounds = ((0, wide), (wide, wide + kv_wide), (wide + kv_wide, wide + 2 * kv_wide))
    seconds = (query_adapter_up, key_adapter_up, value_adapter_up)
    dinner = jnp.concatenate(
        [dot_t(dqkv16[:, a:b], second) for (a, b), second in zip(bounds, seconds)], 1
    ).astype(b16)
    dnormed = (dot_t(dqkv16, qkv_w) + dot_t(dinner, downs)).astype(b16)
    down_terms = t_dot(dinner, normed)
    inner16 = inner.astype(b16)
    up_terms = [
        t_dot(inner16[:, i * rank : (i + 1) * rank], dqkv16[:, a:b]) for i, (a, b) in enumerate(bounds)
    ]
    dnormed, upper_in2, lower_in2 = lax.optimization_barrier((dnormed, upper_in2, lower_in2))
    mlp_out = jnp.concatenate(
        [
            up_keep[1].astype(f32) + upper_in[1].astype(f32) + upper_in2.astype(f32),
            low_keep[1].astype(f32) + lower_in[1].astype(f32) + lower_in2.astype(f32),
        ],
        0,
    )
    output = both_halves((resid + mlp_out).astype(b16)).reshape(seq_count, rows_here, width)
    tokens_grad, attn_gain_rows = norm_close(
        dnormed, swap_core(dnormed), tok2, dresid16, attention_norm_gain.reshape(1, width)
    )
    tokens_grad = tokens_grad.reshape(seq_count, rows_here, width)
    gains, downs_g, oup, ups, odown, qmaps_g, kmaps_g = grad_total(
        n,
        (down_terms, oup_term, attn_gain_rows, mlp_gain_rows, *up_terms, odown_term, dqmaps, dkmaps),
        8,
    )
    gains = gains.reshape(2, width)
    attn_gain, mlp_gain = gains[0], gains[1]
    qup, kup, vup = ups[:, :wide], ups[:, wide : wide + kv_wide], ups[:, wide + kv_wide :]
    downs_g = downs_g.T
    return (
        output,
        tokens_grad,
        attn_gain,
        mlp_gain,
        downs_g[:, :rank],
        qup,
        downs_g[:, rank : 2 * rank],
        kup,
        downs_g[:, 2 * rank :],
        vup,
        odown.T,
        oup,
        qmaps_g,
        kmaps_g,
    )


def solution(mesh):
    placed = (
        P("dp", "seq", None),
        P("dp", "seq", None),
        P(),
        P(),
        P("seq", "mp"),
        P("seq", "mp"),
        P("seq", "mp"),
        P("mp", "seq"),
        P("seq", "mp"),
        P("seq", "mp"),
        P("mp", "seq"),
        P(),
        P(None, "mp"),
        P(),
        P(None, "mp"),
        P(),
        P(None, "mp"),
        P("mp", None),
        P(),
        P("mp", None, None),
        P("mp", None, None),
    )
    return jax.shard_map(
        per_device,
        mesh=mesh,
        in_specs=placed,
        out_specs=(
            P("dp", "seq", None),
            P("dp", "seq", None),
            P(),
            P(),
            P(),
            P(None, "mp"),
            P(),
            P(None, "mp"),
            P(),
            P(None, "mp"),
            P("mp", None),
            P(),
            P("mp", None, None),
            P("mp", None, None),
        ),
        check_vma=False,
    )
```
